32 devices in a mesh: grp: 2 (over y), blk: 4 (over z), walk: 2 (over x), sub: 2 (over core).
Axes of the slice: x: 2, y: 2, z: 4, core: 2. Of those that a mesh axis runs over, the one named last changes fastest.
Arguments:
- walker_mats: bfloat16 [8, 2048, 2048], P(('grp', 'blk'), 'walk'), parts along dimension 0, may hold values from -0.0029296875 to 0.0029296875
- vertex: int32 [8, 2048], P(('grp', 'blk')), parts along dimension 0, may hold values from 0 to 8191
- weights: float32 [8], P('grp'), parts along dimension 0, may hold values from 0.5 to 1.5
- transfer_table: int32 [16, 2560], replicated, may hold values from 0 to 2559, each once within a row
- g4_old: float32 [32, 16, 2560], P(('grp', 'blk', 'walk', 'sub')), parts along dimension 0, may hold values from -2 to 2
Outputs:
- g4_new: float32 [32, 16, 2560], P(('grp', 'blk', 'walk', 'sub')), parts along dimension 0
The draws below stay inside these ranges and needn't reach their ends.
There are 2 independent parts, one for each index of `grp`. The reference program is written for one: setup_inputs(seed, part) draws one part's arguments, and reference() takes and returns one part's arrays. A program takes and returns all parts, laid end to end along the dimension named above; an argument that names none is the same for every part. Nothing has to cross between parts.
All inputs are finite; a program needn't handle non-finite values.
Results may differ from the reference program's by a relative error of at most 0.0041.
Values may be sent and summed in bfloat16 or wider, within the bound.
No kernel may reach another device: no remote copies, remote signals or barrier semaphores. Data moves between devices by JAX's collectives and lax.ppermute only.
A program may use at most 64 MiB of HBM per device.

```python
import math
import jax
import jax.numpy as jnp
from jax import lax

NV = 2048
K2 = 2560
TQ = 4
RSTEPS = 4
NW = 4
K1 = 16
NQ = 16
STRIDE = 4


def place_ends(drawn, stream_key, smallest, top_value):
    longest = drawn.shape.index(max(drawn.shape))
    spots = []
    for shift in (0, 1):
        where = [jax.random.randint(jax.random.fold_in(stream_key, axis), (), 0, length) for axis, length in enumerate(drawn.shape)]
        where[longest] = (where[longest] + shift) % drawn.shape[longest]
        spots.append(tuple(where))
    return drawn.at[spots[0]].set(smallest).at[spots[1]].set(top_value)


def block_scale(key, dims, cuts, least, high):
    level, own = 1.0, jax.random.fold_in(key, 6)
    for dim, parts in cuts:
        steps = jnp.exp(jax.random.uniform(jax.random.fold_in(own, dim), (parts,), jnp.float32, least / len(cuts), high / len(cuts)))
        level = level * jnp.repeat(steps, dims[dim] // parts).reshape([-1 if axis == dim else 1 for axis in range(len(dims))])
    return level


def noise(stream_key, dims, spread, most, cuts=(), held_as=jnp.bfloat16):
    drawn = spread * jax.random.normal(stream_key, dims, jnp.float32)
    if cuts:
        drawn = drawn * block_scale(stream_key, dims, cuts, -0.22, 0.18)
    return jnp.clip(drawn, -most, most).astype(held_as)


def setup_inputs(seed: int = 0, part: int = 0) -> dict:
    key_of = jax.random.split(jax.random.key(seed), 6)
    own_keys = jax.random.split(jax.random.fold_in(key_of[5], part), 6)
    return {
        "walker_mats": noise(own_keys[0], (NW, NV, NV), (NV * NV) ** -0.5, 0.0029296875, ((0, 4), (1, 2))),
        "vertex": place_ends(jax.random.randint(own_keys[1], (NW, NV), 0, 8192), jax.random.fold_in(own_keys[1], 1), 0, 8191).astype(jnp.int32),
        "weights": jnp.clip(jax.random.uniform(own_keys[2], (NW,), jnp.float32, 0.5, 1.5), 0.5, 1.5),
        "transfer_table": jax.vmap(lambda own: jax.random.permutation(own, K2))(jax.random.split(key_of[3], NQ)).reshape((NQ, K2)).astype(jnp.int32),
        "g4_old": noise(own_keys[4], (K1, NQ, K2), 0.3, 2.0, ((0, 16),), jnp.float32),
    }


phase_period = 8192


def cas_table(vertices, frequencies):
    residue = (vertices[:, None] * frequencies[None, :]) % phase_period
    angles = residue.astype(jnp.float32) * (2.0 * math.pi / phase_period)
    return (jnp.cos(angles) + jnp.sin(angles)).astype(jnp.bfloat16)


def reference(walker_mats, vertex, weights, transfer_table, g4_old):
    frequencies = jnp.arange(K2, dtype=jnp.int32)

    def transform_walker(walker_item):
        matrix, vertices = walker_item
        cas_rows = cas_table(vertices, frequencies)
        half_transform = jnp.dot(matrix, cas_rows, preferred_element_type=jnp.float32).astype(jnp.bfloat16)
        return jnp.dot(cas_rows[:, :K1].T, half_transform, preferred_element_type=jnp.float32).astype(jnp.bfloat16)

    greens = lax.map(transform_walker, (walker_mats, vertex))
    scaled = greens.astype(jnp.float32) * (weights / NW)[:, None, None]
    panels = []
    for cycle_step in range(RSTEPS):
        shifted = jnp.roll(greens, cycle_step * STRIDE, axis=1)
        for transfer in range(TQ):
            picked = jnp.take(shifted, transfer_table[cycle_step * TQ + transfer], axis=2).astype(jnp.float32)
            panels.append(jnp.sum(scaled * picked, axis=0))
    return g4_old + jnp.stack(panels, axis=1)
```

```python
import functools
import math

import jax
import jax.numpy as jnp
from jax import lax
from jax.experimental import pallas as pl
from jax.experimental.pallas import tpu as pltpu
from jax.sharding import PartitionSpec as P

TQ = 4
RSTEPS = 4


phase_period = 8192
quarter_bits = 11
lanes = 128
sublanes = 8


def cos_sin(product):
    residue = product & (phase_period - 1)
    quarter = (residue + phase_period // 8) >> quarter_bits
    angle = (residue - (quarter << quarter_bits)).astype(jnp.float32) * (2.0 * math.pi / phase_period)
    square = angle * angle
    sine = angle + angle * square * (
        -1.0 / 6.0 + square * (1.0 / 120.0 + square * (-1.0 / 5040.0 + square * (1.0 / 362880.0)))
    )
    cosine = 1.0 + square * (
        -0.5 + square * (1.0 / 24.0 + square * (-1.0 / 720.0 + square * (1.0 / 40320.0)))
    )
    odd = (quarter & 1) == 1
    cosine_out = jnp.where(odd, sine, cosine)
    sine_out = jnp.where(odd, cosine, sine)
    cosine_out = jnp.where(((quarter + 1) & 2) == 2, -cosine_out, cosine_out)
    sine_out = jnp.where((quarter & 2) == 2, -sine_out, sine_out)
    return cosine_out, sine_out


def row_ids(count):
    return lax.broadcasted_iota(jnp.int32, (count, lanes), 0)


def transform_kernel(
    sizes, matrix_hbm, vertex_ref, sent_ref, matrix_ref, table_ref, left_ref, weight_ref, copy_sem
):
    blk_count, walk_count, sub_count, rows_own = sizes
    walk_index = lax.axis_index("walk")
    sub_index = lax.axis_index("sub")
    rows_local, vertices = matrix_ref.shape
    columns = table_ref.shape[0]
    sent_rows = left_ref.shape[0]
    copy = pltpu.make_async_copy(matrix_hbm.at[0], matrix_ref, copy_sem)
    copy.start()

    coarse_count = columns // lanes
    coarse_rows = -(-coarse_count // sublanes) * sublanes
    middle_count = lanes // sublanes

    @pl.loop(0, vertices // lanes)
    def _(step):
        here = pl.ds(pl.multiple_of(step * lanes, lanes), lanes)
        vertex = vertex_ref[:, here]
        cos_fine, sin_fine = cos_sin(vertex * row_ids(sublanes))
        cas_fine, cam_fine = cos_fine + sin_fine, cos_fine - sin_fine
        cos_middle, sin_middle = cos_sin(vertex * (row_ids(middle_count) * sublanes))
        cos_coarse, sin_coarse = cos_sin(
            vertex * ((row_ids(coarse_rows) + sub_index * coarse_count) * lanes)
        )
        for pair in range(middle_count // 2):
            cas, cam = [], []
            for middle in (2 * pair, 2 * pair + 1):
                c, s = cos_middle[middle : middle + 1], sin_middle[middle : middle + 1]
                cas.append(c * cas_fine + s * cam_fine)
                cam.append(c * cam_fine - s * cas_fine)
            cas, cam = jnp.concatenate(cas, axis=0), jnp.concatenate(cam, axis=0)
            for coarse in range(coarse_count):
                c, s = cos_coarse[coarse : coarse + 1], sin_coarse[coarse : coarse + 1]
                start = coarse * lanes + pair * 2 * sublanes
                table_ref[start : start + 2 * sublanes, here] = (c * cas + s * cam).astype(jnp.bfloat16)

    ids = row_ids(sent_rows)
    inner = ids % rows_own
    cycle_step = ids // rows_own % RSTEPS
    destination = ids // (rows_own * RSTEPS)
    sub_part = destination % sub_count
    walk_part = destination // sub_count % walk_count
    blk_part = (destination // (sub_count * walk_count) + blk_count - cycle_step % blk_count) % blk_count
    window = ((blk_part * walk_count + walk_part) * sub_count + sub_part) * rows_own + inner

    @pl.loop(0, rows_local // lanes)
    def _(step):
        here = pl.ds(pl.multiple_of(step * lanes, lanes), lanes)
        own = pl.ds(pl.multiple_of(walk_index * rows_local + step * lanes, lanes), lanes)
        cosine, sine = cos_sin(vertex_ref[:, own] * window)
        left_ref[:, here] = (cosine + sine).astype(jnp.bfloat16)

    copy.wait()
    chunk = 4 * lanes
    for start in range(0, vertices, chunk):
        product = jnp.dot(
            left_ref[...], matrix_ref[:, start : start + chunk], preferred_element_type=jnp.float32
        )
        high = product.astype(jnp.bfloat16)
        weight_ref[:sent_rows, start : start + chunk] = high
        weight_ref[sent_rows:, start : start + chunk] = (product - high.astype(jnp.float32)).astype(
            jnp.bfloat16
        )
    green = lax.dot_general(
        table_ref[...], weight_ref[...], (((1,), (1,)), ((), ())), preferred_element_type=jnp.float32
    ).T
    green = (green[:sent_rows] + green[sent_rows:]).astype(sent_ref.dtype)
    sent_ref[...] = green.reshape(sent_ref.shape)


def accumulate_kernel(
    sizes, weights_ref, arrived_ref, transfer_ref, old_ref, new_ref, source_ref, left_ref
):
    blk_count, walk_count, sub_count, rows_own = sizes
    columns_part = arrived_ref.shape[2]
    columns = transfer_ref.shape[1]
    transfers = transfer_ref.shape[0]
    steps_group = sublanes // TQ
    groups = transfers // sublanes
    tiles = columns // lanes
    for own in range(rows_own):
        for walker in range(blk_count):
            for sub_part in range(sub_count):
                here = slice(sub_part * columns_part, (sub_part + 1) * columns_part)
                rows = sum(
                    arrived_ref[(walker * walk_count + walk_part) * sub_count + sub_part].astype(jnp.float32)
                    for walk_part in range(walk_count)
                )
                left_ref[walker, :, here] = rows[own : own + 1] * (
                    weights_ref[walker] * (1.0 / blk_count)
                )
                for group in range(groups):
                    parts = []
                    for step in range(group * steps_group, (group + 1) * steps_group):
                        row = rows[step * rows_own + own : step * rows_own + own + 1]
                        parts.append(jnp.broadcast_to(row, (TQ, columns_part)))
                    source_ref[group, walker, :, here] = jnp.concatenate(parts, axis=0)

        together = math.gcd(blk_count, 4)

        @pl.loop(0, tiles)
        def _(tile):
            here = pl.ds(pl.multiple_of(tile * lanes, lanes), lanes)
            for group in range(groups):
                rows = slice(group * sublanes, (group + 1) * sublanes)
                index = transfer_ref[rows, here]
                index_tile, index_lane = index >> 7, index & (lanes - 1)

                def add_walkers(first, total):
                    picked = [jnp.zeros((sublanes, lanes), jnp.float32)] * together
                    for source in range(tiles):
                        match = index_tile == source
                        for k in range(together):
                            values = source_ref[
                                group, first + k, :, source * lanes : (source + 1) * lanes
                            ]
                            values = jnp.take_along_axis(
                                values, index_lane, axis=1, mode="promise_in_bounds"
                            )
                            picked[k] = jnp.where(match, values, picked[k])
                    for k in range(together):
                        total = total + left_ref[first + k, :, here] * picked[k]
                    return total

                total = old_ref[own, rows, here]
                if blk_count == together:
                    total = add_walkers(0, total)
                else:
                    total = lax.fori_loop(
                        0, blk_count // together, lambda i, t: add_walkers(i * together, t), total
                    )
                new_ref[own, rows, here] = total


def local(walker_mats, vertex, weights, transfer_table, g4_old):
    blk_count = lax.axis_size("blk")
    walk_count = lax.axis_size("walk")
    sub_count = lax.axis_size("sub")
    rows_local, vertices = walker_mats.shape[1:]
    rows_own, transfers, columns = g4_old.shape
    columns_local = columns // sub_count
    devices = blk_count * walk_count * sub_count
    sizes = (blk_count, walk_count, sub_count, rows_own)
    rows_each = RSTEPS * rows_own
    sent_rows = devices * rows_each
    vmem = pl.BlockSpec(memory_space=pltpu.VMEM)
    sent = pl.pallas_call(
        functools.partial(transform_kernel, sizes),
        out_shape=jax.ShapeDtypeStruct((devices, rows_each, columns_local), jnp.bfloat16),
        in_specs=[pl.BlockSpec(memory_space=pl.ANY), vmem],
        out_specs=vmem,
        scratch_shapes=[
            pltpu.VMEM((rows_local, vertices), jnp.bfloat16),
            pltpu.VMEM((columns_local, vertices), jnp.bfloat16),
            pltpu.VMEM((sent_rows, rows_local), jnp.bfloat16),
            pltpu.VMEM((2 * sent_rows, vertices), jnp.bfloat16),
            pltpu.SemaphoreType.DMA,
        ],
        compiler_params=pltpu.CompilerParams(vmem_limit_bytes=48 * 2**20),
        name="transform",
    )(walker_mats, vertex)
    arrived = lax.all_to_all(sent, ("blk", "walk", "sub"), split_axis=0, concat_axis=0, tiled=True)
    return pl.pallas_call(
        functools.partial(accumulate_kernel, sizes),
        out_shape=jax.ShapeDtypeStruct(g4_old.shape, jnp.float32),
        in_specs=[pl.BlockSpec(memory_space=pltpu.SMEM), vmem, vmem, vmem],
        out_specs=vmem,
        scratch_shapes=[
            pltpu.VMEM((transfers // sublanes, blk_count, sublanes, columns), jnp.float32),
            pltpu.VMEM((blk_count, 1, columns), jnp.float32),
        ],
        compiler_params=pltpu.CompilerParams(vmem_limit_bytes=48 * 2**20),
        name="accumulate",
    )(weights, arrived, transfer_table, g4_old)


def solution(mesh):
    in_specs = (
        P(("grp", "blk"), "walk", None),
        P(("grp", "blk"), None),
        P("grp"),
        P(),
        P(("grp", "blk", "walk", "sub"), None, None),
    )
    out_specs = P(("grp", "blk", "walk", "sub"), None, None)
    return jax.shard_map(local, mesh=mesh, in_specs=in_specs, out_specs=out_specs, check_vma=False)
```

```python
import functools
import math

import jax
import jax.numpy as jnp
from jax import lax
from jax.experimental import pallas as pl
from jax.experimental.pallas import tpu as pltpu
from jax.sharding import PartitionSpec as P

TQ = 4
RSTEPS = 4


phase_period = 8192
quarter_bits = 11
lanes = 128
lane_bits = 7
sublanes = 8
code_limit = 32767.0
smallest_peak = 1e-30


def cos_sin(product):
    residue = product & (phase_period - 1)
    quarter = (residue + phase_period // 8) >> quarter_bits
    angle = (residue - (quarter << quarter_bits)).astype(jnp.float32) * (2.0 * math.pi / phase_period)
    square = angle * angle
    sine = angle + angle * square * (
        -1.0 / 6.0 + square * (1.0 / 120.0 + square * (-1.0 / 5040.0 + square * (1.0 / 362880.0)))
    )
    cosine = 1.0 + square * (
        -0.5 + square * (1.0 / 24.0 + square * (-1.0 / 720.0 + square * (1.0 / 40320.0)))
    )
    odd = (quarter & 1) == 1
    cosine_out = jnp.where(odd, sine, cosine)
    sine_out = jnp.where(odd, cosine, sine)
    cosine_out = jnp.where(((quarter + 1) & 2) == 2, -cosine_out, cosine_out)
    sine_out = jnp.where((quarter & 2) == 2, -sine_out, sine_out)
    return cosine_out, sine_out


def row_ids(count):
    return lax.broadcasted_iota(jnp.int32, (count, lanes), 0)


def transform_kernel(
    sizes, matrix_hbm, vertex_ref, sent_ref, matrix_ref, table_ref, left_ref, weight_ref, copy_sem
):
    blk_count, walk_count, sub_count, rows_own = sizes
    walk_index = lax.axis_index("walk")
    sub_index = lax.axis_index("sub")
    rows_local, vertices = matrix_ref.shape
    columns = table_ref.shape[0]
    sent_rows = left_ref.shape[0]
    copy = pltpu.make_async_copy(matrix_hbm.at[0], matrix_ref, copy_sem)
    copy.start()

    coarse_count = columns // lanes
    coarse_rows = -(-coarse_count // sublanes) * sublanes
    middle_count = lanes // sublanes

    @pl.loop(0, vertices // lanes)
    def _(step):
        here = pl.ds(pl.multiple_of(step * lanes, lanes), lanes)
        vertex = vertex_ref[:, here]
        cos_fine, sin_fine = cos_sin(vertex * row_ids(sublanes))
        cas_fine, cam_fine = cos_fine + sin_fine, cos_fine - sin_fine
        cos_middle, sin_middle = cos_sin(vertex * (row_ids(middle_count) * sublanes))
        cos_coarse, sin_coarse = cos_sin(
            vertex * ((row_ids(coarse_rows) + sub_index * coarse_count) * lanes)
        )
        for pair in range(middle_count // 2):
            cas, cam = [], []
            for middle in (2 * pair, 2 * pair + 1):
                c, s = cos_middle[middle : middle + 1], sin_middle[middle : middle + 1]
                cas.append(c * cas_fine + s * cam_fine)
                cam.append(c * cam_fine - s * cas_fine)
            cas, cam = jnp.concatenate(cas, axis=0), jnp.concatenate(cam, axis=0)
            for coarse in range(coarse_count):
                c, s = cos_coarse[coarse : coarse + 1], sin_coarse[coarse : coarse + 1]
                start = coarse * lanes + pair * 2 * sublanes
                table_ref[start : start + 2 * sublanes, here] = (c * cas + s * cam).astype(jnp.bfloat16)

    ids = row_ids(sent_rows)
    inner = ids % rows_own
    cycle_step = ids // rows_own % RSTEPS
    destination = ids // (rows_own * RSTEPS)
    sub_part = destination % sub_count
    walk_part = destination // sub_count % walk_count
    blk_part = (destination // (sub_count * walk_count) + blk_count - cycle_step % blk_count) % blk_count
    window = ((blk_part * walk_count + walk_part) * sub_count + sub_part) * rows_own + inner

    @pl.loop(0, rows_local // lanes)
    def _(step):
        here = pl.ds(pl.multiple_of(step * lanes, lanes), lanes)
        own = pl.ds(pl.multiple_of(walk_index * rows_local + step * lanes, lanes), lanes)
        cosine, sine = cos_sin(vertex_ref[:, own] * window)
        left_ref[:, here] = (cosine + sine).astype(jnp.bfloat16)

    copy.wait()
    chunk = 4 * lanes
    for start in range(0, vertices, chunk):
        product = jnp.dot(
            left_ref[...], matrix_ref[:, start : start + chunk], preferred_element_type=jnp.float32
        )
        high = product.astype(jnp.bfloat16)
        weight_ref[:sent_rows, start : start + chunk] = high
        weight_ref[sent_rows:, start : start + chunk] = (product - high.astype(jnp.float32)).astype(
            jnp.bfloat16
        )
    green = lax.dot_general(
        table_ref[...], weight_ref[...], (((1,), (1,)), ((), ())), preferred_element_type=jnp.float32
    ).T
    green = (green[:sent_rows] + green[sent_rows:]).astype(sent_ref.dtype)
    sent_ref[...] = green.reshape(sent_ref.shape)


def accumulate_kernel(
    sizes, weights_ref, arrived_ref, transfer_ref, old_ref, new_ref, source_ref, left_ref, unit_ref
):
    blk_count, walk_count, sub_count, rows_own = sizes
    columns_part = arrived_ref.shape[2]
    columns = transfer_ref.shape[1]
    transfers = transfer_ref.shape[0]
    steps_group = sublanes // TQ
    groups = transfers // sublanes
    tiles = columns // lanes
    pairs = blk_count // 2

    def spread(rows, own, group):
        parts = []
        for step in range(group * steps_group, (group + 1) * steps_group):
            row = rows[step * rows_own + own : step * rows_own + own + 1]
            parts.append(jnp.broadcast_to(row, (TQ, row.shape[1])))
        return jnp.concatenate(parts, axis=0)

    for own in range(rows_own):
        for pair in range(pairs):
            codes = []
            for walker in (2 * pair, 2 * pair + 1):
                rows = jnp.concatenate(
                    [
                        sum(
                            arrived_ref[(walker * walk_count + walk_part) * sub_count + sub_part].astype(
                                jnp.float32
                            )
                            for walk_part in range(walk_count)
                        )
                        for sub_part in range(sub_count)
                    ],
                    axis=1,
                )
                left_ref[walker] = rows[own : own + 1] * (weights_ref[walker] * (1.0 / blk_count))
                peak = jnp.maximum(jnp.max(jnp.abs(rows), axis=1, keepdims=True), smallest_peak)
                codes.append(jnp.floor(rows * (code_limit / peak) + 0.5).astype(jnp.int32))
                peak = jnp.broadcast_to(peak * (1.0 / code_limit), (peak.shape[0], lanes))
                for group in range(groups):
                    unit_ref[walker, group] = spread(peak, own, group)
            packed = (codes[0] << 16) | (codes[1] & 0xFFFF)
            for group in range(groups):
                source_ref[pair, group] = spread(packed, own, group)

        together = math.gcd(pairs, 2)

        @pl.loop(0, tiles)
        def _(tile):
            here = pl.ds(pl.multiple_of(tile * lanes, lanes), lanes)
            for group in range(groups):
                rows = slice(group * sublanes, (group + 1) * sublanes)
                index = transfer_ref[rows, here]
                index_tile, index_lane = index >> lane_bits, index & (lanes - 1)

                def add_pairs(first, total):
                    picked = [jnp.zeros((sublanes, lanes), jnp.int32)] * together
                    for source in range(tiles):
                        match = index_tile == source
                        for k in range(together):
                            words = source_ref[
                                first + k, group, :, source * lanes : (source + 1) * lanes
                            ]
                            words = jnp.take_along_axis(
                                words, index_lane, axis=1, mode="promise_in_bounds"
                            )
                            picked[k] = jnp.where(match, words, picked[k])
                    for k in range(together):
                        for half, code in enumerate((picked[k] >> 16, (picked[k] << 16) >> 16)):
                            walker = (first + k) * 2 + half
                            total = total + left_ref[walker, :, here] * (
                                unit_ref[walker, group] * code.astype(jnp.float32)
                            )
                    return total

                total = old_ref[own, rows, here]
                if pairs == together:
                    total = add_pairs(0, total)
                else:
                    total = lax.fori_loop(
                        0, pairs // together, lambda i, t: add_pairs(i * together, t), total
                    )
                new_ref[own, rows, here] = total


def local(walker_mats, vertex, weights, transfer_table, g4_old):
    blk_count = lax.axis_size("blk")
    walk_count = lax.axis_size("walk")
    sub_count = lax.axis_size("sub")
    rows_local, vertices = walker_mats.shape[1:]
    rows_own, transfers, columns = g4_old.shape
    columns_local = columns // sub_count
    devices = blk_count * walk_count * sub_count
    sizes = (blk_count, walk_count, sub_count, rows_own)
    rows_each = RSTEPS * rows_own
    sent_rows = devices * rows_each
    vmem = pl.BlockSpec(memory_space=pltpu.VMEM)
    sent = pl.pallas_call(
        functools.partial(transform_kernel, sizes),
        out_shape=jax.ShapeDtypeStruct((devices, rows_each, columns_local), jnp.bfloat16),
        in_specs=[pl.BlockSpec(memory_space=pl.ANY), vmem],
        out_specs=vmem,
        scratch_shapes=[
            pltpu.VMEM((rows_local, vertices), jnp.bfloat16),
            pltpu.VMEM((columns_local, vertices), jnp.bfloat16),
            pltpu.VMEM((sent_rows, rows_local), jnp.bfloat16),
            pltpu.VMEM((2 * sent_rows, vertices), jnp.bfloat16),
            pltpu.SemaphoreType.DMA,
        ],
        compiler_params=pltpu.CompilerParams(vmem_limit_bytes=121 * 2**19),
        name="transform",
    )(walker_mats, vertex)
    arrived = lax.all_to_all(sent, ("blk", "walk", "sub"), split_axis=0, concat_axis=0, tiled=True)
    return pl.pallas_call(
        functools.partial(accumulate_kernel, sizes),
        out_shape=jax.ShapeDtypeStruct(g4_old.shape, jnp.float32),
        in_specs=[pl.BlockSpec(memory_space=pltpu.SMEM), vmem, vmem, vmem],
        out_specs=vmem,
        scratch_shapes=[
            pltpu.VMEM((blk_count // 2, transfers // sublanes, sublanes, columns), jnp.int32),
            pltpu.VMEM((blk_count, 1, columns), jnp.float32),
            pltpu.VMEM((blk_count, transfers // sublanes, sublanes, lanes), jnp.float32),
        ],
        compiler_params=pltpu.CompilerParams(vmem_limit_bytes=48 * 2**20),
        name="accumulate",
    )(weights, arrived, transfer_table, g4_old)


def solution(mesh):
    in_specs = (
        P(("grp", "blk"), "walk", None),
        P(("grp", "blk"), None),
        P("grp"),
        P(),
        P(("grp", "blk", "walk", "sub"), None, None),
    )
    out_specs = P(("grp", "blk", "walk", "sub"), None, None)
    return jax.shard_map(local, mesh=mesh, in_specs=in_specs, out_specs=out_specs, check_vma=False)
```

```python
import functools
import math

import jax
import jax.numpy as jnp
from jax import lax
from jax.experimental import pallas as pl
from jax.experimental.pallas import tpu as pltpu
from jax.sharding import PartitionSpec as P

TQ = 4
RSTEPS = 4


phase_period = 8192
quarter_bits = 11
lanes = 128
lane_bits = 7
sublanes = 8
code_limit = 32767.0
smallest_peak = 1e-30


def cos_sin(product):
    residue = product & (phase_period - 1)
    quarter = (residue + phase_period // 8) >> quarter_bits
    angle = (residue - (quarter << quarter_bits)).astype(jnp.float32) * (2.0 * math.pi / phase_period)
    square = angle * angle
    sine = angle + angle * square * (
        -1.0 / 6.0 + square * (1.0 / 120.0 + square * (-1.0 / 5040.0 + square * (1.0 / 362880.0)))
    )
    cosine = 1.0 + square * (
        -0.5 + square * (1.0 / 24.0 + square * (-1.0 / 720.0 + square * (1.0 / 40320.0)))
    )
    odd = (quarter & 1) == 1
    cosine_out = jnp.where(odd, sine, cosine)
    sine_out = jnp.where(odd, cosine, sine)
    cosine_out = jnp.where(((quarter + 1) & 2) == 2, -cosine_out, cosine_out)
    sine_out = jnp.where((quarter & 2) == 2, -sine_out, sine_out)
    return cosine_out, sine_out


def row_ids(count):
    return lax.broadcasted_iota(jnp.int32, (count, lanes), 0)


def transform_kernel(
    sizes,
    matrix_hbm,
    vertex_hbm,
    sent_ref,
    matrix_ref,
    vertex_ref,
    left_ref,
    table_even,
    table_odd,
    weight_even,
    weight_odd,
    total_ref,
    matrix_sems,
    vertex_sem,
):
    blk_count, walk_count, sub_count, rows_own = sizes
    walk_index = lax.axis_index("walk")
    sub_index = lax.axis_index("sub")
    chunks, rows_local, chunk = matrix_ref.shape
    columns = table_even.shape[0]
    sent_rows = left_ref.shape[0]
    window_rows = blk_count * walk_count * sub_count * rows_own

    def matrix_copy(step):
        start = pl.multiple_of(step * chunk, chunk)
        return pltpu.make_async_copy(
            matrix_hbm.at[0, :, pl.ds(start, chunk)], matrix_ref.at[step], matrix_sems.at[step]
        )

    vertex_copy = pltpu.make_async_copy(vertex_hbm, vertex_ref, vertex_sem)
    vertex_copy.start()
    for step in range(chunks):
        matrix_copy(step).start()

    ids = lax.broadcasted_iota(jnp.int32, (sent_rows, window_rows), 0)
    inner = ids % rows_own
    cycle_step = ids // rows_own % RSTEPS
    destination = ids // (rows_own * RSTEPS)
    sub_part = destination % sub_count
    walk_part = destination // sub_count % walk_count
    blk_part = (destination // (sub_count * walk_count) + blk_count - cycle_step % blk_count) % blk_count
    window = ((blk_part * walk_count + walk_part) * sub_count + sub_part) * rows_own + inner
    repeat = jnp.where(
        window == lax.broadcasted_iota(jnp.int32, window.shape, 1), 1.0, 0.0
    ).astype(jnp.bfloat16)
    total_ref[...] = jnp.zeros_like(total_ref)
    table_odd[...] = jnp.zeros_like(table_odd)
    weight_odd[...] = jnp.zeros_like(weight_odd)

    vertex_copy.wait()
    own_start = pl.multiple_of(walk_index * rows_local, lanes)
    own_vertex = vertex_ref[:, pl.ds(own_start, rows_local)]
    cosine, sine = cos_sin(
        own_vertex * lax.broadcasted_iota(jnp.int32, (window_rows, rows_local), 0)
    )
    left_ref[...] = jnp.dot(
        repeat, (cosine + sine).astype(jnp.bfloat16), preferred_element_type=jnp.float32
    ).astype(jnp.bfloat16)

    blocks = columns // lanes
    half_blocks = blocks // 2
    coarse_rows = -(-max(half_blocks, 1) // sublanes) * sublanes
    middle_count = lanes // sublanes
    center = sub_index * columns + (blocks - 1) * (lanes // 2)

    def make_table(table_ref, step):
        for part in range(chunk // lanes):
            vertex = vertex_ref[:, pl.ds(pl.multiple_of(step * chunk + part * lanes, lanes), lanes)]
            here = slice(part * lanes, (part + 1) * lanes)
            cos_fine, sin_fine = cos_sin(vertex * (row_ids(sublanes) + center))
            cas_fine, cam_fine = cos_fine + sin_fine, cos_fine - sin_fine
            cos_middle, sin_middle = cos_sin(vertex * (row_ids(middle_count) * sublanes))
            cos_coarse, sin_coarse = cos_sin(
                vertex * ((blocks - 1 - 2 * row_ids(coarse_rows)) * (lanes // 2))
            )
            for pair in range(middle_count // 2):
                cas, cam = [], []
                for middle in (2 * pair, 2 * pair + 1):
                    c, s = cos_middle[middle : middle + 1], sin_middle[middle : middle + 1]
                    cas.append(c * cas_fine + s * cam_fine)
                    cam.append(c * cam_fine - s * cas_fine)
                cas, cam = jnp.concatenate(cas, axis=0), jnp.concatenate(cam, axis=0)
                start = pair * 2 * sublanes
                for low in range(half_blocks):
                    high = blocks - 1 - low
                    even = cos_coarse[low : low + 1] * cas
                    odd = sin_coarse[low : low + 1] * cam
                    for block, value in ((low, even - odd), (high, even + odd)):
                        first = block * lanes + start
                        table_ref[first : first + 2 * sublanes, here] = value.astype(jnp.bfloat16)
                if blocks % 2:
                    first = half_blocks * lanes + start
                    table_ref[first : first + 2 * sublanes, here] = cas.astype(jnp.bfloat16)

    def product(table_ref, weight_ref):
        return lax.dot_general(
            table_ref[...], weight_ref[...], (((1,), (1,)), ((), ())), preferred_element_type=jnp.float32
        )

    def advance(step, table_ref, weight_ref, table_before, weight_before):
        matrix_copy(step).wait()
        total_ref[...] += product(table_before, weight_before)
        left_product = jnp.dot(left_ref[...], matrix_ref[step], preferred_element_type=jnp.float32)
        high = left_product.astype(jnp.bfloat16)
        weight_ref[:sent_rows] = high
        weight_ref[sent_rows:] = (left_product - high.astype(jnp.float32)).astype(jnp.bfloat16)
        make_table(table_ref, step)

    @pl.loop(0, chunks // 2)
    def _(pair):
        advance(2 * pair, table_even, weight_even, table_odd, weight_odd)
        advance(2 * pair + 1, table_odd, weight_odd, table_even, weight_even)

    green = (total_ref[...] + product(table_odd, weight_odd)).T
    green = (green[:sent_rows] + green[sent_rows:]).astype(sent_ref.dtype)
    sent_ref[...] = green.reshape(sent_ref.shape)


def accumulate_kernel(
    sizes, weights_ref, arrived_ref, transfer_ref, old_ref, new_ref, source_ref, left_ref, unit_ref
):
    blk_count, walk_count, sub_count, rows_own = sizes
    columns_part = arrived_ref.shape[2]
    columns = transfer_ref.shape[1]
    transfers = transfer_ref.shape[0]
    steps_group = sublanes // TQ
    groups = transfers // sublanes
    tiles = columns // lanes
    pairs = blk_count // 2

    def spread(rows, own, group):
        parts = []
        for step in range(group * steps_group, (group + 1) * steps_group):
            row = rows[step * rows_own + own : step * rows_own + own + 1]
            parts.append(jnp.broadcast_to(row, (TQ, row.shape[1])))
        return jnp.concatenate(parts, axis=0)

    for own in range(rows_own):
        for pair in range(pairs):
            codes = []
            for walker in (2 * pair, 2 * pair + 1):
                rows = jnp.concatenate(
                    [
                        sum(
                            arrived_ref[(walker * walk_count + walk_part) * sub_count + sub_part].astype(
                                jnp.float32
                            )
                            for walk_part in range(walk_count)
                        )
                        for sub_part in range(sub_count)
                    ],
                    axis=1,
                )
                left_ref[walker] = rows[own : own + 1] * (weights_ref[:, walker : walker + 1] * (1.0 / blk_count))
                peak = jnp.maximum(jnp.max(jnp.abs(rows), axis=1, keepdims=True), smallest_peak)
                codes.append(jnp.floor(rows * (code_limit / peak) + 0.5).astype(jnp.int32))
                peak = jnp.broadcast_to(peak * (1.0 / code_limit), (peak.shape[0], lanes))
                for group in range(groups):
                    unit_ref[walker, group] = spread(peak, own, group)
            packed = (codes[0] << 16) | (codes[1] & 0xFFFF)
            for group in range(groups):
                source_ref[pair, group] = spread(packed, own, group)

        together = math.gcd(pairs, 2)

        @pl.loop(0, tiles)
        def _(tile):
            here = pl.ds(pl.multiple_of(tile * lanes, lanes), lanes)
            for group in range(groups):
                rows = slice(group * sublanes, (group + 1) * sublanes)
                index = transfer_ref[rows, here]
                index_tile, index_lane = index >> lane_bits, index & (lanes - 1)

                def add_pairs(first, total):
                    picked = [jnp.zeros((sublanes, lanes), jnp.int32)] * together
                    for source in range(tiles):
                        match = index_tile == source
                        for k in range(together):
                            words = source_ref[
                                first + k, group, :, source * lanes : (source + 1) * lanes
                            ]
                            words = jnp.take_along_axis(
                                words, index_lane, axis=1, mode="promise_in_bounds"
                            )
                            picked[k] = jnp.where(match, words, picked[k])
                    for k in range(together):
                        for half, code in enumerate((picked[k] >> 16, (picked[k] << 16) >> 16)):
                            walker = (first + k) * 2 + half
                            total = total + left_ref[walker, :, here] * (
                                unit_ref[walker, group] * code.astype(jnp.float32)
                            )
                    return total

                total = old_ref[own, rows, here]
                if pairs == together:
                    total = add_pairs(0, total)
                else:
                    total = lax.fori_loop(
                        0, pairs // together, lambda i, t: add_pairs(i * together, t), total
                    )
                new_ref[own, rows, here] = total


def local(walker_mats, vertex, weights, transfer_table, g4_old):
    blk_count = lax.axis_size("blk")
    walk_count = lax.axis_size("walk")
    sub_count = lax.axis_size("sub")
    rows_local, vertices = walker_mats.shape[1:]
    rows_own, transfers, columns = g4_old.shape
    columns_local = columns // sub_count
    devices = blk_count * walk_count * sub_count
    sizes = (blk_count, walk_count, sub_count, rows_own)
    rows_each = RSTEPS * rows_own
    chunk = 2 * lanes
    sent_rows = devices * rows_each
    vmem = pl.BlockSpec(memory_space=pltpu.VMEM)
    sent = pl.pallas_call(
        functools.partial(transform_kernel, sizes),
        out_shape=jax.ShapeDtypeStruct((devices, rows_each, columns_local), jnp.bfloat16),
        in_specs=[pl.BlockSpec(memory_space=pl.ANY)] * 2,
        out_specs=vmem,
        scratch_shapes=[
            pltpu.VMEM((vertices // chunk, rows_local, chunk), jnp.bfloat16),
            pltpu.VMEM((1, vertices), jnp.int32),
            pltpu.VMEM((sent_rows, rows_local), jnp.bfloat16),
            pltpu.VMEM((columns_local, chunk), jnp.bfloat16),
            pltpu.VMEM((columns_local, chunk), jnp.bfloat16),
            pltpu.VMEM((2 * sent_rows, chunk), jnp.bfloat16),
            pltpu.VMEM((2 * sent_rows, chunk), jnp.bfloat16),
            pltpu.VMEM((columns_local, 2 * sent_rows), jnp.float32),
            pltpu.SemaphoreType.DMA((vertices // chunk,)),
            pltpu.SemaphoreType.DMA,
        ],
        compiler_params=pltpu.CompilerParams(vmem_limit_bytes=121 * 2**19),
        name="transform",
    )(walker_mats, vertex)
    arrived = lax.all_to_all(sent, ("blk", "walk", "sub"), split_axis=0, concat_axis=0, tiled=True)
    return pl.pallas_call(
        functools.partial(accumulate_kernel, sizes),
        out_shape=jax.ShapeDtypeStruct(g4_old.shape, jnp.float32),
        in_specs=[vmem] * 4,
        out_specs=vmem,
        scratch_shapes=[
            pltpu.VMEM((blk_count // 2, transfers // sublanes, sublanes, columns), jnp.int32),
            pltpu.VMEM((blk_count, 1, columns), jnp.float32),
            pltpu.VMEM((blk_count, transfers // sublanes, sublanes, lanes), jnp.float32),
        ],
        compiler_params=pltpu.CompilerParams(vmem_limit_bytes=48 * 2**20),
        name="accumulate",
    )(weights[None], arrived, transfer_table, g4_old)


def solution(mesh):
    in_specs = (
        P(("grp", "blk"), "walk", None),
        P(("grp", "blk"), None),
        P("grp"),
        P(),
        P(("grp", "blk", "walk", "sub"), None, None),
    )
    out_specs = P(("grp", "blk", "walk", "sub"), None, None)
    return jax.shard_map(local, mesh=mesh, in_specs=in_specs, out_specs=out_specs, check_vma=False)
```

```python
import functools
import math

import jax
import jax.numpy as jnp
from jax import lax
from jax.experimental import pallas as pl
from jax.experimental.pallas import tpu as pltpu
from jax.sharding import PartitionSpec as P

TQ = 4
RSTEPS = 4


phase_period = 8192
quarter_bits = 11
lanes = 128
lane_bits = 7
sublanes = 8
code_limit = 32767.0
smallest_peak = 1e-30


def cos_sin(product):
    residue = product & (phase_period - 1)
    quarter = (residue + phase_period // 8) >> quarter_bits
    angle = (residue - (quarter << quarter_bits)).astype(jnp.float32) * (2.0 * math.pi / phase_period)
    square = angle * angle
    sine = angle + angle * square * (
        -1.0 / 6.0 + square * (1.0 / 120.0 + square * (-1.0 / 5040.0 + square * (1.0 / 362880.0)))
    )
    cosine = 1.0 + square * (
        -0.5 + square * (1.0 / 24.0 + square * (-1.0 / 720.0 + square * (1.0 / 40320.0)))
    )
    odd = (quarter & 1) == 1
    cosine_out = jnp.where(odd, sine, cosine)
    sine_out = jnp.where(odd, cosine, sine)
    cosine_out = jnp.where(((quarter + 1) & 2) == 2, -cosine_out, cosine_out)
    sine_out = jnp.where((quarter & 2) == 2, -sine_out, sine_out)
    return cosine_out, sine_out


def row_ids(count):
    return lax.broadcasted_iota(jnp.int32, (count, lanes), 0)


def split_by(ids, size):
    if size & (size - 1) == 0:
        return ids >> (size.bit_length() - 1), ids & (size - 1)
    return ids // size, ids % size


def transform_kernel(
    sizes,
    matrix_hbm,
    vertex_hbm,
    sent_ref,
    matrix_ref,
    vertex_ref,
    left_ref,
    table_ref,
    weight_ref,
    matrix_sem,
    vertex_sem,
):
    blk_count, walk_count, sub_count, rows_own = sizes
    walk_index = lax.axis_index("walk")
    sub_index = lax.axis_index("sub")
    rows_local, vertices = matrix_ref.shape
    columns = table_ref.shape[0]
    sent_rows = left_ref.shape[0]
    window_rows = blk_count * walk_count * sub_count * rows_own

    vertex_copy = pltpu.make_async_copy(vertex_hbm, vertex_ref, vertex_sem)
    vertex_copy.start()
    matrix_copy = pltpu.make_async_copy(matrix_hbm.at[0], matrix_ref, matrix_sem)
    matrix_copy.start()

    ids = lax.broadcasted_iota(jnp.int32, (sent_rows, window_rows), 0)
    ids, inner = split_by(ids, rows_own)
    ids, cycle_step = split_by(ids, RSTEPS)
    ids, sub_part = split_by(ids, sub_count)
    ids, walk_part = split_by(ids, walk_count)
    _, blk_part = split_by(ids + RSTEPS * blk_count - cycle_step, blk_count)
    window = ((blk_part * walk_count + walk_part) * sub_count + sub_part) * rows_own + inner
    repeat = jnp.where(
        window == lax.broadcasted_iota(jnp.int32, window.shape, 1), 1.0, 0.0
    ).astype(jnp.bfloat16)

    vertex_copy.wait()
    own_start = pl.multiple_of(walk_index * rows_local, lanes)
    own_vertex = vertex_ref[:, pl.ds(own_start, rows_local)]
    cosine, sine = cos_sin(
        own_vertex * lax.broadcasted_iota(jnp.int32, (window_rows, rows_local), 0)
    )
    left_ref[...] = jnp.dot(
        repeat, (cosine + sine).astype(jnp.bfloat16), preferred_element_type=jnp.float32
    ).astype(jnp.bfloat16)

    blocks = columns // lanes
    half_blocks = blocks // 2
    coarse_rows = -(-max(half_blocks, 1) // sublanes) * sublanes
    middle_count = lanes // sublanes
    center = sub_index * columns + (blocks - 1) * (lanes // 2)

    @pl.loop(0, vertices // lanes)
    def _(step):
        here = pl.ds(pl.multiple_of(step * lanes, lanes), lanes)
        vertex = vertex_ref[:, here]
        cos_fine, sin_fine = cos_sin(vertex * (row_ids(sublanes) + center))
        cas_fine, cam_fine = cos_fine + sin_fine, cos_fine - sin_fine
        cos_middle, sin_middle = cos_sin(vertex * (row_ids(middle_count) * sublanes))
        cos_coarse, sin_coarse = cos_sin(
            vertex * ((blocks - 1 - 2 * row_ids(coarse_rows)) * (lanes // 2))
        )
        for pair in range(middle_count // 2):
            cas, cam = [], []
            for middle in (2 * pair, 2 * pair + 1):
                c, s = cos_middle[middle : middle + 1], sin_middle[middle : middle + 1]
                cas.append(c * cas_fine + s * cam_fine)
                cam.append(c * cam_fine - s * cas_fine)
            cas, cam = jnp.concatenate(cas, axis=0), jnp.concatenate(cam, axis=0)
            start = pair * 2 * sublanes
            for low in range(half_blocks):
                high = blocks - 1 - low
                even = cos_coarse[low : low + 1] * cas
                odd = sin_coarse[low : low + 1] * cam
                for block, value in ((low, even - odd), (high, even + odd)):
                    first = block * lanes + start
                    table_ref[first : first + 2 * sublanes, here] = value.astype(jnp.bfloat16)
            if blocks % 2:
                first = half_blocks * lanes + start
                table_ref[first : first + 2 * sublanes, here] = cas.astype(jnp.bfloat16)

    matrix_copy.wait()
    chunk = 4 * lanes
    for start in range(0, vertices, chunk):
        left_product = jnp.dot(
            left_ref[...], matrix_ref[:, start : start + chunk], preferred_element_type=jnp.float32
        )
        high = left_product.astype(jnp.bfloat16)
        weight_ref[:sent_rows, start : start + chunk] = high
        weight_ref[sent_rows:, start : start + chunk] = (
            left_product - high.astype(jnp.float32)
        ).astype(jnp.bfloat16)
    green = lax.dot_general(
        table_ref[...], weight_ref[...], (((1,), (1,)), ((), ())), preferred_element_type=jnp.float32
    ).T
    green = (green[:sent_rows] + green[sent_rows:]).astype(sent_ref.dtype)
    sent_ref[...] = green.reshape(sent_ref.shape)


def accumulate_kernel(
    sizes, weights_ref, arrived_ref, transfer_ref, old_ref, new_ref, source_ref, left_ref, unit_ref
):
    blk_count, walk_count, sub_count, rows_own = sizes
    columns_part = arrived_ref.shape[2]
    columns = transfer_ref.shape[1]
    transfers = transfer_ref.shape[0]
    steps_group = sublanes // TQ
    groups = transfers // sublanes
    tiles = columns // lanes
    pairs = blk_count // 2

    def spread(rows, own, group):
        parts = []
        for step in range(group * steps_group, (group + 1) * steps_group):
            row = rows[step * rows_own + own : step * rows_own + own + 1]
            parts.append(jnp.broadcast_to(row, (TQ, row.shape[1])))
        return jnp.concatenate(parts, axis=0)

    for own in range(rows_own):
        for pair in range(pairs):
            codes = []
            for walker in (2 * pair, 2 * pair + 1):
                rows = jnp.concatenate(
                    [
                        sum(
                            arrived_ref[(walker * walk_count + walk_part) * sub_count + sub_part].astype(
                                jnp.float32
                            )
                            for walk_part in range(walk_count)
                        )
                        for sub_part in range(sub_count)
                    ],
                    axis=1,
                )
                left_ref[walker] = rows[own : own + 1] * (weights_ref[:, walker : walker + 1] * (1.0 / blk_count))
                peak = jnp.maximum(jnp.max(jnp.abs(rows), axis=1, keepdims=True), smallest_peak)
                codes.append(jnp.floor(rows * (code_limit / peak) + 0.5).astype(jnp.int32))
                peak = jnp.broadcast_to(peak * (1.0 / code_limit), (peak.shape[0], lanes))
                for group in range(groups):
                    unit_ref[walker, group] = spread(peak, own, group)
            packed = (codes[0] << 16) | (codes[1] & 0xFFFF)
            for group in range(groups):
                source_ref[pair, group] = spread(packed, own, group)

        together = math.gcd(pairs, 2)

        @pl.loop(0, tiles)
        def _(tile):
            here = pl.ds(pl.multiple_of(tile * lanes, lanes), lanes)
            for group in range(groups):
                rows = slice(group * sublanes, (group + 1) * sublanes)
                index = transfer_ref[rows, here]
                index_tile, index_lane = index >> lane_bits, index & (lanes - 1)

                def add_pairs(first, total):
                    picked = [jnp.zeros((sublanes, lanes), jnp.int32)] * together
                    for source in range(tiles):
                        match = index_tile == source
                        for k in range(together):
                            words = source_ref[
                                first + k, group, :, source * lanes : (source + 1) * lanes
                            ]
                            words = jnp.take_along_axis(
                                words, index_lane, axis=1, mode="promise_in_bounds"
                            )
                            picked[k] = jnp.where(match, words, picked[k])
                    for k in range(together):
                        for half, code in enumerate((picked[k] >> 16, (picked[k] << 16) >> 16)):
                            walker = (first + k) * 2 + half
                            total = total + left_ref[walker, :, here] * (
                                unit_ref[walker, group] * code.astype(jnp.float32)
                            )
                    return total

                total = old_ref[own, rows, here]
                if pairs == together:
                    total = add_pairs(0, total)
                else:
                    total = lax.fori_loop(
                        0, pairs // together, lambda i, t: add_pairs(i * together, t), total
                    )
                new_ref[own, rows, here] = total


def local(walker_mats, vertex, weights, transfer_table, g4_old):
    blk_count = lax.axis_size("blk")
    walk_count = lax.axis_size("walk")
    sub_count = lax.axis_size("sub")
    rows_local, vertices = walker_mats.shape[1:]
    rows_own, transfers, columns = g4_old.shape
    columns_local = columns // sub_count
    devices = blk_count * walk_count * sub_count
    sizes = (blk_count, walk_count, sub_count, rows_own)
    rows_each = RSTEPS * rows_own
    sent_rows = devices * rows_each
    vmem = pl.BlockSpec(memory_space=pltpu.VMEM)
    sent = pl.pallas_call(
        functools.partial(transform_kernel, sizes),
        out_shape=jax.ShapeDtypeStruct((devices, rows_each, columns_local), jnp.bfloat16),
        in_specs=[pl.BlockSpec(memory_space=pl.ANY)] * 2,
        out_specs=vmem,
        scratch_shapes=[
            pltpu.VMEM((rows_local, vertices), jnp.bfloat16),
            pltpu.VMEM((1, vertices), jnp.int32),
            pltpu.VMEM((sent_rows, rows_local), jnp.bfloat16),
            pltpu.VMEM((columns_local, vertices), jnp.bfloat16),
            pltpu.VMEM((2 * sent_rows, vertices), jnp.bfloat16),
            pltpu.SemaphoreType.DMA,
            pltpu.SemaphoreType.DMA,
        ],
        compiler_params=pltpu.CompilerParams(vmem_limit_bytes=121 * 2**19),
        name="transform",
    )(walker_mats, vertex)
    arrived = lax.all_to_all(sent, ("blk", "walk", "sub"), split_axis=0, concat_axis=0, tiled=True)
    return pl.pallas_call(
        functools.partial(accumulate_kernel, sizes),
        out_shape=jax.ShapeDtypeStruct(g4_old.shape, jnp.float32),
        in_specs=[vmem] * 4,
        out_specs=vmem,
        scratch_shapes=[
            pltpu.VMEM((blk_count // 2, transfers // sublanes, sublanes, columns), jnp.int32),
            pltpu.VMEM((blk_count, 1, columns), jnp.float32),
            pltpu.VMEM((blk_count, transfers // sublanes, sublanes, lanes), jnp.float32),
        ],
        compiler_params=pltpu.CompilerParams(vmem_limit_bytes=48 * 2**20),
        name="accumulate",
    )(weights[None], arrived, transfer_table, g4_old)


def solution(mesh):
    in_specs = (
        P(("grp", "blk"), "walk", None),
        P(("grp", "blk"), None),
        P("grp"),
        P(),
        P(("grp", "blk", "walk", "sub"), None, None),
    )
    out_specs = P(("grp", "blk", "walk", "sub"), None, None)
    return jax.shard_map(local, mesh=mesh, in_specs=in_specs, out_specs=out_specs, check_vma=False)
```

```python
import functools
import math

import jax
import jax.numpy as jnp
from jax import lax
from jax.experimental import pallas as pl
from jax.experimental.pallas import tpu as pltpu
from jax.sharding import PartitionSpec as P

TQ = 4
RSTEPS = 4


phase_period = 8192
quarter_bits = 11
lanes = 128
lane_bits = 7
sublanes = 8
code_limit = 32767.0
smallest_peak = 1e-30


def cos_sin(product):
    residue = product & (phase_period - 1)
    quarter = (residue + phase_period // 8) >> quarter_bits
    angle = (residue - (quarter << quarter_bits)).astype(jnp.float32) * (2.0 * math.pi / phase_period)
    square = angle * angle
    sine = angle + angle * square * (
        -1.0 / 6.0 + square * (1.0 / 120.0 + square * (-1.0 / 5040.0 + square * (1.0 / 362880.0)))
    )
    cosine = 1.0 + square * (
        -0.5 + square * (1.0 / 24.0 + square * (-1.0 / 720.0 + square * (1.0 / 40320.0)))
    )
    odd = (quarter & 1) == 1
    cosine_out = jnp.where(odd, sine, cosine)
    sine_out = jnp.where(odd, cosine, sine)
    cosine_out = jnp.where(((quarter + 1) & 2) == 2, -cosine_out, cosine_out)
    sine_out = jnp.where((quarter & 2) == 2, -sine_out, sine_out)
    return cosine_out, sine_out


def row_ids(count):
    return lax.broadcasted_iota(jnp.int32, (count, lanes), 0)


def split_by(ids, size):
    if size & (size - 1) == 0:
        return ids >> (size.bit_length() - 1), ids & (size - 1)
    return ids // size, ids % size


def transform_kernel(
    sizes,
    matrix_hbm,
    vertex_hbm,
    sent_ref,
    matrix_ref,
    vertex_ref,
    left_ref,
    table_ref,
    weight_ref,
    matrix_sem,
    vertex_sem,
):
    blk_count, walk_count, sub_count, rows_own = sizes
    walk_index = lax.axis_index("walk")
    sub_index = lax.axis_index("sub")
    rows_local, vertices = matrix_ref.shape
    columns = table_ref.shape[0]
    sent_rows = left_ref.shape[0]
    window_rows = blk_count * walk_count * sub_count * rows_own

    vertex_copy = pltpu.make_async_copy(vertex_hbm, vertex_ref, vertex_sem)
    vertex_copy.start()
    matrix_copy = pltpu.make_async_copy(matrix_hbm.at[0], matrix_ref, matrix_sem)
    matrix_copy.start()

    ids = lax.broadcasted_iota(jnp.int32, (sent_rows, window_rows), 0)
    ids, inner = split_by(ids, rows_own)
    ids, cycle_step = split_by(ids, RSTEPS)
    ids, sub_part = split_by(ids, sub_count)
    ids, walk_part = split_by(ids, walk_count)
    _, blk_part = split_by(ids + RSTEPS * blk_count - cycle_step, blk_count)
    window = ((blk_part * walk_count + walk_part) * sub_count + sub_part) * rows_own + inner
    repeat = jnp.where(
        window == lax.broadcasted_iota(jnp.int32, window.shape, 1), 1.0, 0.0
    ).astype(jnp.bfloat16)

    vertex_copy.wait()
    own_start = pl.multiple_of(walk_index * rows_local, lanes)
    own_vertex = vertex_ref[:, pl.ds(own_start, rows_local)]
    cosine, sine = cos_sin(
        own_vertex * lax.broadcasted_iota(jnp.int32, (window_rows, rows_local), 0)
    )
    left_ref[...] = jnp.dot(
        repeat, (cosine + sine).astype(jnp.bfloat16), preferred_element_type=jnp.float32
    ).astype(jnp.bfloat16)

    blocks = columns // lanes
    half_blocks = blocks // 2
    coarse_rows = -(-max(half_blocks, 1) // sublanes) * sublanes
    middle_count = lanes // sublanes
    center = sub_index * columns + (blocks - 1) * (lanes // 2)

    @pl.loop(0, vertices // lanes)
    def _(step):
        here = pl.ds(pl.multiple_of(step * lanes, lanes), lanes)
        vertex = vertex_ref[:, here]
        cos_fine, sin_fine = cos_sin(vertex * (row_ids(sublanes) + center))
        cas_fine, cam_fine = cos_fine + sin_fine, cos_fine - sin_fine
        cos_middle, sin_middle = cos_sin(vertex * (row_ids(middle_count) * sublanes))
        cos_coarse, sin_coarse = cos_sin(
            vertex * ((blocks - 1 - 2 * row_ids(coarse_rows)) * (lanes // 2))
        )
        for pair in range(middle_count // 2):
            cas, cam = [], []
            for middle in (2 * pair, 2 * pair + 1):
                c, s = cos_middle[middle : middle + 1], sin_middle[middle : middle + 1]
                cas.append(c * cas_fine + s * cam_fine)
                cam.append(c * cam_fine - s * cas_fine)
            cas, cam = jnp.concatenate(cas, axis=0), jnp.concatenate(cam, axis=0)
            start = pair * 2 * sublanes
            for low in range(half_blocks):
                high = blocks - 1 - low
                even = cos_coarse[low : low + 1] * cas
                odd = sin_coarse[low : low + 1] * cam
                for block, value in ((low, even - odd), (high, even + odd)):
                    first = block * lanes + start
                    table_ref[first : first + 2 * sublanes, here] = value.astype(jnp.bfloat16)
            if blocks % 2:
                first = half_blocks * lanes + start
                table_ref[first : first + 2 * sublanes, here] = cas.astype(jnp.bfloat16)

    matrix_copy.wait()
    chunk = 4 * lanes
    for start in range(0, vertices, chunk):
        left_product = jnp.dot(
            left_ref[...], matrix_ref[:, start : start + chunk], preferred_element_type=jnp.float32
        )
        high = left_product.astype(jnp.bfloat16)
        weight_ref[:sent_rows, start : start + chunk] = high
        weight_ref[sent_rows:, start : start + chunk] = (
            left_product - high.astype(jnp.float32)
        ).astype(jnp.bfloat16)
    green = lax.dot_general(
        weight_ref[...], table_ref[...], (((1,), (1,)), ((), ())), preferred_element_type=jnp.float32
    )
    green = (green[:sent_rows] + green[sent_rows:]).astype(sent_ref.dtype)
    sent_ref[...] = green.reshape(sent_ref.shape)


def accumulate_kernel(
    sizes, weights_ref, arrived_ref, transfer_ref, old_ref, new_ref, source_ref, left_ref, unit_ref
):
    blk_count, walk_count, sub_count, rows_own = sizes
    columns_part = arrived_ref.shape[2]
    columns = transfer_ref.shape[1]
    transfers = transfer_ref.shape[0]
    steps_group = sublanes // TQ
    groups = transfers // sublanes
    tiles = columns // lanes
    pairs = blk_count // 2

    def spread(rows, own, group):
        parts = []
        for step in range(group * steps_group, (group + 1) * steps_group):
            row = rows[step * rows_own + own : step * rows_own + own + 1]
            parts.append(jnp.broadcast_to(row, (TQ, row.shape[1])))
        return jnp.concatenate(parts, axis=0)

    for own in range(rows_own):
        for pair in range(pairs):
            codes = []
            for walker in (2 * pair, 2 * pair + 1):
                rows = jnp.concatenate(
                    [
                        sum(
                            arrived_ref[(walker * walk_count + walk_part) * sub_count + sub_part].astype(
                                jnp.float32
                            )
                            for walk_part in range(walk_count)
                        )
                        for sub_part in range(sub_count)
                    ],
                    axis=1,
                )
                left_ref[walker] = rows[own : own + 1] * (weights_ref[:, walker : walker + 1] * (1.0 / blk_count))
                peak = jnp.maximum(jnp.max(jnp.abs(rows), axis=1, keepdims=True), smallest_peak)
                codes.append(jnp.floor(rows * (code_limit / peak) + 0.5).astype(jnp.int32))
                peak = jnp.broadcast_to(peak * (1.0 / code_limit), (peak.shape[0], lanes))
                for group in range(groups):
                    unit_ref[walker, group] = spread(peak, own, group)
            packed = (codes[0] << 16) | (codes[1] & 0xFFFF)
            for group in range(groups):
                source_ref[pair, group] = spread(packed, own, group)

        together = math.gcd(pairs, 2)

        @pl.loop(0, tiles)
        def _(tile):
            here = pl.ds(pl.multiple_of(tile * lanes, lanes), lanes)
            for group in range(groups):
                rows = slice(group * sublanes, (group + 1) * sublanes)
                index = transfer_ref[rows, here]
                index_tile, index_lane = index >> lane_bits, index & (lanes - 1)

                def add_pairs(first, total):
                    picked = [jnp.zeros((sublanes, lanes), jnp.int32)] * together
                    for source in range(tiles):
                        match = index_tile == source
                        for k in range(together):
                            words = source_ref[
                                first + k, group, :, source * lanes : (source + 1) * lanes
                            ]
                            words = jnp.take_along_axis(
                                words, index_lane, axis=1, mode="promise_in_bounds"
                            )
                            picked[k] = jnp.where(match, words, picked[k])
                    for k in range(together):
                        for half, code in enumerate((picked[k] >> 16, (picked[k] << 16) >> 16)):
                            walker = (first + k) * 2 + half
                            total = total + left_ref[walker, :, here] * (
                                unit_ref[walker, group] * code.astype(jnp.float32)
                            )
                    return total

                total = old_ref[own, rows, here]
                if pairs == together:
                    total = add_pairs(0, total)
                else:
                    total = lax.fori_loop(
                        0, pairs // together, lambda i, t: add_pairs(i * together, t), total
                    )
                new_ref[own, rows, here] = total


def local(walker_mats, vertex, weights, transfer_table, g4_old):
    blk_count = lax.axis_size("blk")
    walk_count = lax.axis_size("walk")
    sub_count = lax.axis_size("sub")
    rows_local, vertices = walker_mats.shape[1:]
    rows_own, transfers, columns = g4_old.shape
    columns_local = columns // sub_count
    devices = blk_count * walk_count * sub_count
    sizes = (blk_count, walk_count, sub_count, rows_own)
    rows_each = RSTEPS * rows_own
    sent_rows = devices * rows_each
    vmem = pl.BlockSpec(memory_space=pltpu.VMEM)
    sent = pl.pallas_call(
        functools.partial(transform_kernel, sizes),
        out_shape=jax.ShapeDtypeStruct((devices, rows_each, columns_local), jnp.bfloat16),
        in_specs=[pl.BlockSpec(memory_space=pl.ANY)] * 2,
        out_specs=vmem,
        scratch_shapes=[
            pltpu.VMEM((rows_local, vertices), jnp.bfloat16),
            pltpu.VMEM((1, vertices), jnp.int32),
            pltpu.VMEM((sent_rows, rows_local), jnp.bfloat16),
            pltpu.VMEM((columns_local, vertices), jnp.bfloat16),
            pltpu.VMEM((2 * sent_rows, vertices), jnp.bfloat16),
            pltpu.SemaphoreType.DMA,
            pltpu.SemaphoreType.DMA,
        ],
        compiler_params=pltpu.CompilerParams(vmem_limit_bytes=121 * 2**19),
        name="transform",
    )(walker_mats, vertex)
    arrived = lax.all_to_all(sent, ("blk", "walk", "sub"), split_axis=0, concat_axis=0, tiled=True)
    return pl.pallas_call(
        functools.partial(accumulate_kernel, sizes),
        out_shape=jax.ShapeDtypeStruct(g4_old.shape, jnp.float32),
        in_specs=[vmem] * 4,
        out_specs=vmem,
        scratch_shapes=[
            pltpu.VMEM((blk_count // 2, transfers // sublanes, sublanes, columns), jnp.int32),
            pltpu.VMEM((blk_count, 1, columns), jnp.float32),
            pltpu.VMEM((blk_count, transfers // sublanes, sublanes, lanes), jnp.float32),
        ],
        compiler_params=pltpu.CompilerParams(vmem_limit_bytes=48 * 2**20),
        name="accumulate",
    )(weights[None], arrived, transfer_table, g4_old)


def solution(mesh):
    in_specs = (
        P(("grp", "blk"), "walk", None),
        P(("grp", "blk"), None),
        P("grp"),
        P(),
        P(("grp", "blk", "walk", "sub"), None, None),
    )
    out_specs = P(("grp", "blk", "walk", "sub"), None, None)
    return jax.shard_map(local, mesh=mesh, in_specs=in_specs, out_specs=out_specs, check_vma=False)
```

```python
import functools
import math

import jax
import jax.numpy as jnp
from jax import lax
from jax.experimental import pallas as pl
from jax.experimental.pallas import tpu as pltpu
from jax.sharding import PartitionSpec as P

TQ = 4
RSTEPS = 4


phase_period = 8192
quarter_bits = 11
lanes = 128
lane_bits = 7
sublanes = 8
code_limit = 32767.0
smallest_peak = 1e-30


def cos_sin(product):
    residue = product & (phase_period - 1)
    quarter = (residue + phase_period // 8) >> quarter_bits
    angle = (residue - (quarter << quarter_bits)).astype(jnp.float32) * (2.0 * math.pi / phase_period)
    square = angle * angle
    sine = angle + angle * square * (
        -1.0 / 6.0 + square * (1.0 / 120.0 + square * (-1.0 / 5040.0 + square * (1.0 / 362880.0)))
    )
    cosine = 1.0 + square * (
        -0.5 + square * (1.0 / 24.0 + square * (-1.0 / 720.0 + square * (1.0 / 40320.0)))
    )
    odd = (quarter & 1) == 1
    cosine_out = jnp.where(odd, sine, cosine)
    sine_out = jnp.where(odd, cosine, sine)
    cosine_out = jnp.where(((quarter + 1) & 2) == 2, -cosine_out, cosine_out)
    sine_out = jnp.where((quarter & 2) == 2, -sine_out, sine_out)
    return cosine_out, sine_out


def row_ids(count):
    return lax.broadcasted_iota(jnp.int32, (count, lanes), 0)


def split_by(ids, size):
    if size & (size - 1) == 0:
        return ids >> (size.bit_length() - 1), ids & (size - 1)
    return ids // size, ids % size


def transform_kernel(
    sizes,
    matrix_hbm,
    vertex_hbm,
    sent_ref,
    matrix_ref,
    vertex_ref,
    left_ref,
    table_ref,
    weight_ref,
    fine_ref,
    middle_ref,
    coarse_ref,
    matrix_sem,
    vertex_sem,
):
    blk_count, walk_count, sub_count, rows_own = sizes
    walk_index = lax.axis_index("walk")
    sub_index = lax.axis_index("sub")
    rows_local, vertices = matrix_ref.shape
    columns = table_ref.shape[0]
    sent_rows = left_ref.shape[0]
    window_rows = blk_count * walk_count * sub_count * rows_own

    vertex_copy = pltpu.make_async_copy(vertex_hbm, vertex_ref, vertex_sem)
    vertex_copy.start()
    matrix_copy = pltpu.make_async_copy(matrix_hbm.at[0], matrix_ref, matrix_sem)
    matrix_copy.start()

    ids = lax.broadcasted_iota(jnp.int32, (sent_rows, window_rows), 0)
    ids, inner = split_by(ids, rows_own)
    ids, cycle_step = split_by(ids, RSTEPS)
    ids, sub_part = split_by(ids, sub_count)
    ids, walk_part = split_by(ids, walk_count)
    _, blk_part = split_by(ids + RSTEPS * blk_count - cycle_step, blk_count)
    window = ((blk_part * walk_count + walk_part) * sub_count + sub_part) * rows_own + inner
    repeat = jnp.where(
        window == lax.broadcasted_iota(jnp.int32, window.shape, 1), 1.0, 0.0
    ).astype(jnp.bfloat16)

    vertex_copy.wait()
    own_start = pl.multiple_of(walk_index * rows_local, lanes)
    own_vertex = vertex_ref[:, pl.ds(own_start, rows_local)]
    cosine, sine = cos_sin(
        own_vertex * lax.broadcasted_iota(jnp.int32, (window_rows, rows_local), 0)
    )
    left_ref[...] = jnp.dot(
        repeat, (cosine + sine).astype(jnp.bfloat16), preferred_element_type=jnp.float32
    ).astype(jnp.bfloat16)

    blocks = columns // lanes
    half_blocks = blocks // 2
    coarse_rows = coarse_ref.shape[1]
    middle_count = lanes // sublanes
    center = sub_index * columns + (blocks - 1) * (lanes // 2)

    def wide_rows(count):
        return lax.broadcasted_iota(jnp.int32, (count, vertices), 0)

    vertex = vertex_ref[...]
    cosine, sine = cos_sin(vertex * (wide_rows(sublanes) + center))
    fine_ref[0], fine_ref[1] = cosine + sine, cosine - sine
    middle_ref[0], middle_ref[1] = cos_sin(vertex * (wide_rows(middle_count) * sublanes))
    coarse_ref[0], coarse_ref[1] = cos_sin(
        vertex * ((blocks - 1 - 2 * wide_rows(coarse_rows)) * (lanes // 2))
    )

    @pl.loop(0, vertices // lanes, unroll=2)
    def _(step):
        here = pl.ds(pl.multiple_of(step * lanes, lanes), lanes)
        cas_fine, cam_fine = fine_ref[0, :, here], fine_ref[1, :, here]
        cos_middle, sin_middle = middle_ref[0, :, here], middle_ref[1, :, here]
        cos_coarse, sin_coarse = coarse_ref[0, :, here], coarse_ref[1, :, here]
        for pair in range(middle_count // 2):
            cas, cam = [], []
            for middle in (2 * pair, 2 * pair + 1):
                c, s = cos_middle[middle : middle + 1], sin_middle[middle : middle + 1]
                cas.append(c * cas_fine + s * cam_fine)
                cam.append(c * cam_fine - s * cas_fine)
            cas, cam = jnp.concatenate(cas, axis=0), jnp.concatenate(cam, axis=0)
            start = pair * 2 * sublanes
            for low in range(half_blocks):
                high = blocks - 1 - low
                even = cos_coarse[low : low + 1] * cas
                odd = sin_coarse[low : low + 1] * cam
                for block, value in ((low, even - odd), (high, even + odd)):
                    first = block * lanes + start
                    table_ref[first : first + 2 * sublanes, here] = value.astype(jnp.bfloat16)
            if blocks % 2:
                first = half_blocks * lanes + start
                table_ref[first : first + 2 * sublanes, here] = cas.astype(jnp.bfloat16)

    matrix_copy.wait()
    chunk = 4 * lanes
    for start in range(0, vertices, chunk):
        left_product = jnp.dot(
            left_ref[...], matrix_ref[:, start : start + chunk], preferred_element_type=jnp.float32
        )
        high = left_product.astype(jnp.bfloat16)
        weight_ref[:sent_rows, start : start + chunk] = high
        weight_ref[sent_rows:, start : start + chunk] = (
            left_product - high.astype(jnp.float32)
        ).astype(jnp.bfloat16)
    green = lax.dot_general(
        table_ref[...], weight_ref[...], (((1,), (1,)), ((), ())), preferred_element_type=jnp.float32
    ).T
    green = (green[:sent_rows] + green[sent_rows:]).astype(sent_ref.dtype)
    sent_ref[...] = green.reshape(sent_ref.shape)


def accumulate_kernel(
    sizes, weights_ref, arrived_ref, transfer_ref, old_ref, new_ref, source_ref, left_ref, unit_ref
):
    blk_count, walk_count, sub_count, rows_own = sizes
    columns_part = arrived_ref.shape[2]
    columns = transfer_ref.shape[1]
    transfers = transfer_ref.shape[0]
    steps_group = sublanes // TQ
    groups = transfers // sublanes
    tiles = columns // lanes
    pairs = blk_count // 2

    def spread(rows, own, group):
        parts = []
        for step in range(group * steps_group, (group + 1) * steps_group):
            row = rows[step * rows_own + own : step * rows_own + own + 1]
            parts.append(jnp.broadcast_to(row, (TQ, row.shape[1])))
        return jnp.concatenate(parts, axis=0)

    for own in range(rows_own):
        for pair in range(pairs):
            codes = []
            for walker in (2 * pair, 2 * pair + 1):
                rows = jnp.concatenate(
                    [
                        sum(
                            arrived_ref[(walker * walk_count + walk_part) * sub_count + sub_part].astype(
                                jnp.float32
                            )
                            for walk_part in range(walk_count)
                        )
                        for sub_part in range(sub_count)
                    ],
                    axis=1,
                )
                left_ref[walker] = rows[own : own + 1] * (weights_ref[:, walker : walker + 1] * (1.0 / blk_count))
                peak = jnp.maximum(jnp.max(jnp.abs(rows), axis=1, keepdims=True), smallest_peak)
                codes.append(jnp.floor(rows * (code_limit / peak) + 0.5).astype(jnp.int32))
                peak = jnp.broadcast_to(peak * (1.0 / code_limit), (peak.shape[0], lanes))
                for group in range(groups):
                    unit_ref[walker, group] = spread(peak, own, group)
            packed = (codes[0] << 16) | (codes[1] & 0xFFFF)
            for group in range(groups):
                source_ref[pair, group] = spread(packed, own, group)

        together = math.gcd(pairs, 2)

        @pl.loop(0, tiles, unroll=math.gcd(tiles, 4))
        def _(tile):
            here = pl.ds(pl.multiple_of(tile * lanes, lanes), lanes)
            for group in range(groups):
                rows = slice(group * sublanes, (group + 1) * sublanes)
                index = transfer_ref[rows, here]
                index_tile, index_lane = index >> lane_bits, index & (lanes - 1)

                def add_pairs(first, total):
                    picked = [jnp.zeros((sublanes, lanes), jnp.int32)] * together
                    for source in range(tiles):
                        match = index_tile == source
                        for k in range(together):
                            words = source_ref[
                                first + k, group, :, source * lanes : (source + 1) * lanes
                            ]
                            words = jnp.take_along_axis(
                                words, index_lane, axis=1, mode="promise_in_bounds"
                            )
                            picked[k] = jnp.where(match, words, picked[k])
                    for k in range(together):
                        for half, code in enumerate((picked[k] >> 16, (picked[k] << 16) >> 16)):
                            walker = (first + k) * 2 + half
                            total = total + left_ref[walker, :, here] * (
                                unit_ref[walker, group] * code.astype(jnp.float32)
                            )
                    return total

                total = old_ref[own, rows, here]
                if pairs == together:
                    total = add_pairs(0, total)
                else:
                    total = lax.fori_loop(
                        0, pairs // together, lambda i, t: add_pairs(i * together, t), total
                    )
                new_ref[own, rows, here] = total


def local(walker_mats, vertex, weights, transfer_table, g4_old):
    blk_count = lax.axis_size("blk")
    walk_count = lax.axis_size("walk")
    sub_count = lax.axis_size("sub")
    rows_local, vertices = walker_mats.shape[1:]
    rows_own, transfers, columns = g4_old.shape
    columns_local = columns // sub_count
    devices = blk_count * walk_count * sub_count
    sizes = (blk_count, walk_count, sub_count, rows_own)
    rows_each = RSTEPS * rows_own
    coarse_rows = -(-max(columns_local // (2 * lanes), 1) // sublanes) * sublanes
    sent_rows = devices * rows_each
    vmem = pl.BlockSpec(memory_space=pltpu.VMEM)
    sent = pl.pallas_call(
        functools.partial(transform_kernel, sizes),
        out_shape=jax.ShapeDtypeStruct((devices, rows_each, columns_local), jnp.bfloat16),
        in_specs=[pl.BlockSpec(memory_space=pl.ANY)] * 2,
        out_specs=vmem,
        scratch_shapes=[
            pltpu.VMEM((rows_local, vertices), jnp.bfloat16),
            pltpu.VMEM((1, vertices), jnp.int32),
            pltpu.VMEM((sent_rows, rows_local), jnp.bfloat16),
            pltpu.VMEM((columns_local, vertices), jnp.bfloat16),
            pltpu.VMEM((2 * sent_rows, vertices), jnp.bfloat16),
            pltpu.VMEM((2, sublanes, vertices), jnp.float32),
            pltpu.VMEM((2, lanes // sublanes, vertices), jnp.float32),
            pltpu.VMEM((2, coarse_rows, vertices), jnp.float32),
            pltpu.SemaphoreType.DMA,
            pltpu.SemaphoreType.DMA,
        ],
        compiler_params=pltpu.CompilerParams(vmem_limit_bytes=121 * 2**19),
        name="transform",
    )(walker_mats, vertex)
    arrived = lax.all_to_all(sent, ("blk", "walk", "sub"), split_axis=0, concat_axis=0, tiled=True)
    return pl.pallas_call(
        functools.partial(accumulate_kernel, sizes),
        out_shape=jax.ShapeDtypeStruct(g4_old.shape, jnp.float32),
        in_specs=[vmem] * 4,
        out_specs=vmem,
        scratch_shapes=[
            pltpu.VMEM((blk_count // 2, transfers // sublanes, sublanes, columns), jnp.int32),
            pltpu.VMEM((blk_count, 1, columns), jnp.float32),
            pltpu.VMEM((blk_count, transfers // sublanes, sublanes, lanes), jnp.float32),
        ],
        compiler_params=pltpu.CompilerParams(vmem_limit_bytes=48 * 2**20),
        name="accumulate",
    )(weights[None], arrived, transfer_table, g4_old)


def solution(mesh):
    in_specs = (
        P(("grp", "blk"), "walk", None),
        P(("grp", "blk"), None),
        P("grp"),
        P(),
        P(("grp", "blk", "walk", "sub"), None, None),
    )
    out_specs = P(("grp", "blk", "walk", "sub"), None, None)
    return jax.shard_map(local, mesh=mesh, in_specs=in_specs, out_specs=out_specs, check_vma=False)
```

```python
import functools
import math

import jax
import jax.numpy as jnp
from jax import lax
from jax.experimental import pallas as pl
from jax.experimental.pallas import tpu as pltpu
from jax.sharding import PartitionSpec as P

TQ = 4
RSTEPS = 4


phase_period = 8192
quarter_bits = 11
lanes = 128
lane_bits = 7
sublanes = 8
copies = 8
code_limit = 32767.0
smallest_peak = 1e-30


def cos_sin(product):
    residue = product & (phase_period - 1)
    quarter = (residue + phase_period // 8) >> quarter_bits
    angle = (residue - (quarter << quarter_bits)).astype(jnp.float32) * (2.0 * math.pi / phase_period)
    square = angle * angle
    sine = angle + angle * square * (
        -1.0 / 6.0 + square * (1.0 / 120.0 + square * (-1.0 / 5040.0 + square * (1.0 / 362880.0)))
    )
    cosine = 1.0 + square * (
        -0.5 + square * (1.0 / 24.0 + square * (-1.0 / 720.0 + square * (1.0 / 40320.0)))
    )
    odd = (quarter & 1) == 1
    cosine_out = jnp.where(odd, sine, cosine)
    sine_out = jnp.where(odd, cosine, sine)
    cosine_out = jnp.where(((quarter + 1) & 2) == 2, -cosine_out, cosine_out)
    sine_out = jnp.where((quarter & 2) == 2, -sine_out, sine_out)
    return cosine_out, sine_out


def row_ids(count):
    return lax.broadcasted_iota(jnp.int32, (count, lanes), 0)


def split_by(ids, size):
    if size & (size - 1) == 0:
        return ids >> (size.bit_length() - 1), ids & (size - 1)
    return ids // size, ids % size


def transform_kernel(
    sizes,
    matrix_hbm,
    vertex_hbm,
    sent_ref,
    matrix_ref,
    vertex_ref,
    left_ref,
    table_ref,
    weight_ref,
    matrix_sem,
    vertex_sem,
):
    blk_count, walk_count, sub_count, rows_own = sizes
    walk_index = lax.axis_index("walk")
    sub_index = lax.axis_index("sub")
    rows_local, vertices = matrix_ref.shape
    columns = table_ref.shape[0]
    sent_rows = left_ref.shape[0]
    window_rows = blk_count * walk_count * sub_count * rows_own

    vertex_copy = pltpu.make_async_copy(vertex_hbm, vertex_ref, vertex_sem)
    vertex_copy.start()
    part = rows_local // copies
    matrix_copies = [
        pltpu.make_async_copy(
            matrix_hbm.at[0, i * part : (i + 1) * part],
            matrix_ref.at[i * part : (i + 1) * part],
            matrix_sem.at[i],
        )
        for i in range(copies)
    ]
    for copy in matrix_copies:
        copy.start()

    ids = lax.broadcasted_iota(jnp.int32, (sent_rows, window_rows), 0)
    ids, inner = split_by(ids, rows_own)
    ids, cycle_step = split_by(ids, RSTEPS)
    ids, sub_part = split_by(ids, sub_count)
    ids, walk_part = split_by(ids, walk_count)
    _, blk_part = split_by(ids + RSTEPS * blk_count - cycle_step, blk_count)
    window = ((blk_part * walk_count + walk_part) * sub_count + sub_part) * rows_own + inner
    repeat = jnp.where(
        window == lax.broadcasted_iota(jnp.int32, window.shape, 1), 1.0, 0.0
    ).astype(jnp.bfloat16)

    vertex_copy.wait()
    own_start = pl.multiple_of(walk_index * rows_local, lanes)
    own_vertex = vertex_ref[:, pl.ds(own_start, rows_local)]
    cosine, sine = cos_sin(
        own_vertex * lax.broadcasted_iota(jnp.int32, (window_rows, rows_local), 0)
    )
    left_ref[...] = jnp.dot(
        repeat, (cosine + sine).astype(jnp.bfloat16), preferred_element_type=jnp.float32
    ).astype(jnp.bfloat16)

    blocks = columns // lanes
    half_blocks = blocks // 2
    coarse_rows = -(-max(half_blocks, 1) // sublanes) * sublanes
    middle_count = lanes // sublanes
    center = sub_index * columns + (blocks - 1) * (lanes // 2)

    @pl.loop(0, vertices // lanes)
    def _(step):
        here = pl.ds(pl.multiple_of(step * lanes, lanes), lanes)
        vertex = vertex_ref[:, here]
        cos_fine, sin_fine = cos_sin(vertex * (row_ids(sublanes) + center))
        cas_fine, cam_fine = cos_fine + sin_fine, cos_fine - sin_fine
        cos_middle, sin_middle = cos_sin(vertex * (row_ids(middle_count) * sublanes))
        cos_coarse, sin_coarse = cos_sin(
            vertex * ((blocks - 1 - 2 * row_ids(coarse_rows)) * (lanes // 2))
        )
        for pair in range(middle_count // 2):
            cas, cam = [], []
            for middle in (2 * pair, 2 * pair + 1):
                c, s = cos_middle[middle : middle + 1], sin_middle[middle : middle + 1]
                cas.append(c * cas_fine + s * cam_fine)
                cam.append(c * cam_fine - s * cas_fine)
            cas, cam = jnp.concatenate(cas, axis=0), jnp.concatenate(cam, axis=0)
            start = pair * 2 * sublanes
            for low in range(half_blocks):
                high = blocks - 1 - low
                even = cos_coarse[low : low + 1] * cas
                odd = sin_coarse[low : low + 1] * cam
                for block, value in ((low, even - odd), (high, even + odd)):
                    first = block * lanes + start
                    table_ref[first : first + 2 * sublanes, here] = value.astype(jnp.bfloat16)
            if blocks % 2:
                first = half_blocks * lanes + start
                table_ref[first : first + 2 * sublanes, here] = cas.astype(jnp.bfloat16)

    for copy in matrix_copies:
        copy.wait()
    chunk = 4 * lanes
    for start in range(0, vertices, chunk):
        left_product = jnp.dot(
            left_ref[...], matrix_ref[:, start : start + chunk], preferred_element_type=jnp.float32
        )
        high = left_product.astype(jnp.bfloat16)
        weight_ref[:sent_rows, start : start + chunk] = high
        weight_ref[sent_rows:, start : start + chunk] = (
            left_product - high.astype(jnp.float32)
        ).astype(jnp.bfloat16)
    green = lax.dot_general(
        table_ref[...], weight_ref[...], (((1,), (1,)), ((), ())), preferred_element_type=jnp.float32
    ).T
    green = (green[:sent_rows] + green[sent_rows:]).astype(sent_ref.dtype)
    sent_ref[...] = green.reshape(sent_ref.shape)


def accumulate_kernel(
    sizes, weights_ref, arrived_ref, transfer_ref, old_ref, new_ref, source_ref, left_ref, unit_ref
):
    blk_count, walk_count, sub_count, rows_own = sizes
    columns_part = arrived_ref.shape[2]
    columns = transfer_ref.shape[1]
    transfers = transfer_ref.shape[0]
    steps_group = sublanes // TQ
    groups = transfers // sublanes
    tiles = columns // lanes
    pairs = blk_count // 2

    def spread(rows, own, group):
        parts = []
        for step in range(group * steps_group, (group + 1) * steps_group):
            row = rows[step * rows_own + own : step * rows_own + own + 1]
            parts.append(jnp.broadcast_to(row, (TQ, row.shape[1])))
        return jnp.concatenate(parts, axis=0)

    for own in range(rows_own):
        for pair in range(pairs):
            codes = []
            for walker in (2 * pair, 2 * pair + 1):
                rows = jnp.concatenate(
                    [
                        sum(
                            arrived_ref[(walker * walk_count + walk_part) * sub_count + sub_part].astype(
                                jnp.float32
                            )
                            for walk_part in range(walk_count)
                        )
                        for sub_part in range(sub_count)
                    ],
                    axis=1,
                )
                left_ref[walker] = rows[own : own + 1] * (weights_ref[:, walker : walker + 1] * (1.0 / blk_count))
                peak = jnp.maximum(jnp.max(jnp.abs(rows), axis=1, keepdims=True), smallest_peak)
                codes.append(jnp.floor(rows * (code_limit / peak) + 0.5).astype(jnp.int32))
                peak = jnp.broadcast_to(peak * (1.0 / code_limit), (peak.shape[0], lanes))
                for group in range(groups):
                    unit_ref[walker, group] = spread(peak, own, group)
            packed = (codes[0] << 16) | (codes[1] & 0xFFFF)
            for group in range(groups):
                source_ref[pair, group] = spread(packed, own, group)

        together = math.gcd(pairs, 2)

        @pl.loop(0, tiles, unroll=math.gcd(tiles, 4))
        def _(tile):
            here = pl.ds(pl.multiple_of(tile * lanes, lanes), lanes)
            for group in range(groups):
                rows = slice(group * sublanes, (group + 1) * sublanes)
                index = transfer_ref[rows, here]
                index_tile, index_lane = index >> lane_bits, index & (lanes - 1)

                def add_pairs(first, total):
                    picked = [jnp.zeros((sublanes, lanes), jnp.int32)] * together
                    for source in range(tiles):
                        match = index_tile == source
                        for k in range(together):
                            words = source_ref[
                                first + k, group, :, source * lanes : (source + 1) * lanes
                            ]
                            words = jnp.take_along_axis(
                                words, index_lane, axis=1, mode="promise_in_bounds"
                            )
                            picked[k] = jnp.where(match, words, picked[k])
                    for k in range(together):
                        for half, code in enumerate((picked[k] >> 16, (picked[k] << 16) >> 16)):
                            walker = (first + k) * 2 + half
                            total = total + left_ref[walker, :, here] * (
                                unit_ref[walker, group] * code.astype(jnp.float32)
                            )
                    return total

                total = old_ref[own, rows, here]
                if pairs == together:
                    total = add_pairs(0, total)
                else:
                    total = lax.fori_loop(
                        0, pairs // together, lambda i, t: add_pairs(i * together, t), total
                    )
                new_ref[own, rows, here] = total


def local(walker_mats, vertex, weights, transfer_table, g4_old):
    blk_count = lax.axis_size("blk")
    walk_count = lax.axis_size("walk")
    sub_count = lax.axis_size("sub")
    rows_local, vertices = walker_mats.shape[1:]
    rows_own, transfers, columns = g4_old.shape
    columns_local = columns // sub_count
    devices = blk_count * walk_count * sub_count
    sizes = (blk_count, walk_count, sub_count, rows_own)
    rows_each = RSTEPS * rows_own
    sent_rows = devices * rows_each
    vmem = pl.BlockSpec(memory_space=pltpu.VMEM)
    sent = pl.pallas_call(
        functools.partial(transform_kernel, sizes),
        out_shape=jax.ShapeDtypeStruct((devices, rows_each, columns_local), jnp.bfloat16),
        in_specs=[pl.BlockSpec(memory_space=pl.ANY)] * 2,
        out_specs=vmem,
        scratch_shapes=[
            pltpu.VMEM((rows_local, vertices), jnp.bfloat16),
            pltpu.VMEM((1, vertices), jnp.int32),
            pltpu.VMEM((sent_rows, rows_local), jnp.bfloat16),
            pltpu.VMEM((columns_local, vertices), jnp.bfloat16),
            pltpu.VMEM((2 * sent_rows, vertices), jnp.bfloat16),
            pltpu.SemaphoreType.DMA((copies,)),
            pltpu.SemaphoreType.DMA,
        ],
        compiler_params=pltpu.CompilerParams(vmem_limit_bytes=121 * 2**19),
        name="transform",
    )(walker_mats, vertex)
    arrived = lax.all_to_all(sent, ("blk", "walk", "sub"), split_axis=0, concat_axis=0, tiled=True)
    return pl.pallas_call(
        functools.partial(accumulate_kernel, sizes),
        out_shape=jax.ShapeDtypeStruct(g4_old.shape, jnp.float32),
        in_specs=[vmem] * 4,
        out_specs=vmem,
        scratch_shapes=[
            pltpu.VMEM((blk_count // 2, transfers // sublanes, sublanes, columns), jnp.int32),
            pltpu.VMEM((blk_count, 1, columns), jnp.float32),
            pltpu.VMEM((blk_count, transfers // sublanes, sublanes, lanes), jnp.float32),
        ],
        compiler_params=pltpu.CompilerParams(vmem_limit_bytes=48 * 2**20),
        name="accumulate",
    )(weights[None], arrived, transfer_table, g4_old)


def solution(mesh):
    in_specs = (
        P(("grp", "blk"), "walk", None),
        P(("grp", "blk"), None),
        P("grp"),
        P(),
        P(("grp", "blk", "walk", "sub"), None, None),
    )
    out_specs = P(("grp", "blk", "walk", "sub"), None, None)
    return jax.shard_map(local, mesh=mesh, in_specs=in_specs, out_specs=out_specs, check_vma=False)
```

```python
import functools
import math

import jax
import jax.numpy as jnp
from jax import lax
from jax.experimental import pallas as pl
from jax.experimental.pallas import tpu as pltpu
from jax.sharding import PartitionSpec as P

TQ = 4
RSTEPS = 4


phase_period = 8192
quarter_bits = 11
lanes = 128
lane_bits = 7
sublanes = 8
code_limit = 32767.0
smallest_peak = 1e-30


def cos_sin(product):
    residue = product & (phase_period - 1)
    quarter = (residue + phase_period // 8) >> quarter_bits
    angle = (residue - (quarter << quarter_bits)).astype(jnp.float32) * (2.0 * math.pi / phase_period)
    square = angle * angle
    sine = angle + angle * square * (
        -1.0 / 6.0 + square * (1.0 / 120.0 + square * (-1.0 / 5040.0 + square * (1.0 / 362880.0)))
    )
    cosine = 1.0 + square * (
        -0.5 + square * (1.0 / 24.0 + square * (-1.0 / 720.0 + square * (1.0 / 40320.0)))
    )
    odd = (quarter & 1) == 1
    cosine_out = jnp.where(odd, sine, cosine)
    sine_out = jnp.where(odd, cosine, sine)
    cosine_out = jnp.where(((quarter + 1) & 2) == 2, -cosine_out, cosine_out)
    sine_out = jnp.where((quarter & 2) == 2, -sine_out, sine_out)
    return cosine_out, sine_out


def row_ids(count):
    return lax.broadcasted_iota(jnp.int32, (count, lanes), 0)


def split_by(ids, size):
    if size & (size - 1) == 0:
        return ids >> (size.bit_length() - 1), ids & (size - 1)
    return ids // size, ids % size


def transform_kernel(
    sizes,
    matrix_hbm,
    vertex_hbm,
    sent_ref,
    matrix_ref,
    vertex_ref,
    left_ref,
    table_ref,
    weight_ref,
    matrix_sem,
    vertex_sem,
):
    blk_count, walk_count, sub_count, rows_own = sizes
    walk_index = lax.axis_index("walk")
    sub_index = lax.axis_index("sub")
    rows_local, vertices = matrix_ref.shape
    columns = table_ref.shape[0]
    window_rows = left_ref.shape[0]
    sent_rows = math.prod(sent_ref.shape[:-1])

    vertex_copy = pltpu.make_async_copy(vertex_hbm, vertex_ref, vertex_sem)
    vertex_copy.start()
    matrix_copy = pltpu.make_async_copy(matrix_hbm.at[0], matrix_ref, matrix_sem)
    matrix_copy.start()

    ids = lax.broadcasted_iota(jnp.int32, (sent_rows, window_rows), 0)
    ids, inner = split_by(ids, rows_own)
    ids, cycle_step = split_by(ids, RSTEPS)
    ids, sub_part = split_by(ids, sub_count)
    ids, walk_part = split_by(ids, walk_count)
    _, blk_part = split_by(ids + RSTEPS * blk_count - cycle_step, blk_count)
    window = ((blk_part * walk_count + walk_part) * sub_count + sub_part) * rows_own + inner
    repeat = jnp.where(
        window == lax.broadcasted_iota(jnp.int32, window.shape, 1), 1.0, 0.0
    ).astype(jnp.bfloat16)

    vertex_copy.wait()
    own_start = pl.multiple_of(walk_index * rows_local, lanes)
    own_vertex = vertex_ref[:, pl.ds(own_start, rows_local)]
    cosine, sine = cos_sin(
        own_vertex * lax.broadcasted_iota(jnp.int32, (window_rows, rows_local), 0)
    )
    left_ref[...] = (cosine + sine).astype(jnp.bfloat16)

    blocks = columns // lanes
    half_blocks = blocks // 2
    coarse_rows = -(-max(half_blocks, 1) // sublanes) * sublanes
    middle_count = lanes // sublanes
    center = sub_index * columns + (blocks - 1) * (lanes // 2)

    @pl.loop(0, vertices // lanes)
    def _(step):
        here = pl.ds(pl.multiple_of(step * lanes, lanes), lanes)
        vertex = vertex_ref[:, here]
        cos_fine, sin_fine = cos_sin(vertex * (row_ids(sublanes) + center))
        cas_fine, cam_fine = cos_fine + sin_fine, cos_fine - sin_fine
        cos_middle, sin_middle = cos_sin(vertex * (row_ids(middle_count) * sublanes))
        cos_coarse, sin_coarse = cos_sin(
            vertex * ((blocks - 1 - 2 * row_ids(coarse_rows)) * (lanes // 2))
        )
        for pair in range(middle_count // 2):
            cas, cam = [], []
            for middle in (2 * pair, 2 * pair + 1):
                c, s = cos_middle[middle : middle + 1], sin_middle[middle : middle + 1]
                cas.append(c * cas_fine + s * cam_fine)
                cam.append(c * cam_fine - s * cas_fine)
            cas, cam = jnp.concatenate(cas, axis=0), jnp.concatenate(cam, axis=0)
            start = pair * 2 * sublanes
            for low in range(half_blocks):
                high = blocks - 1 - low
                even = cos_coarse[low : low + 1] * cas
                odd = sin_coarse[low : low + 1] * cam
                for block, value in ((low, even - odd), (high, even + odd)):
                    first = block * lanes + start
                    table_ref[first : first + 2 * sublanes, here] = value.astype(jnp.bfloat16)
            if blocks % 2:
                first = half_blocks * lanes + start
                table_ref[first : first + 2 * sublanes, here] = cas.astype(jnp.bfloat16)

    matrix_copy.wait()
    chunk = 4 * lanes
    for start in range(0, vertices, chunk):
        left_product = jnp.dot(
            left_ref[...], matrix_ref[:, start : start + chunk], preferred_element_type=jnp.float32
        )
        high = left_product.astype(jnp.bfloat16)
        weight_ref[:window_rows, start : start + chunk] = high
        weight_ref[window_rows:, start : start + chunk] = (
            left_product - high.astype(jnp.float32)
        ).astype(jnp.bfloat16)
    green = lax.dot_general(
        weight_ref[...], table_ref[...], (((1,), (1,)), ((), ())), preferred_element_type=jnp.float32
    )
    green = (green[:window_rows] + green[window_rows:]).astype(jnp.bfloat16)
    green = jnp.dot(repeat, green, preferred_element_type=jnp.float32).astype(sent_ref.dtype)
    sent_ref[...] = green.reshape(sent_ref.shape)


def accumulate_kernel(
    sizes, weights_ref, arrived_ref, transfer_ref, old_ref, new_ref, source_ref, left_ref, unit_ref
):
    blk_count, walk_count, sub_count, rows_own = sizes
    columns_part = arrived_ref.shape[2]
    columns = transfer_ref.shape[1]
    transfers = transfer_ref.shape[0]
    steps_group = sublanes // TQ
    groups = transfers // sublanes
    tiles = columns // lanes
    pairs = blk_count // 2

    def spread(rows, own, group):
        parts = []
        for step in range(group * steps_group, (group + 1) * steps_group):
            row = rows[step * rows_own + own : step * rows_own + own + 1]
            parts.append(jnp.broadcast_to(row, (TQ, row.shape[1])))
        return jnp.concatenate(parts, axis=0)

    for own in range(rows_own):
        for pair in range(pairs):
            codes = []
            for walker in (2 * pair, 2 * pair + 1):
                rows = jnp.concatenate(
                    [
                        sum(
                            arrived_ref[(walker * walk_count + walk_part) * sub_count + sub_part].astype(
                                jnp.float32
                            )
                            for walk_part in range(walk_count)
                        )
                        for sub_part in range(sub_count)
                    ],
                    axis=1,
                )
                left_ref[walker] = rows[own : own + 1] * (weights_ref[:, walker : walker + 1] * (1.0 / blk_count))
                peak = jnp.maximum(jnp.max(jnp.abs(rows), axis=1, keepdims=True), smallest_peak)
                codes.append(jnp.floor(rows * (code_limit / peak) + 0.5).astype(jnp.int32))
                peak = jnp.broadcast_to(peak * (1.0 / code_limit), (peak.shape[0], lanes))
                for group in range(groups):
                    unit_ref[walker, group] = spread(peak, own, group)
            packed = (codes[0] << 16) | (codes[1] & 0xFFFF)
            for group in range(groups):
                source_ref[pair, group] = spread(packed, own, group)

        together = math.gcd(pairs, 2)

        @pl.loop(0, tiles, unroll=math.gcd(tiles, 4))
        def _(tile):
            here = pl.ds(pl.multiple_of(tile * lanes, lanes), lanes)
            for group in range(groups):
                rows = slice(group * sublanes, (group + 1) * sublanes)
                index = transfer_ref[rows, here]
                index_tile, index_lane = index >> lane_bits, index & (lanes - 1)

                def add_pairs(first, total):
                    picked = [jnp.zeros((sublanes, lanes), jnp.int32)] * together
                    for source in range(tiles):
                        match = index_tile == source
                        for k in range(together):
                            words = source_ref[
                                first + k, group, :, source * lanes : (source + 1) * lanes
                            ]
                            words = jnp.take_along_axis(
                                words, index_lane, axis=1, mode="promise_in_bounds"
                            )
                            picked[k] = jnp.where(match, words, picked[k])
                    for k in range(together):
                        for half, code in enumerate((picked[k] >> 16, (picked[k] << 16) >> 16)):
                            walker = (first + k) * 2 + half
                            total = total + left_ref[walker, :, here] * (
                                unit_ref[walker, group] * code.astype(jnp.float32)
                            )
                    return total

                total = old_ref[own, rows, here]
                if pairs == together:
                    total = add_pairs(0, total)
                else:
                    total = lax.fori_loop(
                        0, pairs // together, lambda i, t: add_pairs(i * together, t), total
                    )
                new_ref[own, rows, here] = total


def local(walker_mats, vertex, weights, transfer_table, g4_old):
    blk_count = lax.axis_size("blk")
    walk_count = lax.axis_size("walk")
    sub_count = lax.axis_size("sub")
    rows_local, vertices = walker_mats.shape[1:]
    rows_own, transfers, columns = g4_old.shape
    columns_local = columns // sub_count
    devices = blk_count * walk_count * sub_count
    sizes = (blk_count, walk_count, sub_count, rows_own)
    rows_each = RSTEPS * rows_own
    vmem = pl.BlockSpec(memory_space=pltpu.VMEM)
    sent = pl.pallas_call(
        functools.partial(transform_kernel, sizes),
        out_shape=jax.ShapeDtypeStruct((devices, rows_each, columns_local), jnp.bfloat16),
        in_specs=[pl.BlockSpec(memory_space=pl.ANY)] * 2,
        out_specs=vmem,
        scratch_shapes=[
            pltpu.VMEM((rows_local, vertices), jnp.bfloat16),
            pltpu.VMEM((1, vertices), jnp.int32),
            pltpu.VMEM((devices * rows_own, rows_local), jnp.bfloat16),
            pltpu.VMEM((columns_local, vertices), jnp.bfloat16),
            pltpu.VMEM((2 * devices * rows_own, vertices), jnp.bfloat16),
            pltpu.SemaphoreType.DMA,
            pltpu.SemaphoreType.DMA,
        ],
        compiler_params=pltpu.CompilerParams(vmem_limit_bytes=121 * 2**19),
        name="transform",
    )(walker_mats, vertex)
    arrived = lax.all_to_all(sent, ("blk", "walk", "sub"), split_axis=0, concat_axis=0, tiled=True)
    return pl.pallas_call(
        functools.partial(accumulate_kernel, sizes),
        out_shape=jax.ShapeDtypeStruct(g4_old.shape, jnp.float32),
        in_specs=[vmem] * 4,
        out_specs=vmem,
        scratch_shapes=[
            pltpu.VMEM((blk_count // 2, transfers // sublanes, sublanes, columns), jnp.int32),
            pltpu.VMEM((blk_count, 1, columns), jnp.float32),
            pltpu.VMEM((blk_count, transfers // sublanes, sublanes, lanes), jnp.float32),
        ],
        compiler_params=pltpu.CompilerParams(vmem_limit_bytes=48 * 2**20),
        name="accumulate",
    )(weights[None], arrived, transfer_table, g4_old)


def solution(mesh):
    in_specs = (
        P(("grp", "blk"), "walk", None),
        P(("grp", "blk"), None),
        P("grp"),
        P(),
        P(("grp", "blk", "walk", "sub"), None, None),
    )
    out_specs = P(("grp", "blk", "walk", "sub"), None, None)
    return jax.shard_map(local, mesh=mesh, in_specs=in_specs, out_specs=out_specs, check_vma=False)
```

```python
import functools
import math

import jax
import jax.numpy as jnp
from jax import lax
from jax.experimental import pallas as pl
from jax.experimental.pallas import tpu as pltpu
from jax.sharding import PartitionSpec as P

TQ = 4
RSTEPS = 4


phase_period = 8192
quarter_bits = 11
lanes = 128
lane_bits = 7
sublanes = 8
code_limit = 32767.0
smallest_peak = 1e-30


def cos_sin(product):
    residue = product & (phase_period - 1)
    quarter = (residue + phase_period // 8) >> quarter_bits
    angle = (residue - (quarter << quarter_bits)).astype(jnp.float32) * (2.0 * math.pi / phase_period)
    square = angle * angle
    sine = angle + angle * square * (
        -1.0 / 6.0 + square * (1.0 / 120.0 + square * (-1.0 / 5040.0 + square * (1.0 / 362880.0)))
    )
    cosine = 1.0 + square * (
        -0.5 + square * (1.0 / 24.0 + square * (-1.0 / 720.0 + square * (1.0 / 40320.0)))
    )
    odd = (quarter & 1) == 1
    cosine_out = jnp.where(odd, sine, cosine)
    sine_out = jnp.where(odd, cosine, sine)
    cosine_out = jnp.where(((quarter + 1) & 2) == 2, -cosine_out, cosine_out)
    sine_out = jnp.where((quarter & 2) == 2, -sine_out, sine_out)
    return cosine_out, sine_out


def row_ids(count):
    return lax.broadcasted_iota(jnp.int32, (count, lanes), 0)


def split_by(ids, size):
    if size & (size - 1) == 0:
        return ids >> (size.bit_length() - 1), ids & (size - 1)
    return ids // size, ids % size


def table_kernel(vertex_ref, table_ref, left_ref):
    walk_index = lax.axis_index("walk")
    sub_index = lax.axis_index("sub")
    columns, vertices = table_ref.shape
    window_rows, rows_local = left_ref.shape
    own_start = pl.multiple_of(walk_index * rows_local, lanes)
    own_vertex = vertex_ref[:, pl.ds(own_start, rows_local)]
    cosine, sine = cos_sin(
        own_vertex * lax.broadcasted_iota(jnp.int32, (window_rows, rows_local), 0)
    )
    left_ref[...] = (cosine + sine).astype(jnp.bfloat16)

    blocks = columns // lanes
    half_blocks = blocks // 2
    coarse_rows = -(-max(half_blocks, 1) // sublanes) * sublanes
    middle_count = lanes // sublanes
    center = sub_index * columns + (blocks - 1) * (lanes // 2)

    @pl.loop(0, vertices // lanes)
    def _(step):
        here = pl.ds(pl.multiple_of(step * lanes, lanes), lanes)
        vertex = vertex_ref[:, here]
        cos_fine, sin_fine = cos_sin(vertex * (row_ids(sublanes) + center))
        cas_fine, cam_fine = cos_fine + sin_fine, cos_fine - sin_fine
        cos_middle, sin_middle = cos_sin(vertex * (row_ids(middle_count) * sublanes))
        cos_coarse, sin_coarse = cos_sin(
            vertex * ((blocks - 1 - 2 * row_ids(coarse_rows)) * (lanes // 2))
        )
        for pair in range(middle_count // 2):
            cas, cam = [], []
            for middle in (2 * pair, 2 * pair + 1):
                c, s = cos_middle[middle : middle + 1], sin_middle[middle : middle + 1]
                cas.append(c * cas_fine + s * cam_fine)
                cam.append(c * cam_fine - s * cas_fine)
            cas, cam = jnp.concatenate(cas, axis=0), jnp.concatenate(cam, axis=0)
            start = pair * 2 * sublanes
            for low in range(half_blocks):
                high = blocks - 1 - low
                even = cos_coarse[low : low + 1] * cas
                odd = sin_coarse[low : low + 1] * cam
                for block, value in ((low, even - odd), (high, even + odd)):
                    first = block * lanes + start
                    table_ref[first : first + 2 * sublanes, here] = value.astype(jnp.bfloat16)
            if blocks % 2:
                first = half_blocks * lanes + start
                table_ref[first : first + 2 * sublanes, here] = cas.astype(jnp.bfloat16)


def product_kernel(sizes, matrix_ref, table_ref, left_ref, sent_ref, weight_ref):
    blk_count, walk_count, sub_count, rows_own = sizes
    vertices = matrix_ref.shape[2]
    window_rows = left_ref.shape[0]
    sent_rows = math.prod(sent_ref.shape[:-1])

    ids = lax.broadcasted_iota(jnp.int32, (sent_rows, window_rows), 0)
    ids, inner = split_by(ids, rows_own)
    ids, cycle_step = split_by(ids, RSTEPS)
    ids, sub_part = split_by(ids, sub_count)
    ids, walk_part = split_by(ids, walk_count)
    _, blk_part = split_by(ids + RSTEPS * blk_count - cycle_step, blk_count)
    window = ((blk_part * walk_count + walk_part) * sub_count + sub_part) * rows_own + inner
    repeat = jnp.where(
        window == lax.broadcasted_iota(jnp.int32, window.shape, 1), 1.0, 0.0
    ).astype(jnp.bfloat16)

    chunk = 4 * lanes
    for start in range(0, vertices, chunk):
        left_product = jnp.dot(
            left_ref[...], matrix_ref[0, :, start : start + chunk], preferred_element_type=jnp.float32
        )
        high = left_product.astype(jnp.bfloat16)
        weight_ref[:window_rows, start : start + chunk] = high
        weight_ref[window_rows:, start : start + chunk] = (
            left_product - high.astype(jnp.float32)
        ).astype(jnp.bfloat16)
    green = lax.dot_general(
        weight_ref[...], table_ref[...], (((1,), (1,)), ((), ())), preferred_element_type=jnp.float32
    )
    green = (green[:window_rows] + green[window_rows:]).astype(jnp.bfloat16)
    green = jnp.dot(repeat, green, preferred_element_type=jnp.float32).astype(sent_ref.dtype)
    sent_ref[...] = green.reshape(sent_ref.shape)


def accumulate_kernel(
    sizes, weights_ref, arrived_ref, transfer_ref, old_ref, new_ref, source_ref, left_ref, unit_ref
):
    blk_count, walk_count, sub_count, rows_own = sizes
    columns_part = arrived_ref.shape[2]
    columns = transfer_ref.shape[1]
    transfers = transfer_ref.shape[0]
    steps_group = sublanes // TQ
    groups = transfers // sublanes
    tiles = columns // lanes
    pairs = blk_count // 2

    def spread(rows, own, group):
        parts = []
        for step in range(group * steps_group, (group + 1) * steps_group):
            row = rows[step * rows_own + own : step * rows_own + own + 1]
            parts.append(jnp.broadcast_to(row, (TQ, row.shape[1])))
        return jnp.concatenate(parts, axis=0)

    for own in range(rows_own):
        for pair in range(pairs):
            codes = []
            for walker in (2 * pair, 2 * pair + 1):
                rows = jnp.concatenate(
                    [
                        sum(
                            arrived_ref[(walker * walk_count + walk_part) * sub_count + sub_part].astype(
                                jnp.float32
                            )
                            for walk_part in range(walk_count)
                        )
                        for sub_part in range(sub_count)
                    ],
                    axis=1,
                )
                left_ref[walker] = rows[own : own + 1] * (weights_ref[:, walker : walker + 1] * (1.0 / blk_count))
                peak = jnp.maximum(jnp.max(jnp.abs(rows), axis=1, keepdims=True), smallest_peak)
                codes.append(jnp.floor(rows * (code_limit / peak) + 0.5).astype(jnp.int32))
                peak = jnp.broadcast_to(peak * (1.0 / code_limit), (peak.shape[0], lanes))
                for group in range(groups):
                    unit_ref[walker, group] = spread(peak, own, group)
            packed = (codes[0] << 16) | (codes[1] & 0xFFFF)
            for group in range(groups):
                source_ref[pair, group] = spread(packed, own, group)

        together = math.gcd(pairs, 2)

        @pl.loop(0, tiles, unroll=math.gcd(tiles, 4))
        def _(tile):
            here = pl.ds(pl.multiple_of(tile * lanes, lanes), lanes)
            for group in range(groups):
                rows = slice(group * sublanes, (group + 1) * sublanes)
                index = transfer_ref[rows, here]
                index_tile, index_lane = index >> lane_bits, index & (lanes - 1)

                def add_pairs(first, total):
                    picked = [jnp.zeros((sublanes, lanes), jnp.int32)] * together
                    for source in range(tiles):
                        match = index_tile == source
                        for k in range(together):
                            words = source_ref[
                                first + k, group, :, source * lanes : (source + 1) * lanes
                            ]
                            words = jnp.take_along_axis(
                                words, index_lane, axis=1, mode="promise_in_bounds"
                            )
                            picked[k] = jnp.where(match, words, picked[k])
                    for k in range(together):
                        for half, code in enumerate((picked[k] >> 16, (picked[k] << 16) >> 16)):
                            walker = (first + k) * 2 + half
                            total = total + left_ref[walker, :, here] * (
                                unit_ref[walker, group] * code.astype(jnp.float32)
                            )
                    return total

                total = old_ref[own, rows, here]
                if pairs == together:
                    total = add_pairs(0, total)
                else:
                    total = lax.fori_loop(
                        0, pairs // together, lambda i, t: add_pairs(i * together, t), total
                    )
                new_ref[own, rows, here] = total


def local(walker_mats, vertex, weights, transfer_table, g4_old):
    blk_count = lax.axis_size("blk")
    walk_count = lax.axis_size("walk")
    sub_count = lax.axis_size("sub")
    rows_local, vertices = walker_mats.shape[1:]
    rows_own, transfers, columns = g4_old.shape
    columns_local = columns // sub_count
    devices = blk_count * walk_count * sub_count
    sizes = (blk_count, walk_count, sub_count, rows_own)
    rows_each = RSTEPS * rows_own
    vmem = pl.BlockSpec(memory_space=pltpu.VMEM)
    table, left = pl.pallas_call(
        table_kernel,
        out_shape=[
            jax.ShapeDtypeStruct((columns_local, vertices), jnp.bfloat16),
            jax.ShapeDtypeStruct((devices * rows_own, rows_local), jnp.bfloat16),
        ],
        in_specs=[vmem],
        out_specs=[vmem] * 2,
        compiler_params=pltpu.CompilerParams(vmem_limit_bytes=24 * 2**20),
        cost_estimate=pl.CostEstimate(
            flops=2000 * columns_local * vertices,
            bytes_accessed=6 * columns_local * vertices,
            transcendentals=0,
        ),
        name="table",
    )(vertex)
    sent = pl.pallas_call(
        functools.partial(product_kernel, sizes),
        out_shape=jax.ShapeDtypeStruct((devices, rows_each, columns_local), jnp.bfloat16),
        in_specs=[vmem] * 3,
        out_specs=vmem,
        scratch_shapes=[pltpu.VMEM((2 * devices * rows_own, vertices), jnp.bfloat16)],
        compiler_params=pltpu.CompilerParams(vmem_limit_bytes=24 * 2**20),
        name="product",
    )(walker_mats, table, left)
    arrived = lax.all_to_all(sent, ("blk", "walk", "sub"), split_axis=0, concat_axis=0, tiled=True)
    return pl.pallas_call(
        functools.partial(accumulate_kernel, sizes),
        out_shape=jax.ShapeDtypeStruct(g4_old.shape, jnp.float32),
        in_specs=[vmem] * 4,
        out_specs=vmem,
        scratch_shapes=[
            pltpu.VMEM((blk_count // 2, transfers // sublanes, sublanes, columns), jnp.int32),
            pltpu.VMEM((blk_count, 1, columns), jnp.float32),
            pltpu.VMEM((blk_count, transfers // sublanes, sublanes, lanes), jnp.float32),
        ],
        compiler_params=pltpu.CompilerParams(vmem_limit_bytes=48 * 2**20),
        name="accumulate",
    )(weights[None], arrived, transfer_table, g4_old)


def solution(mesh):
    in_specs = (
        P(("grp", "blk"), "walk", None),
        P(("grp", "blk"), None),
        P("grp"),
        P(),
        P(("grp", "blk", "walk", "sub"), None, None),
    )
    out_specs = P(("grp", "blk", "walk", "sub"), None, None)
    return jax.shard_map(local, mesh=mesh, in_specs=in_specs, out_specs=out_specs, check_vma=False)
```

```python
import functools
import itertools
import math

import jax
import jax.numpy as jnp
from jax import lax
from jax.experimental import pallas as pl
from jax.experimental.pallas import tpu as pltpu
from jax.sharding import PartitionSpec as P

TQ = 4
RSTEPS = 4


phase_period = 8192
quarter_bits = 11
lanes = 128
lane_bits = 7
sublanes = 8
code_limit = 32767.0
smallest_peak = 1e-30


def cos_sin(product):
    residue = product & (phase_period - 1)
    quarter = (residue + phase_period // 8) >> quarter_bits
    angle = (residue - (quarter << quarter_bits)).astype(jnp.float32) * (2.0 * math.pi / phase_period)
    square = angle * angle
    sine = angle + angle * square * (
        -1.0 / 6.0 + square * (1.0 / 120.0 + square * (-1.0 / 5040.0 + square * (1.0 / 362880.0)))
    )
    cosine = 1.0 + square * (
        -0.5 + square * (1.0 / 24.0 + square * (-1.0 / 720.0 + square * (1.0 / 40320.0)))
    )
    odd = (quarter & 1) == 1
    cosine_out = jnp.where(odd, sine, cosine)
    sine_out = jnp.where(odd, cosine, sine)
    cosine_out = jnp.where(((quarter + 1) & 2) == 2, -cosine_out, cosine_out)
    sine_out = jnp.where((quarter & 2) == 2, -sine_out, sine_out)
    return cosine_out, sine_out


def row_ids(count):
    return lax.broadcasted_iota(jnp.int32, (count, lanes), 0)


def split_by(ids, size):
    if size & (size - 1) == 0:
        return ids >> (size.bit_length() - 1), ids & (size - 1)
    return ids // size, ids % size


def table_kernel(vertex_ref, table_ref, left_ref):
    walk_index = lax.axis_index("walk")
    sub_index = lax.axis_index("sub")
    columns, vertices = table_ref.shape
    window_rows, rows_local = left_ref.shape
    own_start = pl.multiple_of(walk_index * rows_local, lanes)
    own_vertex = vertex_ref[:, pl.ds(own_start, rows_local)]
    cosine, sine = cos_sin(
        own_vertex * lax.broadcasted_iota(jnp.int32, (window_rows, rows_local), 0)
    )
    left_ref[...] = (cosine + sine).astype(jnp.bfloat16)

    blocks = columns // lanes
    half_blocks = blocks // 2
    coarse_rows = -(-max(half_blocks, 1) // sublanes) * sublanes
    middle_count = lanes // sublanes
    center = sub_index * columns + (blocks - 1) * (lanes // 2)

    @pl.loop(0, vertices // lanes)
    def _(step):
        here = pl.ds(pl.multiple_of(step * lanes, lanes), lanes)
        vertex = vertex_ref[:, here]
        cos_fine, sin_fine = cos_sin(vertex * (row_ids(sublanes) + center))
        cas_fine, cam_fine = cos_fine + sin_fine, cos_fine - sin_fine
        cos_middle, sin_middle = cos_sin(vertex * (row_ids(middle_count) * sublanes))
        cos_coarse, sin_coarse = cos_sin(
            vertex * ((blocks - 1 - 2 * row_ids(coarse_rows)) * (lanes // 2))
        )
        for pair in range(middle_count // 2):
            cas, cam = [], []
            for middle in (2 * pair, 2 * pair + 1):
                c, s = cos_middle[middle : middle + 1], sin_middle[middle : middle + 1]
                cas.append(c * cas_fine + s * cam_fine)
                cam.append(c * cam_fine - s * cas_fine)
            cas, cam = jnp.concatenate(cas, axis=0), jnp.concatenate(cam, axis=0)
            start = pair * 2 * sublanes
            for low in range(half_blocks):
                high = blocks - 1 - low
                even = cos_coarse[low : low + 1] * cas
                odd = sin_coarse[low : low + 1] * cam
                for block, value in ((low, even - odd), (high, even + odd)):
                    first = block * lanes + start
                    table_ref[first : first + 2 * sublanes, here] = value.astype(jnp.bfloat16)
            if blocks % 2:
                first = half_blocks * lanes + start
                table_ref[first : first + 2 * sublanes, here] = cas.astype(jnp.bfloat16)


def product_kernel(sizes, matrix_ref, table_ref, left_ref, *rest):
    *sent_refs, weight_ref = rest
    blk_count, walk_count, sub_count, rows_own = sizes
    blk_index = lax.axis_index("blk")
    walk_index = lax.axis_index("walk")
    sub_index = lax.axis_index("sub")
    vertices = matrix_ref.shape[2]
    window_rows = left_ref.shape[0]

    ids = lax.broadcasted_iota(jnp.int32, (window_rows, window_rows), 0)
    ids, inner = split_by(ids, rows_own)
    ids, blk_part = split_by(ids, blk_count)
    walk_part, sub_part = split_by(ids, sub_count)
    _, sub_part = split_by(sub_part + sub_index, sub_count)
    _, walk_part = split_by(walk_part + walk_index, walk_count)
    _, blk_part = split_by(blk_part + blk_index, blk_count)
    window = ((blk_part * walk_count + walk_part) * sub_count + sub_part) * rows_own + inner
    order = jnp.where(
        window == lax.broadcasted_iota(jnp.int32, window.shape, 1), 1.0, 0.0
    ).astype(jnp.bfloat16)

    chunk = 4 * lanes
    for start in range(0, vertices, chunk):
        left_product = jnp.dot(
            left_ref[...], matrix_ref[0, :, start : start + chunk], preferred_element_type=jnp.float32
        )
        high = left_product.astype(jnp.bfloat16)
        weight_ref[:window_rows, start : start + chunk] = high
        weight_ref[window_rows:, start : start + chunk] = (
            left_product - high.astype(jnp.float32)
        ).astype(jnp.bfloat16)
    green = lax.dot_general(
        weight_ref[...], table_ref[...], (((1,), (1,)), ((), ())), preferred_element_type=jnp.float32
    )
    green = green[:window_rows] + green[window_rows:]
    high = green.astype(jnp.bfloat16)
    low = (green - high.astype(jnp.float32)).astype(jnp.bfloat16)
    green = jnp.dot(order, high, preferred_element_type=jnp.float32) + jnp.dot(
        order, low, preferred_element_type=jnp.float32
    )
    rows_each = blk_count * rows_own
    for place, sent_ref in enumerate(sent_refs):
        sent_ref[...] = green[place * rows_each : (place + 1) * rows_each]


def rows_for(distance, blk_count):
    return [(distance - step) % blk_count for step in range(RSTEPS)]


def combine_kernel(sizes, *refs):
    blk_count, walk_count, sub_count, rows_own = sizes
    sub_index = lax.axis_index("sub")
    part_refs, whole_refs = refs[: walk_count * sub_count], refs[walk_count * sub_count :]
    columns_part = part_refs[0].shape[1]
    for distance in range(sub_count):
        _, sub_part = split_by(sub_index + sub_count - distance, sub_count)
        here = pl.ds(pl.multiple_of(sub_part * columns_part, lanes), columns_part)
        total = sum(
            part_refs[walk_part * sub_count + distance][...]
            for walk_part in range(walk_count)
        )
        if len(whole_refs) == 1:
            whole_refs[0][:, here] = total.astype(whole_refs[0].dtype)
            continue
        for blk_part, whole_ref in enumerate(whole_refs):
            rows = [total[i * rows_own : (i + 1) * rows_own] for i in rows_for(blk_part, blk_count)]
            whole_ref[:, here] = jnp.concatenate(rows, axis=0).astype(whole_ref.dtype)


def accumulate_kernel(sizes, weights_ref, transfer_ref, old_ref, *rest):
    *arrived_refs, new_ref, source_ref, left_ref, unit_ref = rest
    blk_count, walk_count, sub_count, rows_own = sizes
    blk_index = lax.axis_index("blk")
    columns = transfer_ref.shape[1]
    transfers = transfer_ref.shape[0]
    steps_group = sublanes // TQ
    groups = transfers // sublanes
    tiles = columns // lanes
    pairs = blk_count // 2
    weights = weights_ref[...] * (1.0 / blk_count)
    walker_ids = lax.broadcasted_iota(jnp.int32, weights.shape, 1)

    def places(distance):
        if arrived_refs[0].shape[0] == blk_count * rows_own:
            return rows_for(distance, blk_count)
        return list(range(RSTEPS))

    def spread(rows, distance, own, group):
        parts = []
        for place in places(distance)[group * steps_group : (group + 1) * steps_group]:
            row = rows[place * rows_own + own : place * rows_own + own + 1]
            parts.append(jnp.broadcast_to(row, (TQ, row.shape[1])))
        return jnp.concatenate(parts, axis=0)

    for own in range(rows_own):
        for pair in range(pairs):
            codes = []
            for distance in (2 * pair, 2 * pair + 1):
                rows = arrived_refs[distance][...].astype(jnp.float32)
                _, walker = split_by(blk_index + blk_count - distance, blk_count)
                weight = jnp.sum(jnp.where(walker_ids == walker, weights, 0.0), axis=1, keepdims=True)
                first = places(distance)[0] * rows_own + own
                left_ref[distance] = rows[first : first + 1] * weight
                peak = jnp.maximum(jnp.max(jnp.abs(rows), axis=1, keepdims=True), smallest_peak)
                codes.append(jnp.floor(rows * (code_limit / peak) + 0.5).astype(jnp.int32))
                peak = jnp.broadcast_to(peak * (1.0 / code_limit), (peak.shape[0], lanes))
                for group in range(groups):
                    unit_ref[distance, group] = spread(peak, distance, own, group)
            for group in range(groups):
                high = spread(codes[0], 2 * pair, own, group)
                low = spread(codes[1], 2 * pair + 1, own, group)
                source_ref[pair, group] = (high << 16) | (low & 0xFFFF)

        together = math.gcd(pairs, 2)

        @pl.loop(0, tiles, unroll=math.gcd(tiles, 4))
        def _(tile):
            here = pl.ds(pl.multiple_of(tile * lanes, lanes), lanes)
            for group in range(groups):
                rows = slice(group * sublanes, (group + 1) * sublanes)
                index = transfer_ref[rows, here]
                index_tile, index_lane = index >> lane_bits, index & (lanes - 1)

                def add_pairs(first, total):
                    picked = [jnp.zeros((sublanes, lanes), jnp.int32)] * together
                    for source in range(tiles):
                        match = index_tile == source
                        for k in range(together):
                            words = source_ref[
                                first + k, group, :, source * lanes : (source + 1) * lanes
                            ]
                            words = jnp.take_along_axis(
                                words, index_lane, axis=1, mode="promise_in_bounds"
                            )
                            picked[k] = jnp.where(match, words, picked[k])
                    for k in range(together):
                        for half, code in enumerate((picked[k] >> 16, (picked[k] << 16) >> 16)):
                            walker = (first + k) * 2 + half
                            total = total + left_ref[walker, :, here] * (
                                unit_ref[walker, group] * code.astype(jnp.float32)
                            )
                    return total

                total = old_ref[own, rows, here]
                if pairs == together:
                    total = add_pairs(0, total)
                else:
                    total = lax.fori_loop(
                        0, pairs // together, lambda i, t: add_pairs(i * together, t), total
                    )
                new_ref[own, rows, here] = total


def exchange(pieces, axes, counts):
    positions = list(itertools.product(*map(range, counts)))
    place = {position: i for i, position in enumerate(positions)}

    def away(position, distance):
        return tuple((p + d) % n for p, d, n in zip(position, distance, counts))

    arrived = [pieces[0]]
    for distance, piece in list(zip(positions, pieces))[1:]:
        route = [(place[position], place[away(position, distance)]) for position in positions]
        arrived.append(lax.ppermute(piece, axes, route))
    return arrived


def local(walker_mats, vertex, weights, transfer_table, g4_old):
    blk_count = lax.axis_size("blk")
    walk_count = lax.axis_size("walk")
    sub_count = lax.axis_size("sub")
    rows_local, vertices = walker_mats.shape[1:]
    rows_own, transfers, columns = g4_old.shape
    columns_local = columns // sub_count
    devices = blk_count * walk_count * sub_count
    sizes = (blk_count, walk_count, sub_count, rows_own)
    vmem = pl.BlockSpec(memory_space=pltpu.VMEM)
    table, left = pl.pallas_call(
        table_kernel,
        out_shape=[
            jax.ShapeDtypeStruct((columns_local, vertices), jnp.bfloat16),
            jax.ShapeDtypeStruct((devices * rows_own, rows_local), jnp.bfloat16),
        ],
        in_specs=[vmem],
        out_specs=[vmem] * 2,
        compiler_params=pltpu.CompilerParams(vmem_limit_bytes=24 * 2**20),
        cost_estimate=pl.CostEstimate(
            flops=2000 * columns_local * vertices,
            bytes_accessed=6 * columns_local * vertices,
            transcendentals=0,
        ),
        name="table",
    )(vertex)
    sent = pl.pallas_call(
        functools.partial(product_kernel, sizes),
        out_shape=[jax.ShapeDtypeStruct((blk_count * rows_own, columns_local), jnp.float32)]
        * (walk_count * sub_count),
        in_specs=[vmem] * 3,
        out_specs=[vmem] * (walk_count * sub_count),
        scratch_shapes=[pltpu.VMEM((2 * devices * rows_own, vertices), jnp.bfloat16)],
        compiler_params=pltpu.CompilerParams(vmem_limit_bytes=24 * 2**20),
        name="product",
    )(walker_mats, table, left)
    parts = exchange(sent, ("walk", "sub"), (walk_count, sub_count))
    shared = blk_count <= RSTEPS
    rows_each = (blk_count if shared else RSTEPS) * rows_own
    whole_count = 1 if shared else blk_count
    whole = pl.pallas_call(
        functools.partial(combine_kernel, sizes),
        out_shape=[jax.ShapeDtypeStruct((rows_each, columns), jnp.bfloat16)] * whole_count,
        in_specs=[vmem] * len(parts),
        out_specs=[vmem] * whole_count,
        compiler_params=pltpu.CompilerParams(vmem_limit_bytes=24 * 2**20),
        name="combine",
    )(*parts)
    arrived = exchange(whole * blk_count if shared else whole, ("blk",), (blk_count,))
    return pl.pallas_call(
        functools.partial(accumulate_kernel, sizes),
        out_shape=jax.ShapeDtypeStruct(g4_old.shape, jnp.float32),
        in_specs=[vmem] * (3 + len(arrived)),
        out_specs=vmem,
        scratch_shapes=[
            pltpu.VMEM((blk_count // 2, transfers // sublanes, sublanes, columns), jnp.int32),
            pltpu.VMEM((blk_count, 1, columns), jnp.float32),
            pltpu.VMEM((blk_count, transfers // sublanes, sublanes, lanes), jnp.float32),
        ],
        compiler_params=pltpu.CompilerParams(vmem_limit_bytes=48 * 2**20),
        name="accumulate",
    )(weights[None], transfer_table, g4_old, *arrived)


def solution(mesh):
    in_specs = (
        P(("grp", "blk"), "walk", None),
        P(("grp", "blk"), None),
        P("grp"),
        P(),
        P(("grp", "blk", "walk", "sub"), None, None),
    )
    out_specs = P(("grp", "blk", "walk", "sub"), None, None)
    return jax.shard_map(local, mesh=mesh, in_specs=in_specs, out_specs=out_specs, check_vma=False)
```

```python
import functools
import math

import jax
import jax.numpy as jnp
from jax import lax
from jax.experimental import pallas as pl
from jax.experimental.pallas import tpu as pltpu
from jax.sharding import PartitionSpec as P

TQ = 4
RSTEPS = 4


phase_period = 8192
quarter_bits = 11
lanes = 128
lane_bits = 7
sublanes = 8
code_limit = 32767.0
smallest_peak = 1e-30


def cos_sin(product):
    residue = product & (phase_period - 1)
    quarter = (residue + phase_period // 8) >> quarter_bits
    angle = (residue - (quarter << quarter_bits)).astype(jnp.float32) * (2.0 * math.pi / phase_period)
    square = angle * angle
    sine = angle + angle * square * (
        -1.0 / 6.0 + square * (1.0 / 120.0 + square * (-1.0 / 5040.0 + square * (1.0 / 362880.0)))
    )
    cosine = 1.0 + square * (
        -0.5 + square * (1.0 / 24.0 + square * (-1.0 / 720.0 + square * (1.0 / 40320.0)))
    )
    odd = (quarter & 1) == 1
    cosine_out = jnp.where(odd, sine, cosine)
    sine_out = jnp.where(odd, cosine, sine)
    cosine_out = jnp.where(((quarter + 1) & 2) == 2, -cosine_out, cosine_out)
    sine_out = jnp.where((quarter & 2) == 2, -sine_out, sine_out)
    return cosine_out, sine_out


def row_ids(count):
    return lax.broadcasted_iota(jnp.int32, (count, lanes), 0)


def split_by(ids, size):
    if size & (size - 1) == 0:
        return ids >> (size.bit_length() - 1), ids & (size - 1)
    return ids // size, ids % size


def table_kernel(vertex_ref, table_ref, left_ref):
    walk_index = lax.axis_index("walk")
    sub_index = lax.axis_index("sub")
    columns, vertices = table_ref.shape
    window_rows, rows_local = left_ref.shape
    own_start = pl.multiple_of(walk_index * rows_local, lanes)
    own_vertex = vertex_ref[:, pl.ds(own_start, rows_local)]
    cosine, sine = cos_sin(
        own_vertex * lax.broadcasted_iota(jnp.int32, (window_rows, rows_local), 0)
    )
    left_ref[...] = (cosine + sine).astype(jnp.bfloat16)

    blocks = columns // lanes
    half_blocks = blocks // 2
    coarse_rows = -(-max(half_blocks, 1) // sublanes) * sublanes
    middle_count = lanes // sublanes
    center = sub_index * columns + (blocks - 1) * (lanes // 2)

    @pl.loop(0, vertices // lanes)
    def _(step):
        here = pl.ds(pl.multiple_of(step * lanes, lanes), lanes)
        vertex = vertex_ref[:, here]
        cos_fine, sin_fine = cos_sin(vertex * (row_ids(sublanes) + center))
        cas_fine, cam_fine = cos_fine + sin_fine, cos_fine - sin_fine
        cos_middle, sin_middle = cos_sin(vertex * (row_ids(middle_count) * sublanes))
        cos_coarse, sin_coarse = cos_sin(
            vertex * ((blocks - 1 - 2 * row_ids(coarse_rows)) * (lanes // 2))
        )
        for pair in range(middle_count // 2):
            cas, cam = [], []
            for middle in (2 * pair, 2 * pair + 1):
                c, s = cos_middle[middle : middle + 1], sin_middle[middle : middle + 1]
                cas.append(c * cas_fine + s * cam_fine)
                cam.append(c * cam_fine - s * cas_fine)
            cas, cam = jnp.concatenate(cas, axis=0), jnp.concatenate(cam, axis=0)
            start = pair * 2 * sublanes
            for low in range(half_blocks):
                high = blocks - 1 - low
                even = cos_coarse[low : low + 1] * cas
                odd = sin_coarse[low : low + 1] * cam
                for block, value in ((low, even - odd), (high, even + odd)):
                    first = block * lanes + start
                    table_ref[first : first + 2 * sublanes, here] = value.astype(jnp.bfloat16)
            if blocks % 2:
                first = half_blocks * lanes + start
                table_ref[first : first + 2 * sublanes, here] = cas.astype(jnp.bfloat16)


def product_kernel(sizes, matrix_ref, table_ref, left_ref, sent_ref, weight_ref):
    blk_count, walk_count, sub_count, rows_own = sizes
    vertices = matrix_ref.shape[2]
    window_rows = left_ref.shape[0]

    ids = lax.broadcasted_iota(jnp.int32, (window_rows, window_rows), 0)
    ids, inner = split_by(ids, rows_own)
    ids, blk_part = split_by(ids, blk_count)
    walk_part, sub_part = split_by(ids, sub_count)
    window = ((blk_part * walk_count + walk_part) * sub_count + sub_part) * rows_own + inner
    order = jnp.where(
        window == lax.broadcasted_iota(jnp.int32, window.shape, 1), 1.0, 0.0
    ).astype(jnp.bfloat16)

    chunk = 4 * lanes
    for start in range(0, vertices, chunk):
        left_product = jnp.dot(
            left_ref[...], matrix_ref[0, :, start : start + chunk], preferred_element_type=jnp.float32
        )
        high = left_product.astype(jnp.bfloat16)
        weight_ref[:window_rows, start : start + chunk] = high
        weight_ref[window_rows:, start : start + chunk] = (
            left_product - high.astype(jnp.float32)
        ).astype(jnp.bfloat16)
    green = lax.dot_general(
        weight_ref[...], table_ref[...], (((1,), (1,)), ((), ())), preferred_element_type=jnp.float32
    )
    green = green[:window_rows] + green[window_rows:]
    high = green.astype(jnp.bfloat16)
    low = (green - high.astype(jnp.float32)).astype(jnp.bfloat16)
    green = jnp.dot(order, high, preferred_element_type=jnp.float32) + jnp.dot(
        order, low, preferred_element_type=jnp.float32
    )
    rows_each = blk_count * rows_own
    for place in range(walk_count * sub_count):
        sent_ref[place] = green[place * rows_each : (place + 1) * rows_each]


def combine_kernel(sizes, part_ref, whole_ref):
    blk_count, walk_count, sub_count, rows_own = sizes
    columns_part = part_ref.shape[2]
    for sub_part in range(sub_count):
        here = slice(sub_part * columns_part, (sub_part + 1) * columns_part)
        total = sum(part_ref[walk_part * sub_count + sub_part] for walk_part in range(walk_count))
        for blk_part in range(blk_count):
            rows = []
            for step in range(RSTEPS):
                place = (blk_part - step) % blk_count * rows_own
                rows.append(total[place : place + rows_own])
            whole_ref[blk_part, :, here] = jnp.concatenate(rows, axis=0).astype(whole_ref.dtype)


def accumulate_kernel(
    sizes, weights_ref, arrived_ref, transfer_ref, old_ref, new_ref, source_ref, left_ref, unit_ref
):
    blk_count, walk_count, sub_count, rows_own = sizes
    columns = transfer_ref.shape[1]
    transfers = transfer_ref.shape[0]
    steps_group = sublanes // TQ
    groups = transfers // sublanes
    tiles = columns // lanes
    pairs = blk_count // 2

    def spread(rows, own, group):
        parts = []
        for step in range(group * steps_group, (group + 1) * steps_group):
            row = rows[step * rows_own + own : step * rows_own + own + 1]
            parts.append(jnp.broadcast_to(row, (TQ, row.shape[1])))
        return jnp.concatenate(parts, axis=0)

    for own in range(rows_own):
        for pair in range(pairs):
            codes = []
            for walker in (2 * pair, 2 * pair + 1):
                rows = arrived_ref[walker].astype(jnp.float32)
                left_ref[walker] = rows[own : own + 1] * (
                    weights_ref[:, walker : walker + 1] * (1.0 / blk_count)
                )
                peak = jnp.maximum(jnp.max(jnp.abs(rows), axis=1, keepdims=True), smallest_peak)
                codes.append(jnp.floor(rows * (code_limit / peak) + 0.5).astype(jnp.int32))
                peak = jnp.broadcast_to(peak * (1.0 / code_limit), (peak.shape[0], lanes))
                for group in range(groups):
                    unit_ref[walker, group] = spread(peak, own, group)
            packed = (codes[0] << 16) | (codes[1] & 0xFFFF)
            for group in range(groups):
                source_ref[pair, group] = spread(packed, own, group)

        together = math.gcd(pairs, 2)

        @pl.loop(0, tiles, unroll=math.gcd(tiles, 4))
        def _(tile):
            here = pl.ds(pl.multiple_of(tile * lanes, lanes), lanes)
            for group in range(groups):
                rows = slice(group * sublanes, (group + 1) * sublanes)
                index = transfer_ref[rows, here]
                index_tile, index_lane = index >> lane_bits, index & (lanes - 1)

                def add_pairs(first, total):
                    picked = [jnp.zeros((sublanes, lanes), jnp.int32)] * together
                    for source in range(tiles):
                        match = index_tile == source
                        for k in range(together):
                            words = source_ref[
                                first + k, group, :, source * lanes : (source + 1) * lanes
                            ]
                            words = jnp.take_along_axis(
                                words, index_lane, axis=1, mode="promise_in_bounds"
                            )
                            picked[k] = jnp.where(match, words, picked[k])
                    for k in range(together):
                        for half, code in enumerate((picked[k] >> 16, (picked[k] << 16) >> 16)):
                            walker = (first + k) * 2 + half
                            total = total + left_ref[walker, :, here] * (
                                unit_ref[walker, group] * code.astype(jnp.float32)
                            )
                    return total

                total = old_ref[own, rows, here]
                if pairs == together:
                    total = add_pairs(0, total)
                else:
                    total = lax.fori_loop(
                        0, pairs // together, lambda i, t: add_pairs(i * together, t), total
                    )
                new_ref[own, rows, here] = total


def local(walker_mats, vertex, weights, transfer_table, g4_old):
    blk_count = lax.axis_size("blk")
    walk_count = lax.axis_size("walk")
    sub_count = lax.axis_size("sub")
    rows_local, vertices = walker_mats.shape[1:]
    rows_own, transfers, columns = g4_old.shape
    columns_local = columns // sub_count
    devices = blk_count * walk_count * sub_count
    sizes = (blk_count, walk_count, sub_count, rows_own)
    vmem = pl.BlockSpec(memory_space=pltpu.VMEM)
    table, left = pl.pallas_call(
        table_kernel,
        out_shape=[
            jax.ShapeDtypeStruct((columns_local, vertices), jnp.bfloat16),
            jax.ShapeDtypeStruct((devices * rows_own, rows_local), jnp.bfloat16),
        ],
        in_specs=[vmem],
        out_specs=[vmem] * 2,
        compiler_params=pltpu.CompilerParams(vmem_limit_bytes=24 * 2**20),
        cost_estimate=pl.CostEstimate(
            flops=2000 * columns_local * vertices,
            bytes_accessed=6 * columns_local * vertices,
            transcendentals=0,
        ),
        name="table",
    )(vertex)
    sent = pl.pallas_call(
        functools.partial(product_kernel, sizes),
        out_shape=jax.ShapeDtypeStruct(
            (walk_count * sub_count, blk_count * rows_own, columns_local), jnp.float32
        ),
        in_specs=[vmem] * 3,
        out_specs=vmem,
        scratch_shapes=[pltpu.VMEM((2 * devices * rows_own, vertices), jnp.bfloat16)],
        compiler_params=pltpu.CompilerParams(vmem_limit_bytes=24 * 2**20),
        name="product",
    )(walker_mats, table, left)
    parts = lax.all_to_all(sent, ("walk", "sub"), split_axis=0, concat_axis=0, tiled=True)
    whole = pl.pallas_call(
        functools.partial(combine_kernel, sizes),
        out_shape=jax.ShapeDtypeStruct((blk_count, RSTEPS * rows_own, columns), jnp.bfloat16),
        in_specs=[vmem],
        out_specs=vmem,
        compiler_params=pltpu.CompilerParams(vmem_limit_bytes=24 * 2**20),
        name="combine",
    )(parts)
    arrived = lax.all_to_all(whole, "blk", split_axis=0, concat_axis=0, tiled=True)
    return pl.pallas_call(
        functools.partial(accumulate_kernel, sizes),
        out_shape=jax.ShapeDtypeStruct(g4_old.shape, jnp.float32),
        in_specs=[vmem] * 4,
        out_specs=vmem,
        scratch_shapes=[
            pltpu.VMEM((blk_count // 2, transfers // sublanes, sublanes, columns), jnp.int32),
            pltpu.VMEM((blk_count, 1, columns), jnp.float32),
            pltpu.VMEM((blk_count, transfers // sublanes, sublanes, lanes), jnp.float32),
        ],
        compiler_params=pltpu.CompilerParams(vmem_limit_bytes=48 * 2**20),
        name="accumulate",
    )(weights[None], arrived, transfer_table, g4_old)


def solution(mesh):
    in_specs = (
        P(("grp", "blk"), "walk", None),
        P(("grp", "blk"), None),
        P("grp"),
        P(),
        P(("grp", "blk", "walk", "sub"), None, None),
    )
    out_specs = P(("grp", "blk", "walk", "sub"), None, None)
    return jax.shard_map(local, mesh=mesh, in_specs=in_specs, out_specs=out_specs, check_vma=False)
```

```python
import functools
import itertools
import math

import jax
import jax.numpy as jnp
from jax import lax
from jax.experimental import pallas as pl
from jax.experimental.pallas import tpu as pltpu
from jax.sharding import PartitionSpec as P

TQ = 4
RSTEPS = 4


phase_period = 8192
quarter_bits = 11
lanes = 128
lane_bits = 7
sublanes = 8
code_limit = 32767.0
smallest_peak = 1e-30


def toward(index, distance, count):
    if count & (count - 1) == 0:
        return index ^ distance
    return (index + distance) % count


def back(index, distance, count):
    if count & (count - 1) == 0:
        return index ^ distance
    return (index + count - distance) % count


def cos_sin(product):
    residue = product & (phase_period - 1)
    quarter = (residue + phase_period // 8) >> quarter_bits
    angle = (residue - (quarter << quarter_bits)).astype(jnp.float32) * (2.0 * math.pi / phase_period)
    square = angle * angle
    sine = angle + angle * square * (
        -1.0 / 6.0 + square * (1.0 / 120.0 + square * (-1.0 / 5040.0 + square * (1.0 / 362880.0)))
    )
    cosine = 1.0 + square * (
        -0.5 + square * (1.0 / 24.0 + square * (-1.0 / 720.0 + square * (1.0 / 40320.0)))
    )
    odd = (quarter & 1) == 1
    cosine_out = jnp.where(odd, sine, cosine)
    sine_out = jnp.where(odd, cosine, sine)
    cosine_out = jnp.where(((quarter + 1) & 2) == 2, -cosine_out, cosine_out)
    sine_out = jnp.where((quarter & 2) == 2, -sine_out, sine_out)
    return cosine_out, sine_out


def row_ids(count):
    return lax.broadcasted_iota(jnp.int32, (count, lanes), 0)


def split_by(ids, size):
    if size & (size - 1) == 0:
        return ids >> (size.bit_length() - 1), ids & (size - 1)
    return ids // size, ids % size


def table_kernel(vertex_ref, table_ref, left_ref):
    walk_index = lax.axis_index("walk")
    sub_index = lax.axis_index("sub")
    columns, vertices = table_ref.shape
    window_rows, rows_local = left_ref.shape
    own_start = pl.multiple_of(walk_index * rows_local, lanes)
    for start in range(0, rows_local, lanes):
        own_vertex = vertex_ref[:, pl.ds(own_start + start, lanes)]
        cosine, sine = cos_sin(own_vertex * row_ids(window_rows))
        left_ref[:, start : start + lanes] = (cosine + sine).astype(jnp.bfloat16)

    blocks = columns // lanes
    half_blocks = blocks // 2
    coarse_rows = -(-max(half_blocks, 1) // sublanes) * sublanes
    middle_count = lanes // sublanes
    center = sub_index * columns + (blocks - 1) * (lanes // 2)

    def angles(step):
        vertex = vertex_ref[:, pl.ds(pl.multiple_of(step * lanes, lanes), lanes)]
        cosine, sine = cos_sin(vertex * (row_ids(sublanes) + center))
        return (
            cosine + sine,
            cosine - sine,
            *cos_sin(vertex * (row_ids(middle_count) * sublanes)),
            *cos_sin(vertex * ((blocks - 1 - 2 * row_ids(coarse_rows)) * (lanes // 2))),
        )

    def table_step(step, carried):
        following = angles(jnp.minimum(step + 1, steps - 1))
        cas_fine, cam_fine, cos_middle, sin_middle, cos_coarse, sin_coarse = carried
        here = pl.ds(pl.multiple_of(step * lanes, lanes), lanes)
        for pair in range(middle_count // 2):
            cas, cam = [], []
            for middle in (2 * pair, 2 * pair + 1):
                c, s = cos_middle[middle : middle + 1], sin_middle[middle : middle + 1]
                cas.append(c * cas_fine + s * cam_fine)
                cam.append(c * cam_fine - s * cas_fine)
            cas, cam = jnp.concatenate(cas, axis=0), jnp.concatenate(cam, axis=0)
            start = pair * 2 * sublanes
            for low in range(half_blocks):
                high = blocks - 1 - low
                even = cos_coarse[low : low + 1] * cas
                odd = sin_coarse[low : low + 1] * cam
                for block, value in ((low, even - odd), (high, even + odd)):
                    first = block * lanes + start
                    table_ref[first : first + 2 * sublanes, here] = value.astype(jnp.bfloat16)
            if blocks % 2:
                first = half_blocks * lanes + start
                table_ref[first : first + 2 * sublanes, here] = cas.astype(jnp.bfloat16)
        return following

    steps = vertices // lanes
    lax.fori_loop(0, steps, table_step, angles(0))


def product_kernel(sizes, matrix_ref, table_ref, left_ref, *rest):
    *sent_refs, weight_ref = rest
    blk_count, walk_count, sub_count, rows_own = sizes
    walk_index = lax.axis_index("walk")
    sub_index = lax.axis_index("sub")
    vertices = matrix_ref.shape[2]
    window_rows = left_ref.shape[0]

    ids = lax.broadcasted_iota(jnp.int32, (window_rows, window_rows), 0)
    ids, inner = split_by(ids, rows_own)
    ids, blk_part = split_by(ids, blk_count)
    walk_part, sub_part = split_by(ids, sub_count)
    sub_part = toward(sub_index, sub_part, sub_count)
    walk_part = toward(walk_index, walk_part, walk_count)
    window = ((blk_part * walk_count + walk_part) * sub_count + sub_part) * rows_own + inner
    order = jnp.where(
        window == lax.broadcasted_iota(jnp.int32, window.shape, 1), 1.0, 0.0
    ).astype(jnp.bfloat16)

    chunk = 4 * lanes
    for start in range(0, vertices, chunk):
        left_product = jnp.dot(
            left_ref[...], matrix_ref[0, :, start : start + chunk], preferred_element_type=jnp.float32
        )
        high = left_product.astype(jnp.bfloat16)
        weight_ref[:window_rows, start : start + chunk] = high
        weight_ref[window_rows:, start : start + chunk] = (
            left_product - high.astype(jnp.float32)
        ).astype(jnp.bfloat16)
    green = lax.dot_general(
        weight_ref[...], table_ref[...], (((1,), (1,)), ((), ())), preferred_element_type=jnp.float32
    )
    green = green[:window_rows] + green[window_rows:]
    high = green.astype(jnp.bfloat16)
    low = (green - high.astype(jnp.float32)).astype(jnp.bfloat16)
    green = jnp.dot(order, high, preferred_element_type=jnp.float32) + jnp.dot(
        order, low, preferred_element_type=jnp.float32
    )
    rows_each = blk_count * rows_own
    for place, sent_ref in enumerate(sent_refs):
        sent_ref[...] = green[place * rows_each : (place + 1) * rows_each]


def pick_rows(rows, wanted):
    ids = lax.broadcasted_iota(jnp.int32, (wanted.shape[0], rows.shape[0]), 1)
    chosen = jnp.where(ids == wanted, 1.0, 0.0).astype(jnp.bfloat16)
    return jnp.dot(chosen, rows, preferred_element_type=jnp.float32)


def combine_kernel(sizes, *refs):
    blk_count, walk_count, sub_count, rows_own = sizes
    blk_index = lax.axis_index("blk")
    sub_index = lax.axis_index("sub")
    part_refs, whole_refs = refs[: walk_count * sub_count], refs[walk_count * sub_count :]
    columns_part = part_refs[0].shape[1]
    for distance in range(sub_count):
        sub_part = back(sub_index, distance, sub_count)
        here = pl.ds(pl.multiple_of(sub_part * columns_part, lanes), columns_part)
        total = sum(
            part_refs[walk_part * sub_count + distance][...] for walk_part in range(walk_count)
        ).astype(jnp.bfloat16)
        if len(whole_refs) == 1:
            whole_refs[0][:, here] = total
            continue
        for place, whole_ref in enumerate(whole_refs):
            ids = lax.broadcasted_iota(jnp.int32, (whole_ref.shape[0], 1), 0)
            step, inner = split_by(ids, rows_own)
            _, blk_part = split_by(toward(blk_index, place, blk_count) + RSTEPS * blk_count - step, blk_count)
            whole_ref[:, here] = pick_rows(total, blk_part * rows_own + inner).astype(whole_ref.dtype)


def accumulate_kernel(sizes, weights_ref, transfer_ref, old_ref, *rest):
    *arrived_refs, new_ref, source_ref, left_ref, unit_ref = rest
    blk_count, walk_count, sub_count, rows_own = sizes
    blk_index = lax.axis_index("blk")
    columns = transfer_ref.shape[1]
    transfers = transfer_ref.shape[0]
    groups = transfers // sublanes
    tiles = columns // lanes
    pairs = blk_count // 2
    weights = weights_ref[...] * (1.0 / blk_count)
    walker_ids = lax.broadcasted_iota(jnp.int32, weights.shape, 1)

    ids = lax.broadcasted_iota(jnp.int32, (transfers, 1), 0)
    step, _ = split_by(ids, TQ)
    if arrived_refs[0].shape[0] == blk_count * rows_own:
        _, step = split_by(blk_index + RSTEPS * blk_count - step, blk_count)

    for own in range(rows_own):
        for pair in range(pairs):
            codes = []
            for distance in (2 * pair, 2 * pair + 1):
                rows = pick_rows(arrived_refs[distance][...], step * rows_own + own)
                walker = back(blk_index, distance, blk_count)
                weight = jnp.sum(jnp.where(walker_ids == walker, weights, 0.0), axis=1, keepdims=True)
                left_ref[distance] = rows[:1] * weight
                peak = jnp.maximum(jnp.max(jnp.abs(rows), axis=1, keepdims=True), smallest_peak)
                codes.append(jnp.floor(rows * (code_limit / peak) + 0.5).astype(jnp.int32))
                unit_ref[distance] = jnp.broadcast_to(peak * (1.0 / code_limit), (transfers, lanes))
            source_ref[pair] = (codes[0] << 16) | (codes[1] & 0xFFFF)

        together = math.gcd(pairs, 2)

        @pl.loop(0, tiles, unroll=math.gcd(tiles, 4))
        def _(tile):
            here = pl.ds(pl.multiple_of(tile * lanes, lanes), lanes)
            for group in range(groups):
                rows = slice(group * sublanes, (group + 1) * sublanes)
                index = transfer_ref[rows, here]
                index_tile, index_lane = index >> lane_bits, index & (lanes - 1)

                def add_pairs(first, total):
                    picked = [jnp.zeros((sublanes, lanes), jnp.int32)] * together
                    for source in range(tiles):
                        match = index_tile == source
                        for k in range(together):
                            words = source_ref[
                                first + k, rows, source * lanes : (source + 1) * lanes
                            ]
                            words = jnp.take_along_axis(
                                words, index_lane, axis=1, mode="promise_in_bounds"
                            )
                            picked[k] = jnp.where(match, words, picked[k])
                    for k in range(together):
                        for half, code in enumerate((picked[k] >> 16, (picked[k] << 16) >> 16)):
                            walker = (first + k) * 2 + half
                            total = total + left_ref[walker, :, here] * (
                                unit_ref[walker, rows] * code.astype(jnp.float32)
                            )
                    return total

                total = old_ref[own, rows, here]
                if pairs == together:
                    total = add_pairs(0, total)
                else:
                    total = lax.fori_loop(
                        0, pairs // together, lambda i, t: add_pairs(i * together, t), total
                    )
                new_ref[own, rows, here] = total


def exchange(pieces, axes, counts):
    positions = list(itertools.product(*map(range, counts)))
    place = {position: i for i, position in enumerate(positions)}
    arrived = [pieces[0]]
    for distance, piece in list(zip(positions, pieces))[1:]:
        route = [
            (place[position], place[tuple(map(toward, position, distance, counts))])
            for position in positions
        ]
        arrived.append(lax.ppermute(piece, axes, route))
    return arrived


def local(walker_mats, vertex, weights, transfer_table, g4_old):
    blk_count = lax.axis_size("blk")
    walk_count = lax.axis_size("walk")
    sub_count = lax.axis_size("sub")
    rows_local, vertices = walker_mats.shape[1:]
    rows_own, transfers, columns = g4_old.shape
    columns_local = columns // sub_count
    devices = blk_count * walk_count * sub_count
    sizes = (blk_count, walk_count, sub_count, rows_own)
    vmem = pl.BlockSpec(memory_space=pltpu.VMEM)
    table, left = pl.pallas_call(
        table_kernel,
        out_shape=[
            jax.ShapeDtypeStruct((columns_local, vertices), jnp.bfloat16),
            jax.ShapeDtypeStruct((devices * rows_own, rows_local), jnp.bfloat16),
        ],
        in_specs=[vmem],
        out_specs=[vmem] * 2,
        compiler_params=pltpu.CompilerParams(vmem_limit_bytes=24 * 2**20),
        cost_estimate=pl.CostEstimate(
            flops=2000 * columns_local * vertices,
            bytes_accessed=6 * columns_local * vertices,
            transcendentals=0,
        ),
        name="table",
    )(vertex)
    sent = pl.pallas_call(
        functools.partial(product_kernel, sizes),
        out_shape=[jax.ShapeDtypeStruct((blk_count * rows_own, columns_local), jnp.float32)]
        * (walk_count * sub_count),
        in_specs=[vmem] * 3,
        out_specs=[vmem] * (walk_count * sub_count),
        scratch_shapes=[pltpu.VMEM((2 * devices * rows_own, vertices), jnp.bfloat16)],
        compiler_params=pltpu.CompilerParams(vmem_limit_bytes=24 * 2**20),
        name="product",
    )(walker_mats, table, left)
    parts = exchange(sent, ("walk", "sub"), (walk_count, sub_count))
    shared = blk_count <= RSTEPS
    rows_each = (blk_count if shared else RSTEPS) * rows_own
    whole_count = 1 if shared else blk_count
    whole = pl.pallas_call(
        functools.partial(combine_kernel, sizes),
        out_shape=[jax.ShapeDtypeStruct((rows_each, columns), jnp.bfloat16)] * whole_count,
        in_specs=[vmem] * len(parts),
        out_specs=[vmem] * whole_count,
        compiler_params=pltpu.CompilerParams(vmem_limit_bytes=24 * 2**20),
        name="combine",
    )(*parts)
    arrived = exchange(whole * blk_count if shared else whole, ("blk",), (blk_count,))
    return pl.pallas_call(
        functools.partial(accumulate_kernel, sizes),
        out_shape=jax.ShapeDtypeStruct(g4_old.shape, jnp.float32),
        in_specs=[vmem] * (3 + len(arrived)),
        out_specs=vmem,
        scratch_shapes=[
            pltpu.VMEM((blk_count // 2, transfers, columns), jnp.int32),
            pltpu.VMEM((blk_count, 1, columns), jnp.float32),
            pltpu.VMEM((blk_count, transfers, lanes), jnp.float32),
        ],
        compiler_params=pltpu.CompilerParams(vmem_limit_bytes=48 * 2**20),
        name="accumulate",
    )(weights[None], transfer_table, g4_old, *arrived)


def solution(mesh):
    in_specs = (
        P(("grp", "blk"), "walk", None),
        P(("grp", "blk"), None),
        P("grp"),
        P(),
        P(("grp", "blk", "walk", "sub"), None, None),
    )
    out_specs = P(("grp", "blk", "walk", "sub"), None, None)
    return jax.shard_map(local, mesh=mesh, in_specs=in_specs, out_specs=out_specs, check_vma=False)
```

```python
import functools
import itertools
import math

import jax
import jax.numpy as jnp
from jax import lax
from jax.experimental import pallas as pl
from jax.experimental.pallas import tpu as pltpu
from jax.sharding import PartitionSpec as P

TQ = 4
RSTEPS = 4


phase_period = 8192
quarter_bits = 11
lanes = 128
lane_bits = 7
sublanes = 8
code_limit = 32767.0
smallest_peak = 1e-30


def toward(index, distance, count):
    if count & (count - 1) == 0:
        return index ^ distance
    return (index + distance) % count


def back(index, distance, count):
    if count & (count - 1) == 0:
        return index ^ distance
    return (index + count - distance) % count


def cos_sin(product):
    residue = product & (phase_period - 1)
    quarter = (residue + phase_period // 8) >> quarter_bits
    angle = (residue - (quarter << quarter_bits)).astype(jnp.float32) * (2.0 * math.pi / phase_period)
    square = angle * angle
    sine = angle + angle * square * (
        -1.0 / 6.0 + square * (1.0 / 120.0 + square * (-1.0 / 5040.0 + square * (1.0 / 362880.0)))
    )
    cosine = 1.0 + square * (
        -0.5 + square * (1.0 / 24.0 + square * (-1.0 / 720.0 + square * (1.0 / 40320.0)))
    )
    odd = (quarter & 1) == 1
    cosine_out = jnp.where(odd, sine, cosine)
    sine_out = jnp.where(odd, cosine, sine)
    cosine_out = jnp.where(((quarter + 1) & 2) == 2, -cosine_out, cosine_out)
    sine_out = jnp.where((quarter & 2) == 2, -sine_out, sine_out)
    return cosine_out, sine_out


def row_ids(count):
    return lax.broadcasted_iota(jnp.int32, (count, lanes), 0)


def split_by(ids, size):
    if size & (size - 1) == 0:
        return ids >> (size.bit_length() - 1), ids & (size - 1)
    return ids // size, ids % size


def make_table(vertex_ref, table_ref, first, place, sub_index):
    columns = table_ref.shape[0]
    blocks = columns // lanes
    half_blocks = blocks // 2
    coarse_rows = -(-max(half_blocks, 1) // sublanes) * sublanes
    middle_count = lanes // sublanes
    center = sub_index * columns + (blocks - 1) * (lanes // 2)
    here = pl.ds(pl.multiple_of(place, lanes), lanes)
    vertex = vertex_ref[:, pl.ds(pl.multiple_of(first, lanes), lanes)]
    cosine, sine = cos_sin(vertex * (row_ids(sublanes) + center))
    cas_fine, cam_fine = cosine + sine, cosine - sine
    cos_middle, sin_middle = cos_sin(vertex * (row_ids(middle_count) * sublanes))
    cos_coarse, sin_coarse = cos_sin(
        vertex * ((blocks - 1 - 2 * row_ids(coarse_rows)) * (lanes // 2))
    )
    for pair in range(middle_count // 2):
        cas, cam = [], []
        for middle in (2 * pair, 2 * pair + 1):
            c, s = cos_middle[middle : middle + 1], sin_middle[middle : middle + 1]
            cas.append(c * cas_fine + s * cam_fine)
            cam.append(c * cam_fine - s * cas_fine)
        cas, cam = jnp.concatenate(cas, axis=0), jnp.concatenate(cam, axis=0)
        start = pair * 2 * sublanes
        for low in range(half_blocks):
            high = blocks - 1 - low
            even = cos_coarse[low : low + 1] * cas
            odd = sin_coarse[low : low + 1] * cam
            for block, value in ((low, even - odd), (high, even + odd)):
                row = block * lanes + start
                table_ref[row : row + 2 * sublanes, here] = value.astype(jnp.bfloat16)
        if blocks % 2:
            row = half_blocks * lanes + start
            table_ref[row : row + 2 * sublanes, here] = cas.astype(jnp.bfloat16)


def table_kernel(vertex_ref, table_ref, left_ref):
    walk_index = lax.axis_index("walk")
    sub_index = lax.axis_index("sub")
    window_rows, rows_local = left_ref.shape
    own_start = pl.multiple_of(walk_index * rows_local, lanes)
    for start in range(0, rows_local, lanes):
        own_vertex = vertex_ref[:, pl.ds(own_start + start, lanes)]
        cosine, sine = cos_sin(own_vertex * row_ids(window_rows))
        left_ref[:, start : start + lanes] = (cosine + sine).astype(jnp.bfloat16)

    @pl.loop(0, table_ref.shape[1] // lanes, unroll=2)
    def _(step):
        make_table(vertex_ref, table_ref, step * lanes, step * lanes, sub_index)


def product_kernel(sizes, matrix_ref, vertex_ref, first_table, left_ref, *rest):
    *sent_refs, second_table, weight_ref, total_ref = rest
    blk_count, walk_count, sub_count, rows_own = sizes
    walk_index = lax.axis_index("walk")
    sub_index = lax.axis_index("sub")
    vertices = matrix_ref.shape[2]
    half = first_table.shape[1]
    window_rows = left_ref.shape[0]

    ids = lax.broadcasted_iota(jnp.int32, (window_rows, window_rows), 0)
    ids, inner = split_by(ids, rows_own)
    ids, blk_part = split_by(ids, blk_count)
    walk_part, sub_part = split_by(ids, sub_count)
    sub_part = toward(sub_index, sub_part, sub_count)
    walk_part = toward(walk_index, walk_part, walk_count)
    window = ((blk_part * walk_count + walk_part) * sub_count + sub_part) * rows_own + inner
    order = jnp.where(
        window == lax.broadcasted_iota(jnp.int32, window.shape, 1), 1.0, 0.0
    ).astype(jnp.bfloat16)

    def table_product(here, table):
        return lax.dot_general(
            weight_ref[:, here], table, (((1,), (1,)), ((), ())), preferred_element_type=jnp.float32
        )

    chunk = 2 * lanes
    total_ref[...] = jnp.zeros_like(total_ref)

    @pl.loop(0, half // chunk)
    def _(step):
        for part in range(2):
            here = pl.ds(pl.multiple_of((2 * step + part) * chunk, chunk), chunk)
            left_product = jnp.dot(
                left_ref[...], matrix_ref[0, :, here], preferred_element_type=jnp.float32
            )
            high = left_product.astype(jnp.bfloat16)
            weight_ref[:window_rows, here] = high
            weight_ref[window_rows:, here] = (left_product - high.astype(jnp.float32)).astype(
                jnp.bfloat16
            )
        for part in range(2):
            place = step * chunk + part * lanes
            make_table(vertex_ref, second_table, half + place, place, sub_index)
        here = pl.ds(pl.multiple_of(step * chunk, chunk), chunk)
        total_ref[...] += table_product(here, first_table[:, here])

    green = total_ref[...] + table_product(slice(half, vertices), second_table[...])
    green = green[:window_rows] + green[window_rows:]
    high = green.astype(jnp.bfloat16)
    low = (green - high.astype(jnp.float32)).astype(jnp.bfloat16)
    green = jnp.dot(order, high, preferred_element_type=jnp.float32) + jnp.dot(
        order, low, preferred_element_type=jnp.float32
    )
    rows_each = blk_count * rows_own
    for place, sent_ref in enumerate(sent_refs):
        sent_ref[...] = green[place * rows_each : (place + 1) * rows_each]


def pick_rows(rows, wanted):
    ids = lax.broadcasted_iota(jnp.int32, (wanted.shape[0], rows.shape[0]), 1)
    chosen = jnp.where(ids == wanted, 1.0, 0.0).astype(jnp.bfloat16)
    return jnp.dot(chosen, rows, preferred_element_type=jnp.float32)


def combine_kernel(sizes, *refs):
    blk_count, walk_count, sub_count, rows_own = sizes
    blk_index = lax.axis_index("blk")
    sub_index = lax.axis_index("sub")
    part_refs, whole_refs = refs[: walk_count * sub_count], refs[walk_count * sub_count :]
    columns_part = part_refs[0].shape[1]
    for distance in range(sub_count):
        sub_part = back(sub_index, distance, sub_count)
        here = pl.ds(pl.multiple_of(sub_part * columns_part, lanes), columns_part)
        total = sum(
            part_refs[walk_part * sub_count + distance][...] for walk_part in range(walk_count)
        ).astype(jnp.bfloat16)
        if len(whole_refs) == 1:
            whole_refs[0][:, here] = total
            continue
        for place, whole_ref in enumerate(whole_refs):
            ids = lax.broadcasted_iota(jnp.int32, (whole_ref.shape[0], 1), 0)
            step, inner = split_by(ids, rows_own)
            _, blk_part = split_by(toward(blk_index, place, blk_count) + RSTEPS * blk_count - step, blk_count)
            whole_ref[:, here] = pick_rows(total, blk_part * rows_own + inner).astype(whole_ref.dtype)


def accumulate_kernel(sizes, weights_ref, transfer_ref, old_ref, *rest):
    *arrived_refs, new_ref, source_ref, left_ref, unit_ref = rest
    blk_count, walk_count, sub_count, rows_own = sizes
    blk_index = lax.axis_index("blk")
    columns = transfer_ref.shape[1]
    transfers = transfer_ref.shape[0]
    groups = transfers // sublanes
    tiles = columns // lanes
    pairs = blk_count // 2
    weights = weights_ref[...] * (1.0 / blk_count)
    walker_ids = lax.broadcasted_iota(jnp.int32, weights.shape, 1)

    ids = lax.broadcasted_iota(jnp.int32, (transfers, 1), 0)
    step, _ = split_by(ids, TQ)
    if arrived_refs[0].shape[0] == blk_count * rows_own:
        _, step = split_by(blk_index + RSTEPS * blk_count - step, blk_count)

    for own in range(rows_own):
        for pair in range(pairs):
            codes = []
            for distance in (2 * pair, 2 * pair + 1):
                rows = pick_rows(arrived_refs[distance][...], step * rows_own + own)
                walker = back(blk_index, distance, blk_count)
                weight = jnp.sum(jnp.where(walker_ids == walker, weights, 0.0), axis=1, keepdims=True)
                left_ref[distance] = rows[:1] * weight
                peak = jnp.maximum(jnp.max(jnp.abs(rows), axis=1, keepdims=True), smallest_peak)
                codes.append(jnp.floor(rows * (code_limit / peak) + 0.5).astype(jnp.int32))
                unit_ref[distance] = jnp.broadcast_to(peak * (1.0 / code_limit), (transfers, lanes))
            source_ref[pair] = (codes[0] << 16) | (codes[1] & 0xFFFF)

        together = math.gcd(pairs, 2)

        @pl.loop(0, tiles, unroll=math.gcd(tiles, 10))
        def _(tile):
            here = pl.ds(pl.multiple_of(tile * lanes, lanes), lanes)
            for group in range(groups):
                rows = slice(group * sublanes, (group + 1) * sublanes)
                index = transfer_ref[rows, here]
                index_tile, index_lane = index >> lane_bits, index & (lanes - 1)

                def add_pairs(first, total):
                    picked = [jnp.zeros((sublanes, lanes), jnp.int32)] * together
                    for source in range(tiles):
                        match = index_tile == source
                        for k in range(together):
                            words = source_ref[
                                first + k, rows, source * lanes : (source + 1) * lanes
                            ]
                            words = jnp.take_along_axis(
                                words, index_lane, axis=1, mode="promise_in_bounds"
                            )
                            picked[k] = jnp.where(match, words, picked[k])
                    for k in range(together):
                        for half, code in enumerate((picked[k] >> 16, (picked[k] << 16) >> 16)):
                            walker = (first + k) * 2 + half
                            total = total + left_ref[walker, :, here] * (
                                unit_ref[walker, rows] * code.astype(jnp.float32)
                            )
                    return total

                total = old_ref[own, rows, here]
                if pairs == together:
                    total = add_pairs(0, total)
                else:
                    total = lax.fori_loop(
                        0, pairs // together, lambda i, t: add_pairs(i * together, t), total
                    )
                new_ref[own, rows, here] = total


def exchange(pieces, axes, counts):
    positions = list(itertools.product(*map(range, counts)))
    place = {position: i for i, position in enumerate(positions)}
    arrived = [pieces[0]]
    for distance, piece in list(zip(positions, pieces))[1:]:
        route = [
            (place[position], place[tuple(map(toward, position, distance, counts))])
            for position in positions
        ]
        arrived.append(lax.ppermute(piece, axes, route))
    return arrived


def local(walker_mats, vertex, weights, transfer_table, g4_old):
    blk_count = lax.axis_size("blk")
    walk_count = lax.axis_size("walk")
    sub_count = lax.axis_size("sub")
    rows_local, vertices = walker_mats.shape[1:]
    rows_own, transfers, columns = g4_old.shape
    columns_local = columns // sub_count
    devices = blk_count * walk_count * sub_count
    sizes = (blk_count, walk_count, sub_count, rows_own)
    vmem = pl.BlockSpec(memory_space=pltpu.VMEM)
    half = vertices // 2
    table, left = pl.pallas_call(
        table_kernel,
        out_shape=[
            jax.ShapeDtypeStruct((columns_local, half), jnp.bfloat16),
            jax.ShapeDtypeStruct((devices * rows_own, rows_local), jnp.bfloat16),
        ],
        in_specs=[vmem],
        out_specs=[vmem] * 2,
        compiler_params=pltpu.CompilerParams(vmem_limit_bytes=24 * 2**20),
        cost_estimate=pl.CostEstimate(
            flops=2000 * columns_local * vertices,
            bytes_accessed=6 * columns_local * vertices,
            transcendentals=0,
        ),
        name="table",
    )(vertex)
    sent = pl.pallas_call(
        functools.partial(product_kernel, sizes),
        out_shape=[jax.ShapeDtypeStruct((blk_count * rows_own, columns_local), jnp.float32)]
        * (walk_count * sub_count),
        in_specs=[vmem] * 4,
        out_specs=[vmem] * (walk_count * sub_count),
        scratch_shapes=[
            pltpu.VMEM((columns_local, half), jnp.bfloat16),
            pltpu.VMEM((2 * devices * rows_own, vertices), jnp.bfloat16),
            pltpu.VMEM((2 * devices * rows_own, columns_local), jnp.float32),
        ],
        compiler_params=pltpu.CompilerParams(vmem_limit_bytes=24 * 2**20),
        name="product",
    )(walker_mats, vertex, table, left)
    parts = exchange(sent, ("walk", "sub"), (walk_count, sub_count))
    shared = blk_count <= RSTEPS
    rows_each = (blk_count if shared else RSTEPS) * rows_own
    whole_count = 1 if shared else blk_count
    whole = pl.pallas_call(
        functools.partial(combine_kernel, sizes),
        out_shape=[jax.ShapeDtypeStruct((rows_each, columns), jnp.bfloat16)] * whole_count,
        in_specs=[vmem] * len(parts),
        out_specs=[vmem] * whole_count,
        compiler_params=pltpu.CompilerParams(vmem_limit_bytes=24 * 2**20),
        name="combine",
    )(*parts)
    arrived = exchange(whole * blk_count if shared else whole, ("blk",), (blk_count,))
    return pl.pallas_call(
        functools.partial(accumulate_kernel, sizes),
        out_shape=jax.ShapeDtypeStruct(g4_old.shape, jnp.float32),
        in_specs=[vmem] * (3 + len(arrived)),
        out_specs=vmem,
        scratch_shapes=[
            pltpu.VMEM((blk_count // 2, transfers, columns), jnp.int32),
            pltpu.VMEM((blk_count, 1, columns), jnp.float32),
            pltpu.VMEM((blk_count, transfers, lanes), jnp.float32),
        ],
        compiler_params=pltpu.CompilerParams(vmem_limit_bytes=48 * 2**20),
        name="accumulate",
    )(weights[None], transfer_table, g4_old, *arrived)


def solution(mesh):
    in_specs = (
        P(("grp", "blk"), "walk", None),
        P(("grp", "blk"), None),
        P("grp"),
        P(),
        P(("grp", "blk", "walk", "sub"), None, None),
    )
    out_specs = P(("grp", "blk", "walk", "sub"), None, None)
    return jax.shard_map(local, mesh=mesh, in_specs=in_specs, out_specs=out_specs, check_vma=False)
```

```python
import functools
import itertools
import math

import jax
import jax.numpy as jnp
from jax import lax
from jax.experimental import pallas as pl
from jax.experimental.pallas import tpu as pltpu
from jax.sharding import PartitionSpec as P

TQ = 4
RSTEPS = 4


phase_period = 8192
quarter_bits = 11
lanes = 128
lane_bits = 7
sublanes = 8
code_limit = 32767.0
smallest_peak = 1e-30


def toward(index, distance, count):
    if count & (count - 1) == 0:
        return index ^ distance
    return (index + distance) % count


def back(index, distance, count):
    if count & (count - 1) == 0:
        return index ^ distance
    return (index + count - distance) % count


def cos_sin(product):
    residue = product & (phase_period - 1)
    quarter = (residue + phase_period // 8) >> quarter_bits
    angle = (residue - (quarter << quarter_bits)).astype(jnp.float32) * (2.0 * math.pi / phase_period)
    square = angle * angle
    sine = angle + angle * square * (
        -1.0 / 6.0 + square * (1.0 / 120.0 + square * (-1.0 / 5040.0 + square * (1.0 / 362880.0)))
    )
    cosine = 1.0 + square * (
        -0.5 + square * (1.0 / 24.0 + square * (-1.0 / 720.0 + square * (1.0 / 40320.0)))
    )
    odd = (quarter & 1) == 1
    cosine_out = jnp.where(odd, sine, cosine)
    sine_out = jnp.where(odd, cosine, sine)
    cosine_out = jnp.where(((quarter + 1) & 2) == 2, -cosine_out, cosine_out)
    sine_out = jnp.where((quarter & 2) == 2, -sine_out, sine_out)
    return cosine_out, sine_out


def row_ids(count):
    return lax.broadcasted_iota(jnp.int32, (count, lanes), 0)


def split_by(ids, size):
    if size & (size - 1) == 0:
        return ids >> (size.bit_length() - 1), ids & (size - 1)
    return ids // size, ids % size


def table_kernel(sizes, vertex_ref, table_ref, left_ref):
    blk_count, walk_count, sub_count, rows_own = sizes
    walk_index = lax.axis_index("walk")
    sub_index = lax.axis_index("sub")
    columns, vertices = table_ref.shape
    window_rows, rows_local = left_ref.shape

    ids, inner = split_by(row_ids(window_rows), rows_own)
    ids, blk_part = split_by(ids, blk_count)
    walk_part, sub_part = split_by(ids, sub_count)
    sub_part = toward(sub_index, sub_part, sub_count)
    walk_part = toward(walk_index, walk_part, walk_count)
    window = ((blk_part * walk_count + walk_part) * sub_count + sub_part) * rows_own + inner
    own_start = pl.multiple_of(walk_index * rows_local, lanes)
    for start in range(0, rows_local, lanes):
        own_vertex = vertex_ref[:, pl.ds(own_start + start, lanes)]
        cosine, sine = cos_sin(own_vertex * window)
        left_ref[:, start : start + lanes] = (cosine + sine).astype(jnp.bfloat16)

    blocks = columns // lanes
    half_blocks = blocks // 2
    coarse_rows = -(-max(half_blocks, 1) // sublanes) * sublanes
    middle_count = lanes // sublanes
    center = sub_index * columns + (blocks - 1) * (lanes // 2)

    def angles(step):
        vertex = vertex_ref[:, pl.ds(pl.multiple_of(step * lanes, lanes), lanes)]
        cosine, sine = cos_sin(vertex * (row_ids(sublanes) + center))
        return (
            cosine + sine,
            cosine - sine,
            *cos_sin(vertex * (row_ids(middle_count) * sublanes)),
            *cos_sin(vertex * ((blocks - 1 - 2 * row_ids(coarse_rows)) * (lanes // 2))),
        )

    def table_step(step, carried):
        following = angles(jnp.minimum(step + 1, steps - 1))
        cas_fine, cam_fine, cos_middle, sin_middle, cos_coarse, sin_coarse = carried
        here = pl.ds(pl.multiple_of(step * lanes, lanes), lanes)
        for pair in range(middle_count // 2):
            cas, cam = [], []
            for middle in (2 * pair, 2 * pair + 1):
                c, s = cos_middle[middle : middle + 1], sin_middle[middle : middle + 1]
                cas.append(c * cas_fine + s * cam_fine)
                cam.append(c * cam_fine - s * cas_fine)
            cas, cam = jnp.concatenate(cas, axis=0), jnp.concatenate(cam, axis=0)
            start = pair * 2 * sublanes
            for low in range(half_blocks):
                high = blocks - 1 - low
                even = cos_coarse[low : low + 1] * cas
                odd = sin_coarse[low : low + 1] * cam
                for block, value in ((low, even - odd), (high, even + odd)):
                    first = block * lanes + start
                    table_ref[first : first + 2 * sublanes, here] = value.astype(jnp.bfloat16)
            if blocks % 2:
                first = half_blocks * lanes + start
                table_ref[first : first + 2 * sublanes, here] = cas.astype(jnp.bfloat16)
        return following

    steps = vertices // lanes
    lax.fori_loop(0, steps, table_step, angles(0))


def product_kernel(sizes, matrix_ref, table_ref, left_ref, *rest):
    *sent_refs, weight_ref = rest
    blk_count, _, _, rows_own = sizes
    vertices = matrix_ref.shape[2]
    window_rows = left_ref.shape[0]

    chunk = 4 * lanes
    for start in range(0, vertices, chunk):
        left_product = jnp.dot(
            left_ref[...], matrix_ref[0, :, start : start + chunk], preferred_element_type=jnp.float32
        )
        high = left_product.astype(jnp.bfloat16)
        weight_ref[:window_rows, start : start + chunk] = high
        weight_ref[window_rows:, start : start + chunk] = (
            left_product - high.astype(jnp.float32)
        ).astype(jnp.bfloat16)
    green = lax.dot_general(
        weight_ref[...], table_ref[...], (((1,), (1,)), ((), ())), preferred_element_type=jnp.float32
    )
    green = green[:window_rows] + green[window_rows:]
    rows_each = blk_count * rows_own
    for place, sent_ref in enumerate(sent_refs):
        sent_ref[...] = green[place * rows_each : (place + 1) * rows_each]


def pick_rows(rows, wanted):
    ids = lax.broadcasted_iota(jnp.int32, (wanted.shape[0], rows.shape[0]), 1)
    chosen = jnp.where(ids == wanted, 1.0, 0.0).astype(jnp.bfloat16)
    return jnp.dot(chosen, rows, preferred_element_type=jnp.float32)


def combine_kernel(sizes, *refs):
    blk_count, walk_count, sub_count, rows_own = sizes
    blk_index = lax.axis_index("blk")
    sub_index = lax.axis_index("sub")
    part_refs, whole_refs = refs[: walk_count * sub_count], refs[walk_count * sub_count :]
    columns_part = part_refs[0].shape[1]
    for distance in range(sub_count):
        sub_part = back(sub_index, distance, sub_count)
        here = pl.ds(pl.multiple_of(sub_part * columns_part, lanes), columns_part)
        total = sum(
            part_refs[walk_part * sub_count + distance][...] for walk_part in range(walk_count)
        ).astype(jnp.bfloat16)
        if len(whole_refs) == 1:
            whole_refs[0][:, here] = total
            continue
        for place, whole_ref in enumerate(whole_refs):
            ids = lax.broadcasted_iota(jnp.int32, (whole_ref.shape[0], 1), 0)
            step, inner = split_by(ids, rows_own)
            _, blk_part = split_by(toward(blk_index, place, blk_count) + RSTEPS * blk_count - step, blk_count)
            whole_ref[:, here] = pick_rows(total, blk_part * rows_own + inner).astype(whole_ref.dtype)


def accumulate_kernel(sizes, distances, weights_ref, transfer_ref, old_ref, *rest):
    *arrived_refs, new_ref, source_ref, left_ref, unit_ref = rest
    blk_count, walk_count, sub_count, rows_own = sizes
    blk_index = lax.axis_index("blk")
    columns = transfer_ref.shape[1]
    transfers = transfer_ref.shape[0]
    groups = transfers // sublanes
    tiles = columns // lanes
    pairs = blk_count // 2
    weights = weights_ref[...] * (1.0 / blk_count)
    walker_ids = lax.broadcasted_iota(jnp.int32, weights.shape, 1)

    ids = lax.broadcasted_iota(jnp.int32, (transfers, 1), 0)
    step, _ = split_by(ids, TQ)
    if arrived_refs[0].shape[0] == blk_count * rows_own:
        _, step = split_by(blk_index + RSTEPS * blk_count - step, blk_count)

    for own in range(rows_own):
        for pair in range(pairs):
            codes = []
            for place in (2 * pair, 2 * pair + 1):
                rows = pick_rows(arrived_refs[place][...], step * rows_own + own)
                walker = back(blk_index, distances[place], blk_count)
                weight = jnp.sum(jnp.where(walker_ids == walker, weights, 0.0), axis=1, keepdims=True)
                left_ref[place] = rows[:1] * weight
                peak = jnp.maximum(jnp.max(jnp.abs(rows), axis=1, keepdims=True), smallest_peak)
                codes.append(jnp.floor(rows * (code_limit / peak) + 0.5).astype(jnp.int32))
                unit_ref[place] = jnp.broadcast_to(peak * (1.0 / code_limit), (transfers, lanes))
            source_ref[pair] = (codes[0] << 16) | (codes[1] & 0xFFFF)

        together = math.gcd(pairs, 2)

        @pl.loop(0, tiles, unroll=math.gcd(tiles, 10))
        def _(tile):
            here = pl.ds(pl.multiple_of(tile * lanes, lanes), lanes)
            for group in range(groups):
                rows = slice(group * sublanes, (group + 1) * sublanes)
                index = transfer_ref[rows, here]
                index_tile, index_lane = index >> lane_bits, index & (lanes - 1)

                def add_pairs(first, total):
                    picked = [jnp.zeros((sublanes, lanes), jnp.int32)] * together
                    for source in range(tiles):
                        match = index_tile == source
                        for k in range(together):
                            words = source_ref[
                                first + k, rows, source * lanes : (source + 1) * lanes
                            ]
                            words = jnp.take_along_axis(
                                words, index_lane, axis=1, mode="promise_in_bounds"
                            )
                            picked[k] = jnp.where(match, words, picked[k])
                    for k in range(together):
                        for half, code in enumerate((picked[k] >> 16, (picked[k] << 16) >> 16)):
                            walker = (first + k) * 2 + half
                            total = total + left_ref[walker, :, here] * (
                                unit_ref[walker, rows] * code.astype(jnp.float32)
                            )
                    return total

                total = old_ref[own, rows, here]
                if pairs == together:
                    total = add_pairs(0, total)
                else:
                    total = lax.fori_loop(
                        0, pairs // together, lambda i, t: add_pairs(i * together, t), total
                    )
                new_ref[own, rows, here] = total


def exchange(pieces, axes, counts):
    positions = list(itertools.product(*map(range, counts)))
    place = {position: i for i, position in enumerate(positions)}
    arrived = [pieces[0]] * len(positions)
    for i in range(1, len(positions)):
        route = [
            (place[position], place[tuple(map(toward, position, positions[i], counts))])
            for position in positions
        ]
        arrived[i] = lax.ppermute(pieces[i], axes, route)
    return arrived


def local(walker_mats, vertex, weights, transfer_table, g4_old):
    blk_count = lax.axis_size("blk")
    walk_count = lax.axis_size("walk")
    sub_count = lax.axis_size("sub")
    rows_local, vertices = walker_mats.shape[1:]
    rows_own, transfers, columns = g4_old.shape
    columns_local = columns // sub_count
    devices = blk_count * walk_count * sub_count
    sizes = (blk_count, walk_count, sub_count, rows_own)
    vmem = pl.BlockSpec(memory_space=pltpu.VMEM)
    table, left = pl.pallas_call(
        functools.partial(table_kernel, sizes),
        out_shape=[
            jax.ShapeDtypeStruct((columns_local, vertices), jnp.bfloat16),
            jax.ShapeDtypeStruct((devices * rows_own, rows_local), jnp.bfloat16),
        ],
        in_specs=[vmem],
        out_specs=[vmem] * 2,
        compiler_params=pltpu.CompilerParams(vmem_limit_bytes=24 * 2**20),
        cost_estimate=pl.CostEstimate(
            flops=2000 * columns_local * vertices,
            bytes_accessed=6 * columns_local * vertices,
            transcendentals=0,
        ),
        name="table",
    )(vertex)
    sent = pl.pallas_call(
        functools.partial(product_kernel, sizes),
        out_shape=[jax.ShapeDtypeStruct((blk_count * rows_own, columns_local), jnp.float32)]
        * (walk_count * sub_count),
        in_specs=[vmem] * 3,
        out_specs=[vmem] * (walk_count * sub_count),
        scratch_shapes=[pltpu.VMEM((2 * devices * rows_own, vertices), jnp.bfloat16)],
        compiler_params=pltpu.CompilerParams(vmem_limit_bytes=24 * 2**20),
        name="product",
    )(walker_mats, table, left)
    parts = exchange(sent, ("walk", "sub"), (walk_count, sub_count))
    shared = blk_count <= RSTEPS
    rows_each = (blk_count if shared else RSTEPS) * rows_own
    whole_count = 1 if shared else blk_count
    whole = pl.pallas_call(
        functools.partial(combine_kernel, sizes),
        out_shape=[jax.ShapeDtypeStruct((rows_each, columns), jnp.bfloat16)] * whole_count,
        in_specs=[vmem] * len(parts),
        out_specs=[vmem] * whole_count,
        compiler_params=pltpu.CompilerParams(vmem_limit_bytes=24 * 2**20),
        name="combine",
    )(*parts)
    arrived = exchange(whole * blk_count if shared else whole, ("blk",), (blk_count,))
    distances = [i ^ (i >> 1) for i in range(blk_count)]
    if sorted(distances) != list(range(blk_count)):
        distances = list(range(blk_count))
    arrived = [arrived[distance] for distance in distances]
    return pl.pallas_call(
        functools.partial(accumulate_kernel, sizes, distances),
        out_shape=jax.ShapeDtypeStruct(g4_old.shape, jnp.float32),
        in_specs=[vmem] * (3 + len(arrived)),
        out_specs=vmem,
        scratch_shapes=[
            pltpu.VMEM((blk_count // 2, transfers, columns), jnp.int32),
            pltpu.VMEM((blk_count, 1, columns), jnp.float32),
            pltpu.VMEM((blk_count, transfers, lanes), jnp.float32),
        ],
        compiler_params=pltpu.CompilerParams(vmem_limit_bytes=48 * 2**20),
        name="accumulate",
    )(weights[None], transfer_table, g4_old, *arrived)


def solution(mesh):
    in_specs = (
        P(("grp", "blk"), "walk", None),
        P(("grp", "blk"), None),
        P("grp"),
        P(),
        P(("grp", "blk", "walk", "sub"), None, None),
    )
    out_specs = P(("grp", "blk", "walk", "sub"), None, None)
    return jax.shard_map(local, mesh=mesh, in_specs=in_specs, out_specs=out_specs, check_vma=False)
```

```python
import functools
import itertools
import math

import jax
import jax.numpy as jnp
from jax import lax
from jax.experimental import pallas as pl
from jax.experimental.pallas import tpu as pltpu
from jax.sharding import PartitionSpec as P

TQ = 4
RSTEPS = 4


phase_period = 8192
quarter_bits = 11
lanes = 128
lane_bits = 7
sublanes = 8
code_limit = 32767.0
smallest_peak = 1e-30


def toward(index, distance, count):
    if count & (count - 1) == 0:
        return index ^ distance
    return (index + distance) % count


def back(index, distance, count):
    if count & (count - 1) == 0:
        return index ^ distance
    return (index + count - distance) % count


def cos_sin(product):
    residue = product & (phase_period - 1)
    quarter = (residue + phase_period // 8) >> quarter_bits
    angle = (residue - (quarter << quarter_bits)).astype(jnp.float32) * (2.0 * math.pi / phase_period)
    square = angle * angle
    sine = angle + angle * square * (
        -1.0 / 6.0 + square * (1.0 / 120.0 + square * (-1.0 / 5040.0 + square * (1.0 / 362880.0)))
    )
    cosine = 1.0 + square * (
        -0.5 + square * (1.0 / 24.0 + square * (-1.0 / 720.0 + square * (1.0 / 40320.0)))
    )
    odd = (quarter & 1) == 1
    cosine_out = jnp.where(odd, sine, cosine)
    sine_out = jnp.where(odd, cosine, sine)
    cosine_out = jnp.where(((quarter + 1) & 2) == 2, -cosine_out, cosine_out)
    sine_out = jnp.where((quarter & 2) == 2, -sine_out, sine_out)
    return cosine_out, sine_out


def row_ids(count):
    return lax.broadcasted_iota(jnp.int32, (count, lanes), 0)


def split_by(ids, size):
    if size & (size - 1) == 0:
        return ids >> (size.bit_length() - 1), ids & (size - 1)
    return ids // size, ids % size


def table_kernel(sizes, vertex_ref, table_ref, left_ref):
    blk_count, walk_count, sub_count, rows_own = sizes
    walk_index = lax.axis_index("walk")
    sub_index = lax.axis_index("sub")
    columns, vertices = table_ref.shape
    window_rows, rows_local = left_ref.shape

    ids, inner = split_by(row_ids(window_rows), rows_own)
    ids, blk_part = split_by(ids, blk_count)
    walk_part, sub_part = split_by(ids, sub_count)
    sub_part = toward(sub_index, sub_part, sub_count)
    walk_part = toward(walk_index, walk_part, walk_count)
    window = ((blk_part * walk_count + walk_part) * sub_count + sub_part) * rows_own + inner
    own_start = pl.multiple_of(walk_index * rows_local, lanes)
    for start in range(0, rows_local, lanes):
        own_vertex = vertex_ref[:, pl.ds(own_start + start, lanes)]
        cosine, sine = cos_sin(own_vertex * window)
        left_ref[:, start : start + lanes] = (cosine + sine).astype(jnp.bfloat16)

    blocks = columns // lanes
    half_blocks = blocks // 2
    coarse_rows = -(-max(half_blocks, 1) // sublanes) * sublanes
    middle_count = lanes // sublanes
    center = sub_index * columns + (blocks - 1) * (lanes // 2)

    def angles(step):
        vertex = vertex_ref[:, pl.ds(pl.multiple_of(step * lanes, lanes), lanes)]
        cosine, sine = cos_sin(vertex * (row_ids(sublanes) + center))
        return (
            cosine + sine,
            cosine - sine,
            *cos_sin(vertex * (row_ids(middle_count) * sublanes)),
            *cos_sin(vertex * ((blocks - 1 - 2 * row_ids(coarse_rows)) * (lanes // 2))),
        )

    def table_step(step, carried):
        following = angles(jnp.minimum(step + 1, steps - 1))
        cas_fine, cam_fine, cos_middle, sin_middle, cos_coarse, sin_coarse = carried
        here = pl.ds(pl.multiple_of(step * lanes, lanes), lanes)
        for pair in range(middle_count // 2):
            cas, cam = [], []
            for middle in (2 * pair, 2 * pair + 1):
                c, s = cos_middle[middle : middle + 1], sin_middle[middle : middle + 1]
                cas.append(c * cas_fine + s * cam_fine)
                cam.append(c * cam_fine - s * cas_fine)
            cas, cam = jnp.concatenate(cas, axis=0), jnp.concatenate(cam, axis=0)
            start = pair * 2 * sublanes
            for low in range(half_blocks):
                high = blocks - 1 - low
                even = cos_coarse[low : low + 1] * cas
                odd = sin_coarse[low : low + 1] * cam
                for block, value in ((low, even - odd), (high, even + odd)):
                    first = block * lanes + start
                    table_ref[first : first + 2 * sublanes, here] = value.astype(jnp.bfloat16)
            if blocks % 2:
                first = half_blocks * lanes + start
                table_ref[first : first + 2 * sublanes, here] = cas.astype(jnp.bfloat16)
        return following

    steps = vertices // lanes
    lax.fori_loop(0, steps, table_step, angles(0))


def product_kernel(sizes, matrix_ref, table_ref, left_ref, *rest):
    *sent_refs, weight_ref = rest
    blk_count, _, _, rows_own = sizes
    vertices = matrix_ref.shape[2]
    window_rows = left_ref.shape[0]

    chunk = 4 * lanes
    for start in range(0, vertices, chunk):
        left_product = jnp.dot(
            left_ref[...], matrix_ref[0, :, start : start + chunk], preferred_element_type=jnp.float32
        )
        high = left_product.astype(jnp.bfloat16)
        weight_ref[:window_rows, start : start + chunk] = high
        weight_ref[window_rows:, start : start + chunk] = (
            left_product - high.astype(jnp.float32)
        ).astype(jnp.bfloat16)
    green = lax.dot_general(
        weight_ref[...], table_ref[...], (((1,), (1,)), ((), ())), preferred_element_type=jnp.float32
    )
    green = green[:window_rows] + green[window_rows:]
    rows_each = blk_count * rows_own
    for place, sent_ref in enumerate(sent_refs):
        sent_ref[...] = green[place * rows_each : (place + 1) * rows_each]


def pick_rows(rows, wanted):
    ids = lax.broadcasted_iota(jnp.int32, (wanted.shape[0], rows.shape[0]), 1)
    chosen = jnp.where(ids == wanted, 1.0, 0.0).astype(jnp.bfloat16)
    return jnp.dot(chosen, rows, preferred_element_type=jnp.float32)


def combine_kernel(sizes, *refs):
    blk_count, walk_count, sub_count, rows_own = sizes
    blk_index = lax.axis_index("blk")
    sub_index = lax.axis_index("sub")
    part_refs, whole_refs = refs[: walk_count * sub_count], refs[walk_count * sub_count :]
    columns_part = part_refs[0].shape[1]
    for distance in range(sub_count):
        sub_part = back(sub_index, distance, sub_count)
        here = pl.ds(pl.multiple_of(sub_part * columns_part, lanes), columns_part)
        total = sum(
            part_refs[walk_part * sub_count + distance][...] for walk_part in range(walk_count)
        ).astype(jnp.bfloat16)
        if len(whole_refs) == 1:
            whole_refs[0][:, here] = total
            continue
        for place, whole_ref in enumerate(whole_refs):
            ids = lax.broadcasted_iota(jnp.int32, (whole_ref.shape[0], 1), 0)
            step, inner = split_by(ids, rows_own)
            _, blk_part = split_by(toward(blk_index, place, blk_count) + RSTEPS * blk_count - step, blk_count)
            whole_ref[:, here] = pick_rows(total, blk_part * rows_own + inner).astype(whole_ref.dtype)


def accumulate_kernel(sizes, distances, weights_ref, transfer_ref, old_ref, *rest):
    *arrived_refs, new_ref, source_ref, left_ref, unit_ref = rest
    blk_count, walk_count, sub_count, rows_own = sizes
    blk_index = lax.axis_index("blk")
    columns = transfer_ref.shape[1]
    transfers = transfer_ref.shape[0]
    groups = transfers // sublanes
    tiles = columns // lanes
    pairs = len(distances) // 2
    weights = weights_ref[...] * (1.0 / blk_count)
    walker_ids = lax.broadcasted_iota(jnp.int32, weights.shape, 1)

    ids = lax.broadcasted_iota(jnp.int32, (transfers, 1), 0)
    step, _ = split_by(ids, TQ)
    if arrived_refs[0].shape[0] == blk_count * rows_own:
        _, step = split_by(blk_index + RSTEPS * blk_count - step, blk_count)

    for own in range(rows_own):
        for pair in range(pairs):
            codes = []
            for place in (2 * pair, 2 * pair + 1):
                rows = pick_rows(arrived_refs[place][...], step * rows_own + own)
                walker = back(blk_index, distances[place], blk_count)
                weight = jnp.sum(jnp.where(walker_ids == walker, weights, 0.0), axis=1, keepdims=True)
                left_ref[place] = rows[:1] * weight
                peak = jnp.maximum(jnp.max(jnp.abs(rows), axis=1, keepdims=True), smallest_peak)
                codes.append(jnp.floor(rows * (code_limit / peak) + 0.5).astype(jnp.int32))
                unit_ref[place] = jnp.broadcast_to(peak * (1.0 / code_limit), (transfers, lanes))
            source_ref[pair] = (codes[0] << 16) | (codes[1] & 0xFFFF)

        together = math.gcd(pairs, 2)

        @pl.loop(0, tiles, unroll=math.gcd(tiles, 10))
        def _(tile):
            here = pl.ds(pl.multiple_of(tile * lanes, lanes), lanes)
            for group in range(groups):
                rows = slice(group * sublanes, (group + 1) * sublanes)
                index = transfer_ref[rows, here]
                index_tile, index_lane = index >> lane_bits, index & (lanes - 1)

                def add_pairs(first, total):
                    picked = [jnp.zeros((sublanes, lanes), jnp.int32)] * together
                    for source in range(tiles):
                        match = index_tile == source
                        for k in range(together):
                            words = source_ref[
                                first + k, rows, source * lanes : (source + 1) * lanes
                            ]
                            words = jnp.take_along_axis(
                                words, index_lane, axis=1, mode="promise_in_bounds"
                            )
                            picked[k] = jnp.where(match, words, picked[k])
                    for k in range(together):
                        for half, code in enumerate((picked[k] >> 16, (picked[k] << 16) >> 16)):
                            walker = (first + k) * 2 + half
                            total = total + left_ref[walker, :, here] * (
                                unit_ref[walker, rows] * code.astype(jnp.float32)
                            )
                    return total

                total = old_ref[own, rows, here]
                if pairs == together:
                    total = add_pairs(0, total)
                else:
                    total = lax.fori_loop(
                        0, pairs // together, lambda i, t: add_pairs(i * together, t), total
                    )
                new_ref[own, rows, here] = total


def exchange(pieces, axes, counts):
    positions = list(itertools.product(*map(range, counts)))
    place = {position: i for i, position in enumerate(positions)}
    arrived = [pieces[0]] * len(positions)
    for i in range(1, len(positions)):
        route = [
            (place[position], place[tuple(map(toward, position, positions[i], counts))])
            for position in positions
        ]
        arrived[i] = lax.ppermute(pieces[i], axes, route)
    return arrived


def local(walker_mats, vertex, weights, transfer_table, g4_old):
    blk_count = lax.axis_size("blk")
    walk_count = lax.axis_size("walk")
    sub_count = lax.axis_size("sub")
    rows_local, vertices = walker_mats.shape[1:]
    rows_own, transfers, columns = g4_old.shape
    columns_local = columns // sub_count
    devices = blk_count * walk_count * sub_count
    sizes = (blk_count, walk_count, sub_count, rows_own)
    vmem = pl.BlockSpec(memory_space=pltpu.VMEM)
    table, left = pl.pallas_call(
        functools.partial(table_kernel, sizes),
        out_shape=[
            jax.ShapeDtypeStruct((columns_local, vertices), jnp.bfloat16),
            jax.ShapeDtypeStruct((devices * rows_own, rows_local), jnp.bfloat16),
        ],
        in_specs=[vmem],
        out_specs=[vmem] * 2,
        compiler_params=pltpu.CompilerParams(vmem_limit_bytes=24 * 2**20),
        cost_estimate=pl.CostEstimate(
            flops=2000 * columns_local * vertices,
            bytes_accessed=6 * columns_local * vertices,
            transcendentals=0,
        ),
        name="table",
    )(vertex)
    sent = pl.pallas_call(
        functools.partial(product_kernel, sizes),
        out_shape=[jax.ShapeDtypeStruct((blk_count * rows_own, columns_local), jnp.float32)]
        * (walk_count * sub_count),
        in_specs=[vmem] * 3,
        out_specs=[vmem] * (walk_count * sub_count),
        scratch_shapes=[pltpu.VMEM((2 * devices * rows_own, vertices), jnp.bfloat16)],
        compiler_params=pltpu.CompilerParams(vmem_limit_bytes=24 * 2**20),
        name="product",
    )(walker_mats, table, left)
    parts = exchange(sent, ("walk", "sub"), (walk_count, sub_count))
    shared = blk_count <= RSTEPS
    rows_each = (blk_count if shared else RSTEPS) * rows_own
    whole_count = 1 if shared else blk_count
    whole = pl.pallas_call(
        functools.partial(combine_kernel, sizes),
        out_shape=[jax.ShapeDtypeStruct((rows_each, columns), jnp.bfloat16)] * whole_count,
        in_specs=[vmem] * len(parts),
        out_specs=[vmem] * whole_count,
        compiler_params=pltpu.CompilerParams(vmem_limit_bytes=24 * 2**20),
        name="combine",
    )(*parts)
    arrived = exchange(whole * blk_count if shared else whole, ("blk",), (blk_count,))
    far = blk_count // 2
    first = [0, *range(far, 2 * far - 1)]
    others = [place for place in range(blk_count) if place not in first]
    totals = g4_old
    for places in (first, others):
        totals = pl.pallas_call(
            functools.partial(accumulate_kernel, sizes, places),
            out_shape=jax.ShapeDtypeStruct(g4_old.shape, jnp.float32),
            in_specs=[vmem] * (3 + len(places)),
            out_specs=vmem,
            scratch_shapes=[
                pltpu.VMEM((len(places) // 2, transfers, columns), jnp.int32),
                pltpu.VMEM((len(places), 1, columns), jnp.float32),
                pltpu.VMEM((len(places), transfers, lanes), jnp.float32),
            ],
            compiler_params=pltpu.CompilerParams(vmem_limit_bytes=24 * 2**20),
            cost_estimate=pl.CostEstimate(
                flops=1000 * len(places) * transfers * columns,
                bytes_accessed=12 * transfers * columns,
                transcendentals=0,
            ),
            name="accumulate",
        )(weights[None], transfer_table, totals, *[arrived[place] for place in places])
    return totals


def solution(mesh):
    in_specs = (
        P(("grp", "blk"), "walk", None),
        P(("grp", "blk"), None),
        P("grp"),
        P(),
        P(("grp", "blk", "walk", "sub"), None, None),
    )
    out_specs = P(("grp", "blk", "walk", "sub"), None, None)
    return jax.shard_map(local, mesh=mesh, in_specs=in_specs, out_specs=out_specs, check_vma=False)
```

```python
import functools
import itertools
import math

import jax
import jax.numpy as jnp
from jax import lax
from jax.experimental import pallas as pl
from jax.experimental.pallas import tpu as pltpu
from jax.sharding import PartitionSpec as P

TQ = 4
RSTEPS = 4


phase_period = 8192
quarter_bits = 11
lanes = 128
lane_bits = 7
sublanes = 8
code_limit = 32767.0
smallest_peak = 1e-30


def toward(index, distance, count):
    if count & (count - 1) == 0:
        return index ^ distance
    return (index + distance) % count


def back(index, distance, count):
    if count & (count - 1) == 0:
        return index ^ distance
    return (index + count - distance) % count


def cos_sin(product):
    residue = product & (phase_period - 1)
    quarter = (residue + phase_period // 8) >> quarter_bits
    angle = (residue - (quarter << quarter_bits)).astype(jnp.float32) * (2.0 * math.pi / phase_period)
    square = angle * angle
    sine = angle + angle * square * (
        -1.0 / 6.0 + square * (1.0 / 120.0 + square * (-1.0 / 5040.0 + square * (1.0 / 362880.0)))
    )
    cosine = 1.0 + square * (
        -0.5 + square * (1.0 / 24.0 + square * (-1.0 / 720.0 + square * (1.0 / 40320.0)))
    )
    odd = (quarter & 1) == 1
    cosine_out = jnp.where(odd, sine, cosine)
    sine_out = jnp.where(odd, cosine, sine)
    cosine_out = jnp.where(((quarter + 1) & 2) == 2, -cosine_out, cosine_out)
    sine_out = jnp.where((quarter & 2) == 2, -sine_out, sine_out)
    return cosine_out, sine_out


def row_ids(count):
    return lax.broadcasted_iota(jnp.int32, (count, lanes), 0)


def split_by(ids, size):
    if size & (size - 1) == 0:
        return ids >> (size.bit_length() - 1), ids & (size - 1)
    return ids // size, ids % size


def table_kernel(sizes, vertex_ref, table_ref, left_ref):
    blk_count, walk_count, sub_count, rows_own = sizes
    walk_index = lax.axis_index("walk")
    sub_index = lax.axis_index("sub")
    columns, vertices = table_ref.shape
    window_rows, rows_local = left_ref.shape

    ids, inner = split_by(row_ids(window_rows), rows_own)
    ids, blk_part = split_by(ids, blk_count)
    walk_part, sub_part = split_by(ids, sub_count)
    sub_part = toward(sub_index, sub_part, sub_count)
    walk_part = toward(walk_index, walk_part, walk_count)
    window = ((blk_part * walk_count + walk_part) * sub_count + sub_part) * rows_own + inner
    own_start = pl.multiple_of(walk_index * rows_local, lanes)
    for start in range(0, rows_local, lanes):
        own_vertex = vertex_ref[:, pl.ds(own_start + start, lanes)]
        cosine, sine = cos_sin(own_vertex * window)
        left_ref[:, start : start + lanes] = (cosine + sine).astype(jnp.bfloat16)

    blocks = columns // lanes
    half_blocks = blocks // 2
    coarse_rows = -(-max(half_blocks, 1) // sublanes) * sublanes
    middle_count = lanes // sublanes
    center = sub_index * columns + (blocks - 1) * (lanes // 2)

    def angles(step):
        vertex = vertex_ref[:, pl.ds(pl.multiple_of(step * lanes, lanes), lanes)]
        cosine, sine = cos_sin(vertex * (row_ids(sublanes) + center))
        return (
            cosine + sine,
            cosine - sine,
            *cos_sin(vertex * (row_ids(middle_count) * sublanes)),
            *cos_sin(vertex * ((blocks - 1 - 2 * row_ids(coarse_rows)) * (lanes // 2))),
        )

    def table_step(step, carried):
        following = angles(jnp.minimum(step + 1, steps - 1))
        cas_fine, cam_fine, cos_middle, sin_middle, cos_coarse, sin_coarse = carried
        here = pl.ds(pl.multiple_of(step * lanes, lanes), lanes)
        for pair in range(middle_count // 2):
            cas, cam = [], []
            for middle in (2 * pair, 2 * pair + 1):
                c, s = cos_middle[middle : middle + 1], sin_middle[middle : middle + 1]
                cas.append(c * cas_fine + s * cam_fine)
                cam.append(c * cam_fine - s * cas_fine)
            cas, cam = jnp.concatenate(cas, axis=0), jnp.concatenate(cam, axis=0)
            start = pair * 2 * sublanes
            for low in range(half_blocks):
                high = blocks - 1 - low
                even = cos_coarse[low : low + 1] * cas
                odd = sin_coarse[low : low + 1] * cam
                for block, value in ((low, even - odd), (high, even + odd)):
                    first = block * lanes + start
                    table_ref[first : first + 2 * sublanes, here] = value.astype(jnp.bfloat16)
            if blocks % 2:
                first = half_blocks * lanes + start
                table_ref[first : first + 2 * sublanes, here] = cas.astype(jnp.bfloat16)
        return following

    steps = vertices // lanes
    lax.fori_loop(0, steps, table_step, angles(0))


def product_kernel(sizes, matrix_ref, table_ref, left_ref, *rest):
    *sent_refs, weight_ref = rest
    blk_count, _, _, rows_own = sizes
    vertices = matrix_ref.shape[2]
    window_rows = left_ref.shape[0]

    chunk = 4 * lanes
    for start in range(0, vertices, chunk):
        left_product = jnp.dot(
            left_ref[...], matrix_ref[0, :, start : start + chunk], preferred_element_type=jnp.float32
        )
        high = left_product.astype(jnp.bfloat16)
        weight_ref[:window_rows, start : start + chunk] = high
        weight_ref[window_rows:, start : start + chunk] = (
            left_product - high.astype(jnp.float32)
        ).astype(jnp.bfloat16)
    green = lax.dot_general(
        weight_ref[...], table_ref[...], (((1,), (1,)), ((), ())), preferred_element_type=jnp.float32
    )
    green = green[:window_rows] + green[window_rows:]
    rows_each = blk_count * rows_own
    for place, sent_ref in enumerate(sent_refs):
        sent_ref[...] = green[place * rows_each : (place + 1) * rows_each]


def pick_rows(rows, wanted):
    ids = lax.broadcasted_iota(jnp.int32, (wanted.shape[0], rows.shape[0]), 1)
    chosen = jnp.where(ids == wanted, 1.0, 0.0).astype(jnp.bfloat16)
    return jnp.dot(chosen, rows, preferred_element_type=jnp.float32)


def combine_kernel(sizes, *refs):
    blk_count, walk_count, sub_count, rows_own = sizes
    blk_index = lax.axis_index("blk")
    sub_index = lax.axis_index("sub")
    part_refs, whole_refs = refs[: walk_count * sub_count], refs[walk_count * sub_count :]
    columns_part = part_refs[0].shape[1]
    for distance in range(sub_count):
        sub_part = back(sub_index, distance, sub_count)
        here = pl.ds(pl.multiple_of(sub_part * columns_part, lanes), columns_part)
        total = sum(
            part_refs[walk_part * sub_count + distance][...] for walk_part in range(walk_count)
        ).astype(jnp.bfloat16)
        if len(whole_refs) == 1:
            whole_refs[0][:, here] = total
            continue
        for place, whole_ref in enumerate(whole_refs):
            ids = lax.broadcasted_iota(jnp.int32, (whole_ref.shape[0], 1), 0)
            step, inner = split_by(ids, rows_own)
            _, blk_part = split_by(toward(blk_index, place, blk_count) + RSTEPS * blk_count - step, blk_count)
            whole_ref[:, here] = pick_rows(total, blk_part * rows_own + inner).astype(whole_ref.dtype)


def accumulate_kernel(sizes, distances, weights_ref, transfer_ref, old_ref, *rest):
    *arrived_refs, new_ref, source_ref, left_ref, unit_ref = rest
    blk_count, _, _, rows_own = sizes
    blk_index = lax.axis_index("blk")
    transfers, columns = transfer_ref.shape
    half = columns // 2
    groups = transfers // sublanes
    tiles = columns // lanes
    weights = weights_ref[...] * (1.0 / blk_count)
    walker_ids = lax.broadcasted_iota(jnp.int32, weights.shape, 1)

    ids = lax.broadcasted_iota(jnp.int32, (transfers, 1), 0)
    step, _ = split_by(ids, TQ)
    if arrived_refs[0].shape[0] == blk_count * rows_own:
        _, step = split_by(blk_index + RSTEPS * blk_count - step, blk_count)

    for own in range(rows_own):
        for place, distance in enumerate(distances):
            rows = pick_rows(arrived_refs[place][...], step * rows_own + own)
            walker = back(blk_index, distance, blk_count)
            weight = jnp.sum(jnp.where(walker_ids == walker, weights, 0.0), axis=1, keepdims=True)
            left_ref[place] = rows[:1] * weight
            peak = jnp.maximum(jnp.max(jnp.abs(rows), axis=1, keepdims=True), smallest_peak)
            codes = jnp.floor(rows * (code_limit / peak) + 0.5).astype(jnp.int32)
            unit_ref[place] = jnp.broadcast_to(peak * (1.0 / code_limit), (transfers, lanes))
            source_ref[place] = (codes[:, :half] << 16) | (codes[:, half:] & 0xFFFF)

        together = len(distances) if len(distances) <= 4 else math.gcd(len(distances), 4)

        @pl.loop(0, tiles, unroll=math.gcd(tiles, 10))
        def _(tile):
            here = pl.ds(pl.multiple_of(tile * lanes, lanes), lanes)
            for group in range(groups):
                rows = slice(group * sublanes, (group + 1) * sublanes)
                index = transfer_ref[rows, here]
                index_lane = index & (lanes - 1)
                in_first = index < half
                index_tile = jnp.where(in_first, index, index - half) >> lane_bits

                def add_walkers(first, total):
                    picked = [jnp.zeros((sublanes, lanes), jnp.int32)] * together
                    for source in range(half // lanes):
                        match = index_tile == source
                        for k in range(together):
                            words = source_ref[
                                first + k, rows, source * lanes : (source + 1) * lanes
                            ]
                            words = jnp.take_along_axis(
                                words, index_lane, axis=1, mode="promise_in_bounds"
                            )
                            picked[k] = jnp.where(match, words, picked[k])
                    for k in range(together):
                        code = jnp.where(in_first, picked[k], picked[k] << 16) >> 16
                        total = total + left_ref[first + k, :, here] * (
                            unit_ref[first + k, rows] * code.astype(jnp.float32)
                        )
                    return total

                total = old_ref[own, rows, here]
                if len(distances) == together:
                    total = add_walkers(0, total)
                else:
                    total = lax.fori_loop(
                        0, len(distances) // together, lambda i, t: add_walkers(i * together, t), total
                    )
                new_ref[own, rows, here] = total


def exchange(pieces, axes, counts):
    positions = list(itertools.product(*map(range, counts)))
    place = {position: i for i, position in enumerate(positions)}
    arrived = [pieces[0]] * len(positions)
    for i in range(1, len(positions)):
        route = [
            (place[position], place[tuple(map(toward, position, positions[i], counts))])
            for position in positions
        ]
        arrived[i] = lax.ppermute(pieces[i], axes, route)
    return arrived


def local(walker_mats, vertex, weights, transfer_table, g4_old):
    blk_count = lax.axis_size("blk")
    walk_count = lax.axis_size("walk")
    sub_count = lax.axis_size("sub")
    rows_local, vertices = walker_mats.shape[1:]
    rows_own, transfers, columns = g4_old.shape
    columns_local = columns // sub_count
    devices = blk_count * walk_count * sub_count
    sizes = (blk_count, walk_count, sub_count, rows_own)
    vmem = pl.BlockSpec(memory_space=pltpu.VMEM)
    table, left = pl.pallas_call(
        functools.partial(table_kernel, sizes),
        out_shape=[
            jax.ShapeDtypeStruct((columns_local, vertices), jnp.bfloat16),
            jax.ShapeDtypeStruct((devices * rows_own, rows_local), jnp.bfloat16),
        ],
        in_specs=[vmem],
        out_specs=[vmem] * 2,
        compiler_params=pltpu.CompilerParams(vmem_limit_bytes=24 * 2**20),
        cost_estimate=pl.CostEstimate(
            flops=2000 * columns_local * vertices,
            bytes_accessed=6 * columns_local * vertices,
            transcendentals=0,
        ),
        name="table",
    )(vertex)
    sent = pl.pallas_call(
        functools.partial(product_kernel, sizes),
        out_shape=[jax.ShapeDtypeStruct((blk_count * rows_own, columns_local), jnp.float32)]
        * (walk_count * sub_count),
        in_specs=[vmem] * 3,
        out_specs=[vmem] * (walk_count * sub_count),
        scratch_shapes=[pltpu.VMEM((2 * devices * rows_own, vertices), jnp.bfloat16)],
        compiler_params=pltpu.CompilerParams(vmem_limit_bytes=24 * 2**20),
        name="product",
    )(walker_mats, table, left)
    parts = exchange(sent, ("walk", "sub"), (walk_count, sub_count))
    shared = blk_count <= RSTEPS
    rows_each = (blk_count if shared else RSTEPS) * rows_own
    whole_count = 1 if shared else blk_count
    whole = pl.pallas_call(
        functools.partial(combine_kernel, sizes),
        out_shape=[jax.ShapeDtypeStruct((rows_each, columns), jnp.bfloat16)] * whole_count,
        in_specs=[vmem] * len(parts),
        out_specs=[vmem] * whole_count,
        compiler_params=pltpu.CompilerParams(vmem_limit_bytes=24 * 2**20),
        name="combine",
    )(*parts)
    arrived = exchange(whole * blk_count if shared else whole, ("blk",), (blk_count,))
    far = blk_count // 2
    totals = g4_old
    for places in ([0, *range(far + 1, blk_count)], [*range(1, far)], [far]):
        totals = pl.pallas_call(
            functools.partial(accumulate_kernel, sizes, places),
            out_shape=jax.ShapeDtypeStruct(g4_old.shape, jnp.float32),
            in_specs=[vmem] * (3 + len(places)),
            out_specs=vmem,
            scratch_shapes=[
                pltpu.VMEM((len(places), transfers, columns // 2), jnp.int32),
                pltpu.VMEM((len(places), 1, columns), jnp.float32),
                pltpu.VMEM((len(places), transfers, lanes), jnp.float32),
            ],
            compiler_params=pltpu.CompilerParams(vmem_limit_bytes=24 * 2**20),
            cost_estimate=pl.CostEstimate(
                flops=1000 * len(places) * transfers * columns,
                bytes_accessed=12 * transfers * columns,
                transcendentals=0,
            ),
            name="accumulate",
        )(weights[None], transfer_table, totals, *[arrived[place] for place in places])
    return totals


def solution(mesh):
    in_specs = (
        P(("grp", "blk"), "walk", None),
        P(("grp", "blk"), None),
        P("grp"),
        P(),
        P(("grp", "blk", "walk", "sub"), None, None),
    )
    out_specs = P(("grp", "blk", "walk", "sub"), None, None)
    return jax.shard_map(local, mesh=mesh, in_specs=in_specs, out_specs=out_specs, check_vma=False)
```

```python
import functools
import itertools
import math

import jax
import jax.numpy as jnp
from jax import lax
from jax.experimental import pallas as pl
from jax.experimental.pallas import tpu as pltpu
from jax.sharding import PartitionSpec as P

TQ = 4
RSTEPS = 4


phase_period = 8192
quarter_bits = 11
lanes = 128
lane_bits = 7
sublanes = 8
code_limit = 32767.0
smallest_peak = 1e-30


def toward(index, distance, count):
    if count & (count - 1) == 0:
        return index ^ distance
    return (index + distance) % count


def back(index, distance, count):
    if count & (count - 1) == 0:
        return index ^ distance
    return (index + count - distance) % count


def cos_sin(product):
    residue = product & (phase_period - 1)
    quarter = (residue + phase_period // 8) >> quarter_bits
    angle = (residue - (quarter << quarter_bits)).astype(jnp.float32) * (2.0 * math.pi / phase_period)
    square = angle * angle
    sine = angle + angle * square * (
        -1.0 / 6.0 + square * (1.0 / 120.0 + square * (-1.0 / 5040.0 + square * (1.0 / 362880.0)))
    )
    cosine = 1.0 + square * (
        -0.5 + square * (1.0 / 24.0 + square * (-1.0 / 720.0 + square * (1.0 / 40320.0)))
    )
    odd = (quarter & 1) == 1
    cosine_out = jnp.where(odd, sine, cosine)
    sine_out = jnp.where(odd, cosine, sine)
    cosine_out = jnp.where(((quarter + 1) & 2) == 2, -cosine_out, cosine_out)
    sine_out = jnp.where((quarter & 2) == 2, -sine_out, sine_out)
    return cosine_out, sine_out


def row_ids(count):
    return lax.broadcasted_iota(jnp.int32, (count, lanes), 0)


def split_by(ids, size):
    if size & (size - 1) == 0:
        return ids >> (size.bit_length() - 1), ids & (size - 1)
    return ids // size, ids % size


def table_kernel(sizes, vertex_ref, table_ref, left_ref):
    blk_count, walk_count, sub_count, rows_own = sizes
    walk_index = lax.axis_index("walk")
    sub_index = lax.axis_index("sub")
    columns, vertices = table_ref.shape
    window_rows, rows_local = left_ref.shape

    ids, inner = split_by(row_ids(window_rows), rows_own)
    ids, blk_part = split_by(ids, blk_count)
    walk_part, sub_part = split_by(ids, sub_count)
    sub_part = toward(sub_index, sub_part, sub_count)
    walk_part = toward(walk_index, walk_part, walk_count)
    window = ((blk_part * walk_count + walk_part) * sub_count + sub_part) * rows_own + inner
    own_start = pl.multiple_of(walk_index * rows_local, lanes)

    @pl.loop(0, rows_local // lanes, unroll=2)
    def _(step):
        start = pl.multiple_of(step * lanes, lanes)
        cosine, sine = cos_sin(vertex_ref[:, pl.ds(own_start + start, lanes)] * window)
        left_ref[:, pl.ds(start, lanes)] = (cosine + sine).astype(jnp.bfloat16)

    blocks = columns // lanes
    half_blocks = blocks // 2
    coarse_rows = -(-max(half_blocks, 1) // sublanes) * sublanes
    middle_count = lanes // sublanes
    center = sub_index * columns + (blocks - 1) * (lanes // 2)

    def angles(step):
        vertex = vertex_ref[:, pl.ds(pl.multiple_of(step * lanes, lanes), lanes)]
        cosine, sine = cos_sin(vertex * (row_ids(sublanes) + center))
        return (
            cosine + sine,
            cosine - sine,
            *cos_sin(vertex * (row_ids(middle_count) * sublanes)),
            *cos_sin(vertex * ((blocks - 1 - 2 * row_ids(coarse_rows)) * (lanes // 2))),
        )

    def table_step(step, carried):
        following = angles(jnp.minimum(step + 1, steps - 1))
        cas_fine, cam_fine, cos_middle, sin_middle, cos_coarse, sin_coarse = carried
        here = pl.ds(pl.multiple_of(step * lanes, lanes), lanes)
        for pair in range(middle_count // 2):
            cas, cam = [], []
            for middle in (2 * pair, 2 * pair + 1):
                c, s = cos_middle[middle : middle + 1], sin_middle[middle : middle + 1]
                cas.append(c * cas_fine + s * cam_fine)
                cam.append(c * cam_fine - s * cas_fine)
            cas, cam = jnp.concatenate(cas, axis=0), jnp.concatenate(cam, axis=0)
            start = pair * 2 * sublanes
            for low in range(half_blocks):
                high = blocks - 1 - low
                even = cos_coarse[low : low + 1] * cas
                odd = sin_coarse[low : low + 1] * cam
                for block, value in ((low, even - odd), (high, even + odd)):
                    first = block * lanes + start
                    table_ref[first : first + 2 * sublanes, here] = value.astype(jnp.bfloat16)
            if blocks % 2:
                first = half_blocks * lanes + start
                table_ref[first : first + 2 * sublanes, here] = cas.astype(jnp.bfloat16)
        return following

    steps = vertices // lanes
    lax.fori_loop(0, steps, table_step, angles(0))


def product_kernel(sizes, matrix_ref, table_ref, left_ref, *rest):
    *sent_refs, weight_ref, product_ref, total_ref = rest
    blk_count, _, _, rows_own = sizes
    vertices = matrix_ref.shape[2]
    window_rows = left_ref.shape[0]

    rows_local = matrix_ref.shape[1]
    columns = table_ref.shape[0]
    block = 2 * lanes
    product_ref[...] = jnp.zeros_like(product_ref)

    @pl.loop(0, rows_local // block)
    def _(step):
        here = pl.ds(pl.multiple_of(step * block, block), block)
        product_ref[...] += jnp.dot(
            left_ref[:, here], matrix_ref[0, here, :], preferred_element_type=jnp.float32
        )

    left_product = product_ref[...]
    high = left_product.astype(jnp.bfloat16)
    weight_ref[:window_rows] = high
    weight_ref[window_rows:] = (left_product - high.astype(jnp.float32)).astype(jnp.bfloat16)

    @pl.loop(0, columns // block)
    def _(step):
        here = pl.ds(pl.multiple_of(step * block, block), block)
        total_ref[:, here] = lax.dot_general(
            weight_ref[...],
            table_ref[here, :],
            (((1,), (1,)), ((), ())),
            preferred_element_type=jnp.float32,
        )

    green = total_ref[...]
    green = green[:window_rows] + green[window_rows:]
    rows_each = blk_count * rows_own
    for place, sent_ref in enumerate(sent_refs):
        sent_ref[...] = green[place * rows_each : (place + 1) * rows_each]


def pick_rows(rows, wanted):
    ids = lax.broadcasted_iota(jnp.int32, (wanted.shape[0], rows.shape[0]), 1)
    chosen = jnp.where(ids == wanted, 1.0, 0.0).astype(jnp.bfloat16)
    return jnp.dot(chosen, rows, preferred_element_type=jnp.float32)


def combine_kernel(sizes, *refs):
    blk_count, walk_count, sub_count, rows_own = sizes
    blk_index = lax.axis_index("blk")
    sub_index = lax.axis_index("sub")
    part_refs, whole_refs = refs[: walk_count * sub_count], refs[walk_count * sub_count :]
    columns_part = part_refs[0].shape[1]
    for distance in range(sub_count):
        sub_part = back(sub_index, distance, sub_count)
        here = pl.ds(pl.multiple_of(sub_part * columns_part, lanes), columns_part)
        total = sum(
            part_refs[walk_part * sub_count + distance][...] for walk_part in range(walk_count)
        ).astype(jnp.bfloat16)
        if len(whole_refs) == 1:
            whole_refs[0][:, here] = total
            continue
        for place, whole_ref in enumerate(whole_refs):
            ids = lax.broadcasted_iota(jnp.int32, (whole_ref.shape[0], 1), 0)
            step, inner = split_by(ids, rows_own)
            _, blk_part = split_by(toward(blk_index, place, blk_count) + RSTEPS * blk_count - step, blk_count)
            whole_ref[:, here] = pick_rows(total, blk_part * rows_own + inner).astype(whole_ref.dtype)


def accumulate_kernel(sizes, distances, weights_ref, transfer_ref, old_ref, *rest):
    *arrived_refs, new_ref, source_ref, left_ref, unit_ref = rest
    blk_count, _, _, rows_own = sizes
    blk_index = lax.axis_index("blk")
    transfers, columns = transfer_ref.shape
    half = columns // 2
    groups = transfers // sublanes
    tiles = columns // lanes
    weights = weights_ref[...] * (1.0 / blk_count)
    walker_ids = lax.broadcasted_iota(jnp.int32, weights.shape, 1)

    ids = lax.broadcasted_iota(jnp.int32, (transfers, 1), 0)
    step, _ = split_by(ids, TQ)
    if arrived_refs[0].shape[0] == blk_count * rows_own:
        _, step = split_by(blk_index + RSTEPS * blk_count - step, blk_count)

    for own in range(rows_own):
        for place, distance in enumerate(distances):
            rows = pick_rows(arrived_refs[place][...], step * rows_own + own)
            walker = back(blk_index, distance, blk_count)
            weight = jnp.sum(jnp.where(walker_ids == walker, weights, 0.0), axis=1, keepdims=True)
            left_ref[place] = rows[:1] * weight
            peak = jnp.maximum(jnp.max(jnp.abs(rows), axis=1, keepdims=True), smallest_peak)
            codes = jnp.floor(rows * (code_limit / peak) + 0.5).astype(jnp.int32)
            unit_ref[place] = jnp.broadcast_to(peak * (1.0 / code_limit), (transfers, lanes))
            source_ref[place] = (codes[:, :half] << 16) | (codes[:, half:] & 0xFFFF)

        together = len(distances) if len(distances) <= 4 else math.gcd(len(distances), 4)

        @pl.loop(0, tiles, unroll=math.gcd(tiles, 10))
        def _(tile):
            here = pl.ds(pl.multiple_of(tile * lanes, lanes), lanes)
            for group in range(groups):
                rows = slice(group * sublanes, (group + 1) * sublanes)
                index = transfer_ref[rows, here]
                index_lane = index & (lanes - 1)
                in_first = index < half
                index_tile = jnp.where(in_first, index, index - half) >> lane_bits

                def add_walkers(first, total):
                    picked = [jnp.zeros((sublanes, lanes), jnp.int32)] * together
                    for source in range(half // lanes):
                        match = index_tile == source
                        for k in range(together):
                            words = source_ref[
                                first + k, rows, source * lanes : (source + 1) * lanes
                            ]
                            words = jnp.take_along_axis(
                                words, index_lane, axis=1, mode="promise_in_bounds"
                            )
                            picked[k] = jnp.where(match, words, picked[k])
                    for k in range(together):
                        code = jnp.where(in_first, picked[k], picked[k] << 16) >> 16
                        total = total + left_ref[first + k, :, here] * (
                            unit_ref[first + k, rows] * code.astype(jnp.float32)
                        )
                    return total

                total = old_ref[own, rows, here]
                if len(distances) == together:
                    total = add_walkers(0, total)
                else:
                    total = lax.fori_loop(
                        0, len(distances) // together, lambda i, t: add_walkers(i * together, t), total
                    )
                new_ref[own, rows, here] = total


def exchange(pieces, axes, counts):
    positions = list(itertools.product(*map(range, counts)))
    place = {position: i for i, position in enumerate(positions)}
    arrived = [pieces[0]] * len(positions)
    for i in range(1, len(positions)):
        route = [
            (place[position], place[tuple(map(toward, position, positions[i], counts))])
            for position in positions
        ]
        arrived[i] = lax.ppermute(pieces[i], axes, route)
    return arrived


def local(walker_mats, vertex, weights, transfer_table, g4_old):
    blk_count = lax.axis_size("blk")
    walk_count = lax.axis_size("walk")
    sub_count = lax.axis_size("sub")
    rows_local, vertices = walker_mats.shape[1:]
    rows_own, transfers, columns = g4_old.shape
    columns_local = columns // sub_count
    devices = blk_count * walk_count * sub_count
    sizes = (blk_count, walk_count, sub_count, rows_own)
    vmem = pl.BlockSpec(memory_space=pltpu.VMEM)
    table, left = pl.pallas_call(
        functools.partial(table_kernel, sizes),
        out_shape=[
            jax.ShapeDtypeStruct((columns_local, vertices), jnp.bfloat16),
            jax.ShapeDtypeStruct((devices * rows_own, rows_local), jnp.bfloat16),
        ],
        in_specs=[vmem],
        out_specs=[vmem] * 2,
        compiler_params=pltpu.CompilerParams(vmem_limit_bytes=24 * 2**20),
        cost_estimate=pl.CostEstimate(
            flops=2000 * columns_local * vertices,
            bytes_accessed=6 * columns_local * vertices,
            transcendentals=0,
        ),
        name="table",
    )(vertex)
    sent = pl.pallas_call(
        functools.partial(product_kernel, sizes),
        out_shape=[jax.ShapeDtypeStruct((blk_count * rows_own, columns_local), jnp.float32)]
        * (walk_count * sub_count),
        in_specs=[vmem] * 3,
        out_specs=[vmem] * (walk_count * sub_count),
        scratch_shapes=[
            pltpu.VMEM((2 * devices * rows_own, vertices), jnp.bfloat16),
            pltpu.VMEM((devices * rows_own, vertices), jnp.float32),
            pltpu.VMEM((2 * devices * rows_own, columns_local), jnp.float32),
        ],
        compiler_params=pltpu.CompilerParams(vmem_limit_bytes=24 * 2**20),
        name="product",
    )(walker_mats, table, left)
    parts = exchange(sent, ("walk", "sub"), (walk_count, sub_count))
    shared = blk_count <= RSTEPS
    rows_each = (blk_count if shared else RSTEPS) * rows_own
    whole_count = 1 if shared else blk_count
    whole = pl.pallas_call(
        functools.partial(combine_kernel, sizes),
        out_shape=[jax.ShapeDtypeStruct((rows_each, columns), jnp.bfloat16)] * whole_count,
        in_specs=[vmem] * len(parts),
        out_specs=[vmem] * whole_count,
        compiler_params=pltpu.CompilerParams(vmem_limit_bytes=24 * 2**20),
        name="combine",
    )(*parts)
    arrived = exchange(whole * blk_count if shared else whole, ("blk",), (blk_count,))
    far = blk_count // 2
    totals = g4_old
    for places in ([0, *range(far + 1, blk_count)], [*range(1, far)], [far]):
        totals = pl.pallas_call(
            functools.partial(accumulate_kernel, sizes, places),
            out_shape=jax.ShapeDtypeStruct(g4_old.shape, jnp.float32),
            in_specs=[vmem] * (3 + len(places)),
            out_specs=vmem,
            scratch_shapes=[
                pltpu.VMEM((len(places), transfers, columns // 2), jnp.int32),
                pltpu.VMEM((len(places), 1, columns), jnp.float32),
                pltpu.VMEM((len(places), transfers, lanes), jnp.float32),
            ],
            compiler_params=pltpu.CompilerParams(vmem_limit_bytes=24 * 2**20),
            cost_estimate=pl.CostEstimate(
                flops=1000 * len(places) * transfers * columns,
                bytes_accessed=12 * transfers * columns,
                transcendentals=0,
            ),
            name="accumulate",
        )(weights[None], transfer_table, totals, *[arrived[place] for place in places])
    return totals


def solution(mesh):
    in_specs = (
        P(("grp", "blk"), "walk", None),
        P(("grp", "blk"), None),
        P("grp"),
        P(),
        P(("grp", "blk", "walk", "sub"), None, None),
    )
    out_specs = P(("grp", "blk", "walk", "sub"), None, None)
    return jax.shard_map(local, mesh=mesh, in_specs=in_specs, out_specs=out_specs, check_vma=False)
```

```python
import functools
import itertools
import math

import jax
import jax.numpy as jnp
from jax import lax
from jax.experimental import pallas as pl
from jax.experimental.pallas import tpu as pltpu
from jax.sharding import PartitionSpec as P

TQ = 4
RSTEPS = 4


phase_period = 8192
quarter_bits = 11
lanes = 128
lane_bits = 7
sublanes = 8
code_limit = 32767.0
smallest_peak = 1e-30


def toward(index, distance, count):
    if count & (count - 1) == 0:
        return index ^ distance
    return (index + distance) % count


def back(index, distance, count):
    if count & (count - 1) == 0:
        return index ^ distance
    return (index + count - distance) % count


def cos_sin(product):
    residue = product & (phase_period - 1)
    quarter = (residue + phase_period // 8) >> quarter_bits
    angle = (residue - (quarter << quarter_bits)).astype(jnp.float32) * (2.0 * math.pi / phase_period)
    square = angle * angle
    sine = angle + angle * square * (
        -1.0 / 6.0 + square * (1.0 / 120.0 + square * (-1.0 / 5040.0 + square * (1.0 / 362880.0)))
    )
    cosine = 1.0 + square * (
        -0.5 + square * (1.0 / 24.0 + square * (-1.0 / 720.0 + square * (1.0 / 40320.0)))
    )
    odd = (quarter & 1) == 1
    cosine_out = jnp.where(odd, sine, cosine)
    sine_out = jnp.where(odd, cosine, sine)
    cosine_out = jnp.where(((quarter + 1) & 2) == 2, -cosine_out, cosine_out)
    sine_out = jnp.where((quarter & 2) == 2, -sine_out, sine_out)
    return cosine_out, sine_out


def row_ids(count):
    return lax.broadcasted_iota(jnp.int32, (count, lanes), 0)


def split_by(ids, size):
    if size & (size - 1) == 0:
        return ids >> (size.bit_length() - 1), ids & (size - 1)
    return ids // size, ids % size


def tile_of(start):
    return pl.ds(start if isinstance(start, int) else pl.multiple_of(start, lanes), lanes)


def make_table(vertex_ref, table_ref, first, place, sub_index):
    columns = table_ref.shape[0]
    blocks = columns // lanes
    half_blocks = blocks // 2
    coarse_rows = -(-max(half_blocks, 1) // sublanes) * sublanes
    middle_count = lanes // sublanes
    center = sub_index * columns + (blocks - 1) * (lanes // 2)
    here = tile_of(place)
    vertex = vertex_ref[:, tile_of(first)]
    cosine, sine = cos_sin(vertex * (row_ids(sublanes) + center))
    cas_fine, cam_fine = cosine + sine, cosine - sine
    cos_middle, sin_middle = cos_sin(vertex * (row_ids(middle_count) * sublanes))
    cos_coarse, sin_coarse = cos_sin(
        vertex * ((blocks - 1 - 2 * row_ids(coarse_rows)) * (lanes // 2))
    )
    for pair in range(middle_count // 2):
        cas, cam = [], []
        for middle in (2 * pair, 2 * pair + 1):
            c, s = cos_middle[middle : middle + 1], sin_middle[middle : middle + 1]
            cas.append(c * cas_fine + s * cam_fine)
            cam.append(c * cam_fine - s * cas_fine)
        cas, cam = jnp.concatenate(cas, axis=0), jnp.concatenate(cam, axis=0)
        start = pair * 2 * sublanes
        for low in range(half_blocks):
            high = blocks - 1 - low
            even = cos_coarse[low : low + 1] * cas
            odd = sin_coarse[low : low + 1] * cam
            for block, value in ((low, even - odd), (high, even + odd)):
                row = block * lanes + start
                table_ref[row : row + 2 * sublanes, here] = value.astype(jnp.bfloat16)
        if blocks % 2:
            row = half_blocks * lanes + start
            table_ref[row : row + 2 * sublanes, here] = cas.astype(jnp.bfloat16)


def table_kernel(sizes, vertex_ref, table_ref, left_ref):
    blk_count, walk_count, sub_count, rows_own = sizes
    walk_index = lax.axis_index("walk")
    sub_index = lax.axis_index("sub")
    window_rows, rows_local = left_ref.shape

    ids, inner = split_by(row_ids(window_rows), rows_own)
    ids, blk_part = split_by(ids, blk_count)
    walk_part, sub_part = split_by(ids, sub_count)
    sub_part = toward(sub_index, sub_part, sub_count)
    walk_part = toward(walk_index, walk_part, walk_count)
    window = ((blk_part * walk_count + walk_part) * sub_count + sub_part) * rows_own + inner
    own_start = pl.multiple_of(walk_index * rows_local, lanes)
    for start in range(0, rows_local, lanes):
        own_vertex = vertex_ref[:, pl.ds(own_start + start, lanes)]
        cosine, sine = cos_sin(own_vertex * window)
        left_ref[:, start : start + lanes] = (cosine + sine).astype(jnp.bfloat16)

    @pl.loop(0, table_ref.shape[1] // lanes)
    def _(step):
        make_table(vertex_ref, table_ref, step * lanes, step * lanes, sub_index)


def product_kernel(sizes, matrix_ref, vertex_ref, early_ref, left_ref, *rest):
    *sent_refs, late_ref, weight_ref = rest
    blk_count, _, _, rows_own = sizes
    sub_index = lax.axis_index("sub")
    vertices = matrix_ref.shape[2]
    window_rows = left_ref.shape[0]
    early = early_ref.shape[1]

    chunk = 4 * lanes
    tiles = list(range(0, vertices - early, lanes))
    chunks = list(range(0, vertices, chunk))
    for i, start in enumerate(chunks):
        left_product = jnp.dot(
            left_ref[...], matrix_ref[0, :, start : start + chunk], preferred_element_type=jnp.float32
        )
        for tile in tiles[i * len(tiles) // len(chunks) : (i + 1) * len(tiles) // len(chunks)]:
            make_table(vertex_ref, late_ref, early + tile, tile, sub_index)
        high = left_product.astype(jnp.bfloat16)
        weight_ref[:window_rows, start : start + chunk] = high
        weight_ref[window_rows:, start : start + chunk] = (
            left_product - high.astype(jnp.float32)
        ).astype(jnp.bfloat16)
    green = sum(
        lax.dot_general(
            weight_ref[:, start : start + table_ref.shape[1]],
            table_ref[...],
            (((1,), (1,)), ((), ())),
            preferred_element_type=jnp.float32,
        )
        for start, table_ref in ((0, early_ref), (early, late_ref))
    )
    green = green[:window_rows] + green[window_rows:]
    rows_each = blk_count * rows_own
    for place, sent_ref in enumerate(sent_refs):
        sent_ref[...] = green[place * rows_each : (place + 1) * rows_each]


def pick_rows(rows, wanted):
    ids = lax.broadcasted_iota(jnp.int32, (wanted.shape[0], rows.shape[0]), 1)
    chosen = jnp.where(ids == wanted, 1.0, 0.0).astype(jnp.bfloat16)
    return jnp.dot(chosen, rows, preferred_element_type=jnp.float32)


def combine_kernel(sizes, *refs):
    blk_count, walk_count, sub_count, rows_own = sizes
    blk_index = lax.axis_index("blk")
    sub_index = lax.axis_index("sub")
    part_refs, whole_refs = refs[: walk_count * sub_count], refs[walk_count * sub_count :]
    columns_part = part_refs[0].shape[1]
    for distance in range(sub_count):
        sub_part = back(sub_index, distance, sub_count)
        here = pl.ds(pl.multiple_of(sub_part * columns_part, lanes), columns_part)
        total = sum(
            part_refs[walk_part * sub_count + distance][...] for walk_part in range(walk_count)
        ).astype(jnp.bfloat16)
        if len(whole_refs) == 1:
            whole_refs[0][:, here] = total
            continue
        for place, whole_ref in enumerate(whole_refs):
            ids = lax.broadcasted_iota(jnp.int32, (whole_ref.shape[0], 1), 0)
            step, inner = split_by(ids, rows_own)
            _, blk_part = split_by(toward(blk_index, place, blk_count) + RSTEPS * blk_count - step, blk_count)
            whole_ref[:, here] = pick_rows(total, blk_part * rows_own + inner).astype(whole_ref.dtype)


def accumulate_kernel(sizes, distances, weights_ref, transfer_ref, old_ref, *rest):
    *arrived_refs, new_ref, source_ref, left_ref, unit_ref = rest
    blk_count, _, _, rows_own = sizes
    blk_index = lax.axis_index("blk")
    transfers, columns = transfer_ref.shape
    half = columns // 2
    groups = transfers // sublanes
    tiles = columns // lanes
    weights = weights_ref[...] * (1.0 / blk_count)
    walker_ids = lax.broadcasted_iota(jnp.int32, weights.shape, 1)

    ids = lax.broadcasted_iota(jnp.int32, (transfers, 1), 0)
    step, _ = split_by(ids, TQ)
    if arrived_refs[0].shape[0] == blk_count * rows_own:
        _, step = split_by(blk_index + RSTEPS * blk_count - step, blk_count)

    for own in range(rows_own):
        for place, distance in enumerate(distances):
            rows = pick_rows(arrived_refs[place][...], step * rows_own + own)
            walker = back(blk_index, distance, blk_count)
            weight = jnp.sum(jnp.where(walker_ids == walker, weights, 0.0), axis=1, keepdims=True)
            left_ref[place] = rows[:1] * weight
            peak = jnp.maximum(jnp.max(jnp.abs(rows), axis=1, keepdims=True), smallest_peak)
            codes = jnp.floor(rows * (code_limit / peak) + 0.5).astype(jnp.int32)
            unit_ref[place] = jnp.broadcast_to(peak * (1.0 / code_limit), (transfers, lanes))
            source_ref[place] = (codes[:, :half] << 16) | (codes[:, half:] & 0xFFFF)

        together = len(distances) if len(distances) <= 4 else math.gcd(len(distances), 4)

        @pl.loop(0, tiles, unroll=math.gcd(tiles, 20))
        def _(tile):
            here = pl.ds(pl.multiple_of(tile * lanes, lanes), lanes)
            for group in range(groups):
                rows = slice(group * sublanes, (group + 1) * sublanes)
                index = transfer_ref[rows, here]
                index_lane = index & (lanes - 1)
                in_first = index < half
                index_tile = jnp.where(in_first, index, index - half) >> lane_bits

                def add_walkers(first, total):
                    picked = [jnp.zeros((sublanes, lanes), jnp.int32)] * together
                    for source in range(half // lanes):
                        match = index_tile == source
                        for k in range(together):
                            words = source_ref[
                                first + k, rows, source * lanes : (source + 1) * lanes
                            ]
                            words = jnp.take_along_axis(
                                words, index_lane, axis=1, mode="promise_in_bounds"
                            )
                            picked[k] = jnp.where(match, words, picked[k])
                    for k in range(together):
                        code = jnp.where(in_first, picked[k], picked[k] << 16) >> 16
                        total = total + left_ref[first + k, :, here] * (
                            unit_ref[first + k, rows] * code.astype(jnp.float32)
                        )
                    return total

                total = old_ref[own, rows, here]
                if len(distances) == together:
                    total = add_walkers(0, total)
                else:
                    total = lax.fori_loop(
                        0, len(distances) // together, lambda i, t: add_walkers(i * together, t), total
                    )
                new_ref[own, rows, here] = total


def exchange(pieces, axes, counts):
    positions = list(itertools.product(*map(range, counts)))
    place = {position: i for i, position in enumerate(positions)}
    arrived = [pieces[0]] * len(positions)
    for i in range(1, len(positions)):
        route = [
            (place[position], place[tuple(map(toward, position, positions[i], counts))])
            for position in positions
        ]
        arrived[i] = lax.ppermute(pieces[i], axes, route)
    return arrived


def local(walker_mats, vertex, weights, transfer_table, g4_old):
    blk_count = lax.axis_size("blk")
    walk_count = lax.axis_size("walk")
    sub_count = lax.axis_size("sub")
    rows_local, vertices = walker_mats.shape[1:]
    rows_own, transfers, columns = g4_old.shape
    columns_local = columns // sub_count
    devices = blk_count * walk_count * sub_count
    sizes = (blk_count, walk_count, sub_count, rows_own)
    vmem = pl.BlockSpec(memory_space=pltpu.VMEM)
    early = 5 * vertices // (8 * 2 * lanes) * 2 * lanes
    table, left = pl.pallas_call(
        functools.partial(table_kernel, sizes),
        out_shape=[
            jax.ShapeDtypeStruct((columns_local, early), jnp.bfloat16),
            jax.ShapeDtypeStruct((devices * rows_own, rows_local), jnp.bfloat16),
        ],
        in_specs=[vmem],
        out_specs=[vmem] * 2,
        compiler_params=pltpu.CompilerParams(vmem_limit_bytes=24 * 2**20),
        cost_estimate=pl.CostEstimate(
            flops=2000 * columns_local * vertices,
            bytes_accessed=6 * columns_local * vertices,
            transcendentals=0,
        ),
        name="table",
    )(vertex)
    sent = pl.pallas_call(
        functools.partial(product_kernel, sizes),
        out_shape=[jax.ShapeDtypeStruct((blk_count * rows_own, columns_local), jnp.float32)]
        * (walk_count * sub_count),
        in_specs=[vmem] * 4,
        out_specs=[vmem] * (walk_count * sub_count),
        scratch_shapes=[
            pltpu.VMEM((columns_local, vertices - early), jnp.bfloat16),
            pltpu.VMEM((2 * devices * rows_own, vertices), jnp.bfloat16),
        ],
        compiler_params=pltpu.CompilerParams(vmem_limit_bytes=24 * 2**20),
        name="product",
    )(walker_mats, vertex, table, left)
    parts = exchange(sent, ("walk", "sub"), (walk_count, sub_count))
    shared = blk_count <= RSTEPS
    rows_each = (blk_count if shared else RSTEPS) * rows_own
    whole_count = 1 if shared else blk_count
    whole = pl.pallas_call(
        functools.partial(combine_kernel, sizes),
        out_shape=[jax.ShapeDtypeStruct((rows_each, columns), jnp.bfloat16)] * whole_count,
        in_specs=[vmem] * len(parts),
        out_specs=[vmem] * whole_count,
        compiler_params=pltpu.CompilerParams(vmem_limit_bytes=24 * 2**20),
        name="combine",
    )(*parts)
    arrived = exchange(whole * blk_count if shared else whole, ("blk",), (blk_count,))
    far = blk_count // 2
    totals = g4_old
    for places in ([0, *range(far + 1, blk_count)], [*range(1, far)], [far]):
        totals = pl.pallas_call(
            functools.partial(accumulate_kernel, sizes, places),
            out_shape=jax.ShapeDtypeStruct(g4_old.shape, jnp.float32),
            in_specs=[vmem] * (3 + len(places)),
            out_specs=vmem,
            scratch_shapes=[
                pltpu.VMEM((len(places), transfers, columns // 2), jnp.int32),
                pltpu.VMEM((len(places), 1, columns), jnp.float32),
                pltpu.VMEM((len(places), transfers, lanes), jnp.float32),
            ],
            compiler_params=pltpu.CompilerParams(vmem_limit_bytes=24 * 2**20),
            cost_estimate=pl.CostEstimate(
                flops=1000 * len(places) * transfers * columns,
                bytes_accessed=12 * transfers * columns,
                transcendentals=0,
            ),
            name="accumulate",
        )(weights[None], transfer_table, totals, *[arrived[place] for place in places])
    return totals


def solution(mesh):
    in_specs = (
        P(("grp", "blk"), "walk", None),
        P(("grp", "blk"), None),
        P("grp"),
        P(),
        P(("grp", "blk", "walk", "sub"), None, None),
    )
    out_specs = P(("grp", "blk", "walk", "sub"), None, None)
    return jax.shard_map(local, mesh=mesh, in_specs=in_specs, out_specs=out_specs, check_vma=False)
```

```python
import functools
import itertools
import math

import jax
import jax.numpy as jnp
from jax import lax
from jax.experimental import pallas as pl
from jax.experimental.pallas import tpu as pltpu
from jax.sharding import PartitionSpec as P

TQ = 4
RSTEPS = 4


phase_period = 8192
quarter_bits = 11
lanes = 128
lane_bits = 7
sublanes = 8
code_limit = 32767.0
smallest_peak = 1e-30


def toward(index, distance, count):
    if count & (count - 1) == 0:
        return index ^ distance
    return (index + distance) % count


def back(index, distance, count):
    if count & (count - 1) == 0:
        return index ^ distance
    return (index + count - distance) % count


def cos_sin(product):
    residue = product & (phase_period - 1)
    quarter = (residue + phase_period // 8) >> quarter_bits
    angle = (residue - (quarter << quarter_bits)).astype(jnp.float32) * (2.0 * math.pi / phase_period)
    square = angle * angle
    sine = angle + angle * square * (
        -1.0 / 6.0 + square * (1.0 / 120.0 + square * (-1.0 / 5040.0 + square * (1.0 / 362880.0)))
    )
    cosine = 1.0 + square * (
        -0.5 + square * (1.0 / 24.0 + square * (-1.0 / 720.0 + square * (1.0 / 40320.0)))
    )
    odd = (quarter & 1) == 1
    cosine_out = jnp.where(odd, sine, cosine)
    sine_out = jnp.where(odd, cosine, sine)
    cosine_out = jnp.where(((quarter + 1) & 2) == 2, -cosine_out, cosine_out)
    sine_out = jnp.where((quarter & 2) == 2, -sine_out, sine_out)
    return cosine_out, sine_out


def row_ids(count):
    return lax.broadcasted_iota(jnp.int32, (count, lanes), 0)


def split_by(ids, size):
    if size & (size - 1) == 0:
        return ids >> (size.bit_length() - 1), ids & (size - 1)
    return ids // size, ids % size


def tile_of(start):
    return pl.ds(start if isinstance(start, int) else pl.multiple_of(start, lanes), lanes)


def make_table(vertex_ref, table_ref, first, place, sub_index):
    columns = table_ref.shape[0]
    blocks = columns // lanes
    half_blocks = blocks // 2
    coarse_rows = -(-max(half_blocks, 1) // sublanes) * sublanes
    middle_count = lanes // sublanes
    center = sub_index * columns + (blocks - 1) * (lanes // 2)
    here = tile_of(place)
    vertex = vertex_ref[:, tile_of(first)]
    cosine, sine = cos_sin(vertex * (row_ids(sublanes) + center))
    cas_fine, cam_fine = cosine + sine, cosine - sine
    cos_middle, sin_middle = cos_sin(vertex * (row_ids(middle_count) * sublanes))
    cos_coarse, sin_coarse = cos_sin(
        vertex * ((blocks - 1 - 2 * row_ids(coarse_rows)) * (lanes // 2))
    )
    for pair in range(middle_count // 2):
        cas, cam = [], []
        for middle in (2 * pair, 2 * pair + 1):
            c, s = cos_middle[middle : middle + 1], sin_middle[middle : middle + 1]
            cas.append(c * cas_fine + s * cam_fine)
            cam.append(c * cam_fine - s * cas_fine)
        cas, cam = jnp.concatenate(cas, axis=0), jnp.concatenate(cam, axis=0)
        start = pair * 2 * sublanes
        for low in range(half_blocks):
            high = blocks - 1 - low
            even = cos_coarse[low : low + 1] * cas
            odd = sin_coarse[low : low + 1] * cam
            for block, value in ((low, even - odd), (high, even + odd)):
                row = block * lanes + start
                table_ref[row : row + 2 * sublanes, here] = value.astype(jnp.bfloat16)
        if blocks % 2:
            row = half_blocks * lanes + start
            table_ref[row : row + 2 * sublanes, here] = cas.astype(jnp.bfloat16)


def table_kernel(sizes, vertex_ref, table_ref, left_ref):
    blk_count, walk_count, sub_count, rows_own = sizes
    walk_index = lax.axis_index("walk")
    sub_index = lax.axis_index("sub")
    window_rows, rows_local = left_ref.shape

    ids, inner = split_by(row_ids(window_rows), rows_own)
    ids, blk_part = split_by(ids, blk_count)
    walk_part, sub_part = split_by(ids, sub_count)
    sub_part = toward(sub_index, sub_part, sub_count)
    walk_part = toward(walk_index, walk_part, walk_count)
    window = ((blk_part * walk_count + walk_part) * sub_count + sub_part) * rows_own + inner
    own_start = pl.multiple_of(walk_index * rows_local, lanes)
    for start in range(0, rows_local, lanes):
        own_vertex = vertex_ref[:, pl.ds(own_start + start, lanes)]
        cosine, sine = cos_sin(own_vertex * window)
        left_ref[:, start : start + lanes] = (cosine + sine).astype(jnp.bfloat16)

    @pl.loop(0, table_ref.shape[1] // lanes)
    def _(step):
        make_table(vertex_ref, table_ref, step * lanes, step * lanes, sub_index)


def product_kernel(sizes, matrix_ref, vertex_ref, early_ref, left_ref, *rest):
    *sent_refs, late_ref, weight_ref = rest
    blk_count, _, _, rows_own = sizes
    sub_index = lax.axis_index("sub")
    vertices = matrix_ref.shape[2]
    window_rows = left_ref.shape[0]
    early = early_ref.shape[1]

    chunk = 4 * lanes
    tiles = list(range(0, vertices - early, lanes))
    chunks = list(range(0, vertices, chunk))
    for i, start in enumerate(chunks):
        left_product = jnp.dot(
            left_ref[...], matrix_ref[0, :, start : start + chunk], preferred_element_type=jnp.float32
        )
        for tile in tiles[i * len(tiles) // len(chunks) : (i + 1) * len(tiles) // len(chunks)]:
            make_table(vertex_ref, late_ref, early + tile, tile, sub_index)
        high = left_product.astype(jnp.bfloat16)
        weight_ref[:window_rows, start : start + chunk] = high
        weight_ref[window_rows:, start : start + chunk] = (
            left_product - high.astype(jnp.float32)
        ).astype(jnp.bfloat16)
    green = sum(
        lax.dot_general(
            weight_ref[:, start : start + table_ref.shape[1]],
            table_ref[...],
            (((1,), (1,)), ((), ())),
            preferred_element_type=jnp.float32,
        )
        for start, table_ref in ((0, early_ref), (early, late_ref))
    )
    green = green[:window_rows] + green[window_rows:]
    rows_each = blk_count * rows_own
    for place, sent_ref in enumerate(sent_refs):
        sent_ref[...] = green[place * rows_each : (place + 1) * rows_each]


def pick_rows(rows, wanted):
    ids = lax.broadcasted_iota(jnp.int32, (wanted.shape[0], rows.shape[0]), 1)
    chosen = jnp.where(ids == wanted, 1.0, 0.0).astype(jnp.bfloat16)
    return jnp.dot(chosen, rows, preferred_element_type=jnp.float32)


def combine_kernel(sizes, *refs):
    blk_count, walk_count, sub_count, rows_own = sizes
    blk_index = lax.axis_index("blk")
    sub_index = lax.axis_index("sub")
    part_refs, whole_refs = refs[: walk_count * sub_count], refs[walk_count * sub_count :]
    columns_part = part_refs[0].shape[1]
    for distance in range(sub_count):
        sub_part = back(sub_index, distance, sub_count)
        here = pl.ds(pl.multiple_of(sub_part * columns_part, lanes), columns_part)
        total = sum(
            part_refs[walk_part * sub_count + distance][...] for walk_part in range(walk_count)
        ).astype(jnp.bfloat16)
        if len(whole_refs) == 1:
            whole_refs[0][:, here] = total
            continue
        for place, whole_ref in enumerate(whole_refs):
            ids = lax.broadcasted_iota(jnp.int32, (whole_ref.shape[0], 1), 0)
            step, inner = split_by(ids, rows_own)
            _, blk_part = split_by(toward(blk_index, place, blk_count) + RSTEPS * blk_count - step, blk_count)
            whole_ref[:, here] = pick_rows(total, blk_part * rows_own + inner).astype(whole_ref.dtype)


def accumulate_kernel(sizes, distances, last, weights_ref, transfer_ref, old_ref, *rest):
    if last:
        *arrived_refs, out_ref, source_ref, left_ref, unit_ref, new_ref, out_sems = rest
    else:
        *arrived_refs, new_ref, source_ref, left_ref, unit_ref = rest
    blk_count, _, _, rows_own = sizes
    blk_index = lax.axis_index("blk")
    transfers, columns = transfer_ref.shape
    half = columns // 2
    groups = transfers // sublanes
    tiles = columns // lanes
    weights = weights_ref[...] * (1.0 / blk_count)
    walker_ids = lax.broadcasted_iota(jnp.int32, weights.shape, 1)

    ids = lax.broadcasted_iota(jnp.int32, (transfers, 1), 0)
    step, _ = split_by(ids, TQ)
    if arrived_refs[0].shape[0] == blk_count * rows_own:
        _, step = split_by(blk_index + RSTEPS * blk_count - step, blk_count)

    def out_copy(own, part):
        here = slice(part * half, (part + 1) * half)
        return pltpu.make_async_copy(
            new_ref.at[own, :, here], out_ref.at[own, :, here], out_sems.at[own, part]
        )

    def spread(rows, own):
        wide = (transfers, rows.shape[1])
        picked = jnp.broadcast_to(rows[own : own + 1], wide)
        for place in range(1, rows.shape[0] // rows_own):
            row = place * rows_own + own
            picked = jnp.where(step == place, jnp.broadcast_to(rows[row : row + 1], wide), picked)
        return picked

    for own in range(rows_own):
        for place, distance in enumerate(distances):
            rows = arrived_refs[place][...].astype(jnp.float32)
            walker = back(blk_index, distance, blk_count)
            weight = jnp.sum(jnp.where(walker_ids == walker, weights, 0.0), axis=1, keepdims=True)
            left = rows[own : own + 1]
            for blk_part in range(1, rows.shape[0] // rows_own):
                row = blk_part * rows_own + own
                left = jnp.where(step[:1] == blk_part, rows[row : row + 1], left)
            left_ref[place] = left * weight
            peak = jnp.maximum(jnp.max(jnp.abs(rows), axis=1, keepdims=True), smallest_peak)
            codes = jnp.floor(rows * (code_limit / peak) + 0.5).astype(jnp.int32)
            peak = jnp.broadcast_to(peak * (1.0 / code_limit), (rows.shape[0], lanes))
            unit_ref[place] = spread(peak, own)
            source_ref[place] = spread((codes[:, :half] << 16) | (codes[:, half:] & 0xFFFF), own)

        together = len(distances) if len(distances) <= 4 else math.gcd(len(distances), 4)

        for tile in range(tiles):
            here = slice(tile * lanes, (tile + 1) * lanes)
            for group in range(groups):
                rows = slice(group * sublanes, (group + 1) * sublanes)
                index = transfer_ref[rows, here]
                index_lane = index & (lanes - 1)
                in_first = index < half
                index_tile = jnp.where(in_first, index, index - half) >> lane_bits

                def add_walkers(first, total):
                    picked = [jnp.zeros((sublanes, lanes), jnp.int32)] * together
                    for source in range(half // lanes):
                        match = index_tile == source
                        for k in range(together):
                            words = source_ref[
                                first + k, rows, source * lanes : (source + 1) * lanes
                            ]
                            words = jnp.take_along_axis(
                                words, index_lane, axis=1, mode="promise_in_bounds"
                            )
                            picked[k] = jnp.where(match, words, picked[k])
                    for k in range(together):
                        code = jnp.where(in_first, picked[k], picked[k] << 16) >> 16
                        total = total + left_ref[first + k, :, here] * (
                            unit_ref[first + k, rows] * code.astype(jnp.float32)
                        )
                    return total

                total = old_ref[own, rows, here]
                if len(distances) == together:
                    total = add_walkers(0, total)
                else:
                    total = lax.fori_loop(
                        0, len(distances) // together, lambda i, t: add_walkers(i * together, t), total
                    )
                new_ref[own, rows, here] = total

            if last and (tile + 1) % (tiles // 2) == 0:
                out_copy(own, (tile + 1) // (tiles // 2) - 1).start()
    if last:
        for own in range(rows_own):
            for part in range(2):
                out_copy(own, part).wait()


def exchange(pieces, axes, counts):
    positions = list(itertools.product(*map(range, counts)))
    place = {position: i for i, position in enumerate(positions)}
    arrived = [pieces[0]] * len(positions)
    for i in range(1, len(positions)):
        route = [
            (place[position], place[tuple(map(toward, position, positions[i], counts))])
            for position in positions
        ]
        arrived[i] = lax.ppermute(pieces[i], axes, route)
    return arrived


def local(walker_mats, vertex, weights, transfer_table, g4_old):
    blk_count = lax.axis_size("blk")
    walk_count = lax.axis_size("walk")
    sub_count = lax.axis_size("sub")
    rows_local, vertices = walker_mats.shape[1:]
    rows_own, transfers, columns = g4_old.shape
    columns_local = columns // sub_count
    devices = blk_count * walk_count * sub_count
    sizes = (blk_count, walk_count, sub_count, rows_own)
    vmem = pl.BlockSpec(memory_space=pltpu.VMEM)
    early = 5 * vertices // (8 * 2 * lanes) * 2 * lanes
    table, left = pl.pallas_call(
        functools.partial(table_kernel, sizes),
        out_shape=[
            jax.ShapeDtypeStruct((columns_local, early), jnp.bfloat16),
            jax.ShapeDtypeStruct((devices * rows_own, rows_local), jnp.bfloat16),
        ],
        in_specs=[vmem],
        out_specs=[vmem] * 2,
        compiler_params=pltpu.CompilerParams(vmem_limit_bytes=24 * 2**20),
        cost_estimate=pl.CostEstimate(
            flops=2000 * columns_local * vertices,
            bytes_accessed=6 * columns_local * vertices,
            transcendentals=0,
        ),
        name="table",
    )(vertex)
    sent = pl.pallas_call(
        functools.partial(product_kernel, sizes),
        out_shape=[jax.ShapeDtypeStruct((blk_count * rows_own, columns_local), jnp.float32)]
        * (walk_count * sub_count),
        in_specs=[vmem] * 4,
        out_specs=[vmem] * (walk_count * sub_count),
        scratch_shapes=[
            pltpu.VMEM((columns_local, vertices - early), jnp.bfloat16),
            pltpu.VMEM((2 * devices * rows_own, vertices), jnp.bfloat16),
        ],
        compiler_params=pltpu.CompilerParams(vmem_limit_bytes=24 * 2**20),
        name="product",
    )(walker_mats, vertex, table, left)
    parts = exchange(sent, ("walk", "sub"), (walk_count, sub_count))
    shared = blk_count <= RSTEPS
    rows_each = (blk_count if shared else RSTEPS) * rows_own
    whole_count = 1 if shared else blk_count
    whole = pl.pallas_call(
        functools.partial(combine_kernel, sizes),
        out_shape=[jax.ShapeDtypeStruct((rows_each, columns), jnp.bfloat16)] * whole_count,
        in_specs=[vmem] * len(parts),
        out_specs=[vmem] * whole_count,
        compiler_params=pltpu.CompilerParams(vmem_limit_bytes=24 * 2**20),
        name="combine",
    )(*parts)
    arrived = exchange(whole * blk_count if shared else whole, ("blk",), (blk_count,))
    far = blk_count // 2
    totals = g4_old
    groups = [0, *range(far + 1, blk_count)], [*range(1, far)], [far]
    for places in groups:
        last = places is groups[-1]
        scratch_shapes = [
            pltpu.VMEM((len(places), transfers, columns // 2), jnp.int32),
            pltpu.VMEM((len(places), 1, columns), jnp.float32),
            pltpu.VMEM((len(places), transfers, lanes), jnp.float32),
        ]
        if last:
            scratch_shapes.append(pltpu.VMEM(g4_old.shape, jnp.float32))
            scratch_shapes.append(pltpu.SemaphoreType.DMA((rows_own, 2)))
        totals = pl.pallas_call(
            functools.partial(accumulate_kernel, sizes, places, last),
            out_shape=jax.ShapeDtypeStruct(g4_old.shape, jnp.float32),
            in_specs=[vmem] * (3 + len(places)),
            out_specs=pl.BlockSpec(memory_space=pl.ANY) if last else vmem,
            scratch_shapes=scratch_shapes,
            compiler_params=pltpu.CompilerParams(vmem_limit_bytes=24 * 2**20),
            cost_estimate=pl.CostEstimate(
                flops=1000 * len(places) * transfers * columns,
                bytes_accessed=12 * transfers * columns,
                transcendentals=0,
            ),
            name="accumulate",
        )(weights[None], transfer_table, totals, *[arrived[place] for place in places])
    return totals


def solution(mesh):
    in_specs = (
        P(("grp", "blk"), "walk", None),
        P(("grp", "blk"), None),
        P("grp"),
        P(),
        P(("grp", "blk", "walk", "sub"), None, None),
    )
    out_specs = P(("grp", "blk", "walk", "sub"), None, None)
    return jax.shard_map(local, mesh=mesh, in_specs=in_specs, out_specs=out_specs, check_vma=False)
```

```python
import functools
import itertools
import math

import jax
import jax.numpy as jnp
from jax import lax
from jax.experimental import pallas as pl
from jax.experimental.pallas import tpu as pltpu
from jax.sharding import PartitionSpec as P

TQ = 4
RSTEPS = 4


phase_period = 8192
quarter_bits = 11
lanes = 128
lane_bits = 7
sublanes = 8
code_limit = 32767.0
smallest_peak = 1e-30


def toward(index, distance, count):
    if count & (count - 1) == 0:
        return index ^ distance
    return (index + distance) % count


def back(index, distance, count):
    if count & (count - 1) == 0:
        return index ^ distance
    return (index + count - distance) % count


def cos_sin(product):
    residue = product & (phase_period - 1)
    quarter = (residue + phase_period // 8) >> quarter_bits
    angle = (residue - (quarter << quarter_bits)).astype(jnp.float32) * (2.0 * math.pi / phase_period)
    square = angle * angle
    sine = angle + angle * square * (
        -1.0 / 6.0 + square * (1.0 / 120.0 + square * (-1.0 / 5040.0 + square * (1.0 / 362880.0)))
    )
    cosine = 1.0 + square * (
        -0.5 + square * (1.0 / 24.0 + square * (-1.0 / 720.0 + square * (1.0 / 40320.0)))
    )
    odd = (quarter & 1) == 1
    cosine_out = jnp.where(odd, sine, cosine)
    sine_out = jnp.where(odd, cosine, sine)
    cosine_out = jnp.where(((quarter + 1) & 2) == 2, -cosine_out, cosine_out)
    sine_out = jnp.where((quarter & 2) == 2, -sine_out, sine_out)
    return cosine_out, sine_out


def row_ids(count):
    return lax.broadcasted_iota(jnp.int32, (count, lanes), 0)


def split_by(ids, size):
    if size & (size - 1) == 0:
        return ids >> (size.bit_length() - 1), ids & (size - 1)
    return ids // size, ids % size


def tile_of(start):
    return pl.ds(start if isinstance(start, int) else pl.multiple_of(start, lanes), lanes)


def make_table(vertex_ref, table_ref, first, place, sub_index):
    columns = table_ref.shape[0]
    blocks = columns // lanes
    half_blocks = blocks // 2
    coarse_rows = -(-max(half_blocks, 1) // sublanes) * sublanes
    middle_count = lanes // sublanes
    center = sub_index * columns + (blocks - 1) * (lanes // 2)
    here = tile_of(place)
    vertex = vertex_ref[:, tile_of(first)]
    cosine, sine = cos_sin(vertex * (row_ids(sublanes) + center))
    cas_fine, cam_fine = cosine + sine, cosine - sine
    cos_middle, sin_middle = cos_sin(vertex * (row_ids(middle_count) * sublanes))
    cos_coarse, sin_coarse = cos_sin(
        vertex * ((blocks - 1 - 2 * row_ids(coarse_rows)) * (lanes // 2))
    )
    for pair in range(middle_count // 2):
        cas, cam = [], []
        for middle in (2 * pair, 2 * pair + 1):
            c, s = cos_middle[middle : middle + 1], sin_middle[middle : middle + 1]
            cas.append(c * cas_fine + s * cam_fine)
            cam.append(c * cam_fine - s * cas_fine)
        cas, cam = jnp.concatenate(cas, axis=0), jnp.concatenate(cam, axis=0)
        start = pair * 2 * sublanes
        for low in range(half_blocks):
            high = blocks - 1 - low
            even = cos_coarse[low : low + 1] * cas
            odd = sin_coarse[low : low + 1] * cam
            for block, value in ((low, even - odd), (high, even + odd)):
                row = block * lanes + start
                table_ref[row : row + 2 * sublanes, here] = value.astype(jnp.bfloat16)
        if blocks % 2:
            row = half_blocks * lanes + start
            table_ref[row : row + 2 * sublanes, here] = cas.astype(jnp.bfloat16)


def transform_kernel(sizes, matrix_hbm, vertex_hbm, *rest):
    *sent_refs, matrix_ref, vertex_ref, left_ref, early_ref, late_ref, weight_ref, matrix_sems, vertex_sem = rest
    blk_count, walk_count, sub_count, rows_own = sizes
    walk_index = lax.axis_index("walk")
    sub_index = lax.axis_index("sub")
    rows_local, vertices = matrix_ref.shape
    window_rows = left_ref.shape[0]
    early = early_ref.shape[1]

    vertex_copy = pltpu.make_async_copy(vertex_hbm, vertex_ref, vertex_sem)
    vertex_copy.start()
    parts = matrix_sems.shape[0]
    part = vertices // parts
    matrix_copies = [
        pltpu.make_async_copy(
            matrix_hbm.at[0, :, i * part : (i + 1) * part],
            matrix_ref.at[:, i * part : (i + 1) * part],
            matrix_sems.at[i],
        )
        for i in range(parts)
    ]
    for copy in matrix_copies:
        copy.start()

    ids, inner = split_by(row_ids(window_rows), rows_own)
    ids, blk_part = split_by(ids, blk_count)
    walk_part, sub_part = split_by(ids, sub_count)
    sub_part = toward(sub_index, sub_part, sub_count)
    walk_part = toward(walk_index, walk_part, walk_count)
    window = ((blk_part * walk_count + walk_part) * sub_count + sub_part) * rows_own + inner

    vertex_copy.wait()
    own_start = pl.multiple_of(walk_index * rows_local, lanes)
    for start in range(0, rows_local, lanes):
        own_vertex = vertex_ref[:, pl.ds(own_start + start, lanes)]
        cosine, sine = cos_sin(own_vertex * window)
        left_ref[:, start : start + lanes] = (cosine + sine).astype(jnp.bfloat16)

    @pl.loop(0, early // lanes)
    def _(step):
        make_table(vertex_ref, early_ref, step * lanes, step * lanes, sub_index)

    chunk = 4 * lanes
    tiles = list(range(0, vertices - early, lanes))
    chunks = list(range(0, vertices, chunk))
    for i, start in enumerate(chunks):
        if start % part == 0:
            matrix_copies[start // part].wait()
        left_product = jnp.dot(
            left_ref[...], matrix_ref[:, start : start + chunk], preferred_element_type=jnp.float32
        )
        for tile in tiles[i * len(tiles) // len(chunks) : (i + 1) * len(tiles) // len(chunks)]:
            make_table(vertex_ref, late_ref, early + tile, tile, sub_index)
        high = left_product.astype(jnp.bfloat16)
        weight_ref[:window_rows, start : start + chunk] = high
        weight_ref[window_rows:, start : start + chunk] = (
            left_product - high.astype(jnp.float32)
        ).astype(jnp.bfloat16)
    green = sum(
        lax.dot_general(
            weight_ref[:, start : start + table_ref.shape[1]],
            table_ref[...],
            (((1,), (1,)), ((), ())),
            preferred_element_type=jnp.float32,
        )
        for start, table_ref in ((0, early_ref), (early, late_ref))
    )
    green = green[:window_rows] + green[window_rows:]
    rows_each = blk_count * rows_own
    for place, sent_ref in enumerate(sent_refs):
        sent_ref[...] = green[place * rows_each : (place + 1) * rows_each]


def pick_rows(rows, wanted):
    ids = lax.broadcasted_iota(jnp.int32, (wanted.shape[0], rows.shape[0]), 1)
    chosen = jnp.where(ids == wanted, 1.0, 0.0).astype(jnp.bfloat16)
    return jnp.dot(chosen, rows, preferred_element_type=jnp.float32)


def combine_kernel(sizes, *refs):
    blk_count, walk_count, sub_count, rows_own = sizes
    blk_index = lax.axis_index("blk")
    sub_index = lax.axis_index("sub")
    part_refs, whole_refs = refs[: walk_count * sub_count], refs[walk_count * sub_count :]
    columns_part = part_refs[0].shape[1]
    for distance in range(sub_count):
        sub_part = back(sub_index, distance, sub_count)
        here = pl.ds(pl.multiple_of(sub_part * columns_part, lanes), columns_part)
        total = sum(
            part_refs[walk_part * sub_count + distance][...] for walk_part in range(walk_count)
        ).astype(jnp.bfloat16)
        if len(whole_refs) == 1:
            whole_refs[0][:, here] = total
            continue
        for place, whole_ref in enumerate(whole_refs):
            ids = lax.broadcasted_iota(jnp.int32, (whole_ref.shape[0], 1), 0)
            step, inner = split_by(ids, rows_own)
            _, blk_part = split_by(toward(blk_index, place, blk_count) + RSTEPS * blk_count - step, blk_count)
            whole_ref[:, here] = pick_rows(total, blk_part * rows_own + inner).astype(whole_ref.dtype)


def accumulate_kernel(sizes, distances, last, weights_ref, transfer_ref, old_ref, *rest):
    if last:
        *arrived_refs, out_ref, source_ref, left_ref, unit_ref, new_ref, out_sems = rest
    else:
        *arrived_refs, new_ref, source_ref, left_ref, unit_ref = rest
    blk_count, _, _, rows_own = sizes
    blk_index = lax.axis_index("blk")
    transfers, columns = transfer_ref.shape
    half = columns // 2
    groups = transfers // sublanes
    tiles = columns // lanes
    weights = weights_ref[...] * (1.0 / blk_count)
    walker_ids = lax.broadcasted_iota(jnp.int32, weights.shape, 1)

    ids = lax.broadcasted_iota(jnp.int32, (transfers, 1), 0)
    step, _ = split_by(ids, TQ)
    if arrived_refs[0].shape[0] == blk_count * rows_own:
        _, step = split_by(blk_index + RSTEPS * blk_count - step, blk_count)

    def out_copy(own, part):
        here = slice(part * half, (part + 1) * half)
        return pltpu.make_async_copy(
            new_ref.at[own, :, here], out_ref.at[own, :, here], out_sems.at[own, part]
        )

    def spread(rows, own):
        wide = (transfers, rows.shape[1])
        picked = jnp.broadcast_to(rows[own : own + 1], wide)
        for place in range(1, rows.shape[0] // rows_own):
            row = place * rows_own + own
            picked = jnp.where(step == place, jnp.broadcast_to(rows[row : row + 1], wide), picked)
        return picked

    for own in range(rows_own):
        for place, distance in enumerate(distances):
            rows = arrived_refs[place][...].astype(jnp.float32)
            walker = back(blk_index, distance, blk_count)
            weight = jnp.sum(jnp.where(walker_ids == walker, weights, 0.0), axis=1, keepdims=True)
            left = rows[own : own + 1]
            for blk_part in range(1, rows.shape[0] // rows_own):
                row = blk_part * rows_own + own
                left = jnp.where(step[:1] == blk_part, rows[row : row + 1], left)
            left_ref[place] = left * weight
            peak = jnp.maximum(jnp.max(jnp.abs(rows), axis=1, keepdims=True), smallest_peak)
            codes = jnp.floor(rows * (code_limit / peak) + 0.5).astype(jnp.int32)
            peak = jnp.broadcast_to(peak * (1.0 / code_limit), (rows.shape[0], lanes))
            unit_ref[place] = spread(peak, own)
            source_ref[place] = spread((codes[:, :half] << 16) | (codes[:, half:] & 0xFFFF), own)

        together = len(distances) if len(distances) <= 4 else math.gcd(len(distances), 4)

        for tile in range(tiles):
            here = slice(tile * lanes, (tile + 1) * lanes)
            for group in range(groups):
                rows = slice(group * sublanes, (group + 1) * sublanes)
                index = transfer_ref[rows, here]
                index_lane = index & (lanes - 1)
                in_first = index < half
                index_tile = jnp.where(in_first, index, index - half) >> lane_bits

                def add_walkers(first, total):
                    picked = [jnp.zeros((sublanes, lanes), jnp.int32)] * together
                    for source in range(half // lanes):
                        match = index_tile == source
                        for k in range(together):
                            words = source_ref[
                                first + k, rows, source * lanes : (source + 1) * lanes
                            ]
                            words = jnp.take_along_axis(
                                words, index_lane, axis=1, mode="promise_in_bounds"
                            )
                            picked[k] = jnp.where(match, words, picked[k])
                    for k in range(together):
                        code = jnp.where(in_first, picked[k], picked[k] << 16) >> 16
                        total = total + left_ref[first + k, :, here] * (
                            unit_ref[first + k, rows] * code.astype(jnp.float32)
                        )
                    return total

                total = old_ref[own, rows, here]
                if len(distances) == together:
                    total = add_walkers(0, total)
                else:
                    total = lax.fori_loop(
                        0, len(distances) // together, lambda i, t: add_walkers(i * together, t), total
                    )
                new_ref[own, rows, here] = total

            if last and (tile + 1) % (tiles // 2) == 0:
                out_copy(own, (tile + 1) // (tiles // 2) - 1).start()
    if last:
        for own in range(rows_own):
            for part in range(2):
                out_copy(own, part).wait()


def exchange(pieces, axes, counts):
    positions = list(itertools.product(*map(range, counts)))
    place = {position: i for i, position in enumerate(positions)}
    arrived = [pieces[0]] * len(positions)
    for i in range(1, len(positions)):
        route = [
            (place[position], place[tuple(map(toward, position, positions[i], counts))])
            for position in positions
        ]
        arrived[i] = lax.ppermute(pieces[i], axes, route)
    return arrived


def local(walker_mats, vertex, weights, transfer_table, g4_old):
    blk_count = lax.axis_size("blk")
    walk_count = lax.axis_size("walk")
    sub_count = lax.axis_size("sub")
    rows_local, vertices = walker_mats.shape[1:]
    rows_own, transfers, columns = g4_old.shape
    columns_local = columns // sub_count
    devices = blk_count * walk_count * sub_count
    sizes = (blk_count, walk_count, sub_count, rows_own)
    vmem = pl.BlockSpec(memory_space=pltpu.VMEM)
    early = 3 * vertices // (8 * 2 * lanes) * 2 * lanes
    sent = pl.pallas_call(
        functools.partial(transform_kernel, sizes),
        out_shape=[jax.ShapeDtypeStruct((blk_count * rows_own, columns_local), jnp.float32)]
        * (walk_count * sub_count),
        in_specs=[pl.BlockSpec(memory_space=pltpu.HBM)] * 2,
        out_specs=[vmem] * (walk_count * sub_count),
        scratch_shapes=[
            pltpu.VMEM((rows_local, vertices), jnp.bfloat16),
            pltpu.VMEM((1, vertices), jnp.int32),
            pltpu.VMEM((devices * rows_own, rows_local), jnp.bfloat16),
            pltpu.VMEM((columns_local, early), jnp.bfloat16),
            pltpu.VMEM((columns_local, vertices - early), jnp.bfloat16),
            pltpu.VMEM((2 * devices * rows_own, vertices), jnp.bfloat16),
            pltpu.SemaphoreType.DMA((2,)),
            pltpu.SemaphoreType.DMA,
        ],
        compiler_params=pltpu.CompilerParams(vmem_limit_bytes=24 * 2**20),
        name="transform",
    )(*[pltpu.with_memory_space_constraint(x, pltpu.HBM) for x in (walker_mats, vertex)])
    parts = exchange(sent, ("walk", "sub"), (walk_count, sub_count))
    shared = blk_count <= RSTEPS
    rows_each = (blk_count if shared else RSTEPS) * rows_own
    whole_count = 1 if shared else blk_count
    whole = pl.pallas_call(
        functools.partial(combine_kernel, sizes),
        out_shape=[jax.ShapeDtypeStruct((rows_each, columns), jnp.bfloat16)] * whole_count,
        in_specs=[vmem] * len(parts),
        out_specs=[vmem] * whole_count,
        compiler_params=pltpu.CompilerParams(vmem_limit_bytes=24 * 2**20),
        name="combine",
    )(*parts)
    arrived = exchange(whole * blk_count if shared else whole, ("blk",), (blk_count,))
    far = blk_count // 2
    totals = g4_old
    groups = [0, *range(far + 1, blk_count)], [*range(1, far)], [far]
    for places in groups:
        last = places is groups[-1]
        scratch_shapes = [
            pltpu.VMEM((len(places), transfers, columns // 2), jnp.int32),
            pltpu.VMEM((len(places), 1, columns), jnp.float32),
            pltpu.VMEM((len(places), transfers, lanes), jnp.float32),
        ]
        if last:
            scratch_shapes.append(pltpu.VMEM(g4_old.shape, jnp.float32))
            scratch_shapes.append(pltpu.SemaphoreType.DMA((rows_own, 2)))
        totals = pl.pallas_call(
            functools.partial(accumulate_kernel, sizes, places, last),
            out_shape=jax.ShapeDtypeStruct(g4_old.shape, jnp.float32),
            in_specs=[vmem] * (3 + len(places)),
            out_specs=pl.BlockSpec(memory_space=pl.ANY) if last else vmem,
            scratch_shapes=scratch_shapes,
            compiler_params=pltpu.CompilerParams(vmem_limit_bytes=24 * 2**20),
            cost_estimate=pl.CostEstimate(
                flops=1000 * len(places) * transfers * columns,
                bytes_accessed=12 * transfers * columns,
                transcendentals=0,
            ),
            name="accumulate",
        )(weights[None], transfer_table, totals, *[arrived[place] for place in places])
    return totals


def solution(mesh):
    in_specs = (
        P(("grp", "blk"), "walk", None),
        P(("grp", "blk"), None),
        P("grp"),
        P(),
        P(("grp", "blk", "walk", "sub"), None, None),
    )
    out_specs = P(("grp", "blk", "walk", "sub"), None, None)
    return jax.shard_map(local, mesh=mesh, in_specs=in_specs, out_specs=out_specs, check_vma=False)
```

```python
import functools
import itertools
import math

import jax
import jax.numpy as jnp
from jax import lax
from jax.experimental import pallas as pl
from jax.experimental.pallas import tpu as pltpu
from jax.sharding import PartitionSpec as P

TQ = 4
RSTEPS = 4


phase_period = 8192
quarter_bits = 11
lanes = 128
lane_bits = 7
sublanes = 8
code_limit = 32767.0
smallest_peak = 1e-30


def toward(index, distance, count):
    if count & (count - 1) == 0:
        return index ^ distance
    return (index + distance) % count


def back(index, distance, count):
    if count & (count - 1) == 0:
        return index ^ distance
    return (index + count - distance) % count


def cos_sin(product):
    residue = product & (phase_period - 1)
    quarter = (residue + phase_period // 8) >> quarter_bits
    angle = (residue - (quarter << quarter_bits)).astype(jnp.float32) * (2.0 * math.pi / phase_period)
    square = angle * angle
    sine = angle + angle * square * (
        -1.0 / 6.0 + square * (1.0 / 120.0 + square * (-1.0 / 5040.0 + square * (1.0 / 362880.0)))
    )
    cosine = 1.0 + square * (
        -0.5 + square * (1.0 / 24.0 + square * (-1.0 / 720.0 + square * (1.0 / 40320.0)))
    )
    odd = (quarter & 1) == 1
    cosine_out = jnp.where(odd, sine, cosine)
    sine_out = jnp.where(odd, cosine, sine)
    cosine_out = jnp.where(((quarter + 1) & 2) == 2, -cosine_out, cosine_out)
    sine_out = jnp.where((quarter & 2) == 2, -sine_out, sine_out)
    return cosine_out, sine_out


def row_ids(count):
    return lax.broadcasted_iota(jnp.int32, (count, lanes), 0)


def split_by(ids, size):
    if size & (size - 1) == 0:
        return ids >> (size.bit_length() - 1), ids & (size - 1)
    return ids // size, ids % size


def tile_of(start):
    return pl.ds(start if isinstance(start, int) else pl.multiple_of(start, lanes), lanes)


def make_table(vertex_ref, table_ref, first, place, sub_index):
    columns = table_ref.shape[0]
    blocks = columns // lanes
    half_blocks = blocks // 2
    coarse_rows = -(-max(half_blocks, 1) // sublanes) * sublanes
    middle_count = lanes // sublanes
    center = sub_index * columns + (blocks - 1) * (lanes // 2)
    here = tile_of(place)
    vertex = vertex_ref[:, tile_of(first)]
    cosine, sine = cos_sin(vertex * (row_ids(sublanes) + center))
    cas_fine, cam_fine = cosine + sine, cosine - sine
    cos_middle, sin_middle = cos_sin(vertex * (row_ids(middle_count) * sublanes))
    cos_coarse, sin_coarse = cos_sin(
        vertex * ((blocks - 1 - 2 * row_ids(coarse_rows)) * (lanes // 2))
    )
    for pair in range(middle_count // 2):
        cas, cam = [], []
        for middle in (2 * pair, 2 * pair + 1):
            c, s = cos_middle[middle : middle + 1], sin_middle[middle : middle + 1]
            cas.append(c * cas_fine + s * cam_fine)
            cam.append(c * cam_fine - s * cas_fine)
        cas, cam = jnp.concatenate(cas, axis=0), jnp.concatenate(cam, axis=0)
        start = pair * 2 * sublanes
        for low in range(half_blocks):
            high = blocks - 1 - low
            even = cos_coarse[low : low + 1] * cas
            odd = sin_coarse[low : low + 1] * cam
            for block, value in ((low, even - odd), (high, even + odd)):
                row = block * lanes + start
                table_ref[row : row + 2 * sublanes, here] = value.astype(jnp.bfloat16)
        if blocks % 2:
            row = half_blocks * lanes + start
            table_ref[row : row + 2 * sublanes, here] = cas.astype(jnp.bfloat16)


def table_kernel(sizes, vertex_ref, table_ref, left_ref):
    blk_count, walk_count, sub_count, rows_own = sizes
    walk_index = lax.axis_index("walk")
    sub_index = lax.axis_index("sub")
    window_rows, rows_local = left_ref.shape

    ids, inner = split_by(row_ids(window_rows), rows_own)
    ids, blk_part = split_by(ids, blk_count)
    walk_part, sub_part = split_by(ids, sub_count)
    sub_part = toward(sub_index, sub_part, sub_count)
    walk_part = toward(walk_index, walk_part, walk_count)
    window = ((blk_part * walk_count + walk_part) * sub_count + sub_part) * rows_own + inner
    own_start = pl.multiple_of(walk_index * rows_local, lanes)
    for start in range(0, rows_local, lanes):
        own_vertex = vertex_ref[:, pl.ds(own_start + start, lanes)]
        cosine, sine = cos_sin(own_vertex * window)
        left_ref[:, start : start + lanes] = (cosine + sine).astype(jnp.bfloat16)

    @pl.loop(0, table_ref.shape[1] // lanes)
    def _(step):
        make_table(vertex_ref, table_ref, step * lanes, step * lanes, sub_index)


def product_kernel(sizes, matrix_ref, vertex_ref, early_ref, left_ref, *rest):
    *sent_refs, late_ref, weight_ref = rest
    blk_count, _, _, rows_own = sizes
    sub_index = lax.axis_index("sub")
    vertices = matrix_ref.shape[2]
    window_rows = left_ref.shape[0]
    early = early_ref.shape[1]

    chunk = 4 * lanes
    tiles = list(range(0, vertices - early, lanes))
    chunks = list(range(0, vertices, chunk))
    for i, start in enumerate(chunks):
        left_product = jnp.dot(
            left_ref[...], matrix_ref[0, :, start : start + chunk], preferred_element_type=jnp.float32
        )
        for tile in tiles[i * len(tiles) // len(chunks) : (i + 1) * len(tiles) // len(chunks)]:
            make_table(vertex_ref, late_ref, early + tile, tile, sub_index)
        high = left_product.astype(jnp.bfloat16)
        weight_ref[:window_rows, start : start + chunk] = high
        weight_ref[window_rows:, start : start + chunk] = (
            left_product - high.astype(jnp.float32)
        ).astype(jnp.bfloat16)
    green = sum(
        lax.dot_general(
            table_ref[...],
            weight_ref[:, start : start + table_ref.shape[1]],
            (((1,), (1,)), ((), ())),
            preferred_element_type=jnp.float32,
        )
        for start, table_ref in ((0, early_ref), (early, late_ref))
    ).T
    green = green[:window_rows] + green[window_rows:]
    rows_each = blk_count * rows_own
    for place, sent_ref in enumerate(sent_refs):
        sent_ref[...] = green[place * rows_each : (place + 1) * rows_each]


def pick_rows(rows, wanted):
    ids = lax.broadcasted_iota(jnp.int32, (wanted.shape[0], rows.shape[0]), 1)
    chosen = jnp.where(ids == wanted, 1.0, 0.0).astype(jnp.bfloat16)
    return jnp.dot(chosen, rows, preferred_element_type=jnp.float32)


def combine_kernel(sizes, *refs):
    blk_count, walk_count, sub_count, rows_own = sizes
    blk_index = lax.axis_index("blk")
    sub_index = lax.axis_index("sub")
    part_refs, whole_refs = refs[: walk_count * sub_count], refs[walk_count * sub_count :]
    columns_part = part_refs[0].shape[1]
    for distance in range(sub_count):
        sub_part = back(sub_index, distance, sub_count)
        here = pl.ds(pl.multiple_of(sub_part * columns_part, lanes), columns_part)
        total = sum(
            part_refs[walk_part * sub_count + distance][...] for walk_part in range(walk_count)
        ).astype(jnp.bfloat16)
        if len(whole_refs) == 1:
            whole_refs[0][:, here] = total
            continue
        for place, whole_ref in enumerate(whole_refs):
            ids = lax.broadcasted_iota(jnp.int32, (whole_ref.shape[0], 1), 0)
            step, inner = split_by(ids, rows_own)
            _, blk_part = split_by(toward(blk_index, place, blk_count) + RSTEPS * blk_count - step, blk_count)
            whole_ref[:, here] = pick_rows(total, blk_part * rows_own + inner).astype(whole_ref.dtype)


def accumulate_kernel(sizes, distances, last, weights_ref, transfer_ref, old_ref, *rest):
    if last:
        *arrived_refs, out_ref, source_ref, left_ref, unit_ref, new_ref, out_sems = rest
    else:
        *arrived_refs, new_ref, source_ref, left_ref, unit_ref = rest
    blk_count, _, _, rows_own = sizes
    blk_index = lax.axis_index("blk")
    transfers, columns = transfer_ref.shape
    half = columns // 2
    groups = transfers // sublanes
    tiles = columns // lanes
    weights = weights_ref[...] * (1.0 / blk_count)
    walker_ids = lax.broadcasted_iota(jnp.int32, weights.shape, 1)

    ids = lax.broadcasted_iota(jnp.int32, (transfers, 1), 0)
    step, _ = split_by(ids, TQ)
    if arrived_refs[0].shape[0] == blk_count * rows_own:
        _, step = split_by(blk_index + RSTEPS * blk_count - step, blk_count)

    def out_copy(own, part):
        here = slice(part * half, (part + 1) * half)
        return pltpu.make_async_copy(
            new_ref.at[own, :, here], out_ref.at[own, :, here], out_sems.at[own, part]
        )

    def spread(rows, own):
        wide = (transfers, rows.shape[1])
        picked = jnp.broadcast_to(rows[own : own + 1], wide)
        for place in range(1, rows.shape[0] // rows_own):
            row = place * rows_own + own
            picked = jnp.where(step == place, jnp.broadcast_to(rows[row : row + 1], wide), picked)
        return picked

    for own in range(rows_own):
        for place, distance in enumerate(distances):
            rows = arrived_refs[place][...].astype(jnp.float32)
            walker = back(blk_index, distance, blk_count)
            weight = jnp.sum(jnp.where(walker_ids == walker, weights, 0.0), axis=1, keepdims=True)
            left = rows[own : own + 1]
            for blk_part in range(1, rows.shape[0] // rows_own):
                row = blk_part * rows_own + own
                left = jnp.where(step[:1] == blk_part, rows[row : row + 1], left)
            left_ref[place] = left * weight
            peak = jnp.maximum(jnp.max(jnp.abs(rows), axis=1, keepdims=True), smallest_peak)
            codes = jnp.floor(rows * (code_limit / peak) + 0.5).astype(jnp.int32)
            peak = jnp.broadcast_to(peak * (1.0 / code_limit), (rows.shape[0], lanes))
            unit_ref[place] = spread(peak, own)
            source_ref[place] = spread((codes[:, :half] << 16) | (codes[:, half:] & 0xFFFF), own)

        together = len(distances) if len(distances) <= 4 else math.gcd(len(distances), 4)

        for tile in range(tiles):
            here = slice(tile * lanes, (tile + 1) * lanes)
            for group in range(groups):
                rows = slice(group * sublanes, (group + 1) * sublanes)
                index = transfer_ref[rows, here]
                index_lane = index & (lanes - 1)
                in_first = index < half
                index_tile = jnp.where(in_first, index, index - half) >> lane_bits

                def add_walkers(first, total):
                    picked = [jnp.zeros((sublanes, lanes), jnp.int32)] * together
                    for source in range(half // lanes):
                        match = index_tile == source
                        for k in range(together):
                            words = source_ref[
                                first + k, rows, source * lanes : (source + 1) * lanes
                            ]
                            words = jnp.take_along_axis(
                                words, index_lane, axis=1, mode="promise_in_bounds"
                            )
                            picked[k] = jnp.where(match, words, picked[k])
                    for k in range(together):
                        code = jnp.where(in_first, picked[k], picked[k] << 16) >> 16
                        total = total + left_ref[first + k, :, here] * (
                            unit_ref[first + k, rows] * code.astype(jnp.float32)
                        )
                    return total

                total = old_ref[own, rows, here]
                if len(distances) == together:
                    total = add_walkers(0, total)
                else:
                    total = lax.fori_loop(
                        0, len(distances) // together, lambda i, t: add_walkers(i * together, t), total
                    )
                new_ref[own, rows, here] = total

            if last and (tile + 1) % (tiles // 2) == 0:
                out_copy(own, (tile + 1) // (tiles // 2) - 1).start()
    if last:
        for own in range(rows_own):
            for part in range(2):
                out_copy(own, part).wait()


def exchange(pieces, axes, counts):
    positions = list(itertools.product(*map(range, counts)))
    place = {position: i for i, position in enumerate(positions)}
    arrived = [pieces[0]] * len(positions)
    for i in range(1, len(positions)):
        route = [
            (place[position], place[tuple(map(toward, position, positions[i], counts))])
            for position in positions
        ]
        arrived[i] = lax.ppermute(pieces[i], axes, route)
    return arrived


def local(walker_mats, vertex, weights, transfer_table, g4_old):
    blk_count = lax.axis_size("blk")
    walk_count = lax.axis_size("walk")
    sub_count = lax.axis_size("sub")
    rows_local, vertices = walker_mats.shape[1:]
    rows_own, transfers, columns = g4_old.shape
    columns_local = columns // sub_count
    devices = blk_count * walk_count * sub_count
    sizes = (blk_count, walk_count, sub_count, rows_own)
    vmem = pl.BlockSpec(memory_space=pltpu.VMEM)
    early = 5 * vertices // (8 * 2 * lanes) * 2 * lanes
    table, left = pl.pallas_call(
        functools.partial(table_kernel, sizes),
        out_shape=[
            jax.ShapeDtypeStruct((columns_local, early), jnp.bfloat16),
            jax.ShapeDtypeStruct((devices * rows_own, rows_local), jnp.bfloat16),
        ],
        in_specs=[vmem],
        out_specs=[vmem] * 2,
        compiler_params=pltpu.CompilerParams(vmem_limit_bytes=24 * 2**20),
        cost_estimate=pl.CostEstimate(
            flops=2000 * columns_local * vertices,
            bytes_accessed=6 * columns_local * vertices,
            transcendentals=0,
        ),
        name="table",
    )(vertex)
    sent = pl.pallas_call(
        functools.partial(product_kernel, sizes),
        out_shape=[jax.ShapeDtypeStruct((blk_count * rows_own, columns_local), jnp.float32)]
        * (walk_count * sub_count),
        in_specs=[vmem] * 4,
        out_specs=[vmem] * (walk_count * sub_count),
        scratch_shapes=[
            pltpu.VMEM((columns_local, vertices - early), jnp.bfloat16),
            pltpu.VMEM((2 * devices * rows_own, vertices), jnp.bfloat16),
        ],
        compiler_params=pltpu.CompilerParams(vmem_limit_bytes=24 * 2**20),
        name="product",
    )(walker_mats, vertex, table, left)
    parts = exchange(sent, ("walk", "sub"), (walk_count, sub_count))
    shared = blk_count <= RSTEPS
    rows_each = (blk_count if shared else RSTEPS) * rows_own
    whole_count = 1 if shared else blk_count
    whole = pl.pallas_call(
        functools.partial(combine_kernel, sizes),
        out_shape=[jax.ShapeDtypeStruct((rows_each, columns), jnp.bfloat16)] * whole_count,
        in_specs=[vmem] * len(parts),
        out_specs=[vmem] * whole_count,
        compiler_params=pltpu.CompilerParams(vmem_limit_bytes=24 * 2**20),
        name="combine",
    )(*parts)
    arrived = exchange(whole * blk_count if shared else whole, ("blk",), (blk_count,))
    far = blk_count // 2
    totals = g4_old
    groups = [0, *range(far + 1, blk_count)], [*range(1, far)], [far]
    for places in groups:
        last = places is groups[-1]
        scratch_shapes = [
            pltpu.VMEM((len(places), transfers, columns // 2), jnp.int32),
            pltpu.VMEM((len(places), 1, columns), jnp.float32),
            pltpu.VMEM((len(places), transfers, lanes), jnp.float32),
        ]
        if last:
            scratch_shapes.append(pltpu.VMEM(g4_old.shape, jnp.float32))
            scratch_shapes.append(pltpu.SemaphoreType.DMA((rows_own, 2)))
        totals = pl.pallas_call(
            functools.partial(accumulate_kernel, sizes, places, last),
            out_shape=jax.ShapeDtypeStruct(g4_old.shape, jnp.float32),
            in_specs=[vmem] * (3 + len(places)),
            out_specs=pl.BlockSpec(memory_space=pl.ANY) if last else vmem,
            scratch_shapes=scratch_shapes,
            compiler_params=pltpu.CompilerParams(vmem_limit_bytes=24 * 2**20),
            cost_estimate=pl.CostEstimate(
                flops=1000 * len(places) * transfers * columns,
                bytes_accessed=12 * transfers * columns,
                transcendentals=0,
            ),
            name="accumulate",
        )(weights[None], transfer_table, totals, *[arrived[place] for place in places])
    return totals


def solution(mesh):
    in_specs = (
        P(("grp", "blk"), "walk", None),
        P(("grp", "blk"), None),
        P("grp"),
        P(),
        P(("grp", "blk", "walk", "sub"), None, None),
    )
    out_specs = P(("grp", "blk", "walk", "sub"), None, None)
    return jax.shard_map(local, mesh=mesh, in_specs=in_specs, out_specs=out_specs, check_vma=False)
```

```python
import functools
import itertools
import math

import jax
import jax.numpy as jnp
from jax import lax
from jax.experimental import pallas as pl
from jax.experimental.pallas import tpu as pltpu
from jax.sharding import PartitionSpec as P

TQ = 4
RSTEPS = 4


phase_period = 8192
quarter_bits = 11
lanes = 128
lane_bits = 7
sublanes = 8
code_limit = 32767.0
smallest_peak = 1e-30
exponent_margin = 1e-3


def toward(index, distance, count):
    if count & (count - 1) == 0:
        return index ^ distance
    return (index + distance) % count


def back(index, distance, count):
    if count & (count - 1) == 0:
        return index ^ distance
    return (index + count - distance) % count


def cos_sin(product):
    residue = product & (phase_period - 1)
    quarter = (residue + phase_period // 8) >> quarter_bits
    angle = (residue - (quarter << quarter_bits)).astype(jnp.float32) * (2.0 * math.pi / phase_period)
    square = angle * angle
    sine = angle + angle * square * (
        -1.0 / 6.0 + square * (1.0 / 120.0 + square * (-1.0 / 5040.0 + square * (1.0 / 362880.0)))
    )
    cosine = 1.0 + square * (
        -0.5 + square * (1.0 / 24.0 + square * (-1.0 / 720.0 + square * (1.0 / 40320.0)))
    )
    odd = (quarter & 1) == 1
    cosine_out = jnp.where(odd, sine, cosine)
    sine_out = jnp.where(odd, cosine, sine)
    cosine_out = jnp.where(((quarter + 1) & 2) == 2, -cosine_out, cosine_out)
    sine_out = jnp.where((quarter & 2) == 2, -sine_out, sine_out)
    return cosine_out, sine_out


def row_ids(count):
    return lax.broadcasted_iota(jnp.int32, (count, lanes), 0)


def split_by(ids, size):
    if size & (size - 1) == 0:
        return ids >> (size.bit_length() - 1), ids & (size - 1)
    return ids // size, ids % size


def tile_of(start):
    return pl.ds(start if isinstance(start, int) else pl.multiple_of(start, lanes), lanes)


def make_table(vertex_ref, table_ref, first, place):
    columns = table_ref.shape[0]
    blocks = columns // lanes
    half_blocks = blocks // 2
    coarse_rows = -(-max(half_blocks, 1) // sublanes) * sublanes
    middle_count = lanes // sublanes
    center = (blocks - 1) * (lanes // 2)
    here = tile_of(place)
    vertex = vertex_ref[:, tile_of(first)]
    cosine, sine = cos_sin(vertex * (row_ids(sublanes) + center))
    cas_fine, cam_fine = cosine + sine, cosine - sine
    cos_middle, sin_middle = cos_sin(vertex * (row_ids(middle_count) * sublanes))
    cos_coarse, sin_coarse = cos_sin(
        vertex * ((blocks - 1 - 2 * row_ids(coarse_rows)) * (lanes // 2))
    )
    for pair in range(middle_count // 2):
        cas, cam = [], []
        for middle in (2 * pair, 2 * pair + 1):
            c, s = cos_middle[middle : middle + 1], sin_middle[middle : middle + 1]
            cas.append(c * cas_fine + s * cam_fine)
            cam.append(c * cam_fine - s * cas_fine)
        cas, cam = jnp.concatenate(cas, axis=0), jnp.concatenate(cam, axis=0)
        start = pair * 2 * sublanes
        for low in range(half_blocks):
            high = blocks - 1 - low
            even = cos_coarse[low : low + 1] * cas
            odd = sin_coarse[low : low + 1] * cam
            for block, value in ((low, even - odd), (high, even + odd)):
                row = block * lanes + start
                table_ref[row : row + 2 * sublanes, here] = value.astype(jnp.bfloat16)
        if blocks % 2:
            row = half_blocks * lanes + start
            table_ref[row : row + 2 * sublanes, here] = cas.astype(jnp.bfloat16)


def encode(rows):
    half = rows.shape[1] // 2
    peak = jnp.maximum(jnp.max(jnp.abs(rows), axis=1, keepdims=True), smallest_peak)
    exponent = jnp.ceil(jnp.log2(peak * (1.0 / code_limit)) + exponent_margin)
    codes = jnp.floor(rows * (1.0 / jnp.exp2(exponent)) + 0.5).astype(jnp.int32)
    words = (codes[:, :half] << 16) | (codes[:, half:] & 0xFFFF)
    tail = jnp.broadcast_to(exponent.astype(jnp.int32), (rows.shape[0], lanes))
    return jnp.concatenate([words, tail], axis=1)


def units(coded):
    return jnp.exp2(coded[:, coded.shape[1] - lanes :].astype(jnp.float32))


def decode(coded):
    words = coded[:, : coded.shape[1] - lanes]
    codes = jnp.concatenate([words >> 16, (words << 16) >> 16], axis=1)
    return codes.astype(jnp.float32) * units(coded)[:, :1]


def transform_kernel(sizes, matrix_hbm, vertex_hbm, *rest):
    *sent_refs, matrix_ref, vertex_ref, left_ref, early_ref, late_ref, weight_ref, matrix_sem, vertex_sem = rest
    blk_count, walk_count, sub_count, rows_own = sizes
    walk_index = lax.axis_index("walk")
    sub_index = lax.axis_index("sub")
    rows_local, vertices_local = matrix_ref.shape
    window_rows = left_ref.shape[0]
    early = early_ref.shape[1]

    vertex_copy = pltpu.make_async_copy(vertex_hbm, vertex_ref, vertex_sem)
    vertex_copy.start()
    first = pl.multiple_of(sub_index * vertices_local, lanes)
    matrix_copy = pltpu.make_async_copy(
        matrix_hbm.at[0, :, pl.ds(first, vertices_local)], matrix_ref, matrix_sem
    )
    matrix_copy.start()

    ids, inner = split_by(row_ids(window_rows), rows_own)
    ids, blk_part = split_by(ids, blk_count)
    walk_part, sub_part = split_by(ids, sub_count)
    sub_part = toward(sub_index, sub_part, sub_count)
    walk_part = toward(walk_index, walk_part, walk_count)
    window = ((blk_part * walk_count + walk_part) * sub_count + sub_part) * rows_own + inner

    vertex_copy.wait()
    own_start = pl.multiple_of(walk_index * rows_local, lanes)
    for start in range(0, rows_local, lanes):
        own_vertex = vertex_ref[:, pl.ds(own_start + start, lanes)]
        cosine, sine = cos_sin(own_vertex * window)
        left_ref[:, start : start + lanes] = (cosine + sine).astype(jnp.bfloat16)

    @pl.loop(0, early // lanes)
    def _(step):
        make_table(vertex_ref, early_ref, first + step * lanes, step * lanes)

    matrix_copy.wait()
    late = vertices_local - early
    for start, size in ((0, early), (early, late)):
        left_product = jnp.dot(
            left_ref[...], matrix_ref[:, start : start + size], preferred_element_type=jnp.float32
        )
        high = left_product.astype(jnp.bfloat16)
        weight_ref[:window_rows, start : start + size] = high
        weight_ref[window_rows:, start : start + size] = (
            left_product - high.astype(jnp.float32)
        ).astype(jnp.bfloat16)
    for tile in range(0, late, lanes):
        make_table(vertex_ref, late_ref, first + early + tile, tile)
    green = sum(
        lax.dot_general(
            table_ref[...],
            weight_ref[:, start : start + table_ref.shape[1]],
            (((1,), (1,)), ((), ())),
            preferred_element_type=jnp.float32,
        )
        for start, table_ref in ((0, early_ref), (early, late_ref))
    ).T
    green = green[:window_rows] + green[window_rows:]
    rows_each = blk_count * rows_own
    for place, sent_ref in enumerate(sent_refs):
        rows = green[place * rows_each : (place + 1) * rows_each]
        sent_ref[...] = rows if place == 0 else encode(rows)


def combine_kernel(sizes, *refs):
    blk_count, walk_count, sub_count, rows_own = sizes
    blk_index = lax.axis_index("blk")
    parts = walk_count * sub_count
    part_refs, whole_refs, row_ref = refs[:parts], refs[parts:-1], refs[-1]
    total = part_refs[0][...] + sum(decode(part_ref[...]) for part_ref in part_refs[1:])
    coded = encode(total)
    if len(whole_refs) == 1:
        whole_refs[0][...] = coded
        return
    for row in range(blk_count * rows_own):
        row_ref[row] = coded[row : row + 1]
    for place, whole_ref in enumerate(whole_refs):
        for step in range(RSTEPS):
            blk_part = toward(blk_index, place, blk_count) + RSTEPS * blk_count - step
            _, blk_part = split_by(blk_part, blk_count)
            for inner in range(rows_own):
                row = step * rows_own + inner
                whole_ref[row : row + 1] = row_ref[blk_part * rows_own + inner]


def accumulate_kernel(sizes, distances, last, weights_ref, transfer_ref, old_ref, *rest):
    if last:
        *arrived_refs, out_ref, source_ref, left_ref, unit_ref, new_ref, out_sems = rest
    else:
        *arrived_refs, new_ref, source_ref, left_ref, unit_ref = rest
    blk_count, _, _, rows_own = sizes
    blk_index = lax.axis_index("blk")
    transfers, columns = transfer_ref.shape
    half = columns // 2
    groups = transfers // sublanes
    tiles = columns // lanes
    weights = weights_ref[...] * (1.0 / blk_count)
    walker_ids = lax.broadcasted_iota(jnp.int32, weights.shape, 1)

    ids = lax.broadcasted_iota(jnp.int32, (transfers, 1), 0)
    step, _ = split_by(ids, TQ)
    if arrived_refs[0].shape[0] == blk_count * rows_own:
        _, step = split_by(blk_index + RSTEPS * blk_count - step, blk_count)

    def out_copy(own, part):
        here = slice(part * half, (part + 1) * half)
        return pltpu.make_async_copy(
            new_ref.at[own, :, here], out_ref.at[own, :, here], out_sems.at[own, part]
        )

    def spread(rows, own):
        wide = (transfers, rows.shape[1])
        picked = jnp.broadcast_to(rows[own : own + 1], wide)
        for place in range(1, rows.shape[0] // rows_own):
            row = place * rows_own + own
            picked = jnp.where(step == place, jnp.broadcast_to(rows[row : row + 1], wide), picked)
        return picked

    for own in range(rows_own):
        for place, distance in enumerate(distances):
            coded = arrived_refs[place][...]
            walker = back(blk_index, distance, blk_count)
            weight = jnp.sum(jnp.where(walker_ids == walker, weights, 0.0), axis=1, keepdims=True)
            left = coded[own : own + 1]
            for blk_part in range(1, coded.shape[0] // rows_own):
                row = blk_part * rows_own + own
                left = jnp.where(step[:1] == blk_part, coded[row : row + 1], left)
            left_ref[place] = decode(left) * weight
            unit_ref[place] = spread(units(coded), own)
            source_ref[place] = spread(coded[:, :half], own)

        together = len(distances) if len(distances) <= 4 else math.gcd(len(distances), 4)

        for tile in range(tiles):
            here = slice(tile * lanes, (tile + 1) * lanes)
            for group in range(groups):
                rows = slice(group * sublanes, (group + 1) * sublanes)
                index = transfer_ref[rows, here]
                index_lane = index & (lanes - 1)
                in_first = index < half
                index_tile = jnp.where(in_first, index, index - half) >> lane_bits

                def add_walkers(first, total):
                    picked = [jnp.zeros((sublanes, lanes), jnp.int32)] * together
                    for source in range(half // lanes):
                        match = index_tile == source
                        for k in range(together):
                            words = source_ref[
                                first + k, rows, source * lanes : (source + 1) * lanes
                            ]
                            words = jnp.take_along_axis(
                                words, index_lane, axis=1, mode="promise_in_bounds"
                            )
                            picked[k] = jnp.where(match, words, picked[k])
                    for k in range(together):
                        code = jnp.where(in_first, picked[k], picked[k] << 16) >> 16
                        total = total + left_ref[first + k, :, here] * (
                            unit_ref[first + k, rows] * code.astype(jnp.float32)
                        )
                    return total

                total = old_ref[own, rows, here]
                if len(distances) == together:
                    total = add_walkers(0, total)
                else:
                    total = lax.fori_loop(
                        0, len(distances) // together, lambda i, t: add_walkers(i * together, t), total
                    )
                new_ref[own, rows, here] = total

            if last and (tile + 1) % (tiles // 2) == 0:
                out_copy(own, (tile + 1) // (tiles // 2) - 1).start()
    if last:
        for own in range(rows_own):
            for part in range(2):
                out_copy(own, part).wait()


def exchange(pieces, axes, counts):
    positions = list(itertools.product(*map(range, counts)))
    place = {position: i for i, position in enumerate(positions)}
    arrived = [pieces[0]] * len(positions)
    for i in range(1, len(positions)):
        route = [
            (place[position], place[tuple(map(toward, position, positions[i], counts))])
            for position in positions
        ]
        arrived[i] = lax.ppermute(pieces[i], axes, route)
    return arrived


def local(walker_mats, vertex, weights, transfer_table, g4_old):
    blk_count = lax.axis_size("blk")
    walk_count = lax.axis_size("walk")
    sub_count = lax.axis_size("sub")
    rows_local, vertices = walker_mats.shape[1:]
    rows_own, transfers, columns = g4_old.shape
    devices = blk_count * walk_count * sub_count
    sizes = (blk_count, walk_count, sub_count, rows_own)
    vmem = pl.BlockSpec(memory_space=pltpu.VMEM)
    vertices_local = vertices // sub_count
    early = vertices_local // (4 * lanes) * 2 * lanes
    coded = columns // 2 + lanes
    sent = pl.pallas_call(
        functools.partial(transform_kernel, sizes),
        out_shape=[
            jax.ShapeDtypeStruct((blk_count * rows_own, coded if place else columns), jnp.int32 if place else jnp.float32)
            for place in range(walk_count * sub_count)
        ],
        in_specs=[pl.BlockSpec(memory_space=pl.ANY)] * 2,
        out_specs=[vmem] * (walk_count * sub_count),
        scratch_shapes=[
            pltpu.VMEM((rows_local, vertices_local), jnp.bfloat16),
            pltpu.VMEM((1, vertices), jnp.int32),
            pltpu.VMEM((devices * rows_own, rows_local), jnp.bfloat16),
            pltpu.VMEM((columns, early), jnp.bfloat16),
            pltpu.VMEM((columns, vertices_local - early), jnp.bfloat16),
            pltpu.VMEM((2 * devices * rows_own, vertices_local), jnp.bfloat16),
            pltpu.SemaphoreType.DMA,
            pltpu.SemaphoreType.DMA,
        ],
        compiler_params=pltpu.CompilerParams(vmem_limit_bytes=24 * 2**20),
        name="transform",
    )(*[pltpu.with_memory_space_constraint(x, pltpu.HBM) for x in (walker_mats, vertex)])
    parts = exchange(sent, ("walk", "sub"), (walk_count, sub_count))
    shared = blk_count <= RSTEPS
    rows_each = (blk_count if shared else RSTEPS) * rows_own
    whole_count = 1 if shared else blk_count
    whole = pl.pallas_call(
        functools.partial(combine_kernel, sizes),
        out_shape=[jax.ShapeDtypeStruct((rows_each, coded), jnp.int32)] * whole_count,
        in_specs=[vmem] * len(parts),
        out_specs=[vmem] * whole_count,
        scratch_shapes=[pltpu.VMEM((blk_count * rows_own, 1, coded), jnp.int32)],
        compiler_params=pltpu.CompilerParams(vmem_limit_bytes=24 * 2**20),
        name="combine",
    )(*parts)
    arrived = exchange(whole * blk_count if shared else whole, ("blk",), (blk_count,))
    far = blk_count // 2
    totals = g4_old
    groups = [0, *range(far + 1, blk_count)], [*range(1, far)], [far]
    for places in groups:
        last = places is groups[-1]
        scratch_shapes = [
            pltpu.VMEM((len(places), transfers, columns // 2), jnp.int32),
            pltpu.VMEM((len(places), 1, columns), jnp.float32),
            pltpu.VMEM((len(places), transfers, lanes), jnp.float32),
        ]
        if last:
            scratch_shapes.append(pltpu.VMEM(g4_old.shape, jnp.float32))
            scratch_shapes.append(pltpu.SemaphoreType.DMA((rows_own, 2)))
        totals = pl.pallas_call(
            functools.partial(accumulate_kernel, sizes, places, last),
            out_shape=jax.ShapeDtypeStruct(g4_old.shape, jnp.float32),
            in_specs=[vmem] * (3 + len(places)),
            out_specs=pl.BlockSpec(memory_space=pl.ANY) if last else vmem,
            scratch_shapes=scratch_shapes,
            compiler_params=pltpu.CompilerParams(vmem_limit_bytes=24 * 2**20),
            cost_estimate=pl.CostEstimate(
                flops=1000 * len(places) * transfers * columns,
                bytes_accessed=12 * transfers * columns,
                transcendentals=0,
            ),
            name="accumulate",
        )(weights[None], transfer_table, totals, *[arrived[place] for place in places])
    return totals


def solution(mesh):
    in_specs = (
        P(("grp", "blk"), "walk", None),
        P(("grp", "blk"), None),
        P("grp"),
        P(),
        P(("grp", "blk", "walk", "sub"), None, None),
    )
    out_specs = P(("grp", "blk", "walk", "sub"), None, None)
    return jax.shard_map(local, mesh=mesh, in_specs=in_specs, out_specs=out_specs, check_vma=False)
```

```python
import functools
import itertools
import math

import jax
import jax.numpy as jnp
from jax import lax
from jax.experimental import pallas as pl
from jax.experimental.pallas import tpu as pltpu
from jax.sharding import PartitionSpec as P

TQ = 4
RSTEPS = 4


phase_period = 8192
quarter_bits = 11
lanes = 128
lane_bits = 7
sublanes = 8
code_limit = 32767.0
smallest_peak = 1e-30
exponent_margin = 1e-3


def toward(index, distance, count):
    if count & (count - 1) == 0:
        return index ^ distance
    return (index + distance) % count


def back(index, distance, count):
    if count & (count - 1) == 0:
        return index ^ distance
    return (index + count - distance) % count


def cos_sin(product):
    residue = product & (phase_period - 1)
    quarter = (residue + phase_period // 8) >> quarter_bits
    angle = (residue - (quarter << quarter_bits)).astype(jnp.float32) * (2.0 * math.pi / phase_period)
    square = angle * angle
    sine = angle + angle * square * (
        -1.0 / 6.0 + square * (1.0 / 120.0 + square * (-1.0 / 5040.0 + square * (1.0 / 362880.0)))
    )
    cosine = 1.0 + square * (
        -0.5 + square * (1.0 / 24.0 + square * (-1.0 / 720.0 + square * (1.0 / 40320.0)))
    )
    odd = (quarter & 1) == 1
    cosine_out = jnp.where(odd, sine, cosine)
    sine_out = jnp.where(odd, cosine, sine)
    cosine_out = jnp.where(((quarter + 1) & 2) == 2, -cosine_out, cosine_out)
    sine_out = jnp.where((quarter & 2) == 2, -sine_out, sine_out)
    return cosine_out, sine_out


def row_ids(count):
    return lax.broadcasted_iota(jnp.int32, (count, lanes), 0)


def split_by(ids, size):
    if size & (size - 1) == 0:
        return ids >> (size.bit_length() - 1), ids & (size - 1)
    return ids // size, ids % size


def tile_of(start):
    return pl.ds(start if isinstance(start, int) else pl.multiple_of(start, lanes), lanes)


def make_table(vertex_ref, table_ref, first, place):
    columns = table_ref.shape[0]
    blocks = columns // lanes
    half_blocks = blocks // 2
    coarse_rows = -(-max(half_blocks, 1) // sublanes) * sublanes
    middle_count = lanes // sublanes
    center = (blocks - 1) * (lanes // 2)
    here = tile_of(place)
    vertex = vertex_ref[:, tile_of(first)]
    cosine, sine = cos_sin(vertex * (row_ids(sublanes) + center))
    cas_fine, cam_fine = cosine + sine, cosine - sine
    cos_middle, sin_middle = cos_sin(vertex * (row_ids(middle_count) * sublanes))
    cos_coarse, sin_coarse = cos_sin(
        vertex * ((blocks - 1 - 2 * row_ids(coarse_rows)) * (lanes // 2))
    )
    for pair in range(middle_count // 2):
        cas, cam = [], []
        for middle in (2 * pair, 2 * pair + 1):
            c, s = cos_middle[middle : middle + 1], sin_middle[middle : middle + 1]
            cas.append(c * cas_fine + s * cam_fine)
            cam.append(c * cam_fine - s * cas_fine)
        cas, cam = jnp.concatenate(cas, axis=0), jnp.concatenate(cam, axis=0)
        start = pair * 2 * sublanes
        for low in range(half_blocks):
            high = blocks - 1 - low
            even = cos_coarse[low : low + 1] * cas
            odd = sin_coarse[low : low + 1] * cam
            for block, value in ((low, even - odd), (high, even + odd)):
                row = block * lanes + start
                table_ref[row : row + 2 * sublanes, here] = value.astype(jnp.bfloat16)
        if blocks % 2:
            row = half_blocks * lanes + start
            table_ref[row : row + 2 * sublanes, here] = cas.astype(jnp.bfloat16)


def encode(rows):
    half = rows.shape[1] // 2
    peak = jnp.maximum(jnp.max(jnp.abs(rows), axis=1, keepdims=True), smallest_peak)
    exponent = jnp.ceil(jnp.log2(peak * (1.0 / code_limit)) + exponent_margin)
    codes = jnp.floor(rows * (1.0 / jnp.exp2(exponent)) + 0.5).astype(jnp.int32)
    words = (codes[:, :half] << 16) | (codes[:, half:] & 0xFFFF)
    tail = jnp.broadcast_to(exponent.astype(jnp.int32), (rows.shape[0], lanes))
    return jnp.concatenate([words, tail], axis=1)


def units(coded):
    return jnp.exp2(coded[:, coded.shape[1] - lanes :].astype(jnp.float32))


def decode(coded):
    words = coded[:, : coded.shape[1] - lanes]
    codes = jnp.concatenate([words >> 16, (words << 16) >> 16], axis=1)
    return codes.astype(jnp.float32) * units(coded)[:, :1]


def transform_kernel(sizes, matrix_hbm, vertex_hbm, *rest):
    *sent_refs, matrix_ref, vertex_ref, left_ref, early_ref, middle_ref, late_ref, weight_ref, matrix_sem, vertex_sem = rest
    blk_count, walk_count, sub_count, rows_own = sizes
    walk_index = lax.axis_index("walk")
    sub_index = lax.axis_index("sub")
    rows_local, vertices_local = matrix_ref.shape
    window_rows = left_ref.shape[0]
    early = early_ref.shape[1]

    vertex_copy = pltpu.make_async_copy(vertex_hbm, vertex_ref, vertex_sem)
    vertex_copy.start()
    first = pl.multiple_of(sub_index * vertices_local, lanes)
    matrix_copy = pltpu.make_async_copy(
        matrix_hbm.at[0, :, pl.ds(first, vertices_local)], matrix_ref, matrix_sem
    )
    matrix_copy.start()

    ids, inner = split_by(row_ids(window_rows), rows_own)
    ids, blk_part = split_by(ids, blk_count)
    walk_part, sub_part = split_by(ids, sub_count)
    sub_part = toward(sub_index, sub_part, sub_count)
    walk_part = toward(walk_index, walk_part, walk_count)
    window = ((blk_part * walk_count + walk_part) * sub_count + sub_part) * rows_own + inner

    vertex_copy.wait()
    own_start = pl.multiple_of(walk_index * rows_local, lanes)
    for start in range(0, rows_local, lanes):
        own_vertex = vertex_ref[:, pl.ds(own_start + start, lanes)]
        cosine, sine = cos_sin(own_vertex * window)
        left_ref[:, start : start + lanes] = (cosine + sine).astype(jnp.bfloat16)

    @pl.loop(0, early // lanes, unroll=2)
    def _(step):
        make_table(vertex_ref, early_ref, first + step * lanes, step * lanes)

    matrix_copy.wait()
    chunk = 4 * lanes
    for start in range(0, vertices_local, chunk):
        left_product = jnp.dot(
            left_ref[...], matrix_ref[:, start : start + chunk], preferred_element_type=jnp.float32
        )
        high = left_product.astype(jnp.bfloat16)
        weight_ref[:window_rows, start : start + chunk] = high
        weight_ref[window_rows:, start : start + chunk] = (
            left_product - high.astype(jnp.float32)
        ).astype(jnp.bfloat16)
    green, start = 0.0, 0
    for table_ref in (early_ref, middle_ref, late_ref):
        size = table_ref.shape[1]
        if table_ref is not early_ref:
            for tile in range(0, size, lanes):
                make_table(vertex_ref, table_ref, first + start + tile, tile)
        green += lax.dot_general(
            table_ref[...],
            weight_ref[:, start : start + size],
            (((1,), (1,)), ((), ())),
            preferred_element_type=jnp.float32,
        )
        start += size
    green = green.T
    green = green[:window_rows] + green[window_rows:]
    rows_each = blk_count * rows_own
    for place, sent_ref in enumerate(sent_refs):
        rows = green[place * rows_each : (place + 1) * rows_each]
        sent_ref[...] = rows if place == 0 else encode(rows)


def combine_kernel(sizes, *refs):
    blk_count, walk_count, sub_count, rows_own = sizes
    blk_index = lax.axis_index("blk")
    parts = walk_count * sub_count
    part_refs, whole_refs, row_ref = refs[:parts], refs[parts:-1], refs[-1]
    total = part_refs[0][...] + sum(decode(part_ref[...]) for part_ref in part_refs[1:])
    coded = encode(total)
    if len(whole_refs) == 1:
        whole_refs[0][...] = coded
        return
    for row in range(blk_count * rows_own):
        row_ref[row] = coded[row : row + 1]
    for place, whole_ref in enumerate(whole_refs):
        for step in range(RSTEPS):
            blk_part = toward(blk_index, place, blk_count) + RSTEPS * blk_count - step
            _, blk_part = split_by(blk_part, blk_count)
            for inner in range(rows_own):
                row = step * rows_own + inner
                whole_ref[row : row + 1] = row_ref[blk_part * rows_own + inner]


def accumulate_kernel(sizes, distances, last, weights_ref, transfer_ref, old_ref, *rest):
    if last:
        *arrived_refs, out_ref, source_ref, left_ref, unit_ref, new_ref, out_sems = rest
    else:
        *arrived_refs, new_ref, source_ref, left_ref, unit_ref = rest
    blk_count, _, _, rows_own = sizes
    blk_index = lax.axis_index("blk")
    transfers, columns = transfer_ref.shape
    half = columns // 2
    groups = transfers // sublanes
    tiles = columns // lanes
    weights = weights_ref[...] * (1.0 / blk_count)
    walker_ids = lax.broadcasted_iota(jnp.int32, weights.shape, 1)

    ids = lax.broadcasted_iota(jnp.int32, (transfers, 1), 0)
    step, _ = split_by(ids, TQ)
    if arrived_refs[0].shape[0] == blk_count * rows_own:
        _, step = split_by(blk_index + RSTEPS * blk_count - step, blk_count)

    def out_copy(own, part):
        here = slice(part * half, (part + 1) * half)
        return pltpu.make_async_copy(
            new_ref.at[own, :, here], out_ref.at[own, :, here], out_sems.at[own, part]
        )

    def spread(rows, own):
        wide = (transfers, rows.shape[1])
        picked = jnp.broadcast_to(rows[own : own + 1], wide)
        for place in range(1, rows.shape[0] // rows_own):
            row = place * rows_own + own
            picked = jnp.where(step == place, jnp.broadcast_to(rows[row : row + 1], wide), picked)
        return picked

    for own in range(rows_own):
        for place, distance in enumerate(distances):
            coded = arrived_refs[place][...]
            walker = back(blk_index, distance, blk_count)
            weight = jnp.sum(jnp.where(walker_ids == walker, weights, 0.0), axis=1, keepdims=True)
            left = coded[own : own + 1]
            for blk_part in range(1, coded.shape[0] // rows_own):
                row = blk_part * rows_own + own
                left = jnp.where(step[:1] == blk_part, coded[row : row + 1], left)
            left_ref[place] = decode(left) * weight
            unit_ref[place] = spread(units(coded), own)
            source_ref[place] = spread(coded[:, :half], own)

        together = len(distances) if len(distances) <= 4 else math.gcd(len(distances), 4)

        for tile in range(tiles):
            here = slice(tile * lanes, (tile + 1) * lanes)
            for group in range(groups):
                rows = slice(group * sublanes, (group + 1) * sublanes)
                index = transfer_ref[rows, here]
                index_lane = index & (lanes - 1)
                in_first = index < half
                index_tile = jnp.where(in_first, index, index - half) >> lane_bits

                def add_walkers(first, total):
                    picked = [jnp.zeros((sublanes, lanes), jnp.int32)] * together
                    for source in range(half // lanes):
                        match = index_tile == source
                        for k in range(together):
                            words = source_ref[
                                first + k, rows, source * lanes : (source + 1) * lanes
                            ]
                            words = jnp.take_along_axis(
                                words, index_lane, axis=1, mode="promise_in_bounds"
                            )
                            picked[k] = jnp.where(match, words, picked[k])
                    for k in range(together):
                        code = jnp.where(in_first, picked[k], picked[k] << 16) >> 16
                        total = total + left_ref[first + k, :, here] * (
                            unit_ref[first + k, rows] * code.astype(jnp.float32)
                        )
                    return total

                total = old_ref[own, rows, here]
                if len(distances) == together:
                    total = add_walkers(0, total)
                else:
                    total = lax.fori_loop(
                        0, len(distances) // together, lambda i, t: add_walkers(i * together, t), total
                    )
                new_ref[own, rows, here] = total

            if last and (tile + 1) % (tiles // 2) == 0:
                out_copy(own, (tile + 1) // (tiles // 2) - 1).start()
    if last:
        for own in range(rows_own):
            for part in range(2):
                out_copy(own, part).wait()


def exchange(pieces, axes, counts):
    positions = list(itertools.product(*map(range, counts)))
    place = {position: i for i, position in enumerate(positions)}
    arrived = [pieces[0]] * len(positions)
    for i in range(1, len(positions)):
        route = [
            (place[position], place[tuple(map(toward, position, positions[i], counts))])
            for position in positions
        ]
        arrived[i] = lax.ppermute(pieces[i], axes, route)
    return arrived


def local(walker_mats, vertex, weights, transfer_table, g4_old):
    blk_count = lax.axis_size("blk")
    walk_count = lax.axis_size("walk")
    sub_count = lax.axis_size("sub")
    rows_local, vertices = walker_mats.shape[1:]
    rows_own, transfers, columns = g4_old.shape
    devices = blk_count * walk_count * sub_count
    sizes = (blk_count, walk_count, sub_count, rows_own)
    vmem = pl.BlockSpec(memory_space=pltpu.VMEM)
    vertices_local = vertices // sub_count
    early = vertices_local // (4 * lanes) * 2 * lanes
    middle = early // 2
    coded = columns // 2 + lanes
    sent = pl.pallas_call(
        functools.partial(transform_kernel, sizes),
        out_shape=[
            jax.ShapeDtypeStruct((blk_count * rows_own, coded if place else columns), jnp.int32 if place else jnp.float32)
            for place in range(walk_count * sub_count)
        ],
        in_specs=[pl.BlockSpec(memory_space=pl.ANY)] * 2,
        out_specs=[vmem] * (walk_count * sub_count),
        scratch_shapes=[
            pltpu.VMEM((rows_local, vertices_local), jnp.bfloat16),
            pltpu.VMEM((1, vertices), jnp.int32),
            pltpu.VMEM((devices * rows_own, rows_local), jnp.bfloat16),
            pltpu.VMEM((columns, early), jnp.bfloat16),
            pltpu.VMEM((columns, middle), jnp.bfloat16),
            pltpu.VMEM((columns, vertices_local - early - middle), jnp.bfloat16),
            pltpu.VMEM((2 * devices * rows_own, vertices_local), jnp.bfloat16),
            pltpu.SemaphoreType.DMA,
            pltpu.SemaphoreType.DMA,
        ],
        compiler_params=pltpu.CompilerParams(vmem_limit_bytes=24 * 2**20),
        name="transform",
    )(*[pltpu.with_memory_space_constraint(x, pltpu.HBM) for x in (walker_mats, vertex)])
    sent, weights, transfer_table, g4_old = lax.optimization_barrier(
        (sent, weights, transfer_table, g4_old)
    )
    parts = exchange(sent, ("walk", "sub"), (walk_count, sub_count))
    shared = blk_count <= RSTEPS
    rows_each = (blk_count if shared else RSTEPS) * rows_own
    whole_count = 1 if shared else blk_count
    whole = pl.pallas_call(
        functools.partial(combine_kernel, sizes),
        out_shape=[jax.ShapeDtypeStruct((rows_each, coded), jnp.int32)] * whole_count,
        in_specs=[vmem] * len(parts),
        out_specs=[vmem] * whole_count,
        scratch_shapes=[pltpu.VMEM((blk_count * rows_own, 1, coded), jnp.int32)],
        compiler_params=pltpu.CompilerParams(vmem_limit_bytes=24 * 2**20),
        name="combine",
    )(*parts)
    arrived = exchange(whole * blk_count if shared else whole, ("blk",), (blk_count,))
    far = blk_count // 2
    totals = g4_old
    groups = [0, *range(far + 1, blk_count)], [*range(1, far)], [far]
    for places in groups:
        last = places is groups[-1]
        scratch_shapes = [
            pltpu.VMEM((len(places), transfers, columns // 2), jnp.int32),
            pltpu.VMEM((len(places), 1, columns), jnp.float32),
            pltpu.VMEM((len(places), transfers, lanes), jnp.float32),
        ]
        if last:
            scratch_shapes.append(pltpu.VMEM(g4_old.shape, jnp.float32))
            scratch_shapes.append(pltpu.SemaphoreType.DMA((rows_own, 2)))
        totals = pl.pallas_call(
            functools.partial(accumulate_kernel, sizes, places, last),
            out_shape=jax.ShapeDtypeStruct(g4_old.shape, jnp.float32),
            in_specs=[vmem] * (3 + len(places)),
            out_specs=pl.BlockSpec(memory_space=pl.ANY) if last else vmem,
            scratch_shapes=scratch_shapes,
            compiler_params=pltpu.CompilerParams(vmem_limit_bytes=24 * 2**20),
            cost_estimate=pl.CostEstimate(
                flops=1000 * len(places) * transfers * columns,
                bytes_accessed=12 * transfers * columns,
                transcendentals=0,
            ),
            name="accumulate",
        )(weights[None], transfer_table, totals, *[arrived[place] for place in places])
    return totals


def solution(mesh):
    in_specs = (
        P(("grp", "blk"), "walk", None),
        P(("grp", "blk"), None),
        P("grp"),
        P(),
        P(("grp", "blk", "walk", "sub"), None, None),
    )
    out_specs = P(("grp", "blk", "walk", "sub"), None, None)
    return jax.shard_map(local, mesh=mesh, in_specs=in_specs, out_specs=out_specs, check_vma=False)
```

```python
import functools
import itertools
import math

import jax
import jax.numpy as jnp
from jax import lax
from jax.experimental import pallas as pl
from jax.experimental.pallas import tpu as pltpu
from jax.sharding import PartitionSpec as P

TQ = 4
RSTEPS = 4


phase_period = 8192
quarter_bits = 11
lanes = 128
lane_bits = 7
sublanes = 8
code_limit = 32767.0
smallest_peak = 1e-30
exponent_margin = 1e-3


def toward(index, distance, count):
    if count & (count - 1) == 0:
        return index ^ distance
    return (index + distance) % count


def back(index, distance, count):
    if count & (count - 1) == 0:
        return index ^ distance
    return (index + count - distance) % count


def cos_sin(product):
    residue = product & (phase_period - 1)
    quarter = (residue + phase_period // 8) >> quarter_bits
    angle = (residue - (quarter << quarter_bits)).astype(jnp.float32) * (2.0 * math.pi / phase_period)
    square = angle * angle
    sine = angle + angle * square * (
        -1.0 / 6.0 + square * (1.0 / 120.0 + square * (-1.0 / 5040.0 + square * (1.0 / 362880.0)))
    )
    cosine = 1.0 + square * (
        -0.5 + square * (1.0 / 24.0 + square * (-1.0 / 720.0 + square * (1.0 / 40320.0)))
    )
    odd = (quarter & 1) == 1
    cosine_out = jnp.where(odd, sine, cosine)
    sine_out = jnp.where(odd, cosine, sine)
    cosine_out = jnp.where(((quarter + 1) & 2) == 2, -cosine_out, cosine_out)
    sine_out = jnp.where((quarter & 2) == 2, -sine_out, sine_out)
    return cosine_out, sine_out


def row_ids(count):
    return lax.broadcasted_iota(jnp.int32, (count, lanes), 0)


def split_by(ids, size):
    if size & (size - 1) == 0:
        return ids >> (size.bit_length() - 1), ids & (size - 1)
    return ids // size, ids % size


def tile_of(start):
    return pl.ds(start if isinstance(start, int) else pl.multiple_of(start, lanes), lanes)


def make_table(vertex_ref, table_ref, first, place):
    columns = table_ref.shape[0]
    blocks = columns // lanes
    half_blocks = blocks // 2
    coarse_rows = -(-max(half_blocks, 1) // sublanes) * sublanes
    middle_count = lanes // sublanes
    center = (blocks - 1) * (lanes // 2)
    here = tile_of(place)
    vertex = vertex_ref[:, tile_of(first)]
    cosine, sine = cos_sin(vertex * (row_ids(sublanes) + center))
    cas_fine, cam_fine = cosine + sine, cosine - sine
    cos_middle, sin_middle = cos_sin(vertex * (row_ids(middle_count) * sublanes))
    cos_coarse, sin_coarse = cos_sin(
        vertex * ((blocks - 1 - 2 * row_ids(coarse_rows)) * (lanes // 2))
    )
    for pair in range(middle_count // 2):
        cas, cam = [], []
        for middle in (2 * pair, 2 * pair + 1):
            c, s = cos_middle[middle : middle + 1], sin_middle[middle : middle + 1]
            cas.append(c * cas_fine + s * cam_fine)
            cam.append(c * cam_fine - s * cas_fine)
        cas, cam = jnp.concatenate(cas, axis=0), jnp.concatenate(cam, axis=0)
        start = pair * 2 * sublanes
        for low in range(half_blocks):
            high = blocks - 1 - low
            even = cos_coarse[low : low + 1] * cas
            odd = sin_coarse[low : low + 1] * cam
            for block, value in ((low, even - odd), (high, even + odd)):
                row = block * lanes + start
                table_ref[row : row + 2 * sublanes, here] = value.astype(jnp.bfloat16)
        if blocks % 2:
            row = half_blocks * lanes + start
            table_ref[row : row + 2 * sublanes, here] = cas.astype(jnp.bfloat16)


def encode(rows):
    half = rows.shape[1] // 2
    peak = jnp.maximum(jnp.max(jnp.abs(rows), axis=1, keepdims=True), smallest_peak)
    exponent = jnp.ceil(jnp.log2(peak * (1.0 / code_limit)) + exponent_margin)
    codes = jnp.floor(rows * (1.0 / jnp.exp2(exponent)) + 0.5).astype(jnp.int32)
    words = (codes[:, :half] << 16) | (codes[:, half:] & 0xFFFF)
    tail = jnp.broadcast_to(exponent.astype(jnp.int32), (rows.shape[0], lanes))
    return jnp.concatenate([words, tail], axis=1)


def units(coded):
    return jnp.exp2(coded[:, coded.shape[1] - lanes :].astype(jnp.float32))


def decode(coded):
    words = coded[:, : coded.shape[1] - lanes]
    codes = jnp.concatenate([words >> 16, (words << 16) >> 16], axis=1)
    return codes.astype(jnp.float32) * units(coded)[:, :1]


def transform_kernel(sizes, matrix_hbm, vertex_hbm, *rest):
    *sent_refs, matrix_ref, vertex_ref, left_ref, early_ref, middle_ref, late_ref, weight_ref, matrix_sem, vertex_sem = rest
    blk_count, walk_count, sub_count, rows_own = sizes
    walk_index = lax.axis_index("walk")
    sub_index = lax.axis_index("sub")
    rows_local, vertices_local = matrix_ref.shape
    window_rows = left_ref.shape[0]
    early = early_ref.shape[1]

    vertex_copy = pltpu.make_async_copy(vertex_hbm, vertex_ref, vertex_sem)
    vertex_copy.start()
    first = pl.multiple_of(sub_index * vertices_local, lanes)
    matrix_copy = pltpu.make_async_copy(
        matrix_hbm.at[0, :, pl.ds(first, vertices_local)], matrix_ref, matrix_sem
    )
    matrix_copy.start()

    ids, inner = split_by(row_ids(window_rows), rows_own)
    ids, blk_part = split_by(ids, blk_count)
    walk_part, sub_part = split_by(ids, sub_count)
    sub_part = toward(sub_index, sub_part, sub_count)
    walk_part = toward(walk_index, walk_part, walk_count)
    window = ((blk_part * walk_count + walk_part) * sub_count + sub_part) * rows_own + inner

    vertex_copy.wait()
    own_start = pl.multiple_of(walk_index * rows_local, lanes)
    for start in range(0, rows_local, lanes):
        own_vertex = vertex_ref[:, pl.ds(own_start + start, lanes)]
        cosine, sine = cos_sin(own_vertex * window)
        left_ref[:, start : start + lanes] = (cosine + sine).astype(jnp.bfloat16)

    @pl.loop(0, early // lanes)
    def _(step):
        make_table(vertex_ref, early_ref, first + step * lanes, step * lanes)

    matrix_copy.wait()
    chunk = 4 * lanes
    for start in range(0, vertices_local, chunk):
        left_product = jnp.dot(
            left_ref[...], matrix_ref[:, start : start + chunk], preferred_element_type=jnp.float32
        )
        high = left_product.astype(jnp.bfloat16)
        weight_ref[:window_rows, start : start + chunk] = high
        weight_ref[window_rows:, start : start + chunk] = (
            left_product - high.astype(jnp.float32)
        ).astype(jnp.bfloat16)
    green, start = 0.0, 0
    for table_ref in (early_ref, middle_ref, late_ref):
        size = table_ref.shape[1]
        if table_ref is not early_ref:
            for tile in range(0, size, lanes):
                make_table(vertex_ref, table_ref, first + start + tile, tile)
        green += lax.dot_general(
            table_ref[...],
            weight_ref[:, start : start + size],
            (((1,), (1,)), ((), ())),
            preferred_element_type=jnp.float32,
        )
        start += size
    green = green.T
    green = green[:window_rows] + green[window_rows:]
    rows_each = blk_count * rows_own
    coded = encode(green)
    for place, sent_ref in enumerate(sent_refs):
        rows = coded if place else green
        sent_ref[...] = rows[place * rows_each : (place + 1) * rows_each]


def combine_kernel(sizes, *refs):
    blk_count, walk_count, sub_count, rows_own = sizes
    blk_index = lax.axis_index("blk")
    parts = walk_count * sub_count
    part_refs, whole_refs, row_ref = refs[:parts], refs[parts:-1], refs[-1]
    total = part_refs[0][...] + sum(decode(part_ref[...]) for part_ref in part_refs[1:])
    coded = encode(total)
    if len(whole_refs) == 1:
        whole_refs[0][...] = coded
        return
    for row in range(blk_count * rows_own):
        row_ref[row] = coded[row : row + 1]
    for place, whole_ref in enumerate(whole_refs):
        for step in range(RSTEPS):
            blk_part = toward(blk_index, place, blk_count) + RSTEPS * blk_count - step
            _, blk_part = split_by(blk_part, blk_count)
            for inner in range(rows_own):
                row = step * rows_own + inner
                whole_ref[row : row + 1] = row_ref[blk_part * rows_own + inner]


def accumulate_kernel(sizes, distances, last, weights_ref, transfer_ref, old_ref, *rest):
    if last:
        *arrived_refs, out_ref, source_ref, left_ref, unit_ref, new_ref, out_sems = rest
    else:
        *arrived_refs, new_ref, source_ref, left_ref, unit_ref = rest
    blk_count, _, _, rows_own = sizes
    blk_index = lax.axis_index("blk")
    transfers, columns = transfer_ref.shape
    half = columns // 2
    groups = transfers // sublanes
    tiles = columns // lanes
    weights = weights_ref[...] * (1.0 / blk_count)
    walker_ids = lax.broadcasted_iota(jnp.int32, weights.shape, 1)

    ids = lax.broadcasted_iota(jnp.int32, (transfers, 1), 0)
    step, _ = split_by(ids, TQ)
    if arrived_refs[0].shape[0] == blk_count * rows_own:
        _, step = split_by(blk_index + RSTEPS * blk_count - step, blk_count)

    def out_copy(own, part):
        here = slice(part * half, (part + 1) * half)
        return pltpu.make_async_copy(
            new_ref.at[own, :, here], out_ref.at[own, :, here], out_sems.at[own, part]
        )

    def spread(rows, own):
        wide = (transfers, rows.shape[1])
        picked = jnp.broadcast_to(rows[own : own + 1], wide)
        for place in range(1, rows.shape[0] // rows_own):
            row = place * rows_own + own
            picked = jnp.where(step == place, jnp.broadcast_to(rows[row : row + 1], wide), picked)
        return picked

    for own in range(rows_own):
        for place, distance in enumerate(distances):
            coded = arrived_refs[place][...]
            walker = back(blk_index, distance, blk_count)
            weight = jnp.sum(jnp.where(walker_ids == walker, weights, 0.0), axis=1, keepdims=True)
            left = coded[own : own + 1]
            for blk_part in range(1, coded.shape[0] // rows_own):
                row = blk_part * rows_own + own
                left = jnp.where(step[:1] == blk_part, coded[row : row + 1], left)
            left_ref[place] = decode(left) * weight
            unit_ref[place] = spread(units(coded), own)
            source_ref[place] = spread(coded[:, :half], own)

        together = len(distances) if len(distances) <= 4 else math.gcd(len(distances), 4)

        for tile in range(tiles):
            here = slice(tile * lanes, (tile + 1) * lanes)
            for group in range(groups):
                rows = slice(group * sublanes, (group + 1) * sublanes)
                index = transfer_ref[rows, here]
                index_lane = index & (lanes - 1)
                in_first = index < half
                index_tile = jnp.where(in_first, index, index - half) >> lane_bits

                def add_walkers(first, total):
                    picked = [jnp.zeros((sublanes, lanes), jnp.int32)] * together
                    for source in range(half // lanes):
                        match = index_tile == source
                        for k in range(together):
                            words = source_ref[
                                first + k, rows, source * lanes : (source + 1) * lanes
                            ]
                            words = jnp.take_along_axis(
                                words, index_lane, axis=1, mode="promise_in_bounds"
                            )
                            picked[k] = jnp.where(match, words, picked[k])
                    for k in range(together):
                        code = jnp.where(in_first, picked[k], picked[k] << 16) >> 16
                        total = total + left_ref[first + k, :, here] * (
                            unit_ref[first + k, rows] * code.astype(jnp.float32)
                        )
                    return total

                total = old_ref[own, rows, here]
                if len(distances) == together:
                    total = add_walkers(0, total)
                else:
                    total = lax.fori_loop(
                        0, len(distances) // together, lambda i, t: add_walkers(i * together, t), total
                    )
                new_ref[own, rows, here] = total

            if last and (tile + 1) % (tiles // 2) == 0:
                out_copy(own, (tile + 1) // (tiles // 2) - 1).start()
    if last:
        for own in range(rows_own):
            for part in range(2):
                out_copy(own, part).wait()


def exchange(pieces, axes, counts):
    positions = list(itertools.product(*map(range, counts)))
    place = {position: i for i, position in enumerate(positions)}
    arrived = [pieces[0]] * len(positions)
    for i in range(1, len(positions)):
        route = [
            (place[position], place[tuple(map(toward, position, positions[i], counts))])
            for position in positions
        ]
        arrived[i] = lax.ppermute(pieces[i], axes, route)
    return arrived


def local(walker_mats, vertex, weights, transfer_table, g4_old):
    blk_count = lax.axis_size("blk")
    walk_count = lax.axis_size("walk")
    sub_count = lax.axis_size("sub")
    rows_local, vertices = walker_mats.shape[1:]
    rows_own, transfers, columns = g4_old.shape
    devices = blk_count * walk_count * sub_count
    sizes = (blk_count, walk_count, sub_count, rows_own)
    vmem = pl.BlockSpec(memory_space=pltpu.VMEM)
    vertices_local = vertices // sub_count
    early = vertices_local // (4 * lanes) * 2 * lanes
    middle = early // 2
    coded = columns // 2 + lanes
    sent = pl.pallas_call(
        functools.partial(transform_kernel, sizes),
        out_shape=[
            jax.ShapeDtypeStruct((blk_count * rows_own, coded if place else columns), jnp.int32 if place else jnp.float32)
            for place in range(walk_count * sub_count)
        ],
        in_specs=[pl.BlockSpec(memory_space=pl.ANY)] * 2,
        out_specs=[vmem] * (walk_count * sub_count),
        scratch_shapes=[
            pltpu.VMEM((rows_local, vertices_local), jnp.bfloat16),
            pltpu.VMEM((1, vertices), jnp.int32),
            pltpu.VMEM((devices * rows_own, rows_local), jnp.bfloat16),
            pltpu.VMEM((columns, early), jnp.bfloat16),
            pltpu.VMEM((columns, middle), jnp.bfloat16),
            pltpu.VMEM((columns, vertices_local - early - middle), jnp.bfloat16),
            pltpu.VMEM((2 * devices * rows_own, vertices_local), jnp.bfloat16),
            pltpu.SemaphoreType.DMA,
            pltpu.SemaphoreType.DMA,
        ],
        compiler_params=pltpu.CompilerParams(vmem_limit_bytes=24 * 2**20),
        name="transform",
    )(*[pltpu.with_memory_space_constraint(x, pltpu.HBM) for x in (walker_mats, vertex)])
    parts = exchange(sent, ("walk", "sub"), (walk_count, sub_count))
    shared = blk_count <= RSTEPS
    rows_each = (blk_count if shared else RSTEPS) * rows_own
    whole_count = 1 if shared else blk_count
    whole = pl.pallas_call(
        functools.partial(combine_kernel, sizes),
        out_shape=[jax.ShapeDtypeStruct((rows_each, coded), jnp.int32)] * whole_count,
        in_specs=[vmem] * len(parts),
        out_specs=[vmem] * whole_count,
        scratch_shapes=[pltpu.VMEM((blk_count * rows_own, 1, coded), jnp.int32)],
        compiler_params=pltpu.CompilerParams(vmem_limit_bytes=24 * 2**20),
        name="combine",
    )(*parts)
    arrived = exchange(whole * blk_count if shared else whole, ("blk",), (blk_count,))
    far = blk_count // 2
    totals = g4_old
    groups = [0, *range(far + 1, blk_count)], [*range(1, far)], [far]
    for places in groups:
        last = places is groups[-1]
        scratch_shapes = [
            pltpu.VMEM((len(places), transfers, columns // 2), jnp.int32),
            pltpu.VMEM((len(places), 1, columns), jnp.float32),
            pltpu.VMEM((len(places), transfers, lanes), jnp.float32),
        ]
        if last:
            scratch_shapes.append(pltpu.VMEM(g4_old.shape, jnp.float32))
            scratch_shapes.append(pltpu.SemaphoreType.DMA((rows_own, 2)))
        totals = pl.pallas_call(
            functools.partial(accumulate_kernel, sizes, places, last),
            out_shape=jax.ShapeDtypeStruct(g4_old.shape, jnp.float32),
            in_specs=[vmem] * (3 + len(places)),
            out_specs=pl.BlockSpec(memory_space=pl.ANY) if last else vmem,
            scratch_shapes=scratch_shapes,
            compiler_params=pltpu.CompilerParams(vmem_limit_bytes=24 * 2**20),
            cost_estimate=pl.CostEstimate(
                flops=1000 * len(places) * transfers * columns,
                bytes_accessed=12 * transfers * columns,
                transcendentals=0,
            ),
            name="accumulate",
        )(weights[None], transfer_table, totals, *[arrived[place] for place in places])
    return totals


def solution(mesh):
    in_specs = (
        P(("grp", "blk"), "walk", None),
        P(("grp", "blk"), None),
        P("grp"),
        P(),
        P(("grp", "blk", "walk", "sub"), None, None),
    )
    out_specs = P(("grp", "blk", "walk", "sub"), None, None)
    return jax.shard_map(local, mesh=mesh, in_specs=in_specs, out_specs=out_specs, check_vma=False)
```

```python
import functools
import itertools
import math

import jax
import jax.numpy as jnp
from jax import lax
from jax.experimental import pallas as pl
from jax.experimental.pallas import tpu as pltpu
from jax.sharding import PartitionSpec as P

TQ = 4
RSTEPS = 4


phase_period = 8192
quarter_bits = 11
lanes = 128
lane_bits = 7
sublanes = 8
code_limit = 32767.0
smallest_peak = 1e-30
exponent_margin = 1e-3


def toward(index, distance, count):
    if count & (count - 1) == 0:
        return index ^ distance
    return (index + distance) % count


def back(index, distance, count):
    if count & (count - 1) == 0:
        return index ^ distance
    return (index + count - distance) % count


def cos_sin(product):
    residue = product & (phase_period - 1)
    quarter = (residue + phase_period // 8) >> quarter_bits
    angle = (residue - (quarter << quarter_bits)).astype(jnp.float32) * (2.0 * math.pi / phase_period)
    square = angle * angle
    sine = angle + angle * square * (
        -1.0 / 6.0 + square * (1.0 / 120.0 + square * (-1.0 / 5040.0 + square * (1.0 / 362880.0)))
    )
    cosine = 1.0 + square * (
        -0.5 + square * (1.0 / 24.0 + square * (-1.0 / 720.0 + square * (1.0 / 40320.0)))
    )
    odd = (quarter & 1) == 1
    cosine_out = jnp.where(odd, sine, cosine)
    sine_out = jnp.where(odd, cosine, sine)
    cosine_out = jnp.where(((quarter + 1) & 2) == 2, -cosine_out, cosine_out)
    sine_out = jnp.where((quarter & 2) == 2, -sine_out, sine_out)
    return cosine_out, sine_out


def row_ids(count):
    return lax.broadcasted_iota(jnp.int32, (count, lanes), 0)


def split_by(ids, size):
    if size & (size - 1) == 0:
        return ids >> (size.bit_length() - 1), ids & (size - 1)
    return ids // size, ids % size


def tile_of(start):
    return pl.ds(start if isinstance(start, int) else pl.multiple_of(start, lanes), lanes)


def make_table(vertex_ref, table_ref, first, place):
    columns = table_ref.shape[0]
    blocks = columns // lanes
    half_blocks = blocks // 2
    coarse_rows = -(-max(half_blocks, 1) // sublanes) * sublanes
    middle_count = lanes // sublanes
    center = (blocks - 1) * (lanes // 2)
    here = tile_of(place)
    vertex = vertex_ref[:, tile_of(first)]
    cosine, sine = cos_sin(vertex * (row_ids(sublanes) + center))
    cas_fine, cam_fine = cosine + sine, cosine - sine
    cos_middle, sin_middle = cos_sin(vertex * (row_ids(middle_count) * sublanes))
    cos_coarse, sin_coarse = cos_sin(
        vertex * ((blocks - 1 - 2 * row_ids(coarse_rows)) * (lanes // 2))
    )
    for pair in range(middle_count // 2):
        cas, cam = [], []
        for middle in (2 * pair, 2 * pair + 1):
            c, s = cos_middle[middle : middle + 1], sin_middle[middle : middle + 1]
            cas.append(c * cas_fine + s * cam_fine)
            cam.append(c * cam_fine - s * cas_fine)
        cas, cam = jnp.concatenate(cas, axis=0), jnp.concatenate(cam, axis=0)
        start = pair * 2 * sublanes
        for low in range(half_blocks):
            high = blocks - 1 - low
            even = cos_coarse[low : low + 1] * cas
            odd = sin_coarse[low : low + 1] * cam
            for block, value in ((low, even - odd), (high, even + odd)):
                row = block * lanes + start
                table_ref[row : row + 2 * sublanes, here] = value.astype(jnp.bfloat16)
        if blocks % 2:
            row = half_blocks * lanes + start
            table_ref[row : row + 2 * sublanes, here] = cas.astype(jnp.bfloat16)


def encode(rows):
    half = rows.shape[1] // 2
    peak = jnp.maximum(jnp.max(jnp.abs(rows), axis=1, keepdims=True), smallest_peak)
    exponent = jnp.ceil(jnp.log2(peak * (1.0 / code_limit)) + exponent_margin)
    codes = jnp.floor(rows * (1.0 / jnp.exp2(exponent)) + 0.5).astype(jnp.int32)
    words = (codes[:, :half] << 16) | (codes[:, half:] & 0xFFFF)
    tail = jnp.broadcast_to(exponent.astype(jnp.int32), (rows.shape[0], lanes))
    return jnp.concatenate([words, tail], axis=1)


def units(coded):
    return jnp.exp2(coded[:, coded.shape[1] - lanes :].astype(jnp.float32))


def decode(coded):
    words = coded[:, : coded.shape[1] - lanes]
    codes = jnp.concatenate([words >> 16, (words << 16) >> 16], axis=1)
    return codes.astype(jnp.float32) * units(coded)[:, :1]


def transform_kernel(sizes, matrix_hbm, vertex_hbm, *rest):
    *sent_refs, matrix_ref, vertex_ref, left_ref, early_ref, middle_ref, late_ref, weight_ref, matrix_sem, vertex_sem = rest
    blk_count, walk_count, sub_count, rows_own = sizes
    walk_index = lax.axis_index("walk")
    sub_index = lax.axis_index("sub")
    rows_local, vertices_local = matrix_ref.shape
    window_rows = left_ref.shape[0]
    early = early_ref.shape[1]

    vertex_copy = pltpu.make_async_copy(vertex_hbm, vertex_ref, vertex_sem)
    vertex_copy.start()
    first = pl.multiple_of(sub_index * vertices_local, lanes)
    matrix_copy = pltpu.make_async_copy(
        matrix_hbm.at[0, :, pl.ds(first, vertices_local)], matrix_ref, matrix_sem
    )
    matrix_copy.start()

    ids, inner = split_by(row_ids(window_rows), rows_own)
    ids, blk_part = split_by(ids, blk_count)
    walk_part, sub_part = split_by(ids, sub_count)
    sub_part = toward(sub_index, sub_part, sub_count)
    walk_part = toward(walk_index, walk_part, walk_count)
    window = ((blk_part * walk_count + walk_part) * sub_count + sub_part) * rows_own + inner

    vertex_copy.wait()
    own_start = pl.multiple_of(walk_index * rows_local, lanes)
    for start in range(0, rows_local, lanes):
        own_vertex = vertex_ref[:, pl.ds(own_start + start, lanes)]
        cosine, sine = cos_sin(own_vertex * window)
        left_ref[:, start : start + lanes] = (cosine + sine).astype(jnp.bfloat16)

    @pl.loop(0, early // lanes)
    def _(step):
        make_table(vertex_ref, early_ref, first + step * lanes, step * lanes)

    matrix_copy.wait()
    chunk = 4 * lanes
    for start in range(0, vertices_local, chunk):
        left_product = jnp.dot(
            left_ref[...], matrix_ref[:, start : start + chunk], preferred_element_type=jnp.float32
        )
        high = left_product.astype(jnp.bfloat16)
        weight_ref[:window_rows, start : start + chunk] = high
        weight_ref[window_rows:, start : start + chunk] = (
            left_product - high.astype(jnp.float32)
        ).astype(jnp.bfloat16)
    green, start = 0.0, 0
    for table_ref in (early_ref, middle_ref, late_ref):
        size = table_ref.shape[1]
        if table_ref is not early_ref:
            for tile in range(0, size, lanes):
                make_table(vertex_ref, table_ref, first + start + tile, tile)
        green += lax.dot_general(
            weight_ref[:, start : start + size],
            table_ref[...],
            (((1,), (1,)), ((), ())),
            preferred_element_type=jnp.float32,
        )
        start += size
    green = green[:window_rows] + green[window_rows:]
    rows_each = blk_count * rows_own
    coded = encode(green)
    for place, sent_ref in enumerate(sent_refs):
        rows = coded if place else green
        sent_ref[...] = rows[place * rows_each : (place + 1) * rows_each]


def combine_kernel(sizes, *refs):
    blk_count, walk_count, sub_count, rows_own = sizes
    blk_index = lax.axis_index("blk")
    parts = walk_count * sub_count
    part_refs, whole_refs, row_ref = refs[:parts], refs[parts:-1], refs[-1]
    total = part_refs[0][...] + sum(decode(part_ref[...]) for part_ref in part_refs[1:])
    coded = encode(total)
    if len(whole_refs) == 1:
        whole_refs[0][...] = coded
        return
    for row in range(blk_count * rows_own):
        row_ref[row] = coded[row : row + 1]
    for place, whole_ref in enumerate(whole_refs):
        for step in range(RSTEPS):
            blk_part = toward(blk_index, place, blk_count) + RSTEPS * blk_count - step
            _, blk_part = split_by(blk_part, blk_count)
            for inner in range(rows_own):
                row = step * rows_own + inner
                whole_ref[row : row + 1] = row_ref[blk_part * rows_own + inner]


def accumulate_kernel(sizes, distances, last, weights_ref, transfer_ref, old_ref, *rest):
    if last:
        *arrived_refs, out_ref, source_ref, left_ref, unit_ref, new_ref, out_sems = rest
    else:
        *arrived_refs, new_ref, source_ref, left_ref, unit_ref = rest
    blk_count, _, _, rows_own = sizes
    blk_index = lax.axis_index("blk")
    transfers, columns = transfer_ref.shape
    half = columns // 2
    groups = transfers // sublanes
    tiles = columns // lanes
    weights = weights_ref[...] * (1.0 / blk_count)
    walker_ids = lax.broadcasted_iota(jnp.int32, weights.shape, 1)

    ids = lax.broadcasted_iota(jnp.int32, (transfers, 1), 0)
    step, _ = split_by(ids, TQ)
    if arrived_refs[0].shape[0] == blk_count * rows_own:
        _, step = split_by(blk_index + RSTEPS * blk_count - step, blk_count)

    def out_copy(own, part):
        here = slice(part * half, (part + 1) * half)
        return pltpu.make_async_copy(
            new_ref.at[own, :, here], out_ref.at[own, :, here], out_sems.at[own, part]
        )

    def spread(rows, own):
        wide = (transfers, rows.shape[1])
        picked = jnp.broadcast_to(rows[own : own + 1], wide)
        for place in range(1, rows.shape[0] // rows_own):
            row = place * rows_own + own
            picked = jnp.where(step == place, jnp.broadcast_to(rows[row : row + 1], wide), picked)
        return picked

    for own in range(rows_own):
        for place, distance in enumerate(distances):
            coded = arrived_refs[place][...]
            walker = back(blk_index, distance, blk_count)
            weight = jnp.sum(jnp.where(walker_ids == walker, weights, 0.0), axis=1, keepdims=True)
            left = coded[own : own + 1]
            for blk_part in range(1, coded.shape[0] // rows_own):
                row = blk_part * rows_own + own
                left = jnp.where(step[:1] == blk_part, coded[row : row + 1], left)
            left_ref[place] = decode(left) * weight
            unit_ref[place] = spread(units(coded), own)
            source_ref[place] = spread(coded[:, :half], own)

        together = len(distances) if len(distances) <= 4 else math.gcd(len(distances), 4)

        for tile in range(tiles):
            here = slice(tile * lanes, (tile + 1) * lanes)
            for group in range(groups):
                rows = slice(group * sublanes, (group + 1) * sublanes)
                index = transfer_ref[rows, here]
                index_lane = index & (lanes - 1)
                in_first = index < half
                index_tile = jnp.where(in_first, index, index - half) >> lane_bits

                def add_walkers(first, total):
                    picked = [jnp.zeros((sublanes, lanes), jnp.int32)] * together
                    for source in range(half // lanes):
                        match = index_tile == source
                        for k in range(together):
                            words = source_ref[
                                first + k, rows, source * lanes : (source + 1) * lanes
                            ]
                            words = jnp.take_along_axis(
                                words, index_lane, axis=1, mode="promise_in_bounds"
                            )
                            picked[k] = jnp.where(match, words, picked[k])
                    for k in range(together):
                        code = jnp.where(in_first, picked[k], picked[k] << 16) >> 16
                        total = total + left_ref[first + k, :, here] * (
                            unit_ref[first + k, rows] * code.astype(jnp.float32)
                        )
                    return total

                total = old_ref[own, rows, here]
                if len(distances) == together:
                    total = add_walkers(0, total)
                else:
                    total = lax.fori_loop(
                        0, len(distances) // together, lambda i, t: add_walkers(i * together, t), total
                    )
                new_ref[own, rows, here] = total

            if last and (tile + 1) % (tiles // 2) == 0:
                out_copy(own, (tile + 1) // (tiles // 2) - 1).start()
    if last:
        for own in range(rows_own):
            for part in range(2):
                out_copy(own, part).wait()


def exchange(pieces, axes, counts):
    positions = list(itertools.product(*map(range, counts)))
    place = {position: i for i, position in enumerate(positions)}
    arrived = [pieces[0]] * len(positions)
    for i in range(1, len(positions)):
        route = [
            (place[position], place[tuple(map(toward, position, positions[i], counts))])
            for position in positions
        ]
        arrived[i] = lax.ppermute(pieces[i], axes, route)
    return arrived


def local(walker_mats, vertex, weights, transfer_table, g4_old):
    blk_count = lax.axis_size("blk")
    walk_count = lax.axis_size("walk")
    sub_count = lax.axis_size("sub")
    rows_local, vertices = walker_mats.shape[1:]
    rows_own, transfers, columns = g4_old.shape
    devices = blk_count * walk_count * sub_count
    sizes = (blk_count, walk_count, sub_count, rows_own)
    vmem = pl.BlockSpec(memory_space=pltpu.VMEM)
    vertices_local = vertices // sub_count
    early = vertices_local // (4 * lanes) * 2 * lanes
    middle = early // 2
    coded = columns // 2 + lanes
    sent = pl.pallas_call(
        functools.partial(transform_kernel, sizes),
        out_shape=[
            jax.ShapeDtypeStruct((blk_count * rows_own, coded if place else columns), jnp.int32 if place else jnp.float32)
            for place in range(walk_count * sub_count)
        ],
        in_specs=[pl.BlockSpec(memory_space=pl.ANY)] * 2,
        out_specs=[vmem] * (walk_count * sub_count),
        scratch_shapes=[
            pltpu.VMEM((rows_local, vertices_local), jnp.bfloat16),
            pltpu.VMEM((1, vertices), jnp.int32),
            pltpu.VMEM((devices * rows_own, rows_local), jnp.bfloat16),
            pltpu.VMEM((columns, early), jnp.bfloat16),
            pltpu.VMEM((columns, middle), jnp.bfloat16),
            pltpu.VMEM((columns, vertices_local - early - middle), jnp.bfloat16),
            pltpu.VMEM((2 * devices * rows_own, vertices_local), jnp.bfloat16),
            pltpu.SemaphoreType.DMA,
            pltpu.SemaphoreType.DMA,
        ],
        compiler_params=pltpu.CompilerParams(vmem_limit_bytes=24 * 2**20),
        name="transform",
    )(*[pltpu.with_memory_space_constraint(x, pltpu.HBM) for x in (walker_mats, vertex)])
    parts = exchange(sent, ("walk", "sub"), (walk_count, sub_count))
    shared = blk_count <= RSTEPS
    rows_each = (blk_count if shared else RSTEPS) * rows_own
    whole_count = 1 if shared else blk_count
    whole = pl.pallas_call(
        functools.partial(combine_kernel, sizes),
        out_shape=[jax.ShapeDtypeStruct((rows_each, coded), jnp.int32)] * whole_count,
        in_specs=[vmem] * len(parts),
        out_specs=[vmem] * whole_count,
        scratch_shapes=[pltpu.VMEM((blk_count * rows_own, 1, coded), jnp.int32)],
        compiler_params=pltpu.CompilerParams(vmem_limit_bytes=24 * 2**20),
        name="combine",
    )(*parts)
    arrived = exchange(whole * blk_count if shared else whole, ("blk",), (blk_count,))
    far = blk_count // 2
    totals = g4_old
    groups = [0, *range(far + 1, blk_count)], [*range(1, far)], [far]
    for places in groups:
        last = places is groups[-1]
        scratch_shapes = [
            pltpu.VMEM((len(places), transfers, columns // 2), jnp.int32),
            pltpu.VMEM((len(places), 1, columns), jnp.float32),
            pltpu.VMEM((len(places), transfers, lanes), jnp.float32),
        ]
        if last:
            scratch_shapes.append(pltpu.VMEM(g4_old.shape, jnp.float32))
            scratch_shapes.append(pltpu.SemaphoreType.DMA((rows_own, 2)))
        totals = pl.pallas_call(
            functools.partial(accumulate_kernel, sizes, places, last),
            out_shape=jax.ShapeDtypeStruct(g4_old.shape, jnp.float32),
            in_specs=[vmem] * (3 + len(places)),
            out_specs=pl.BlockSpec(memory_space=pl.ANY) if last else vmem,
            scratch_shapes=scratch_shapes,
            compiler_params=pltpu.CompilerParams(vmem_limit_bytes=24 * 2**20),
            cost_estimate=pl.CostEstimate(
                flops=1000 * len(places) * transfers * columns,
                bytes_accessed=12 * transfers * columns,
                transcendentals=0,
            ),
            name="accumulate",
        )(weights[None], transfer_table, totals, *[arrived[place] for place in places])
    return totals


def solution(mesh):
    in_specs = (
        P(("grp", "blk"), "walk", None),
        P(("grp", "blk"), None),
        P("grp"),
        P(),
        P(("grp", "blk", "walk", "sub"), None, None),
    )
    out_specs = P(("grp", "blk", "walk", "sub"), None, None)
    return jax.shard_map(local, mesh=mesh, in_specs=in_specs, out_specs=out_specs, check_vma=False)
```

```python
import functools
import itertools
import math

import jax
import jax.numpy as jnp
from jax import lax
from jax.experimental import pallas as pl
from jax.experimental.pallas import tpu as pltpu
from jax.sharding import PartitionSpec as P

TQ = 4
RSTEPS = 4


phase_period = 8192
quarter_bits = 11
lanes = 128
lane_bits = 7
sublanes = 8
code_limit = 32767.0
smallest_peak = 1e-30
exponent_margin = 1e-3


def toward(index, distance, count):
    if count & (count - 1) == 0:
        return index ^ distance
    return (index + distance) % count


def back(index, distance, count):
    if count & (count - 1) == 0:
        return index ^ distance
    return (index + count - distance) % count


def cos_sin(product):
    residue = product & (phase_period - 1)
    quarter = (residue + phase_period // 8) >> quarter_bits
    angle = (residue - (quarter << quarter_bits)).astype(jnp.float32) * (2.0 * math.pi / phase_period)
    square = angle * angle
    sine = angle + angle * square * (
        -1.0 / 6.0 + square * (1.0 / 120.0 + square * (-1.0 / 5040.0 + square * (1.0 / 362880.0)))
    )
    cosine = 1.0 + square * (
        -0.5 + square * (1.0 / 24.0 + square * (-1.0 / 720.0 + square * (1.0 / 40320.0)))
    )
    odd = (quarter & 1) == 1
    cosine_out = jnp.where(odd, sine, cosine)
    sine_out = jnp.where(odd, cosine, sine)
    cosine_out = jnp.where(((quarter + 1) & 2) == 2, -cosine_out, cosine_out)
    sine_out = jnp.where((quarter & 2) == 2, -sine_out, sine_out)
    return cosine_out, sine_out


def row_ids(count):
    return lax.broadcasted_iota(jnp.int32, (count, lanes), 0)


def split_by(ids, size):
    if size & (size - 1) == 0:
        return ids >> (size.bit_length() - 1), ids & (size - 1)
    return ids // size, ids % size


def tile_of(start):
    return pl.ds(start if isinstance(start, int) else pl.multiple_of(start, lanes), lanes)


def make_table(vertex_ref, table_ref, first, place):
    columns = table_ref.shape[0]
    blocks = columns // lanes
    half_blocks = blocks // 2
    coarse_rows = -(-max(half_blocks, 1) // sublanes) * sublanes
    middle_count = lanes // sublanes
    center = (blocks - 1) * (lanes // 2)
    here = tile_of(place)
    vertex = vertex_ref[:, tile_of(first)]
    cosine, sine = cos_sin(vertex * (row_ids(sublanes) + center))
    cas_fine, cam_fine = cosine + sine, cosine - sine
    cos_middle, sin_middle = cos_sin(vertex * (row_ids(middle_count) * sublanes))
    cos_coarse, sin_coarse = cos_sin(
        vertex * ((blocks - 1 - 2 * row_ids(coarse_rows)) * (lanes // 2))
    )
    for pair in range(middle_count // 2):
        cas, cam = [], []
        for middle in (2 * pair, 2 * pair + 1):
            c, s = cos_middle[middle : middle + 1], sin_middle[middle : middle + 1]
            cas.append(c * cas_fine + s * cam_fine)
            cam.append(c * cam_fine - s * cas_fine)
        cas, cam = jnp.concatenate(cas, axis=0), jnp.concatenate(cam, axis=0)
        start = pair * 2 * sublanes
        for low in range(half_blocks):
            high = blocks - 1 - low
            even = cos_coarse[low : low + 1] * cas
            odd = sin_coarse[low : low + 1] * cam
            for block, value in ((low, even - odd), (high, even + odd)):
                row = block * lanes + start
                table_ref[row : row + 2 * sublanes, here] = value.astype(jnp.bfloat16)
        if blocks % 2:
            row = half_blocks * lanes + start
            table_ref[row : row + 2 * sublanes, here] = cas.astype(jnp.bfloat16)


def encode(rows):
    half = rows.shape[1] // 2
    peak = jnp.maximum(jnp.max(jnp.abs(rows), axis=1, keepdims=True), smallest_peak)
    exponent = jnp.ceil(jnp.log2(peak * (1.0 / code_limit)) + exponent_margin)
    codes = jnp.floor(rows * (1.0 / jnp.exp2(exponent)) + 0.5).astype(jnp.int32)
    words = (codes[:, :half] << 16) | (codes[:, half:] & 0xFFFF)
    tail = jnp.broadcast_to(exponent.astype(jnp.int32), (rows.shape[0], lanes))
    return jnp.concatenate([words, tail], axis=1)


def units(coded):
    return jnp.exp2(coded[:, coded.shape[1] - lanes :].astype(jnp.float32))


def decode(coded):
    words = coded[:, : coded.shape[1] - lanes]
    codes = jnp.concatenate([words >> 16, (words << 16) >> 16], axis=1)
    return codes.astype(jnp.float32) * units(coded)[:, :1]


def transform_kernel(sizes, matrix_hbm, vertex_hbm, *rest):
    *sent_refs, matrix_ref, vertex_ref, left_ref, early_ref, middle_ref, late_ref, weight_ref, matrix_sem, vertex_sem = rest
    blk_count, walk_count, sub_count, rows_own = sizes
    walk_index = lax.axis_index("walk")
    sub_index = lax.axis_index("sub")
    rows_local, vertices_local = matrix_ref.shape
    window_rows = left_ref.shape[0]
    early = early_ref.shape[1]

    vertex_copy = pltpu.make_async_copy(vertex_hbm, vertex_ref, vertex_sem)
    vertex_copy.start()
    first = pl.multiple_of(sub_index * vertices_local, lanes)
    matrix_copy = pltpu.make_async_copy(
        matrix_hbm.at[0, :, pl.ds(first, vertices_local)], matrix_ref, matrix_sem
    )
    matrix_copy.start()

    ids, inner = split_by(row_ids(window_rows), rows_own)
    ids, blk_part = split_by(ids, blk_count)
    walk_part, sub_part = split_by(ids, sub_count)
    sub_part = toward(sub_index, sub_part, sub_count)
    walk_part = toward(walk_index, walk_part, walk_count)
    window = ((blk_part * walk_count + walk_part) * sub_count + sub_part) * rows_own + inner

    vertex_copy.wait()
    own_start = pl.multiple_of(walk_index * rows_local, lanes)
    for start in range(0, rows_local, lanes):
        own_vertex = vertex_ref[:, pl.ds(own_start + start, lanes)]
        cosine, sine = cos_sin(own_vertex * window)
        left_ref[:, start : start + lanes] = (cosine + sine).astype(jnp.bfloat16)

    @pl.loop(0, early // lanes)
    def _(step):
        make_table(vertex_ref, early_ref, first + step * lanes, step * lanes)

    matrix_copy.wait()
    chunk = 4 * lanes
    for start in range(0, vertices_local, chunk):
        left_product = jnp.dot(
            left_ref[...], matrix_ref[:, start : start + chunk], preferred_element_type=jnp.float32
        )
        high = left_product.astype(jnp.bfloat16)
        weight_ref[:window_rows, start : start + chunk] = high
        weight_ref[window_rows:, start : start + chunk] = (
            left_product - high.astype(jnp.float32)
        ).astype(jnp.bfloat16)
    green, start = 0.0, 0
    for table_ref in (early_ref, middle_ref, late_ref):
        size = table_ref.shape[1]
        if table_ref is not early_ref:
            for tile in range(0, size, lanes):
                make_table(vertex_ref, table_ref, first + start + tile, tile)
        green += lax.dot_general(
            table_ref[...],
            weight_ref[:, start : start + size],
            (((1,), (1,)), ((), ())),
            preferred_element_type=jnp.float32,
        )
        start += size
    green = green.T
    green = green[:window_rows] + green[window_rows:]
    rows_each = blk_count * rows_own
    coded = encode(green)
    for place, sent_ref in enumerate(sent_refs):
        rows = coded if place else green
        sent_ref[...] = rows[place * rows_each : (place + 1) * rows_each]


def combine_kernel(sizes, *refs):
    blk_count, walk_count, sub_count, rows_own = sizes
    blk_index = lax.axis_index("blk")
    parts = walk_count * sub_count
    part_refs, whole_refs, row_ref = refs[:parts], refs[parts:-1], refs[-1]
    total = part_refs[0][...] + sum(decode(part_ref[...]) for part_ref in part_refs[1:])
    coded = encode(total)
    if len(whole_refs) == 1:
        whole_refs[0][...] = coded
        return
    for row in range(blk_count * rows_own):
        row_ref[row] = coded[row : row + 1]
    for place, whole_ref in enumerate(whole_refs):
        for step in range(RSTEPS):
            blk_part = toward(blk_index, place, blk_count) + RSTEPS * blk_count - step
            _, blk_part = split_by(blk_part, blk_count)
            for inner in range(rows_own):
                row = step * rows_own + inner
                whole_ref[row : row + 1] = row_ref[blk_part * rows_own + inner]


def accumulate_kernel(sizes, distances, last, weights_ref, transfer_ref, old_ref, *rest):
    if last:
        *arrived_refs, out_ref, source_ref, left_ref, unit_ref, new_ref, out_sems = rest
    else:
        *arrived_refs, new_ref, source_ref, left_ref, unit_ref = rest
    blk_count, _, _, rows_own = sizes
    blk_index = lax.axis_index("blk")
    transfers, columns = transfer_ref.shape
    half = columns // 2
    groups = transfers // sublanes
    tiles = columns // lanes
    weights = weights_ref[...] * (1.0 / blk_count)
    walker_ids = lax.broadcasted_iota(jnp.int32, weights.shape, 1)

    ids = lax.broadcasted_iota(jnp.int32, (transfers, 1), 0)
    step, _ = split_by(ids, TQ)
    if arrived_refs[0].shape[0] == blk_count * rows_own:
        _, step = split_by(blk_index + RSTEPS * blk_count - step, blk_count)

    def out_copy(own, part):
        here = slice(part * half, (part + 1) * half)
        return pltpu.make_async_copy(
            new_ref.at[own, :, here], out_ref.at[own, :, here], out_sems.at[own, part]
        )

    def spread(rows, own):
        wide = (transfers, rows.shape[1])
        picked = jnp.broadcast_to(rows[own : own + 1], wide)
        for place in range(1, rows.shape[0] // rows_own):
            row = place * rows_own + own
            picked = jnp.where(step == place, jnp.broadcast_to(rows[row : row + 1], wide), picked)
        return picked

    for own in range(rows_own):
        for place, distance in enumerate(distances):
            coded = arrived_refs[place][...]
            walker = back(blk_index, distance, blk_count)
            weight = jnp.sum(jnp.where(walker_ids == walker, weights, 0.0), axis=1, keepdims=True)
            left = coded[own : own + 1]
            for blk_part in range(1, coded.shape[0] // rows_own):
                row = blk_part * rows_own + own
                left = jnp.where(step[:1] == blk_part, coded[row : row + 1], left)
            left_ref[place] = decode(left) * weight
            unit_ref[place] = spread(units(coded), own)
            source_ref[place] = spread(coded[:, :half], own)

        together = len(distances) if len(distances) <= 4 else math.gcd(len(distances), 4)

        for tile in range(tiles):
            here = slice(tile * lanes, (tile + 1) * lanes)
            for group in range(groups):
                rows = slice(group * sublanes, (group + 1) * sublanes)
                index = transfer_ref[rows, here]
                index_lane = index & (lanes - 1)
                in_first = index < half
                index_tile = jnp.where(in_first, index, index - half) >> lane_bits

                def add_walkers(first, total):
                    picked = [jnp.zeros((sublanes, lanes), jnp.int32)] * together
                    for source in range(half // lanes):
                        match = index_tile == source
                        for k in range(together):
                            words = source_ref[
                                first + k, rows, source * lanes : (source + 1) * lanes
                            ]
                            words = jnp.take_along_axis(
                                words, index_lane, axis=1, mode="promise_in_bounds"
                            )
                            picked[k] = jnp.where(match, words, picked[k])
                    for k in range(together):
                        code = jnp.where(in_first, picked[k], picked[k] << 16) >> 16
                        total = total + left_ref[first + k, :, here] * (
                            unit_ref[first + k, rows] * code.astype(jnp.float32)
                        )
                    return total

                total = old_ref[own, rows, here]
                if len(distances) == together:
                    total = add_walkers(0, total)
                else:
                    total = lax.fori_loop(
                        0, len(distances) // together, lambda i, t: add_walkers(i * together, t), total
                    )
                new_ref[own, rows, here] = total

            if last and (tile + 1) % (tiles // 2) == 0:
                out_copy(own, (tile + 1) // (tiles // 2) - 1).start()
    if last:
        for own in range(rows_own):
            for part in range(2):
                out_copy(own, part).wait()


def exchange(pieces, axes, counts):
    positions = list(itertools.product(*map(range, counts)))
    place = {position: i for i, position in enumerate(positions)}
    arrived = [pieces[0]] * len(positions)
    for i in range(1, len(positions)):
        route = [
            (place[position], place[tuple(map(toward, position, positions[i], counts))])
            for position in positions
        ]
        arrived[i] = lax.ppermute(pieces[i], axes, route)
    return arrived


def local(walker_mats, vertex, weights, transfer_table, g4_old):
    blk_count = lax.axis_size("blk")
    walk_count = lax.axis_size("walk")
    sub_count = lax.axis_size("sub")
    rows_local, vertices = walker_mats.shape[1:]
    rows_own, transfers, columns = g4_old.shape
    devices = blk_count * walk_count * sub_count
    sizes = (blk_count, walk_count, sub_count, rows_own)
    vmem = pl.BlockSpec(memory_space=pltpu.VMEM)
    vertices_local = vertices // sub_count
    early = vertices_local // (8 * lanes) * 2 * lanes
    middle = 2 * early
    coded = columns // 2 + lanes
    sent = pl.pallas_call(
        functools.partial(transform_kernel, sizes),
        out_shape=[
            jax.ShapeDtypeStruct((blk_count * rows_own, coded if place else columns), jnp.int32 if place else jnp.float32)
            for place in range(walk_count * sub_count)
        ],
        in_specs=[pl.BlockSpec(memory_space=pl.ANY)] * 2,
        out_specs=[vmem] * (walk_count * sub_count),
        scratch_shapes=[
            pltpu.VMEM((rows_local, vertices_local), jnp.bfloat16),
            pltpu.VMEM((1, vertices), jnp.int32),
            pltpu.VMEM((devices * rows_own, rows_local), jnp.bfloat16),
            pltpu.VMEM((columns, early), jnp.bfloat16),
            pltpu.VMEM((columns, middle), jnp.bfloat16),
            pltpu.VMEM((columns, vertices_local - early - middle), jnp.bfloat16),
            pltpu.VMEM((2 * devices * rows_own, vertices_local), jnp.bfloat16),
            pltpu.SemaphoreType.DMA,
            pltpu.SemaphoreType.DMA,
        ],
        compiler_params=pltpu.CompilerParams(vmem_limit_bytes=24 * 2**20),
        name="transform",
    )(*[pltpu.with_memory_space_constraint(x, pltpu.HBM) for x in (walker_mats, vertex)])
    parts = exchange(sent, ("walk", "sub"), (walk_count, sub_count))
    shared = blk_count <= RSTEPS
    rows_each = (blk_count if shared else RSTEPS) * rows_own
    whole_count = 1 if shared else blk_count
    whole = pl.pallas_call(
        functools.partial(combine_kernel, sizes),
        out_shape=[jax.ShapeDtypeStruct((rows_each, coded), jnp.int32)] * whole_count,
        in_specs=[vmem] * len(parts),
        out_specs=[vmem] * whole_count,
        scratch_shapes=[pltpu.VMEM((blk_count * rows_own, 1, coded), jnp.int32)],
        compiler_params=pltpu.CompilerParams(vmem_limit_bytes=24 * 2**20),
        name="combine",
    )(*parts)
    arrived = exchange(whole * blk_count if shared else whole, ("blk",), (blk_count,))
    far = blk_count // 2
    totals = g4_old
    groups = [0, *range(far + 1, blk_count)], [*range(1, far)], [far]
    for places in groups:
        last = places is groups[-1]
        scratch_shapes = [
            pltpu.VMEM((len(places), transfers, columns // 2), jnp.int32),
            pltpu.VMEM((len(places), 1, columns), jnp.float32),
            pltpu.VMEM((len(places), transfers, lanes), jnp.float32),
        ]
        if last:
            scratch_shapes.append(pltpu.VMEM(g4_old.shape, jnp.float32))
            scratch_shapes.append(pltpu.SemaphoreType.DMA((rows_own, 2)))
        totals = pl.pallas_call(
            functools.partial(accumulate_kernel, sizes, places, last),
            out_shape=jax.ShapeDtypeStruct(g4_old.shape, jnp.float32),
            in_specs=[vmem] * (3 + len(places)),
            out_specs=pl.BlockSpec(memory_space=pl.ANY) if last else vmem,
            scratch_shapes=scratch_shapes,
            compiler_params=pltpu.CompilerParams(vmem_limit_bytes=24 * 2**20),
            cost_estimate=pl.CostEstimate(
                flops=1000 * len(places) * transfers * columns,
                bytes_accessed=12 * transfers * columns,
                transcendentals=0,
            ),
            name="accumulate",
        )(weights[None], transfer_table, totals, *[arrived[place] for place in places])
    return totals


def solution(mesh):
    in_specs = (
        P(("grp", "blk"), "walk", None),
        P(("grp", "blk"), None),
        P("grp"),
        P(),
        P(("grp", "blk", "walk", "sub"), None, None),
    )
    out_specs = P(("grp", "blk", "walk", "sub"), None, None)
    return jax.shard_map(local, mesh=mesh, in_specs=in_specs, out_specs=out_specs, check_vma=False)
```

```python
import functools
import itertools
import math

import jax
import jax.numpy as jnp
from jax import lax
from jax.experimental import pallas as pl
from jax.experimental.pallas import tpu as pltpu
from jax.sharding import PartitionSpec as P

TQ = 4
RSTEPS = 4


phase_period = 8192
quarter_bits = 11
lanes = 128
lane_bits = 7
sublanes = 8
code_limit = 32767.0
smallest_peak = 1e-30
exponent_margin = 1e-3


def toward(index, distance, count):
    if count & (count - 1) == 0:
        return index ^ distance
    return (index + distance) % count


def back(index, distance, count):
    if count & (count - 1) == 0:
        return index ^ distance
    return (index + count - distance) % count


def cos_sin(product):
    residue = product & (phase_period - 1)
    quarter = (residue + phase_period // 8) >> quarter_bits
    angle = (residue - (quarter << quarter_bits)).astype(jnp.float32) * (2.0 * math.pi / phase_period)
    square = angle * angle
    sine = angle + angle * square * (
        -1.0 / 6.0 + square * (1.0 / 120.0 + square * (-1.0 / 5040.0 + square * (1.0 / 362880.0)))
    )
    cosine = 1.0 + square * (
        -0.5 + square * (1.0 / 24.0 + square * (-1.0 / 720.0 + square * (1.0 / 40320.0)))
    )
    odd = (quarter & 1) == 1
    cosine_out = jnp.where(odd, sine, cosine)
    sine_out = jnp.where(odd, cosine, sine)
    cosine_out = jnp.where(((quarter + 1) & 2) == 2, -cosine_out, cosine_out)
    sine_out = jnp.where((quarter & 2) == 2, -sine_out, sine_out)
    return cosine_out, sine_out


def row_ids(count):
    return lax.broadcasted_iota(jnp.int32, (count, lanes), 0)


def split_by(ids, size):
    if size & (size - 1) == 0:
        return ids >> (size.bit_length() - 1), ids & (size - 1)
    return ids // size, ids % size


def tile_of(start):
    return pl.ds(start if isinstance(start, int) else pl.multiple_of(start, lanes), lanes)


def make_table(vertex_ref, table_ref, first, place):
    columns = table_ref.shape[0]
    blocks = columns // lanes
    half_blocks = blocks // 2
    coarse_rows = -(-max(half_blocks, 1) // sublanes) * sublanes
    middle_count = lanes // sublanes
    center = (blocks - 1) * (lanes // 2)
    here = tile_of(place)
    vertex = vertex_ref[:, tile_of(first)]
    cosine, sine = cos_sin(vertex * (row_ids(sublanes) + center))
    cas_fine, cam_fine = cosine + sine, cosine - sine
    cos_middle, sin_middle = cos_sin(vertex * (row_ids(middle_count) * sublanes))
    cos_coarse, sin_coarse = cos_sin(
        vertex * ((blocks - 1 - 2 * row_ids(coarse_rows)) * (lanes // 2))
    )
    for pair in range(middle_count // 2):
        cas, cam = [], []
        for middle in (2 * pair, 2 * pair + 1):
            c, s = cos_middle[middle : middle + 1], sin_middle[middle : middle + 1]
            cas.append(c * cas_fine + s * cam_fine)
            cam.append(c * cam_fine - s * cas_fine)
        cas, cam = jnp.concatenate(cas, axis=0), jnp.concatenate(cam, axis=0)
        start = pair * 2 * sublanes
        for low in range(half_blocks):
            high = blocks - 1 - low
            even = cos_coarse[low : low + 1] * cas
            odd = sin_coarse[low : low + 1] * cam
            for block, value in ((low, even - odd), (high, even + odd)):
                row = block * lanes + start
                table_ref[row : row + 2 * sublanes, here] = value.astype(jnp.bfloat16)
        if blocks % 2:
            row = half_blocks * lanes + start
            table_ref[row : row + 2 * sublanes, here] = cas.astype(jnp.bfloat16)


def encode(rows):
    half = rows.shape[1] // 2
    peak = jnp.maximum(jnp.max(jnp.abs(rows), axis=1, keepdims=True), smallest_peak)
    exponent = jnp.ceil(jnp.log2(peak * (1.0 / code_limit)) + exponent_margin)
    codes = jnp.floor(rows * (1.0 / jnp.exp2(exponent)) + 0.5).astype(jnp.int32)
    words = (codes[:, :half] << 16) | (codes[:, half:] & 0xFFFF)
    tail = jnp.broadcast_to(exponent.astype(jnp.int32), (rows.shape[0], lanes))
    return jnp.concatenate([words, tail], axis=1)


def units(coded):
    return jnp.exp2(coded[:, coded.shape[1] - lanes :].astype(jnp.float32))


def decode(coded):
    words = coded[:, : coded.shape[1] - lanes]
    codes = jnp.concatenate([words >> 16, (words << 16) >> 16], axis=1)
    return codes.astype(jnp.float32) * units(coded)[:, :1]


def transform_kernel(sizes, matrix_hbm, vertex_hbm, *rest):
    *sent_refs, matrix_ref, vertex_ref, left_ref, early_ref, middle_ref, late_ref, weight_ref, matrix_sem, vertex_sem = rest
    blk_count, walk_count, sub_count, rows_own = sizes
    walk_index = lax.axis_index("walk")
    sub_index = lax.axis_index("sub")
    rows_local, vertices_local = matrix_ref.shape
    window_rows = left_ref.shape[0]
    early = early_ref.shape[1]

    vertex_copy = pltpu.make_async_copy(vertex_hbm, vertex_ref, vertex_sem)
    vertex_copy.start()
    first = pl.multiple_of(sub_index * vertices_local, lanes)
    matrix_copy = pltpu.make_async_copy(
        matrix_hbm.at[0, :, pl.ds(first, vertices_local)], matrix_ref, matrix_sem
    )
    matrix_copy.start()

    ids, inner = split_by(row_ids(window_rows), rows_own)
    ids, blk_part = split_by(ids, blk_count)
    walk_part, sub_part = split_by(ids, sub_count)
    sub_part = toward(sub_index, sub_part, sub_count)
    walk_part = toward(walk_index, walk_part, walk_count)
    window = ((blk_part * walk_count + walk_part) * sub_count + sub_part) * rows_own + inner

    vertex_copy.wait()
    own_start = pl.multiple_of(walk_index * rows_local, lanes)
    for start in range(0, rows_local, lanes):
        own_vertex = vertex_ref[:, pl.ds(own_start + start, lanes)]
        cosine, sine = cos_sin(own_vertex * window)
        left_ref[:, start : start + lanes] = (cosine + sine).astype(jnp.bfloat16)

    @pl.loop(0, early // lanes)
    def _(step):
        make_table(vertex_ref, early_ref, first + step * lanes, step * lanes)

    matrix_copy.wait()
    chunk = 4 * lanes
    for start in range(0, vertices_local, chunk):
        left_product = jnp.dot(
            left_ref[...], matrix_ref[:, start : start + chunk], preferred_element_type=jnp.float32
        )
        high = left_product.astype(jnp.bfloat16)
        weight_ref[:window_rows, start : start + chunk] = high
        weight_ref[window_rows:, start : start + chunk] = (
            left_product - high.astype(jnp.float32)
        ).astype(jnp.bfloat16)
    green, start = 0.0, 0
    for table_ref in (early_ref, middle_ref, late_ref):
        size = table_ref.shape[1]
        if table_ref is not early_ref:
            for tile in range(0, size, lanes):
                make_table(vertex_ref, table_ref, first + start + tile, tile)
        green += lax.dot_general(
            table_ref[...],
            weight_ref[:, start : start + size],
            (((1,), (1,)), ((), ())),
            preferred_element_type=jnp.float32,
        )
        start += size
    green = green.T
    green = green[:window_rows] + green[window_rows:]
    rows_each = blk_count * rows_own
    coded = encode(green)
    for place, sent_ref in enumerate(sent_refs):
        sent_ref[...] = coded[place * rows_each : (place + 1) * rows_each]


def combine_kernel(sizes, *refs):
    blk_count, walk_count, sub_count, rows_own = sizes
    blk_index = lax.axis_index("blk")
    parts = walk_count * sub_count
    part_refs, whole_refs, row_ref = refs[:parts], refs[parts:-1], refs[-1]
    half = part_refs[0].shape[1] - lanes

    exponents = [part_ref[:, half:] for part_ref in part_refs]
    exponent = functools.reduce(jnp.maximum, exponents) + (parts - 1).bit_length()
    high, low = 0.5, 0.5
    for part_ref, part_exponent in zip(part_refs, exponents):
        scale = jnp.exp2((part_exponent - exponent).astype(jnp.float32))[:, :1]
        words = part_ref[:, :half]
        high += (words >> 16).astype(jnp.float32) * scale
        low += ((words << 16) >> 16).astype(jnp.float32) * scale
    high, low = jnp.floor(high).astype(jnp.int32), jnp.floor(low).astype(jnp.int32)
    coded = jnp.concatenate([(high << 16) | (low & 0xFFFF), exponent], axis=1)
    if len(whole_refs) == 1:
        whole_refs[0][...] = coded
        return
    for row in range(blk_count * rows_own):
        row_ref[row] = coded[row : row + 1]
    for place, whole_ref in enumerate(whole_refs):
        for step in range(RSTEPS):
            blk_part = toward(blk_index, place, blk_count) + RSTEPS * blk_count - step
            _, blk_part = split_by(blk_part, blk_count)
            for inner in range(rows_own):
                row = step * rows_own + inner
                whole_ref[row : row + 1] = row_ref[blk_part * rows_own + inner]


def accumulate_kernel(sizes, distances, last, weights_ref, transfer_ref, old_ref, *rest):
    if last:
        *arrived_refs, out_ref, source_ref, left_ref, unit_ref, new_ref, out_sems = rest
    else:
        *arrived_refs, new_ref, source_ref, left_ref, unit_ref = rest
    blk_count, _, _, rows_own = sizes
    blk_index = lax.axis_index("blk")
    transfers, columns = transfer_ref.shape
    half = columns // 2
    groups = transfers // sublanes
    tiles = columns // lanes
    weights = weights_ref[...] * (1.0 / blk_count)
    walker_ids = lax.broadcasted_iota(jnp.int32, weights.shape, 1)

    ids = lax.broadcasted_iota(jnp.int32, (transfers, 1), 0)
    step, _ = split_by(ids, TQ)
    if arrived_refs[0].shape[0] == blk_count * rows_own:
        _, step = split_by(blk_index + RSTEPS * blk_count - step, blk_count)

    def out_copy(own, part):
        here = slice(part * half, (part + 1) * half)
        return pltpu.make_async_copy(
            new_ref.at[own, :, here], out_ref.at[own, :, here], out_sems.at[own, part]
        )

    def spread(rows, own):
        wide = (transfers, rows.shape[1])
        picked = jnp.broadcast_to(rows[own : own + 1], wide)
        for place in range(1, rows.shape[0] // rows_own):
            row = place * rows_own + own
            picked = jnp.where(step == place, jnp.broadcast_to(rows[row : row + 1], wide), picked)
        return picked

    for own in range(rows_own):
        for place, distance in enumerate(distances):
            coded = arrived_refs[place][...]
            walker = back(blk_index, distance, blk_count)
            weight = jnp.sum(jnp.where(walker_ids == walker, weights, 0.0), axis=1, keepdims=True)
            left = coded[own : own + 1]
            for blk_part in range(1, coded.shape[0] // rows_own):
                row = blk_part * rows_own + own
                left = jnp.where(step[:1] == blk_part, coded[row : row + 1], left)
            left_ref[place] = decode(left) * weight
            unit_ref[place] = spread(units(coded), own)
            source_ref[place] = spread(coded[:, :half], own)

        together = len(distances) if len(distances) <= 4 else math.gcd(len(distances), 4)

        for tile in range(tiles):
            here = slice(tile * lanes, (tile + 1) * lanes)
            for group in range(groups):
                rows = slice(group * sublanes, (group + 1) * sublanes)
                index = transfer_ref[rows, here]
                index_lane = index & (lanes - 1)
                in_first = index < half
                index_tile = jnp.where(in_first, index, index - half) >> lane_bits

                def add_walkers(first, total):
                    picked = [jnp.zeros((sublanes, lanes), jnp.int32)] * together
                    for source in range(half // lanes):
                        match = index_tile == source
                        for k in range(together):
                            words = source_ref[
                                first + k, rows, source * lanes : (source + 1) * lanes
                            ]
                            words = jnp.take_along_axis(
                                words, index_lane, axis=1, mode="promise_in_bounds"
                            )
                            picked[k] = jnp.where(match, words, picked[k])
                    for k in range(together):
                        code = jnp.where(in_first, picked[k], picked[k] << 16) >> 16
                        total = total + left_ref[first + k, :, here] * (
                            unit_ref[first + k, rows] * code.astype(jnp.float32)
                        )
                    return total

                total = old_ref[own, rows, here]
                if len(distances) == together:
                    total = add_walkers(0, total)
                else:
                    total = lax.fori_loop(
                        0, len(distances) // together, lambda i, t: add_walkers(i * together, t), total
                    )
                new_ref[own, rows, here] = total

            if last and (tile + 1) % (tiles // 2) == 0:
                out_copy(own, (tile + 1) // (tiles // 2) - 1).start()
    if last:
        for own in range(rows_own):
            for part in range(2):
                out_copy(own, part).wait()


def exchange(pieces, axes, counts):
    positions = list(itertools.product(*map(range, counts)))
    place = {position: i for i, position in enumerate(positions)}
    arrived = [pieces[0]] * len(positions)
    for i in range(1, len(positions)):
        route = [
            (place[position], place[tuple(map(toward, position, positions[i], counts))])
            for position in positions
        ]
        arrived[i] = lax.ppermute(pieces[i], axes, route)
    return arrived


def local(walker_mats, vertex, weights, transfer_table, g4_old):
    blk_count = lax.axis_size("blk")
    walk_count = lax.axis_size("walk")
    sub_count = lax.axis_size("sub")
    rows_local, vertices = walker_mats.shape[1:]
    rows_own, transfers, columns = g4_old.shape
    devices = blk_count * walk_count * sub_count
    sizes = (blk_count, walk_count, sub_count, rows_own)
    vmem = pl.BlockSpec(memory_space=pltpu.VMEM)
    vertices_local = vertices // sub_count
    early = vertices_local // (4 * lanes) * 2 * lanes
    middle = early // 2
    coded = columns // 2 + lanes
    sent = pl.pallas_call(
        functools.partial(transform_kernel, sizes),
        out_shape=[jax.ShapeDtypeStruct((blk_count * rows_own, coded), jnp.int32)]
        * (walk_count * sub_count),
        in_specs=[pl.BlockSpec(memory_space=pl.ANY)] * 2,
        out_specs=[vmem] * (walk_count * sub_count),
        scratch_shapes=[
            pltpu.VMEM((rows_local, vertices_local), jnp.bfloat16),
            pltpu.VMEM((1, vertices), jnp.int32),
            pltpu.VMEM((devices * rows_own, rows_local), jnp.bfloat16),
            pltpu.VMEM((columns, early), jnp.bfloat16),
            pltpu.VMEM((columns, middle), jnp.bfloat16),
            pltpu.VMEM((columns, vertices_local - early - middle), jnp.bfloat16),
            pltpu.VMEM((2 * devices * rows_own, vertices_local), jnp.bfloat16),
            pltpu.SemaphoreType.DMA,
            pltpu.SemaphoreType.DMA,
        ],
        compiler_params=pltpu.CompilerParams(vmem_limit_bytes=24 * 2**20),
        name="transform",
    )(*[pltpu.with_memory_space_constraint(x, pltpu.HBM) for x in (walker_mats, vertex)])
    parts = exchange(sent, ("walk", "sub"), (walk_count, sub_count))
    shared = blk_count <= RSTEPS
    rows_each = (blk_count if shared else RSTEPS) * rows_own
    whole_count = 1 if shared else blk_count
    whole = pl.pallas_call(
        functools.partial(combine_kernel, sizes),
        out_shape=[jax.ShapeDtypeStruct((rows_each, coded), jnp.int32)] * whole_count,
        in_specs=[vmem] * len(parts),
        out_specs=[vmem] * whole_count,
        scratch_shapes=[pltpu.VMEM((blk_count * rows_own, 1, coded), jnp.int32)],
        compiler_params=pltpu.CompilerParams(vmem_limit_bytes=24 * 2**20),
        name="combine",
    )(*parts)
    arrived = exchange(whole * blk_count if shared else whole, ("blk",), (blk_count,))
    far = blk_count // 2
    totals = g4_old
    groups = [0, *range(far + 1, blk_count)], [*range(1, far)], [far]
    for places in groups:
        last = places is groups[-1]
        scratch_shapes = [
            pltpu.VMEM((len(places), transfers, columns // 2), jnp.int32),
            pltpu.VMEM((len(places), 1, columns), jnp.float32),
            pltpu.VMEM((len(places), transfers, lanes), jnp.float32),
        ]
        if last:
            scratch_shapes.append(pltpu.VMEM(g4_old.shape, jnp.float32))
            scratch_shapes.append(pltpu.SemaphoreType.DMA((rows_own, 2)))
        totals = pl.pallas_call(
            functools.partial(accumulate_kernel, sizes, places, last),
            out_shape=jax.ShapeDtypeStruct(g4_old.shape, jnp.float32),
            in_specs=[vmem] * (3 + len(places)),
            out_specs=pl.BlockSpec(memory_space=pl.ANY) if last else vmem,
            scratch_shapes=scratch_shapes,
            compiler_params=pltpu.CompilerParams(vmem_limit_bytes=24 * 2**20),
            cost_estimate=pl.CostEstimate(
                flops=1000 * len(places) * transfers * columns,
                bytes_accessed=12 * transfers * columns,
                transcendentals=0,
            ),
            name="accumulate",
        )(weights[None], transfer_table, totals, *[arrived[place] for place in places])
    return totals


def solution(mesh):
    in_specs = (
        P(("grp", "blk"), "walk", None),
        P(("grp", "blk"), None),
        P("grp"),
        P(),
        P(("grp", "blk", "walk", "sub"), None, None),
    )
    out_specs = P(("grp", "blk", "walk", "sub"), None, None)
    return jax.shard_map(local, mesh=mesh, in_specs=in_specs, out_specs=out_specs, check_vma=False)
```

```python
import functools
import itertools
import math

import jax
import jax.numpy as jnp
from jax import lax
from jax.experimental import pallas as pl
from jax.experimental.pallas import tpu as pltpu
from jax.sharding import PartitionSpec as P

TQ = 4
RSTEPS = 4


phase_period = 8192
quarter_bits = 11
lanes = 128
lane_bits = 7
sublanes = 8
code_limit = 32767.0
smallest_peak = 1e-30
exponent_margin = 1e-3


def toward(index, distance, count):
    if count & (count - 1) == 0:
        return index ^ distance
    return (index + distance) % count


def back(index, distance, count):
    if count & (count - 1) == 0:
        return index ^ distance
    return (index + count - distance) % count


def cos_sin(product):
    residue = product & (phase_period - 1)
    quarter = (residue + phase_period // 8) >> quarter_bits
    angle = (residue - (quarter << quarter_bits)).astype(jnp.float32) * (2.0 * math.pi / phase_period)
    square = angle * angle
    sine = angle + angle * square * (
        -1.0 / 6.0 + square * (1.0 / 120.0 + square * (-1.0 / 5040.0 + square * (1.0 / 362880.0)))
    )
    cosine = 1.0 + square * (
        -0.5 + square * (1.0 / 24.0 + square * (-1.0 / 720.0 + square * (1.0 / 40320.0)))
    )
    odd = (quarter & 1) == 1
    cosine_out = jnp.where(odd, sine, cosine)
    sine_out = jnp.where(odd, cosine, sine)
    cosine_out = jnp.where(((quarter + 1) & 2) == 2, -cosine_out, cosine_out)
    sine_out = jnp.where((quarter & 2) == 2, -sine_out, sine_out)
    return cosine_out, sine_out


def row_ids(count):
    return lax.broadcasted_iota(jnp.int32, (count, lanes), 0)


def split_by(ids, size):
    if size & (size - 1) == 0:
        return ids >> (size.bit_length() - 1), ids & (size - 1)
    return ids // size, ids % size


def tile_of(start):
    return pl.ds(start if isinstance(start, int) else pl.multiple_of(start, lanes), lanes)


def make_table(vertex_ref, table_ref, first, place):
    columns = table_ref.shape[0]
    blocks = columns // lanes
    half_blocks = blocks // 2
    coarse_rows = -(-max(half_blocks, 1) // sublanes) * sublanes
    middle_count = lanes // sublanes
    center = (blocks - 1) * (lanes // 2)
    here = tile_of(place)
    vertex = vertex_ref[:, tile_of(first)]
    cosine, sine = cos_sin(vertex * (row_ids(sublanes) + center))
    cas_fine, cam_fine = cosine + sine, cosine - sine
    cos_middle, sin_middle = cos_sin(vertex * (row_ids(middle_count) * sublanes))
    cos_coarse, sin_coarse = cos_sin(
        vertex * ((blocks - 1 - 2 * row_ids(coarse_rows)) * (lanes // 2))
    )
    for pair in range(middle_count // 2):
        cas, cam = [], []
        for middle in (2 * pair, 2 * pair + 1):
            c, s = cos_middle[middle : middle + 1], sin_middle[middle : middle + 1]
            cas.append(c * cas_fine + s * cam_fine)
            cam.append(c * cam_fine - s * cas_fine)
        cas, cam = jnp.concatenate(cas, axis=0), jnp.concatenate(cam, axis=0)
        start = pair * 2 * sublanes
        for low in range(half_blocks):
            high = blocks - 1 - low
            even = cos_coarse[low : low + 1] * cas
            odd = sin_coarse[low : low + 1] * cam
            for block, value in ((low, even - odd), (high, even + odd)):
                row = block * lanes + start
                table_ref[row : row + 2 * sublanes, here] = value.astype(jnp.bfloat16)
        if blocks % 2:
            row = half_blocks * lanes + start
            table_ref[row : row + 2 * sublanes, here] = cas.astype(jnp.bfloat16)


def encode(rows):
    half = rows.shape[1] // 2
    peak = jnp.maximum(jnp.max(jnp.abs(rows), axis=1, keepdims=True), smallest_peak)
    exponent = jnp.ceil(jnp.log2(peak * (1.0 / code_limit)) + exponent_margin)
    codes = jnp.floor(rows * (1.0 / jnp.exp2(exponent)) + 0.5).astype(jnp.int32)
    words = (codes[:, :half] << 16) | (codes[:, half:] & 0xFFFF)
    tail = jnp.broadcast_to(exponent.astype(jnp.int32), (rows.shape[0], lanes))
    return jnp.concatenate([words, tail], axis=1)


def units(coded):
    return jnp.exp2(coded[:, coded.shape[1] - lanes :].astype(jnp.float32))


def decode(coded):
    words = coded[:, : coded.shape[1] - lanes]
    codes = jnp.concatenate([words >> 16, (words << 16) >> 16], axis=1)
    return codes.astype(jnp.float32) * units(coded)[:, :1]


def transform_kernel(sizes, matrix_hbm, vertex_hbm, *rest):
    *sent_refs, matrix_ref, vertex_ref, left_ref, early_ref, late_ref, weight_ref, matrix_sem, vertex_sem = rest
    blk_count, walk_count, sub_count, rows_own = sizes
    walk_index = lax.axis_index("walk")
    sub_index = lax.axis_index("sub")
    rows_local, vertices_local = matrix_ref.shape
    window_rows = left_ref.shape[0]
    early = early_ref.shape[1]

    vertex_copy = pltpu.make_async_copy(vertex_hbm, vertex_ref, vertex_sem)
    vertex_copy.start()
    first = pl.multiple_of(sub_index * vertices_local, lanes)
    matrix_copy = pltpu.make_async_copy(
        matrix_hbm.at[0, :, pl.ds(first, vertices_local)], matrix_ref, matrix_sem
    )
    matrix_copy.start()

    ids, inner = split_by(row_ids(window_rows), rows_own)
    ids, blk_part = split_by(ids, blk_count)
    walk_part, sub_part = split_by(ids, sub_count)
    sub_part = toward(sub_index, sub_part, sub_count)
    walk_part = toward(walk_index, walk_part, walk_count)
    window = ((blk_part * walk_count + walk_part) * sub_count + sub_part) * rows_own + inner

    vertex_copy.wait()
    own_start = pl.multiple_of(walk_index * rows_local, lanes)
    for start in range(0, rows_local, lanes):
        own_vertex = vertex_ref[:, pl.ds(own_start + start, lanes)]
        cosine, sine = cos_sin(own_vertex * window)
        left_ref[:, start : start + lanes] = (cosine + sine).astype(jnp.bfloat16)

    @pl.loop(0, early // lanes)
    def _(step):
        make_table(vertex_ref, early_ref, first + step * lanes, step * lanes)

    matrix_copy.wait()
    chunk = 4 * lanes
    for start in range(0, vertices_local, chunk):
        left_product = jnp.dot(
            left_ref[...], matrix_ref[:, start : start + chunk], preferred_element_type=jnp.float32
        )
        high = left_product.astype(jnp.bfloat16)
        weight_ref[:window_rows, start : start + chunk] = high
        weight_ref[window_rows:, start : start + chunk] = (
            left_product - high.astype(jnp.float32)
        ).astype(jnp.bfloat16)
    green, start = 0.0, 0
    for table_ref in (early_ref, late_ref):
        size = table_ref.shape[1]
        if table_ref is not early_ref:
            for tile in range(0, size, lanes):
                make_table(vertex_ref, table_ref, first + start + tile, tile)
        green += lax.dot_general(
            table_ref[...],
            weight_ref[:, start : start + size],
            (((1,), (1,)), ((), ())),
            preferred_element_type=jnp.float32,
        )
        start += size
    green = green.T
    green = green[:window_rows] + green[window_rows:]
    rows_each = blk_count * rows_own
    coded = encode(green)
    for place, sent_ref in enumerate(sent_refs):
        sent_ref[...] = coded[place * rows_each : (place + 1) * rows_each]


def combine_kernel(sizes, *refs):
    blk_count, walk_count, sub_count, rows_own = sizes
    blk_index = lax.axis_index("blk")
    parts = walk_count * sub_count
    part_refs, whole_refs, row_ref = refs[:parts], refs[parts:-1], refs[-1]
    half = part_refs[0].shape[1] - lanes

    exponents = [part_ref[:, half:] for part_ref in part_refs]
    exponent = functools.reduce(jnp.maximum, exponents) + (parts - 1).bit_length()
    high, low = 0.5, 0.5
    for part_ref, part_exponent in zip(part_refs, exponents):
        scale = jnp.exp2((part_exponent - exponent).astype(jnp.float32))[:, :1]
        words = part_ref[:, :half]
        high += (words >> 16).astype(jnp.float32) * scale
        low += ((words << 16) >> 16).astype(jnp.float32) * scale
    high, low = jnp.floor(high).astype(jnp.int32), jnp.floor(low).astype(jnp.int32)
    coded = jnp.concatenate([(high << 16) | (low & 0xFFFF), exponent], axis=1)
    if len(whole_refs) == 1:
        whole_refs[0][...] = coded
        return
    for row in range(blk_count * rows_own):
        row_ref[row] = coded[row : row + 1]
    for place, whole_ref in enumerate(whole_refs):
        for step in range(RSTEPS):
            blk_part = toward(blk_index, place, blk_count) + RSTEPS * blk_count - step
            _, blk_part = split_by(blk_part, blk_count)
            for inner in range(rows_own):
                row = step * rows_own + inner
                whole_ref[row : row + 1] = row_ref[blk_part * rows_own + inner]


def accumulate_kernel(sizes, distances, last, weights_ref, transfer_ref, old_ref, *rest):
    if last:
        *arrived_refs, out_ref, source_ref, left_ref, unit_ref, new_ref, out_sems = rest
    else:
        *arrived_refs, new_ref, source_ref, left_ref, unit_ref = rest
    blk_count, _, _, rows_own = sizes
    blk_index = lax.axis_index("blk")
    transfers, columns = transfer_ref.shape
    half = columns // 2
    groups = transfers // sublanes
    tiles = columns // lanes
    weights = weights_ref[...] * (1.0 / blk_count)
    walker_ids = lax.broadcasted_iota(jnp.int32, weights.shape, 1)

    ids = lax.broadcasted_iota(jnp.int32, (transfers, 1), 0)
    step, _ = split_by(ids, TQ)
    if arrived_refs[0].shape[0] == blk_count * rows_own:
        _, step = split_by(blk_index + RSTEPS * blk_count - step, blk_count)

    def out_copy(own, part):
        here = slice(part * half, (part + 1) * half)
        return pltpu.make_async_copy(
            new_ref.at[own, :, here], out_ref.at[own, :, here], out_sems.at[own, part]
        )

    def spread(rows, own):
        wide = (transfers, rows.shape[1])
        picked = jnp.broadcast_to(rows[own : own + 1], wide)
        for place in range(1, rows.shape[0] // rows_own):
            row = place * rows_own + own
            picked = jnp.where(step == place, jnp.broadcast_to(rows[row : row + 1], wide), picked)
        return picked

    for own in range(rows_own):
        for place, distance in enumerate(distances):
            coded = arrived_refs[place][...]
            walker = back(blk_index, distance, blk_count)
            weight = jnp.sum(jnp.where(walker_ids == walker, weights, 0.0), axis=1, keepdims=True)
            left = coded[own : own + 1]
            for blk_part in range(1, coded.shape[0] // rows_own):
                row = blk_part * rows_own + own
                left = jnp.where(step[:1] == blk_part, coded[row : row + 1], left)
            left_ref[place] = decode(left) * weight
            unit_ref[place] = spread(units(coded), own)
            source_ref[place] = spread(coded[:, :half], own)

        together = len(distances) if len(distances) <= 4 else math.gcd(len(distances), 4)

        for tile in range(tiles):
            here = slice(tile * lanes, (tile + 1) * lanes)
            for group in range(groups):
                rows = slice(group * sublanes, (group + 1) * sublanes)
                index = transfer_ref[rows, here]
                index_lane = index & (lanes - 1)
                in_first = index < half
                index_tile = jnp.where(in_first, index, index - half) >> lane_bits

                def add_walkers(first, total):
                    picked = [jnp.zeros((sublanes, lanes), jnp.int32)] * together
                    for source in range(half // lanes):
                        match = index_tile == source
                        for k in range(together):
                            words = source_ref[
                                first + k, rows, source * lanes : (source + 1) * lanes
                            ]
                            words = jnp.take_along_axis(
                                words, index_lane, axis=1, mode="promise_in_bounds"
                            )
                            picked[k] = jnp.where(match, words, picked[k])
                    for k in range(together):
                        code = jnp.where(in_first, picked[k], picked[k] << 16) >> 16
                        total = total + left_ref[first + k, :, here] * (
                            unit_ref[first + k, rows] * code.astype(jnp.float32)
                        )
                    return total

                total = old_ref[own, rows, here]
                if len(distances) == together:
                    total = add_walkers(0, total)
                else:
                    total = lax.fori_loop(
                        0, len(distances) // together, lambda i, t: add_walkers(i * together, t), total
                    )
                new_ref[own, rows, here] = total

            if last and (tile + 1) % (tiles // 2) == 0:
                out_copy(own, (tile + 1) // (tiles // 2) - 1).start()
    if last:
        for own in range(rows_own):
            for part in range(2):
                out_copy(own, part).wait()


def exchange(pieces, axes, counts):
    positions = list(itertools.product(*map(range, counts)))
    place = {position: i for i, position in enumerate(positions)}
    arrived = [pieces[0]] * len(positions)
    for i in range(1, len(positions)):
        route = [
            (place[position], place[tuple(map(toward, position, positions[i], counts))])
            for position in positions
        ]
        arrived[i] = lax.ppermute(pieces[i], axes, route)
    return arrived


def local(walker_mats, vertex, weights, transfer_table, g4_old):
    blk_count = lax.axis_size("blk")
    walk_count = lax.axis_size("walk")
    sub_count = lax.axis_size("sub")
    rows_local, vertices = walker_mats.shape[1:]
    rows_own, transfers, columns = g4_old.shape
    devices = blk_count * walk_count * sub_count
    sizes = (blk_count, walk_count, sub_count, rows_own)
    vmem = pl.BlockSpec(memory_space=pltpu.VMEM)
    vertices_local = vertices // sub_count
    early = 3 * vertices_local // (8 * lanes) * 2 * lanes
    coded = columns // 2 + lanes
    sent = pl.pallas_call(
        functools.partial(transform_kernel, sizes),
        out_shape=[jax.ShapeDtypeStruct((blk_count * rows_own, coded), jnp.int32)]
        * (walk_count * sub_count),
        in_specs=[pl.BlockSpec(memory_space=pl.ANY)] * 2,
        out_specs=[vmem] * (walk_count * sub_count),
        scratch_shapes=[
            pltpu.VMEM((rows_local, vertices_local), jnp.bfloat16),
            pltpu.VMEM((1, vertices), jnp.int32),
            pltpu.VMEM((devices * rows_own, rows_local), jnp.bfloat16),
            pltpu.VMEM((columns, early), jnp.bfloat16),
            pltpu.VMEM((columns, vertices_local - early), jnp.bfloat16),
            pltpu.VMEM((2 * devices * rows_own, vertices_local), jnp.bfloat16),
            pltpu.SemaphoreType.DMA,
            pltpu.SemaphoreType.DMA,
        ],
        compiler_params=pltpu.CompilerParams(vmem_limit_bytes=24 * 2**20),
        name="transform",
    )(*[pltpu.with_memory_space_constraint(x, pltpu.HBM) for x in (walker_mats, vertex)])
    parts = exchange(sent, ("walk", "sub"), (walk_count, sub_count))
    shared = blk_count <= RSTEPS
    rows_each = (blk_count if shared else RSTEPS) * rows_own
    whole_count = 1 if shared else blk_count
    whole = pl.pallas_call(
        functools.partial(combine_kernel, sizes),
        out_shape=[jax.ShapeDtypeStruct((rows_each, coded), jnp.int32)] * whole_count,
        in_specs=[vmem] * len(parts),
        out_specs=[vmem] * whole_count,
        scratch_shapes=[pltpu.VMEM((blk_count * rows_own, 1, coded), jnp.int32)],
        compiler_params=pltpu.CompilerParams(vmem_limit_bytes=24 * 2**20),
        name="combine",
    )(*parts)
    arrived = exchange(whole * blk_count if shared else whole, ("blk",), (blk_count,))
    far = blk_count // 2
    totals = g4_old
    groups = [0, *range(far + 1, blk_count)], [*range(1, far)], [far]
    for places in groups:
        last = places is groups[-1]
        scratch_shapes = [
            pltpu.VMEM((len(places), transfers, columns // 2), jnp.int32),
            pltpu.VMEM((len(places), 1, columns), jnp.float32),
            pltpu.VMEM((len(places), transfers, lanes), jnp.float32),
        ]
        if last:
            scratch_shapes.append(pltpu.VMEM(g4_old.shape, jnp.float32))
            scratch_shapes.append(pltpu.SemaphoreType.DMA((rows_own, 2)))
        totals = pl.pallas_call(
            functools.partial(accumulate_kernel, sizes, places, last),
            out_shape=jax.ShapeDtypeStruct(g4_old.shape, jnp.float32),
            in_specs=[vmem] * (3 + len(places)),
            out_specs=pl.BlockSpec(memory_space=pl.ANY) if last else vmem,
            scratch_shapes=scratch_shapes,
            compiler_params=pltpu.CompilerParams(vmem_limit_bytes=24 * 2**20),
            cost_estimate=pl.CostEstimate(
                flops=1000 * len(places) * transfers * columns,
                bytes_accessed=12 * transfers * columns,
                transcendentals=0,
            ),
            name="accumulate",
        )(weights[None], transfer_table, totals, *[arrived[place] for place in places])
    return totals


def solution(mesh):
    in_specs = (
        P(("grp", "blk"), "walk", None),
        P(("grp", "blk"), None),
        P("grp"),
        P(),
        P(("grp", "blk", "walk", "sub"), None, None),
    )
    out_specs = P(("grp", "blk", "walk", "sub"), None, None)
    return jax.shard_map(local, mesh=mesh, in_specs=in_specs, out_specs=out_specs, check_vma=False)
```

```python
import functools
import itertools
import math

import jax
import jax.numpy as jnp
from jax import lax
from jax.experimental import pallas as pl
from jax.experimental.pallas import tpu as pltpu
from jax.sharding import PartitionSpec as P

TQ = 4
RSTEPS = 4


phase_period = 8192
quarter_bits = 11
lanes = 128
lane_bits = 7
sublanes = 8
code_limit = 32767.0
smallest_peak = 1e-30
exponent_margin = 1e-3


def toward(index, distance, count):
    if count & (count - 1) == 0:
        return index ^ distance
    return (index + distance) % count


def back(index, distance, count):
    if count & (count - 1) == 0:
        return index ^ distance
    return (index + count - distance) % count


def cos_sin(product):
    residue = product & (phase_period - 1)
    quarter = (residue + phase_period // 8) >> quarter_bits
    angle = (residue - (quarter << quarter_bits)).astype(jnp.float32) * (2.0 * math.pi / phase_period)
    square = angle * angle
    sine = angle + angle * square * (
        -1.0 / 6.0 + square * (1.0 / 120.0 + square * (-1.0 / 5040.0 + square * (1.0 / 362880.0)))
    )
    cosine = 1.0 + square * (
        -0.5 + square * (1.0 / 24.0 + square * (-1.0 / 720.0 + square * (1.0 / 40320.0)))
    )
    odd = (quarter & 1) == 1
    cosine_out = jnp.where(odd, sine, cosine)
    sine_out = jnp.where(odd, cosine, sine)
    cosine_out = jnp.where(((quarter + 1) & 2) == 2, -cosine_out, cosine_out)
    sine_out = jnp.where((quarter & 2) == 2, -sine_out, sine_out)
    return cosine_out, sine_out


def row_ids(count):
    return lax.broadcasted_iota(jnp.int32, (count, lanes), 0)


def split_by(ids, size):
    if size & (size - 1) == 0:
        return ids >> (size.bit_length() - 1), ids & (size - 1)
    return ids // size, ids % size


def tile_of(start):
    return pl.ds(start if isinstance(start, int) else pl.multiple_of(start, lanes), lanes)


def make_table(vertex_ref, table_ref, first, place):
    columns = table_ref.shape[0]
    blocks = columns // lanes
    half_blocks = blocks // 2
    coarse_rows = -(-max(half_blocks, 1) // sublanes) * sublanes
    middle_count = lanes // sublanes
    center = (blocks - 1) * (lanes // 2)
    here = tile_of(place)
    vertex = vertex_ref[:, tile_of(first)]
    cosine, sine = cos_sin(vertex * (row_ids(sublanes) + center))
    cas_fine, cam_fine = cosine + sine, cosine - sine
    cos_middle, sin_middle = cos_sin(vertex * (row_ids(middle_count) * sublanes))
    cos_coarse, sin_coarse = cos_sin(
        vertex * ((blocks - 1 - 2 * row_ids(coarse_rows)) * (lanes // 2))
    )
    for pair in range(middle_count // 2):
        cas, cam = [], []
        for middle in (2 * pair, 2 * pair + 1):
            c, s = cos_middle[middle : middle + 1], sin_middle[middle : middle + 1]
            cas.append(c * cas_fine + s * cam_fine)
            cam.append(c * cam_fine - s * cas_fine)
        cas, cam = jnp.concatenate(cas, axis=0), jnp.concatenate(cam, axis=0)
        start = pair * 2 * sublanes
        for low in range(half_blocks):
            high = blocks - 1 - low
            even = cos_coarse[low : low + 1] * cas
            odd = sin_coarse[low : low + 1] * cam
            for block, value in ((low, even - odd), (high, even + odd)):
                row = block * lanes + start
                table_ref[row : row + 2 * sublanes, here] = value.astype(jnp.bfloat16)
        if blocks % 2:
            row = half_blocks * lanes + start
            table_ref[row : row + 2 * sublanes, here] = cas.astype(jnp.bfloat16)


def encode(rows):
    half = rows.shape[1] // 2
    peak = jnp.maximum(jnp.max(jnp.abs(rows), axis=1, keepdims=True), smallest_peak)
    exponent = jnp.ceil(jnp.log2(peak * (1.0 / code_limit)) + exponent_margin)
    codes = jnp.floor(rows * (1.0 / jnp.exp2(exponent)) + 0.5).astype(jnp.int32)
    words = (codes[:, :half] << 16) | (codes[:, half:] & 0xFFFF)
    tail = jnp.broadcast_to(exponent.astype(jnp.int32), (rows.shape[0], lanes))
    return jnp.concatenate([words, tail], axis=1)


def units(coded):
    return jnp.exp2(coded[:, coded.shape[1] - lanes :].astype(jnp.float32))


def decode(coded):
    words = coded[:, : coded.shape[1] - lanes]
    codes = jnp.concatenate([words >> 16, (words << 16) >> 16], axis=1)
    return codes.astype(jnp.float32) * units(coded)[:, :1]


def transform_kernel(sizes, matrix_hbm, vertex_hbm, *rest):
    *sent_refs, matrix_ref, vertex_ref, left_ref, early_ref, late_ref, weight_ref, matrix_sem, vertex_sem = rest
    blk_count, walk_count, sub_count, rows_own = sizes
    walk_index = lax.axis_index("walk")
    sub_index = lax.axis_index("sub")
    rows_local, vertices_local = matrix_ref.shape
    window_rows = left_ref.shape[0]
    early = early_ref.shape[1]

    vertex_copy = pltpu.make_async_copy(vertex_hbm, vertex_ref, vertex_sem)
    vertex_copy.start()
    first = pl.multiple_of(sub_index * vertices_local, lanes)
    matrix_copy = pltpu.make_async_copy(
        matrix_hbm.at[0, :, pl.ds(first, vertices_local)], matrix_ref, matrix_sem
    )
    matrix_copy.start()

    ids, inner = split_by(row_ids(window_rows), rows_own)
    ids, blk_part = split_by(ids, blk_count)
    walk_part, sub_part = split_by(ids, sub_count)
    sub_part = toward(sub_index, sub_part, sub_count)
    walk_part = toward(walk_index, walk_part, walk_count)
    window = ((blk_part * walk_count + walk_part) * sub_count + sub_part) * rows_own + inner

    vertex_copy.wait()
    own_start = pl.multiple_of(walk_index * rows_local, lanes)
    for start in range(0, rows_local, lanes):
        own_vertex = vertex_ref[:, pl.ds(own_start + start, lanes)]
        cosine, sine = cos_sin(own_vertex * window)
        left_ref[:, start : start + lanes] = (cosine + sine).astype(jnp.bfloat16)

    @pl.loop(0, early // lanes)
    def _(step):
        make_table(vertex_ref, early_ref, first + step * lanes, step * lanes)

    matrix_copy.wait()
    chunk = 4 * lanes
    for start in range(0, vertices_local, chunk):
        left_product = jnp.dot(
            left_ref[...], matrix_ref[:, start : start + chunk], preferred_element_type=jnp.float32
        )
        high = left_product.astype(jnp.bfloat16)
        weight_ref[:window_rows, start : start + chunk] = high
        weight_ref[window_rows:, start : start + chunk] = (
            left_product - high.astype(jnp.float32)
        ).astype(jnp.bfloat16)
    green, start = 0.0, 0
    for table_ref in (early_ref, late_ref):
        size = table_ref.shape[1]
        if table_ref is not early_ref:
            for tile in range(0, size, lanes):
                make_table(vertex_ref, table_ref, first + start + tile, tile)
        green += lax.dot_general(
            table_ref[...],
            weight_ref[:, start : start + size],
            (((1,), (1,)), ((), ())),
            preferred_element_type=jnp.float32,
        )
        start += size
    green = green.T
    green = green[:window_rows] + green[window_rows:]
    rows_each = blk_count * rows_own
    coded = encode(green)
    for place, sent_ref in enumerate(sent_refs):
        sent_ref[...] = coded[place * rows_each : (place + 1) * rows_each]


def combine_kernel(sizes, *refs):
    blk_count, walk_count, sub_count, rows_own = sizes
    blk_index = lax.axis_index("blk")
    parts = walk_count * sub_count
    part_refs, whole_refs, row_ref = refs[:parts], refs[parts:-1], refs[-1]
    half = part_refs[0].shape[1] - lanes

    exponents = [part_ref[:, half:] for part_ref in part_refs]
    exponent = functools.reduce(jnp.maximum, exponents) + (parts - 1).bit_length()
    high, low = 0.5, 0.5
    for part_ref, part_exponent in zip(part_refs, exponents):
        scale = jnp.exp2((part_exponent - exponent).astype(jnp.float32))[:, :1]
        words = part_ref[:, :half]
        high += (words >> 16).astype(jnp.float32) * scale
        low += ((words << 16) >> 16).astype(jnp.float32) * scale
    high, low = jnp.floor(high).astype(jnp.int32), jnp.floor(low).astype(jnp.int32)
    coded = jnp.concatenate([(high << 16) | (low & 0xFFFF), exponent], axis=1)
    if len(whole_refs) == 1:
        whole_refs[0][...] = coded
        return
    for row in range(blk_count * rows_own):
        row_ref[row] = coded[row : row + 1]
    for place, whole_ref in enumerate(whole_refs):
        for step in range(RSTEPS):
            blk_part = toward(blk_index, place, blk_count) + RSTEPS * blk_count - step
            _, blk_part = split_by(blk_part, blk_count)
            for inner in range(rows_own):
                row = step * rows_own + inner
                whole_ref[row : row + 1] = row_ref[blk_part * rows_own + inner]


def accumulate_kernel(sizes, distances, last, weights_ref, transfer_ref, old_ref, *rest):
    if last:
        *arrived_refs, out_ref, source_ref, left_ref, unit_ref, new_ref, out_sems = rest
    else:
        *arrived_refs, new_ref, source_ref, left_ref, unit_ref = rest
    blk_count, _, _, rows_own = sizes
    blk_index = lax.axis_index("blk")
    transfers, columns = transfer_ref.shape
    half = columns // 2
    groups = transfers // sublanes
    tiles = columns // lanes
    weights = weights_ref[...] * (1.0 / blk_count)
    walker_ids = lax.broadcasted_iota(jnp.int32, weights.shape, 1)

    ids = lax.broadcasted_iota(jnp.int32, (transfers, 1), 0)
    step, _ = split_by(ids, TQ)
    if arrived_refs[0].shape[0] == blk_count * rows_own:
        _, step = split_by(blk_index + RSTEPS * blk_count - step, blk_count)

    def out_copy(own, part):
        here = slice(part * half, (part + 1) * half)
        return pltpu.make_async_copy(
            new_ref.at[own, :, here], out_ref.at[own, :, here], out_sems.at[own, part]
        )

    def spread(rows, own):
        wide = (transfers, rows.shape[1])
        picked = jnp.broadcast_to(rows[own : own + 1], wide)
        for place in range(1, rows.shape[0] // rows_own):
            row = place * rows_own + own
            picked = jnp.where(step == place, jnp.broadcast_to(rows[row : row + 1], wide), picked)
        return picked

    for own in range(rows_own):
        for place, distance in enumerate(distances):
            coded = arrived_refs[place][...]
            walker = back(blk_index, distance, blk_count)
            weight = jnp.sum(jnp.where(walker_ids == walker, weights, 0.0), axis=1, keepdims=True)
            left = coded[own : own + 1]
            for blk_part in range(1, coded.shape[0] // rows_own):
                row = blk_part * rows_own + own
                left = jnp.where(step[:1] == blk_part, coded[row : row + 1], left)
            left_ref[place] = decode(left) * weight
            unit_ref[place] = spread(units(coded), own)
            source_ref[place] = spread(coded[:, :half], own)

        together = len(distances) if len(distances) <= 4 else math.gcd(len(distances), 4)

        for tile in range(tiles):
            here = slice(tile * lanes, (tile + 1) * lanes)
            for group in range(groups):
                rows = slice(group * sublanes, (group + 1) * sublanes)
                index = transfer_ref[rows, here]
                index_lane = index & (lanes - 1)
                in_first = index < half
                index_tile = jnp.where(in_first, index, index - half) >> lane_bits

                def add_walkers(first, total):
                    picked = [jnp.zeros((sublanes, lanes), jnp.int32)] * together
                    for source in range(half // lanes):
                        match = index_tile == source
                        for k in range(together):
                            words = source_ref[
                                first + k, rows, source * lanes : (source + 1) * lanes
                            ]
                            words = jnp.take_along_axis(
                                words, index_lane, axis=1, mode="promise_in_bounds"
                            )
                            picked[k] = jnp.where(match, words, picked[k])
                    for k in range(together):
                        code = jnp.where(in_first, picked[k], picked[k] << 16) >> 16
                        total = total + left_ref[first + k, :, here] * (
                            unit_ref[first + k, rows] * code.astype(jnp.float32)
                        )
                    return total

                total = old_ref[own, rows, here]
                if len(distances) == together:
                    total = add_walkers(0, total)
                else:
                    total = lax.fori_loop(
                        0, len(distances) // together, lambda i, t: add_walkers(i * together, t), total
                    )
                new_ref[own, rows, here] = total

            if last and (tile + 1) % (tiles // 2) == 0:
                out_copy(own, (tile + 1) // (tiles // 2) - 1).start()
    if last:
        for own in range(rows_own):
            for part in range(2):
                out_copy(own, part).wait()


def exchange(pieces, axes, counts):
    positions = list(itertools.product(*map(range, counts)))
    place = {position: i for i, position in enumerate(positions)}
    arrived = [pieces[0]] * len(positions)
    for i in range(1, len(positions)):
        route = [
            (place[position], place[tuple(map(toward, position, positions[i], counts))])
            for position in positions
        ]
        arrived[i] = lax.ppermute(pieces[i], axes, route)
    return arrived


def local(walker_mats, vertex, weights, transfer_table, g4_old):
    blk_count = lax.axis_size("blk")
    walk_count = lax.axis_size("walk")
    sub_count = lax.axis_size("sub")
    rows_local, vertices = walker_mats.shape[1:]
    rows_own, transfers, columns = g4_old.shape
    devices = blk_count * walk_count * sub_count
    sizes = (blk_count, walk_count, sub_count, rows_own)
    vmem = pl.BlockSpec(memory_space=pltpu.VMEM)
    vertices_local = vertices // sub_count
    early = vertices_local // (4 * lanes) * 2 * lanes
    coded = columns // 2 + lanes
    sent = pl.pallas_call(
        functools.partial(transform_kernel, sizes),
        out_shape=[jax.ShapeDtypeStruct((blk_count * rows_own, coded), jnp.int32)]
        * (walk_count * sub_count),
        in_specs=[pl.BlockSpec(memory_space=pl.ANY)] * 2,
        out_specs=[vmem] * (walk_count * sub_count),
        scratch_shapes=[
            pltpu.VMEM((rows_local, vertices_local), jnp.bfloat16),
            pltpu.VMEM((1, vertices), jnp.int32),
            pltpu.VMEM((devices * rows_own, rows_local), jnp.bfloat16),
            pltpu.VMEM((columns, early), jnp.bfloat16),
            pltpu.VMEM((columns, vertices_local - early), jnp.bfloat16),
            pltpu.VMEM((2 * devices * rows_own, vertices_local), jnp.bfloat16),
            pltpu.SemaphoreType.DMA,
            pltpu.SemaphoreType.DMA,
        ],
        compiler_params=pltpu.CompilerParams(vmem_limit_bytes=24 * 2**20),
        name="transform",
    )(*[pltpu.with_memory_space_constraint(x, pltpu.HBM) for x in (walker_mats, vertex)])
    parts = exchange(sent, ("walk", "sub"), (walk_count, sub_count))
    shared = blk_count <= RSTEPS
    rows_each = (blk_count if shared else RSTEPS) * rows_own
    whole_count = 1 if shared else blk_count
    whole = pl.pallas_call(
        functools.partial(combine_kernel, sizes),
        out_shape=[jax.ShapeDtypeStruct((rows_each, coded), jnp.int32)] * whole_count,
        in_specs=[vmem] * len(parts),
        out_specs=[vmem] * whole_count,
        scratch_shapes=[pltpu.VMEM((blk_count * rows_own, 1, coded), jnp.int32)],
        compiler_params=pltpu.CompilerParams(vmem_limit_bytes=24 * 2**20),
        name="combine",
    )(*parts)
    arrived = exchange(whole * blk_count if shared else whole, ("blk",), (blk_count,))
    far = blk_count // 2
    totals = g4_old
    groups = [0, *range(far + 1, blk_count)], [*range(1, far)], [far]
    for places in groups:
        last = places is groups[-1]
        scratch_shapes = [
            pltpu.VMEM((len(places), transfers, columns // 2), jnp.int32),
            pltpu.VMEM((len(places), 1, columns), jnp.float32),
            pltpu.VMEM((len(places), transfers, lanes), jnp.float32),
        ]
        if last:
            scratch_shapes.append(pltpu.VMEM(g4_old.shape, jnp.float32))
            scratch_shapes.append(pltpu.SemaphoreType.DMA((rows_own, 2)))
        totals = pl.pallas_call(
            functools.partial(accumulate_kernel, sizes, places, last),
            out_shape=jax.ShapeDtypeStruct(g4_old.shape, jnp.float32),
            in_specs=[vmem] * (3 + len(places)),
            out_specs=pl.BlockSpec(memory_space=pl.ANY) if last else vmem,
            scratch_shapes=scratch_shapes,
            compiler_params=pltpu.CompilerParams(vmem_limit_bytes=24 * 2**20),
            cost_estimate=pl.CostEstimate(
                flops=1000 * len(places) * transfers * columns,
                bytes_accessed=12 * transfers * columns,
                transcendentals=0,
            ),
            name="accumulate",
        )(weights[None], transfer_table, totals, *[arrived[place] for place in places])
    return totals


def solution(mesh):
    in_specs = (
        P(("grp", "blk"), "walk", None),
        P(("grp", "blk"), None),
        P("grp"),
        P(),
        P(("grp", "blk", "walk", "sub"), None, None),
    )
    out_specs = P(("grp", "blk", "walk", "sub"), None, None)
    return jax.shard_map(local, mesh=mesh, in_specs=in_specs, out_specs=out_specs, check_vma=False)
```

```python
import functools
import itertools
import math

import jax
import jax.numpy as jnp
from jax import lax
from jax.experimental import pallas as pl
from jax.experimental.pallas import tpu as pltpu
from jax.sharding import PartitionSpec as P

TQ = 4
RSTEPS = 4


phase_period = 8192
quarter_bits = 11
lanes = 128
lane_bits = 7
sublanes = 8
code_limit = 32767.0
smallest_peak = 1e-30
exponent_margin = 1e-3


def toward(index, distance, count):
    if count & (count - 1) == 0:
        return index ^ distance
    return (index + distance) % count


def back(index, distance, count):
    if count & (count - 1) == 0:
        return index ^ distance
    return (index + count - distance) % count


def cos_sin(product):
    residue = product & (phase_period - 1)
    quarter = (residue + phase_period // 8) >> quarter_bits
    angle = (residue - (quarter << quarter_bits)).astype(jnp.float32) * (2.0 * math.pi / phase_period)
    square = angle * angle
    sine = angle + angle * square * (
        -1.0 / 6.0 + square * (1.0 / 120.0 + square * (-1.0 / 5040.0 + square * (1.0 / 362880.0)))
    )
    cosine = 1.0 + square * (
        -0.5 + square * (1.0 / 24.0 + square * (-1.0 / 720.0 + square * (1.0 / 40320.0)))
    )
    odd = (quarter & 1) == 1
    cosine_out = jnp.where(odd, sine, cosine)
    sine_out = jnp.where(odd, cosine, sine)
    cosine_out = jnp.where(((quarter + 1) & 2) == 2, -cosine_out, cosine_out)
    sine_out = jnp.where((quarter & 2) == 2, -sine_out, sine_out)
    return cosine_out, sine_out


def row_ids(count):
    return lax.broadcasted_iota(jnp.int32, (count, lanes), 0)


def split_by(ids, size):
    if size & (size - 1) == 0:
        return ids >> (size.bit_length() - 1), ids & (size - 1)
    return ids // size, ids % size


def tile_of(start):
    return pl.ds(start if isinstance(start, int) else pl.multiple_of(start, lanes), lanes)


def make_table(vertex_ref, table_ref, first, place):
    columns = table_ref.shape[0]
    blocks = columns // lanes
    half_blocks = blocks // 2
    coarse_rows = -(-max(half_blocks, 1) // sublanes) * sublanes
    middle_count = lanes // sublanes
    center = (blocks - 1) * (lanes // 2)
    here = tile_of(place)
    vertex = vertex_ref[:, tile_of(first)]
    cosine, sine = cos_sin(vertex * (row_ids(sublanes) + center))
    cas_fine, cam_fine = cosine + sine, cosine - sine
    cos_middle, sin_middle = cos_sin(vertex * (row_ids(middle_count) * sublanes))
    cos_coarse, sin_coarse = cos_sin(
        vertex * ((blocks - 1 - 2 * row_ids(coarse_rows)) * (lanes // 2))
    )
    for pair in range(middle_count // 2):
        cas, cam = [], []
        for middle in (2 * pair, 2 * pair + 1):
            c, s = cos_middle[middle : middle + 1], sin_middle[middle : middle + 1]
            cas.append(c * cas_fine + s * cam_fine)
            cam.append(c * cam_fine - s * cas_fine)
        cas, cam = jnp.concatenate(cas, axis=0), jnp.concatenate(cam, axis=0)
        start = pair * 2 * sublanes
        for low in range(half_blocks):
            high = blocks - 1 - low
            even = cos_coarse[low : low + 1] * cas
            odd = sin_coarse[low : low + 1] * cam
            for block, value in ((low, even - odd), (high, even + odd)):
                row = block * lanes + start
                table_ref[row : row + 2 * sublanes, here] = value.astype(jnp.bfloat16)
        if blocks % 2:
            row = half_blocks * lanes + start
            table_ref[row : row + 2 * sublanes, here] = cas.astype(jnp.bfloat16)


def encode(rows):
    half = rows.shape[1] // 2
    peak = jnp.maximum(jnp.max(jnp.abs(rows), axis=1, keepdims=True), smallest_peak)
    exponent = jnp.ceil(jnp.log2(peak * (1.0 / code_limit)) + exponent_margin)
    codes = jnp.floor(rows * (1.0 / jnp.exp2(exponent)) + 0.5).astype(jnp.int32)
    words = (codes[:, :half] << 16) | (codes[:, half:] & 0xFFFF)
    tail = jnp.broadcast_to(exponent.astype(jnp.int32), (rows.shape[0], lanes))
    return jnp.concatenate([words, tail], axis=1)


def units(coded):
    return jnp.exp2(coded[:, coded.shape[1] - lanes :].astype(jnp.float32))


def decode(coded):
    words = coded[:, : coded.shape[1] - lanes]
    codes = jnp.concatenate([words >> 16, (words << 16) >> 16], axis=1)
    return codes.astype(jnp.float32) * units(coded)[:, :1]


def transform_kernel(sizes, matrix_hbm, vertex_hbm, *rest):
    *sent_refs, matrix_ref, vertex_ref, left_ref, early_ref, late_ref, weight_ref, matrix_sem, vertex_sem = rest
    blk_count, walk_count, sub_count, rows_own = sizes
    walk_index = lax.axis_index("walk")
    sub_index = lax.axis_index("sub")
    rows_local, vertices_local = matrix_ref.shape
    window_rows = left_ref.shape[0]
    early = early_ref.shape[1]

    vertex_copy = pltpu.make_async_copy(vertex_hbm, vertex_ref, vertex_sem)
    vertex_copy.start()
    first = pl.multiple_of(sub_index * vertices_local, lanes)
    matrix_copy = pltpu.make_async_copy(
        matrix_hbm.at[0, :, pl.ds(first, vertices_local)], matrix_ref, matrix_sem
    )
    matrix_copy.start()

    ids, inner = split_by(row_ids(window_rows), rows_own)
    ids, blk_part = split_by(ids, blk_count)
    walk_part, sub_part = split_by(ids, sub_count)
    sub_part = toward(sub_index, sub_part, sub_count)
    walk_part = toward(walk_index, walk_part, walk_count)
    window = ((blk_part * walk_count + walk_part) * sub_count + sub_part) * rows_own + inner

    vertex_copy.wait()
    own_start = pl.multiple_of(walk_index * rows_local, lanes)
    for start in range(0, rows_local, lanes):
        own_vertex = vertex_ref[:, pl.ds(own_start + start, lanes)]
        cosine, sine = cos_sin(own_vertex * window)
        left_ref[:, start : start + lanes] = (cosine + sine).astype(jnp.bfloat16)

    @pl.loop(0, early // lanes)
    def _(step):
        make_table(vertex_ref, early_ref, first + step * lanes, step * lanes)

    matrix_copy.wait()
    late = vertices_local - early
    tiles = list(range(0, late, lanes))
    green = 0.0
    for start, table_ref, beside in (
        (0, early_ref, tiles[: len(tiles) // 2]),
        (early, late_ref, tiles[len(tiles) // 2 :]),
    ):
        size = table_ref.shape[1]
        left_product = jnp.dot(
            left_ref[...], matrix_ref[:, start : start + size], preferred_element_type=jnp.float32
        )
        for tile in beside:
            make_table(vertex_ref, late_ref, first + early + tile, tile)
        high = left_product.astype(jnp.bfloat16)
        weight_ref[:window_rows, start : start + size] = high
        weight_ref[window_rows:, start : start + size] = (
            left_product - high.astype(jnp.float32)
        ).astype(jnp.bfloat16)
        green += lax.dot_general(
            table_ref[...],
            weight_ref[:, start : start + size],
            (((1,), (1,)), ((), ())),
            preferred_element_type=jnp.float32,
        )
    green = green.T
    green = green[:window_rows] + green[window_rows:]
    rows_each = blk_count * rows_own
    coded = encode(green)
    for place, sent_ref in enumerate(sent_refs):
        sent_ref[...] = coded[place * rows_each : (place + 1) * rows_each]


def combine_kernel(sizes, *refs):
    blk_count, walk_count, sub_count, rows_own = sizes
    blk_index = lax.axis_index("blk")
    parts = walk_count * sub_count
    part_refs, whole_refs, row_ref = refs[:parts], refs[parts:-1], refs[-1]
    half = part_refs[0].shape[1] - lanes

    exponents = [part_ref[:, half:] for part_ref in part_refs]
    exponent = functools.reduce(jnp.maximum, exponents) + (parts - 1).bit_length()
    high, low = 0.5, 0.5
    for part_ref, part_exponent in zip(part_refs, exponents):
        scale = jnp.exp2((part_exponent - exponent).astype(jnp.float32))[:, :1]
        words = part_ref[:, :half]
        high += (words >> 16).astype(jnp.float32) * scale
        low += ((words << 16) >> 16).astype(jnp.float32) * scale
    high, low = jnp.floor(high).astype(jnp.int32), jnp.floor(low).astype(jnp.int32)
    coded = jnp.concatenate([(high << 16) | (low & 0xFFFF), exponent], axis=1)
    if len(whole_refs) == 1:
        whole_refs[0][...] = coded
        return
    for row in range(blk_count * rows_own):
        row_ref[row] = coded[row : row + 1]
    for place, whole_ref in enumerate(whole_refs):
        for step in range(RSTEPS):
            blk_part = toward(blk_index, place, blk_count) + RSTEPS * blk_count - step
            _, blk_part = split_by(blk_part, blk_count)
            for inner in range(rows_own):
                row = step * rows_own + inner
                whole_ref[row : row + 1] = row_ref[blk_part * rows_own + inner]


def accumulate_kernel(sizes, distances, last, weights_ref, transfer_ref, old_ref, *rest):
    if last:
        *arrived_refs, out_ref, source_ref, left_ref, unit_ref, new_ref, out_sems = rest
    else:
        *arrived_refs, new_ref, source_ref, left_ref, unit_ref = rest
    blk_count, _, _, rows_own = sizes
    blk_index = lax.axis_index("blk")
    transfers, columns = transfer_ref.shape
    half = columns // 2
    groups = transfers // sublanes
    tiles = columns // lanes
    weights = weights_ref[...] * (1.0 / blk_count)
    walker_ids = lax.broadcasted_iota(jnp.int32, weights.shape, 1)

    ids = lax.broadcasted_iota(jnp.int32, (transfers, 1), 0)
    step, _ = split_by(ids, TQ)
    if arrived_refs[0].shape[0] == blk_count * rows_own:
        _, step = split_by(blk_index + RSTEPS * blk_count - step, blk_count)

    def out_copy(own, part):
        here = slice(part * half, (part + 1) * half)
        return pltpu.make_async_copy(
            new_ref.at[own, :, here], out_ref.at[own, :, here], out_sems.at[own, part]
        )

    def spread(rows, own):
        wide = (transfers, rows.shape[1])
        picked = jnp.broadcast_to(rows[own : own + 1], wide)
        for place in range(1, rows.shape[0] // rows_own):
            row = place * rows_own + own
            picked = jnp.where(step == place, jnp.broadcast_to(rows[row : row + 1], wide), picked)
        return picked

    for own in range(rows_own):
        for place, distance in enumerate(distances):
            coded = arrived_refs[place][...]
            walker = back(blk_index, distance, blk_count)
            weight = jnp.sum(jnp.where(walker_ids == walker, weights, 0.0), axis=1, keepdims=True)
            left = coded[own : own + 1]
            for blk_part in range(1, coded.shape[0] // rows_own):
                row = blk_part * rows_own + own
                left = jnp.where(step[:1] == blk_part, coded[row : row + 1], left)
            left_ref[place] = decode(left) * weight
            unit_ref[place] = spread(units(coded), own)
            source_ref[place] = spread(coded[:, :half], own)

        together = len(distances) if len(distances) <= 4 else math.gcd(len(distances), 4)

        for tile in range(tiles):
            here = slice(tile * lanes, (tile + 1) * lanes)
            for group in range(groups):
                rows = slice(group * sublanes, (group + 1) * sublanes)
                index = transfer_ref[rows, here]
                index_lane = index & (lanes - 1)
                in_first = index < half
                index_tile = jnp.where(in_first, index, index - half) >> lane_bits

                def add_walkers(first, total):
                    picked = [jnp.zeros((sublanes, lanes), jnp.int32)] * together
                    for source in range(half // lanes):
                        match = index_tile == source
                        for k in range(together):
                            words = source_ref[
                                first + k, rows, source * lanes : (source + 1) * lanes
                            ]
                            words = jnp.take_along_axis(
                                words, index_lane, axis=1, mode="promise_in_bounds"
                            )
                            picked[k] = jnp.where(match, words, picked[k])
                    for k in range(together):
                        code = jnp.where(in_first, picked[k], picked[k] << 16) >> 16
                        total = total + left_ref[first + k, :, here] * (
                            unit_ref[first + k, rows] * code.astype(jnp.float32)
                        )
                    return total

                total = old_ref[own, rows, here]
                if len(distances) == together:
                    total = add_walkers(0, total)
                else:
                    total = lax.fori_loop(
                        0, len(distances) // together, lambda i, t: add_walkers(i * together, t), total
                    )
                new_ref[own, rows, here] = total

            if last and (tile + 1) % (tiles // 2) == 0:
                out_copy(own, (tile + 1) // (tiles // 2) - 1).start()
    if last:
        for own in range(rows_own):
            for part in range(2):
                out_copy(own, part).wait()


def exchange(pieces, axes, counts):
    positions = list(itertools.product(*map(range, counts)))
    place = {position: i for i, position in enumerate(positions)}
    arrived = [pieces[0]] * len(positions)
    for i in range(1, len(positions)):
        route = [
            (place[position], place[tuple(map(toward, position, positions[i], counts))])
            for position in positions
        ]
        arrived[i] = lax.ppermute(pieces[i], axes, route)
    return arrived


def local(walker_mats, vertex, weights, transfer_table, g4_old):
    blk_count = lax.axis_size("blk")
    walk_count = lax.axis_size("walk")
    sub_count = lax.axis_size("sub")
    rows_local, vertices = walker_mats.shape[1:]
    rows_own, transfers, columns = g4_old.shape
    devices = blk_count * walk_count * sub_count
    sizes = (blk_count, walk_count, sub_count, rows_own)
    vmem = pl.BlockSpec(memory_space=pltpu.VMEM)
    vertices_local = vertices // sub_count
    early = vertices_local // (4 * lanes) * 2 * lanes
    coded = columns // 2 + lanes
    sent = pl.pallas_call(
        functools.partial(transform_kernel, sizes),
        out_shape=[jax.ShapeDtypeStruct((blk_count * rows_own, coded), jnp.int32)]
        * (walk_count * sub_count),
        in_specs=[pl.BlockSpec(memory_space=pl.ANY)] * 2,
        out_specs=[vmem] * (walk_count * sub_count),
        scratch_shapes=[
            pltpu.VMEM((rows_local, vertices_local), jnp.bfloat16),
            pltpu.VMEM((1, vertices), jnp.int32),
            pltpu.VMEM((devices * rows_own, rows_local), jnp.bfloat16),
            pltpu.VMEM((columns, early), jnp.bfloat16),
            pltpu.VMEM((columns, vertices_local - early), jnp.bfloat16),
            pltpu.VMEM((2 * devices * rows_own, vertices_local), jnp.bfloat16),
            pltpu.SemaphoreType.DMA,
            pltpu.SemaphoreType.DMA,
        ],
        compiler_params=pltpu.CompilerParams(vmem_limit_bytes=24 * 2**20),
        name="transform",
    )(*[pltpu.with_memory_space_constraint(x, pltpu.HBM) for x in (walker_mats, vertex)])
    parts = exchange(sent, ("walk", "sub"), (walk_count, sub_count))
    shared = blk_count <= RSTEPS
    rows_each = (blk_count if shared else RSTEPS) * rows_own
    whole_count = 1 if shared else blk_count
    whole = pl.pallas_call(
        functools.partial(combine_kernel, sizes),
        out_shape=[jax.ShapeDtypeStruct((rows_each, coded), jnp.int32)] * whole_count,
        in_specs=[vmem] * len(parts),
        out_specs=[vmem] * whole_count,
        scratch_shapes=[pltpu.VMEM((blk_count * rows_own, 1, coded), jnp.int32)],
        compiler_params=pltpu.CompilerParams(vmem_limit_bytes=24 * 2**20),
        name="combine",
    )(*parts)
    arrived = exchange(whole * blk_count if shared else whole, ("blk",), (blk_count,))
    far = blk_count // 2
    totals = g4_old
    groups = [0, *range(far + 1, blk_count)], [*range(1, far)], [far]
    for places in groups:
        last = places is groups[-1]
        scratch_shapes = [
            pltpu.VMEM((len(places), transfers, columns // 2), jnp.int32),
            pltpu.VMEM((len(places), 1, columns), jnp.float32),
            pltpu.VMEM((len(places), transfers, lanes), jnp.float32),
        ]
        if last:
            scratch_shapes.append(pltpu.VMEM(g4_old.shape, jnp.float32))
            scratch_shapes.append(pltpu.SemaphoreType.DMA((rows_own, 2)))
        totals = pl.pallas_call(
            functools.partial(accumulate_kernel, sizes, places, last),
            out_shape=jax.ShapeDtypeStruct(g4_old.shape, jnp.float32),
            in_specs=[vmem] * (3 + len(places)),
            out_specs=pl.BlockSpec(memory_space=pl.ANY) if last else vmem,
            scratch_shapes=scratch_shapes,
            compiler_params=pltpu.CompilerParams(vmem_limit_bytes=24 * 2**20),
            cost_estimate=pl.CostEstimate(
                flops=1000 * len(places) * transfers * columns,
                bytes_accessed=12 * transfers * columns,
                transcendentals=0,
            ),
            name="accumulate",
        )(weights[None], transfer_table, totals, *[arrived[place] for place in places])
    return totals


def solution(mesh):
    in_specs = (
        P(("grp", "blk"), "walk", None),
        P(("grp", "blk"), None),
        P("grp"),
        P(),
        P(("grp", "blk", "walk", "sub"), None, None),
    )
    out_specs = P(("grp", "blk", "walk", "sub"), None, None)
    return jax.shard_map(local, mesh=mesh, in_specs=in_specs, out_specs=out_specs, check_vma=False)
```
